32 devices in a mesh: section: 4 (over y, x), dp: 8 (over z, core).
Axes of the slice: x: 2, y: 2, z: 4, core: 2. Of those that a mesh axis runs over, the one named last changes fastest.
Arguments:
- acts: bfloat16 [4, 128, 196, 1024], P('section', 'dp'), may hold values from -8 to 8, as said below
- patches: bfloat16 [128, 196, 768], P('dp', None, 'section'), may hold values from -6 to 6
- labels: int32 [128], P('dp'), may hold values from 0 to 11263
- w_first: bfloat16 [4, 1024, 256], P('section'), may hold values from -0.1875 to 0.1875
- w_second: bfloat16 [4, 256, 1024], P('section'), may hold values from -0.375 to 0.375
- w_decode: bfloat16 [4, 1024, 768], P('section'), may hold values from -0.1875 to 0.1875
- w_aux: bfloat16 [4, 1024, 512], P('section'), may hold values from -0.1875 to 0.1875
- w_class: bfloat16 [4, 11264, 512], P('section', 'dp'), may hold values from -1.5 to 1.5
Outputs:
- grad_first: float32 [4, 1024, 256], P('section', 'dp')
- grad_second: float32 [4, 256, 1024], P('section', 'dp')
- grad_decode: float32 [4, 1024, 768], P('section', 'dp')
- grad_aux: float32 [4, 1024, 512], P('section', 'dp')
- grad_class: float32 [4, 11264, 512], P('section', 'dp')
The draws below stay inside these ranges and needn't reach their ends.
Inputs may be any that keep to these rules, and one draw needn't show every extreme that they name: `acts`: feature maps with a per-image, per-channel offset.
All inputs are finite; a program needn't handle non-finite values.
Results may differ from the reference program's by a relative error of at most 0.03.
The reference program's roundings to bfloat16 on the way count: a program that leaves them out, or rounds other values in their place, can miss the bound.
Values may be sent and summed in bfloat16 or wider, within the bound.
No kernel may reach another device: no remote copies, remote signals or barrier semaphores. Data moves between devices by JAX's collectives and lax.ppermute only.
A program may use at most 192 MiB of HBM per device.

```python
import jax
import jax.numpy as jnp
from jax import lax

C = 1024
BOT = 256
PIX = 196
PATCH = 768
HEAD = 512
CLASSES = 11264
MODULES = 4
IMAGES = 128
ROWS = 25088
N_DP = 8


def draw_acts(key, part):
    key_base = jax.random.fold_in(key, 11)
    key_offset = jax.random.fold_in(key, 12)
    shape = (MODULES, IMAGES, PIX, C)
    base = jax.random.normal(key_base, shape, jnp.float32)
    offset = jax.random.normal(key_offset, (MODULES, IMAGES, 1, C), jnp.float32)
    values = 0.7 * base + offset
    return jnp.clip(values, -8.0, 8.0).astype(jnp.bfloat16)


def draw_w_class(key, part):
    key_base = jax.random.fold_in(key, 21)
    shape = (MODULES, CLASSES, HEAD)
    values = 0.18 * jax.random.normal(key_base, shape, jnp.float32)
    return jnp.clip(values, -1.5, 1.5).astype(jnp.bfloat16)


def plant(values, key, least, high):
    spot = [jax.random.randint(jax.random.fold_in(key, axis), (), 0, length) for axis, length in enumerate(values.shape)]
    main_axis = values.shape.index(max(values.shape))
    neighbour = spot[:main_axis] + [(spot[main_axis] + 1) % values.shape[main_axis]] + spot[main_axis + 1:]
    return values.at[tuple(spot)].set(least).at[tuple(neighbour)].set(high)


def shard_levels(key, shape, split, low, top_value):
    level, own = 1.0, jax.random.fold_in(key, 6)
    for dim, blocks in split:
        draws = jnp.exp(jax.random.uniform(jax.random.fold_in(own, dim), (blocks,), jnp.float32, low / len(split), top_value / len(split)))
        level = level * jnp.repeat(draws, shape[dim] // blocks).reshape([-1 if axis == dim else 1 for axis in range(len(shape))])
    return level


def centred(stream_key, extent, scale, reach, shards=(), kind=jnp.bfloat16):
    factor_of = shard_levels(stream_key, extent, shards, -0.22, 0.18) if shards else 1.0
    values = jax.random.normal(stream_key, extent, jnp.float32) * scale * factor_of
    return jnp.minimum(jnp.maximum(values, -reach), reach).astype(kind)


def setup_inputs(seed: int = 0) -> dict:
    streams_of = jax.random.split(jax.random.key(seed), 9)
    acts = draw_acts(jax.random.fold_in(streams_of[8], 71), 0)
    patches = centred(streams_of[1], (IMAGES, PIX, PATCH), 1.0, 6.0, ((0, 8), (2, 4)))
    labels = plant(jax.random.randint(streams_of[2], (IMAGES,), 0, CLASSES), jax.random.fold_in(streams_of[2], 1), 0, CLASSES - 1).astype(jnp.int32)
    w_first = centred(streams_of[3], (MODULES, C, BOT), C ** -0.5, 0.1875, ((0, 4),))
    w_second = centred(streams_of[4], (MODULES, BOT, C), BOT ** -0.5, 0.375, ((0, 4),))
    w_decode = centred(streams_of[5], (MODULES, C, PATCH), C ** -0.5, 0.1875, ((0, 4),))
    w_aux = centred(streams_of[6], (MODULES, C, HEAD), C ** -0.5, 0.1875, ((0, 4),))
    w_class = draw_w_class(jax.random.fold_in(streams_of[8], 71), 0)
    return dict(acts=acts, patches=patches, labels=labels, w_first=w_first, w_second=w_second, w_decode=w_decode, w_aux=w_aux, w_class=w_class)


def block_sum(left, right):
    lb = left.reshape(N_DP, -1, left.shape[1]).astype(jnp.float32)
    rb = right.reshape(N_DP, -1, right.shape[1]).astype(jnp.float32)
    parts = jnp.einsum("kra,krb->kab", lb, rb)
    parts = lax.optimization_barrier(parts.astype(jnp.bfloat16))
    return jnp.sum(parts.astype(jnp.float32), axis=0)


def one_module(items):
    acts_m, patches, labels, first, second, decode, aux, klass = items
    flat = acts_m.reshape(ROWS, C)
    pre_act = jnp.dot(flat, first, preferred_element_type=jnp.float32)
    hidden = jax.nn.relu(pre_act).astype(jnp.bfloat16)
    feature = (flat.astype(jnp.float32) + jnp.dot(hidden, second, preferred_element_type=jnp.float32)).astype(jnp.bfloat16)
    recon = jnp.dot(feature, decode, preferred_element_type=jnp.float32)
    target = patches.reshape(ROWS, PATCH).astype(jnp.float32)
    recon_grad = ((recon - target) / (ROWS ** 0.5)).astype(jnp.bfloat16)
    pooled = jnp.mean(feature.reshape(IMAGES, PIX, C).astype(jnp.float32), axis=1).astype(jnp.bfloat16)
    aux_pre = jnp.dot(pooled, aux, preferred_element_type=jnp.float32)
    aux_out = jax.nn.relu(aux_pre).astype(jnp.bfloat16)
    logits = jnp.dot(aux_out, klass.T, preferred_element_type=jnp.float32)
    top = jnp.max(logits, axis=1, keepdims=True)
    expo = jnp.exp(logits - top)
    prob = expo / jnp.sum(expo, axis=1, keepdims=True)
    onehot = (labels[:, None] == jnp.arange(CLASSES, dtype=jnp.int32)[None, :]).astype(jnp.float32)
    logit_grad = ((prob - onehot) / (IMAGES ** 0.5)).astype(jnp.bfloat16)
    grad_class = jnp.dot(logit_grad.T, aux_out, preferred_element_type=jnp.float32)
    back = jnp.dot(logit_grad, klass, preferred_element_type=jnp.float32)
    aux_grad = jnp.where(aux_pre > 0, back, 0.0).astype(jnp.bfloat16)
    pooled_grad = jnp.dot(aux_grad, aux.T, preferred_element_type=jnp.float32)
    dec_back = jnp.dot(recon_grad, decode.T, preferred_element_type=jnp.float32)
    feature_grad = (dec_back.reshape(IMAGES, PIX, C) + pooled_grad[:, None, :] / PIX).reshape(ROWS, C).astype(jnp.bfloat16)
    hid_back = jnp.dot(feature_grad, second.T, preferred_element_type=jnp.float32)
    hidden_grad = jnp.where(pre_act > 0, hid_back, 0.0).astype(jnp.bfloat16)
    grad_first = block_sum(flat, hidden_grad)
    grad_second = block_sum(hidden, feature_grad)
    grad_decode = block_sum(feature, recon_grad)
    grad_aux = block_sum(pooled, aux_grad)
    return grad_first, grad_second, grad_decode, grad_aux, grad_class


def reference(acts, patches, labels, w_first, w_second, w_decode, w_aux, w_class):
    results = []
    for module in range(MODULES):
        results.append(one_module((acts[module], patches, labels, w_first[module], w_second[module], w_decode[module], w_aux[module], w_class[module])))
    return (jnp.stack([r[0] for r in results]), jnp.stack([r[1] for r in results]), jnp.stack([r[2] for r in results]), jnp.stack([r[3] for r in results]), jnp.stack([r[4] for r in results]))
```

```python
import jax
import jax.numpy as jnp
from jax import lax
from jax.sharding import PartitionSpec as P

F32 = jnp.float32
BF16 = jnp.bfloat16


def swap(value, axis, bits):
    count = lax.axis_size(axis)
    return lax.ppermute(value, axis, [(i, i ^ bits) for i in range(count)])


def gather_blocks(block, axis):
    count = lax.axis_size(axis)
    blocks = [block] + [None] * (count - 1)
    for k in range(1, count):
        if k & (k - 1) == 0:
            blocks[k] = swap(block, axis, k)
    half = block.shape[0] // 2
    for k in range(1, count):
        if blocks[k] is None:
            low, high = k & -k, 1 << (k.bit_length() - 1)
            first = swap(blocks[k ^ low][:half], axis, low)
            last = swap(blocks[k ^ high][half:], axis, high)
            blocks[k] = jnp.concatenate([first, last], axis=0)
    return blocks


def spread(block, axis):
    return [block] + [swap(block, axis, k) for k in range(1, lax.axis_size(axis))]


def reduce_rows(part):
    count = lax.axis_size("dp")
    me = lax.axis_index("dp")
    rows = part.shape[0] // count
    cut = part.reshape(count // 2, 2, rows, part.shape[1])
    core = lax.rem(me, 2)
    chip = lax.div(me, 2)
    other = swap(lax.dynamic_index_in_dim(cut, 1 - core, 1, keepdims=False), "dp", 1)
    mine = lax.dynamic_index_in_dim(cut, core, 1, keepdims=False)
    both = mine.astype(F32) + other.astype(F32)
    total = lax.dynamic_index_in_dim(both, chip, 0, keepdims=False)
    rounded = both.astype(BF16)
    for k in range(1, count // 2):
        piece = lax.dynamic_index_in_dim(rounded, chip ^ k, 0, keepdims=False)
        total = total + swap(piece, "dp", 2 * k).astype(F32)
    return total


def local(acts, patches, labels, w_first, w_second, w_decode, w_aux, w_class):
    local_acts = acts[0]
    images_here, pix, width = local_acts.shape
    rows_here = images_here * pix
    groups = lax.axis_size("dp")
    me = lax.axis_index("dp")
    section = lax.axis_index("section")
    total_rows = groups * rows_here
    total_images = groups * images_here
    first, second, decode, aux, klass = w_first[0], w_second[0], w_decode[0], w_aux[0], w_class[0]
    classes_here = klass.shape[0]

    target = gather_blocks(patches, "section")
    flat = local_acts.reshape(rows_here, width)
    pre_act = jnp.dot(flat, first, preferred_element_type=F32)
    hidden = jax.nn.relu(pre_act).astype(BF16)
    feature = (flat.astype(F32) + jnp.dot(hidden, second, preferred_element_type=F32)).astype(BF16)
    pooled = jnp.mean(feature.reshape(images_here, pix, width).astype(F32), axis=1).astype(BF16)
    aux_pre = jnp.dot(pooled, aux, preferred_element_type=F32)
    aux_out = jax.nn.relu(aux_pre).astype(BF16)

    sent = jnp.concatenate([aux_out, pooled], axis=1)
    blocks = jnp.stack(spread(sent, "dp"))
    head = aux_out.shape[1]
    all_out = blocks[:, :, :head].reshape(total_images, head)
    all_labels = jnp.stack(spread(labels, "dp")).reshape(total_images)
    logits = jnp.dot(all_out, klass.T, preferred_element_type=F32)
    top = jnp.max(logits, axis=1)
    denom = jnp.sum(jnp.exp(logits - top[:, None]), axis=1)
    stats = jnp.stack(spread(jnp.stack([top, denom]).reshape(2, groups, images_here), "dp"))
    order = jnp.array([[j ^ k for j in range(groups)] for k in range(groups)], jnp.int32)
    stats = jnp.stack([stats[k][:, order[k]] for k in range(groups)]).reshape(groups, 2, total_images)
    all_top = jnp.max(stats[:, 0], axis=0)
    all_denom = jnp.sum(stats[:, 1] * jnp.exp(stats[:, 0] - all_top[None]), axis=0)
    prob = jnp.exp(logits - all_top[:, None]) / all_denom[:, None]
    ids = me * classes_here + jnp.arange(classes_here, dtype=jnp.int32)
    onehot = (all_labels[:, None] == ids[None, :]).astype(F32)
    logit_grad = ((prob - onehot) / total_images**0.5).astype(BF16)
    grad_class = jnp.dot(logit_grad.T, all_out, preferred_element_type=F32)
    back_part = jnp.dot(logit_grad, klass, preferred_element_type=F32).reshape(groups, images_here, head)
    back = back_part[0]
    for k in range(1, groups):
        back = back + swap(back_part[k], "dp", k)
    aux_grad = jnp.where(aux_pre > 0, back, 0.0).astype(BF16)
    pooled_grad = jnp.dot(aux_grad, aux.T, preferred_element_type=F32)

    all_aux_grad = jnp.stack(spread(aux_grad, "dp"))
    rows_aux = width // groups
    all_pooled = lax.dynamic_slice_in_dim(blocks, head + me * rows_aux, rows_aux, 2)
    grad_aux = jnp.sum(
        lax.optimization_barrier(
            jnp.einsum("kia,kib->kab", all_pooled, all_aux_grad, preferred_element_type=F32).astype(BF16)
        ).astype(F32),
        axis=0,
    )

    span = patches.shape[2]
    dec_back = 0.0
    parts = []
    for k in range(len(target)):
        columns = lax.dynamic_slice_in_dim(decode, (section ^ k) * span, span, 1)
        recon = jnp.dot(feature, columns, preferred_element_type=F32)
        recon_grad = ((recon - target[k].reshape(rows_here, span).astype(F32)) / total_rows**0.5).astype(BF16)
        dec_back = dec_back + jnp.dot(recon_grad, columns.T, preferred_element_type=F32)
        parts.append(jnp.dot(feature.T, recon_grad, preferred_element_type=F32).astype(BF16))
    summed = reduce_rows(jnp.concatenate(parts, axis=1)).reshape(width // groups, len(target), span)
    grad_decode = jnp.concatenate(
        [lax.dynamic_index_in_dim(summed, section ^ k, 1, keepdims=False) for k in range(len(target))], axis=1
    )
    feature_grad = (
        (dec_back.reshape(images_here, pix, width) + pooled_grad[:, None, :] / pix)
        .reshape(rows_here, width)
        .astype(BF16)
    )
    hid_back = jnp.dot(feature_grad, second.T, preferred_element_type=F32)
    hidden_grad = jnp.where(pre_act > 0, hid_back, 0.0).astype(BF16)
    grad_first = reduce_rows(jnp.dot(flat.T, hidden_grad, preferred_element_type=F32).astype(BF16))
    grad_second = reduce_rows(jnp.dot(hidden.T, feature_grad, preferred_element_type=F32).astype(BF16))
    return grad_first[None], grad_second[None], grad_decode[None], grad_aux[None], grad_class[None]


def solution(mesh):
    in_specs = (
        P("section", "dp", None, None),
        P("dp", None, "section"),
        P("dp"),
        P("section", None, None),
        P("section", None, None),
        P("section", None, None),
        P("section", None, None),
        P("section", "dp", None),
    )
    out_specs = (P("section", "dp", None),) * 5
    return jax.shard_map(local, mesh=mesh, in_specs=in_specs, out_specs=out_specs, check_vma=False)
```

```python
import functools

import jax
import jax.numpy as jnp
from jax import lax
from jax.experimental import pallas as pl
from jax.experimental.pallas import tpu as pltpu
from jax.sharding import PartitionSpec as P

F32 = jnp.float32
BF16 = jnp.bfloat16
STEP = 4
LANES = 128
VMEM_LIMIT = 56 * 1024 * 1024
ROWS_0 = (((0,), (0,)), ((), ()))
COLS_1 = (((1,), (1,)), ((), ()))


def dot(left, right, dims=(((1,), (0,)), ((), ()))):
    return lax.dot_general(left, right, dims, preferred_element_type=F32)


def call(kernel, out_shape, *, flops=0, moved=0, **kwargs):
    return pl.pallas_call(
        kernel,
        out_shape=out_shape,
        compiler_params=pltpu.CompilerParams(vmem_limit_bytes=VMEM_LIMIT),
        cost_estimate=pl.CostEstimate(flops=int(flops), bytes_accessed=int(moved), transcendentals=0),
        **kwargs,
    )


def shape(dims, kind):
    return jax.ShapeDtypeStruct(dims, kind)


def swap(value, axis, bits):
    count = lax.axis_size(axis)
    return lax.ppermute(value, axis, [(i, i ^ bits) for i in range(count)])


def exchange(value, groups=None):
    return lax.all_to_all(value, "dp", 0, 0, axis_index_groups=groups, tiled=True)


def split_width(span):
    full = span // LANES * LANES
    return full, span - full


def pack_kernel(full, rem, patches_ref, *halves):
    for h, half in enumerate(halves):
        count = patches_ref.shape[0] // 2
        base = h * count
        if rem == 64 and full:
            half[:count] = patches_ref[base : base + count, :, :full]
            for j in range(count // 2):
                half[count + j] = jnp.concatenate(
                    [patches_ref[base + j, :, full:], patches_ref[base + count // 2 + j, :, full:]], axis=1
                )
        else:
            half[...] = patches_ref[base : base + count]


def pack(patches):
    images, pix, span = patches.shape
    full, rem = split_width(span)
    half = images // 2
    dims = (half + half // 2, pix, full) if rem == 64 and full else (half, pix, span)
    return call(
        functools.partial(pack_kernel, full, rem),
        [shape(dims, BF16)] * 2,
        moved=2 * patches.size * 2,
        name="pack_patches",
    )(patches)


def gather_patches(halves):
    count = lax.axis_size("section")
    blocks = [list(halves)] + [None] * (count - 1)
    for k in range(1, count):
        if k & (k - 1) == 0:
            blocks[k] = [swap(half, "section", k) for half in halves]
    for k in range(1, count):
        if blocks[k] is None:
            low, high = k & -k, 1 << (k.bit_length() - 1)
            blocks[k] = [swap(blocks[k ^ low][0], "section", low), swap(blocks[k ^ high][1], "section", high)]
    return blocks


def block_columns(count, span):
    full, rem = split_width(span)
    early = []
    if full:
        early += [(k, 0, full) for k in range(count - 1)]
    if rem:
        early += [(k, full, span) for k in range(count - 1)]
    return early, [(count - 1, 0, span)]


def order_kernel(count, span, where_ref, decode_ref, early_ref, last_ref):
    early, last = block_columns(count, span)
    for s in range(count):

        @pl.when(where_ref[0] == s)
        def _():
            for pieces, out in ((early, early_ref), (last, last_ref)):
                out[...] = jnp.concatenate(
                    [decode_ref[:, (s ^ k) * span + a : (s ^ k) * span + b] for k, a, b in pieces], axis=1
                )


def order_decode(where, decode, count, span):
    width = decode.shape[0]
    return call(
        functools.partial(order_kernel, count, span),
        [shape((width, (count - 1) * span), BF16), shape((width, span), BF16)],
        in_specs=[pl.BlockSpec(memory_space=pltpu.SMEM), pl.BlockSpec(memory_space=pltpu.VMEM)],
        moved=4 * decode.size,
        name="order_decode",
    )(where, decode)


def forward_kernel(
    pix, groups, acts_ref, first_ref, second_ref, aux_ref, labels_ref,
    wide_ref, hidden_ref, feature_ref, aux_pre_ref, sent_ref, pooled,
):
    step = pl.program_id(0)
    count, rows, width = wide_ref.shape
    for i in range(count):
        wide_ref[i, :pix, :] = acts_ref[i]
        wide_ref[i, pix:, :] = jnp.zeros((rows - pix, width), BF16)
    flat = wide_ref[...].reshape(count * rows, width)
    pre_act = dot(flat, first_ref[...])
    hidden = jnp.maximum(pre_act, 0.0).astype(BF16)
    hidden_ref[...] = hidden.reshape(hidden_ref.shape)
    feature = (flat.astype(F32) + dot(hidden, second_ref[...])).astype(BF16)
    feature_ref[...] = feature.reshape(feature_ref.shape)
    sums = jnp.sum(feature.reshape(count, rows, width).astype(F32), axis=1)
    pooled[step] = sums / pix

    @pl.when(step == pl.num_programs(0) - 1)
    def _():
        mean = pooled[...].reshape(-1, width).astype(BF16)
        aux_pre = dot(mean, aux_ref[...])
        aux_pre_ref[...] = aux_pre
        head = aux_pre.shape[1]
        part = width // groups
        out = jnp.maximum(aux_pre, 0.0).astype(BF16)
        label = labels_ref[...]
        lane = lax.broadcasted_iota(jnp.int32, (label.shape[0], LANES), 1)
        digits = jnp.where(lane == 0, label // LANES, jnp.where(lane == 1, label % LANES, 0))
        digits = digits.astype(F32).astype(BF16)
        for d in range(groups):
            sent_ref[d, :, :head] = out
            sent_ref[d, :, head : head + part] = mean[:, d * part : (d + 1) * part]
            sent_ref[d, :, head + LANES :] = digits


def forward(acts, first, second, aux, labels, groups, rows):
    images, pix, width = acts.shape
    inner, head = first.shape[1], aux.shape[1]
    steps = images // STEP
    whole = lambda g: (0, 0)
    block = lambda n: pl.BlockSpec((STEP, rows, n), lambda g: (g, 0, 0))
    return call(
        functools.partial(forward_kernel, pix, groups),
        [
            shape((images, rows, width), BF16),
            shape((images, rows, inner), BF16),
            shape((images, rows, width), BF16),
            shape((images, head), F32),
            shape((groups, images, head + 2 * LANES), BF16),
        ],
        grid=(steps,),
        in_specs=[
            pl.BlockSpec((STEP, pix, width), lambda g: (g, 0, 0)),
            pl.BlockSpec(first.shape, whole),
            pl.BlockSpec(second.shape, whole),
            pl.BlockSpec(aux.shape, whole),
            pl.BlockSpec((images, 1), whole),
        ],
        out_specs=[
            block(width),
            block(inner),
            block(width),
            pl.BlockSpec((images, head), whole),
            pl.BlockSpec((groups, images, head + 2 * LANES), lambda g: (0, 0, 0)),
        ],
        scratch_shapes=[pltpu.VMEM((steps, STEP, width), F32)],
        flops=4 * images * rows * width * inner,
        moved=2 * images * rows * (3 * width + inner),
        name="forward",
    )(acts, first, second, aux, labels)


def recon_kernel(feature_ref, early_ref, last_ref, recon_early_ref, recon_last_ref):
    count, rows, width = feature_ref.shape
    feature = feature_ref[...].reshape(count * rows, width)
    recon_early_ref[...] = dot(feature, early_ref[...]).reshape(recon_early_ref.shape)
    recon_last_ref[...] = dot(feature, last_ref[...]).reshape(recon_last_ref.shape)


def reconstruct(feature, early, last):
    images, rows, width = feature.shape
    block = lambda n: pl.BlockSpec((STEP, rows, n), lambda g: (g, 0, 0))
    whole = lambda g: (0, 0)
    n_early, n_last = early.shape[1], last.shape[1]
    return call(
        recon_kernel,
        [shape((images, rows, n_early), F32), shape((images, rows, n_last), F32)],
        grid=(images // STEP,),
        in_specs=[block(width), pl.BlockSpec(early.shape, whole), pl.BlockSpec(last.shape, whole)],
        out_specs=[block(n_early), block(n_last)],
        flops=2 * images * rows * width * (n_early + n_last),
        moved=images * rows * (2 * width + 4 * (n_early + n_last)),
        name="reconstruct",
    )(feature, early, last)


def patch_specs(halves, images):
    per_half = images // 2 // STEP
    specs = []
    for h, half in enumerate(halves):
        dims = (STEP,) + half.shape[1:]
        index = lambda g, h=h: (jnp.clip(g - h * per_half, 0, per_half - 1), 0, 0)
        specs.append(pl.BlockSpec(dims, index))
        if half.shape[0] != images // 2:
            specs.append(pl.BlockSpec(dims, lambda g: (per_half, 0, 0)))
        else:
            specs.append(pl.BlockSpec(memory_space=pl.ANY))
    return specs


def residual(step, steps, pieces, scale, packed, patch_refs, recon_ref, grad_ref):
    count, rows, _ = recon_ref.shape
    pix = patch_refs[0][0].shape[1]
    per_half = steps // 2
    first_block = pieces[0][0]
    for g in range(steps):

        @pl.when(step == g)
        def _():
            h = g // per_half
            at = 0
            for k, a, b in pieces:
                refs = patch_refs[k - first_block]
                spans = [(refs[2 * h], a, b)]
                if packed:
                    side = 64 * (g % per_half)
                    cut = refs[0].shape[2]
                    spans = []
                    if a < cut:
                        spans.append((refs[2 * h], a, min(b, cut)))
                    if b > cut:
                        spans.append((refs[2 * h + 1], side, side + 64))
                for ref, lo, hi in spans:
                    size = hi - lo
                    for i in range(count):
                        value = recon_ref[i, :pix, at : at + size] - ref[i, :, lo:hi].astype(F32)
                        grad_ref[i, :pix, at : at + size] = (value * scale).astype(BF16)
                    at += size

    @pl.when(step == 0)
    def _():
        grad_ref[:, pix:, :] = jnp.zeros((count, rows - pix, grad_ref.shape[2]), BF16)


def deal(where_ref, sums, part, keep_ref, send_ref):
    core = where_ref[1]
    at = 0
    for value in sums:
        height = value.shape[0]
        for z in range(keep_ref.shape[0]):
            even = value[:, 2 * z * part : (2 * z + 1) * part]
            odd = value[:, (2 * z + 1) * part : (2 * z + 2) * part]
            mine = jnp.where(core == 0, even, odd)
            other = jnp.where(core == 0, odd, even)
            keep_ref[z, at : at + height, :] = mine.astype(BF16)
            send_ref[z, at : at + height, :] = other.astype(BF16)
        at += height


def early_kernel(
    pieces, scale, packed, groups, where_ref, feature_ref, recon_ref, decode_ref, *refs
):
    n_refs = len(refs) - 5
    patch = [refs[4 * j : 4 * j + 4] for j in range(n_refs // 4)]
    back_ref, keep_ref, send_ref, grad, total = refs[n_refs:]
    step = pl.program_id(0)
    count, rows, width = feature_ref.shape
    residual(step, pl.num_programs(0), pieces, scale, packed, patch, recon_ref, grad)
    flat = grad[...].reshape(count * rows, -1)
    feature = feature_ref[...].reshape(count * rows, width)
    back_ref[...] = dot(flat, decode_ref[...], COLS_1).reshape(back_ref.shape)
    now = dot(flat, feature, ROWS_0)

    @pl.when(step == 0)
    def _():
        total[...] = now

    @pl.when(step > 0)
    def _():
        total[...] += now

    @pl.when(step == pl.num_programs(0) - 1)
    def _():
        deal(where_ref, [total], width // groups, keep_ref, send_ref)


def early_blocks(where, feature, recon, decode, blocks, pieces, scale, groups):
    images, rows, width = feature.shape
    n = decode.shape[1]
    block = lambda m: pl.BlockSpec((STEP, rows, m), lambda g: (g, 0, 0))
    packed = blocks[0][0].shape[0] != images // 2
    parts = (groups // 2, n, width // groups)
    dealt = pl.BlockSpec(parts, lambda g: (0, 0, 0))
    patch_args, specs = [], []
    for halves in blocks:
        specs += patch_specs(halves, images)
        patch_args += [halves[0], halves[0], halves[1], halves[1]]
    return call(
        functools.partial(early_kernel, pieces, scale, packed, groups),
        [shape((images, rows, width), F32), shape(parts, BF16), shape(parts, BF16)],
        grid=(images // STEP,),
        in_specs=[
            pl.BlockSpec(memory_space=pltpu.SMEM),
            block(width),
            block(n),
            pl.BlockSpec(decode.shape, lambda g: (0, 0)),
            *specs,
        ],
        out_specs=[block(width), dealt, dealt],
        scratch_shapes=[pltpu.VMEM((STEP, rows, n), BF16), pltpu.VMEM((n, width), F32)],
        flops=4 * images * rows * width * n,
        moved=images * rows * (6 * width + 6 * n),
        name="early_blocks",
    )(where, feature, recon, decode, *patch_args)


def last_kernel(
    pieces, scale, packed, groups, where_ref, feature_ref, recon_ref, decode_ref, *refs
):
    patch = [refs[:4]]
    (back_ref, pooled_ref, hidden_ref, wide_ref, second_ref, keep_ref, send_ref,
     grad, total_decode, total_second, total_first) = refs[4:]
    step = pl.program_id(0)
    count, rows, width = feature_ref.shape
    residual(step, pl.num_programs(0), pieces, scale, packed, patch, recon_ref, grad)
    flat = grad[...].reshape(count * rows, -1)
    feature = feature_ref[...].reshape(count * rows, width)
    decode_back = dot(flat, decode_ref[...], COLS_1).reshape(count, rows, width)
    pooled = pooled_ref[step]
    feature_grad = (back_ref[...] + decode_back + pooled[:, None, :]).astype(BF16).reshape(count * rows, width)
    hidden = hidden_ref[...].reshape(count * rows, -1)
    hidden_back = dot(feature_grad, second_ref[...], COLS_1)
    hidden_grad = jnp.where(hidden.astype(F32) > 0, hidden_back, 0.0).astype(BF16)
    wide = wide_ref[...].reshape(count * rows, width)
    sums = (
        (total_decode, dot(flat, feature, ROWS_0)),
        (total_second, dot(hidden, feature_grad, ROWS_0)),
        (total_first, dot(hidden_grad, wide, ROWS_0)),
    )

    @pl.when(step == 0)
    def _():
        for total, now in sums:
            total[...] = now

    @pl.when(step > 0)
    def _():
        for total, now in sums:
            total[...] += now

    @pl.when(step == pl.num_programs(0) - 1)
    def _():
        part = width // groups
        tall = total_second.shape[0] // groups
        second = jnp.concatenate(
            [
                jnp.concatenate(
                    [total_second[d * tall : (d + 1) * tall, q * part : (q + 1) * part] for q in range(groups)], axis=0
                )
                for d in range(groups)
            ],
            axis=1,
        )
        deal(where_ref, [total_decode, second, total_first], part, keep_ref, send_ref)


def last_block(where, feature, recon, decode, halves, pieces, scale, groups, back, pooled, hidden, wide, second):
    images, rows, width = feature.shape
    n, inner = decode.shape[1], second.shape[0]
    block = lambda m: pl.BlockSpec((STEP, rows, m), lambda g: (g, 0, 0))
    whole = lambda g: (0, 0)
    packed = halves[0].shape[0] != images // 2
    parts = (groups // 2, n + 2 * inner, width // groups)
    dealt = pl.BlockSpec(parts, lambda g: (0, 0, 0))
    return call(
        functools.partial(last_kernel, pieces, scale, packed, groups),
        [shape(parts, BF16), shape(parts, BF16)],
        grid=(images // STEP,),
        in_specs=[
            pl.BlockSpec(memory_space=pltpu.SMEM),
            block(width),
            block(n),
            pl.BlockSpec(decode.shape, whole),
            *patch_specs(halves, images),
            block(width),
            pl.BlockSpec(pooled.shape, lambda g: (0, 0, 0)),
            block(inner),
            block(width),
            pl.BlockSpec(second.shape, whole),
        ],
        out_specs=[dealt, dealt],
        scratch_shapes=[
            pltpu.VMEM((STEP, rows, n), BF16),
            pltpu.VMEM((n, width), F32),
            pltpu.VMEM((inner, width), F32),
            pltpu.VMEM((inner, width), F32),
        ],
        flops=images * rows * width * (4 * n + 6 * inner),
        moved=images * rows * (8 * width + 6 * n + 2 * inner),
        name="last_block",
    )(where, feature, recon, decode, halves[0], halves[0], halves[1], halves[1], back, pooled, hidden, wide, second)


def labels_of(got, head):
    digits = got[:, head + LANES : head + LANES + 2].astype(F32)
    return (digits[:, 0:1] * LANES + digits[:, 1:2]).astype(jnp.int32)


def logits_kernel(where_ref, got_ref, klass_ref, logits_ref, sent_ref):
    groups, images, _ = got_ref.shape
    classes, head = klass_ref.shape
    got = got_ref[...].reshape(groups * images, -1)
    logits = dot(got[:, :head], klass_ref[...], COLS_1)
    logits_ref[...] = logits
    ids = lax.broadcasted_iota(jnp.int32, logits.shape, 1) + where_ref[2] * classes
    hit = labels_of(got, head) == ids
    top = jnp.max(logits, axis=1, keepdims=True)
    expo = jnp.exp(logits - top)
    denom = jnp.sum(expo, axis=1, keepdims=True)
    own = jnp.sum(jnp.where(hit, expo, 0.0), axis=1, keepdims=True)
    rest = jnp.where(hit, 0.0, expo).astype(BF16)
    onehot = jnp.where(hit, 1.0, 0.0).astype(BF16)
    sent_ref[:, :, :head] = dot(rest, klass_ref[...]).reshape(groups, images, head)
    sent_ref[:, :, head : 2 * head] = dot(onehot, klass_ref[...]).reshape(groups, images, head)
    lane = lax.broadcasted_iota(jnp.int32, (groups * images, LANES), 1)
    stats = jnp.where(lane == 0, top, jnp.where(lane == 1, denom, jnp.where(lane == 2, own, 0.0)))
    sent_ref[:, :, 2 * head :] = stats.reshape(groups, images, LANES)


def class_logits(where, got, klass):
    groups, images, _ = got.shape
    classes, head = klass.shape
    smem, vmem = pl.BlockSpec(memory_space=pltpu.SMEM), pl.BlockSpec(memory_space=pltpu.VMEM)
    return call(
        logits_kernel,
        [shape((groups * images, classes), F32), shape((groups, images, 2 * head + LANES), F32)],
        in_specs=[smem, vmem, vmem],
        flops=6 * groups * images * classes * head,
        moved=2 * klass.size + 4 * groups * images * classes,
        name="class_logits",
    )(where, got, klass)


def aux_kernel(pix, norm, got_ref, aux_pre_ref, aux_ref, pooled_ref, sent_ref):
    groups, images, _ = got_ref.shape
    head = aux_pre_ref.shape[1]
    stats = [got_ref[d, :, 2 * head : 2 * head + 3] for d in range(groups)]
    top = functools.reduce(jnp.maximum, [s[:, 0:1] for s in stats])
    scales = [jnp.exp(s[:, 0:1] - top) for s in stats]
    denom = sum(s[:, 1:2] * f for s, f in zip(stats, scales))
    own = sum(s[:, 2:3] * f for s, f in zip(stats, scales)) / denom
    rest = sum(got_ref[d, :, :head] * scales[d] for d in range(groups)) / (denom * norm)
    row = sum(got_ref[d, :, head : 2 * head] for d in range(groups))
    back = rest + row * ((own - 1.0) / norm).astype(BF16).astype(F32)
    aux_grad = jnp.where(aux_pre_ref[...] > 0, back, 0.0).astype(BF16)
    pooled_ref[...] = (dot(aux_grad, aux_ref[...], COLS_1) / pix).reshape(pooled_ref.shape)
    lane = lax.broadcasted_iota(jnp.int32, (images, LANES), 1)
    tail = jnp.where(lane == 0, top, jnp.where(lane == 1, denom, 0.0))
    for d in range(groups):
        sent_ref[d, :, :head] = aux_grad.astype(F32)
        sent_ref[d, :, head:] = tail


def aux_backward(got, aux_pre, aux, pix, norm):
    groups, images, _ = got.shape
    width, head = aux.shape
    return call(
        functools.partial(aux_kernel, pix, norm),
        [shape((images // STEP, STEP, width), F32), shape((groups, images, head + LANES), F32)],
        flops=2 * images * width * head,
        moved=2 * aux.size + 4 * got.size,
        name="aux_backward",
    )(got, aux_pre, aux)


def class_kernel(norm, where_ref, logits_ref, got_ref, grads_ref, class_ref, aux_ref):
    groups, images, _ = got_ref.shape
    classes, head = class_ref.shape
    part = aux_ref.shape[0]
    got = got_ref[...].reshape(groups * images, -1)
    grads = grads_ref[...].reshape(groups * images, -1)
    top, denom = grads[:, head : head + 1], grads[:, head + 1 : head + 2]
    logits = logits_ref[...]
    ids = lax.broadcasted_iota(jnp.int32, logits.shape, 1) + where_ref[2] * classes
    onehot = jnp.where(labels_of(got, head) == ids, 1.0, 0.0)
    logit_grad = ((jnp.exp(logits - top) / denom - onehot) / norm).astype(BF16)
    class_ref[...] = dot(logit_grad, got[:, :head], ROWS_0)
    total = jnp.zeros(aux_ref.shape, F32)
    for d in range(groups):
        pooled = got_ref[d, :, head : head + part]
        total += dot(pooled, grads_ref[d, :, :head].astype(BF16), ROWS_0).astype(BF16).astype(F32)
    aux_ref[...] = total


def class_backward(where, logits, got, grads, classes, part, norm):
    groups, images, wide = grads.shape
    head = wide - LANES
    smem, vmem = pl.BlockSpec(memory_space=pltpu.SMEM), pl.BlockSpec(memory_space=pltpu.VMEM)
    return call(
        functools.partial(class_kernel, norm),
        [shape((classes, head), F32), shape((part, head), F32)],
        in_specs=[smem, vmem, vmem, vmem],
        flops=2 * groups * images * classes * head,
        moved=4 * classes * head + 4 * logits.size,
        name="class_backward",
    )(where, logits, got, grads)


def chip_kernel(keep_ref, got_ref, out_ref):
    out_ref[...] = (keep_ref[...].astype(F32) + got_ref[...].astype(F32)).astype(BF16)


def reduce_parts(keep, send, name):
    count = lax.axis_size("dp")
    got = swap(send, "dp", 1)
    chip = call(
        chip_kernel,
        shape(keep.shape, BF16),
        flops=keep.size,
        moved=6 * keep.size,
        name=name,
    )(keep, got)
    return exchange(chip, [[z + core for z in range(0, count, 2)] for core in range(2)])


def finish_kernel(count, span, inner, where_ref, early_ref, last_ref, first_ref, second_ref, decode_ref):
    chips, _, part = early_ref.shape
    early = sum(early_ref[z].astype(F32) for z in range(chips))
    last = sum(last_ref[z].astype(F32) for z in range(chips))
    first_ref[...] = last[span + inner :].T
    tall, groups = second_ref.shape[0], inner // second_ref.shape[0]
    for q in range(groups):
        second_ref[:, q * part : (q + 1) * part] = last[span + q * tall : span + (q + 1) * tall]
    pieces, tail = block_columns(count, span)
    columns = {}
    at = 0
    for k, a, b in pieces:
        columns[k, a] = early[at : at + b - a].T
        at += b - a
    for k, a, b in tail:
        columns[k, a] = last[:span].T
    for s in range(count):

        @pl.when(where_ref[0] == s)
        def _():
            for (k, a), value in columns.items():
                start = (s ^ k) * span + a
                decode_ref[:, start : start + value.shape[1]] = value


def finish(where, early, last, count, span, inner, groups):
    part = early.shape[2]
    smem, vmem = pl.BlockSpec(memory_space=pltpu.SMEM), pl.BlockSpec(memory_space=pltpu.VMEM)
    return call(
        functools.partial(finish_kernel, count, span, inner),
        [shape((part, inner), F32), shape((inner // groups, part * groups), F32), shape((part, count * span), F32)],
        in_specs=[smem, vmem, vmem],
        moved=2 * early.size + 2 * last.size,
        name="finish",
    )(where, early, last)


def local(acts, patches, labels, w_first, w_second, w_decode, w_aux, w_class):
    acts = acts[0]
    images, pix, width = acts.shape
    groups, count = lax.axis_size("dp"), lax.axis_size("section")
    me, section = lax.axis_index("dp"), lax.axis_index("section")
    where = jnp.stack([section, lax.rem(me, 2), me]).astype(jnp.int32)
    rows = -(-pix // 16) * 16
    scale = (groups * images * pix) ** -0.5
    norm = (groups * images) ** 0.5
    first, second, decode, aux, klass = w_first[0], w_second[0], w_decode[0], w_aux[0], w_class[0]
    span = patches.shape[2]
    inner = first.shape[1]
    pieces, tail = block_columns(count, span)

    blocks = gather_patches(pack(patches))
    early, last = order_decode(where, decode, count, span)
    wide, hidden, feature, aux_pre, sent = forward(acts, first, second, aux, labels[:, None], groups, rows)
    got = exchange(sent)
    recon_early, recon_last = reconstruct(feature, early, last)
    logits, partial = class_logits(where, got, klass)
    pooled_grad, sent = aux_backward(exchange(partial), aux_pre, aux, pix, norm)
    grads = exchange(sent)
    back, keep, send = early_blocks(where, feature, recon_early, early, blocks[:-1], pieces, scale, groups)
    sum_early = reduce_parts(keep, send, "chip_sum_early")
    grad_class, grad_aux = class_backward(where, logits, got, grads, klass.shape[0], width // groups, norm)
    keep, send = last_block(
        where, feature, recon_last, last, blocks[-1], tail, scale, groups, back, pooled_grad, hidden, wide, second
    )
    sum_last = reduce_parts(keep, send, "chip_sum_last")
    grad_first, grad_second, grad_decode = finish(where, sum_early, sum_last, count, span, inner, groups)
    return grad_first[None], grad_second[None], grad_decode[None], grad_aux[None], grad_class[None]


def solution(mesh):
    in_specs = (
        P("section", "dp", None, None),
        P("dp", None, "section"),
        P("dp"),
        P("section", None, None),
        P("section", None, None),
        P("section", None, None),
        P("section", None, None),
        P("section", "dp", None),
    )
    out_specs = (P("section", "dp", None),) * 5
    return jax.shard_map(local, mesh=mesh, in_specs=in_specs, out_specs=out_specs, check_vma=False)
```

```python
import functools

import jax
import jax.numpy as jnp
from jax import lax
from jax.experimental import pallas as pl
from jax.experimental.pallas import tpu as pltpu
from jax.sharding import PartitionSpec as P

F32 = jnp.float32
BF16 = jnp.bfloat16
STEPS = 4
LANES = 128
EARLY = 4
MIB = 1024 * 1024
ROWS_0 = (((0,), (0,)), ((), ()))
COLS_1 = (((1,), (1,)), ((), ()))
PARITY, CORE, ME, TILES = 0, 1, 2, 3


def dot(left, right, dims=(((1,), (0,)), ((), ()))):
    return lax.dot_general(left, right, dims, preferred_element_type=F32)


def call(kernel, out_shape, *, limit, flops=0, moved=0, **kwargs):
    return pl.pallas_call(
        kernel,
        out_shape=out_shape,
        compiler_params=pltpu.CompilerParams(vmem_limit_bytes=limit * MIB),
        cost_estimate=pl.CostEstimate(flops=int(flops), bytes_accessed=int(moved), transcendentals=0),
        **kwargs,
    )


def shape(dims, kind):
    return jax.ShapeDtypeStruct(dims, kind)


SMEM = pl.BlockSpec(memory_space=pltpu.SMEM)
VMEM = pl.BlockSpec(memory_space=pltpu.VMEM)
ANY = pl.BlockSpec(memory_space=pl.ANY)
HBM = pl.BlockSpec(memory_space=pltpu.HBM)


def swap(value, axis, bits):
    count = lax.axis_size(axis)
    return lax.ppermute(value, axis, [(i, i ^ bits) for i in range(count)])


def exchange(value, groups=None):
    return lax.all_to_all(value, "dp", 0, 0, axis_index_groups=groups, tiled=True)


def pack_kernel(where_ref, patches_ref, *refs):
    out_ref, turned, own, shared = refs
    images, span, pix = patches_ref.shape
    padded = turned.shape[1]
    parity = where_ref[PARITY]
    at_own = pl.multiple_of(64 * parity, 64)
    at_shared = pl.multiple_of(128 * (1 - parity), 64)
    unit = lambda n: (
        lax.broadcasted_iota(jnp.int32, (n, n), 0) == lax.broadcasted_iota(jnp.int32, (n, n), 1)
    ).astype(F32).astype(BF16)
    eye = unit(pix)
    for i in range(images):
        turned[i, :pix, :LANES] = dot(eye, patches_ref[i, pl.ds(at_own, LANES), :], COLS_1).astype(BF16)
        turned[i, :pix, LANES:] = dot(eye, patches_ref[i, pl.ds(at_shared, 64), :], COLS_1).astype(BF16)
        turned[i, pix:, :] = jnp.zeros((padded - pix, span), BF16)
    size = 16 * images
    row = lax.broadcasted_iota(jnp.int32, (size, size), 0)
    column = lax.broadcasted_iota(jnp.int32, (size, size), 1)
    order = (row // images == column % 16) & (row % images == column // 16)
    order = order.astype(F32).astype(BF16)
    for b in range(padded // 16):
        rows = turned[:, 16 * b : 16 * b + 16, :].reshape(size, span)
        out = dot(order, rows).astype(BF16)
        own[16 * b : 16 * b + 16] = out[:, :LANES].reshape(16, images, LANES)
        shared[16 * b : 16 * b + 16] = out[:, LANES:].reshape(16, images, 64)
    count = pix // 2
    quarter = count // 2
    for h in range(2):
        base = h * count
        half = out_ref.at[h]
        half[:count] = own[base : base + count]
        half[count:] = jnp.concatenate(
            [shared[base : base + quarter], shared[base + quarter : base + count]], axis=2
        )


def pack(where, patches):
    images, span, pix = patches.shape
    padded = -(-pix // 16) * 16
    half = pix // 2
    return call(
        pack_kernel,
        shape((2, half + half // 2, images, LANES), BF16),
        limit=20,
        in_specs=[SMEM, VMEM],
        scratch_shapes=[
            pltpu.VMEM((images, padded, span), BF16),
            pltpu.VMEM((padded, images, LANES), BF16),
            pltpu.VMEM((padded, images, 64), BF16),
        ],
        name="pack_patches",
    )(where, patches)


def forward_kernel(
    groups, pix, acts_ref, first_ref, second_ref, aux_ref, labels_ref, *refs
):
    hidden_ref, feature_ref, aux_pre_ref, sent_ref, pooled = refs[-5:]
    step = pl.program_id(0)
    block, images, width = acts_ref.shape
    flat = acts_ref[...].reshape(block * images, width)
    hidden = jnp.maximum(dot(flat, first_ref[...]), 0.0).astype(BF16)
    hidden_ref[...] = hidden
    feature = (flat.astype(F32) + dot(hidden, second_ref[...])).astype(BF16)
    feature_ref[...] = feature
    sums = jnp.sum(feature.reshape(block, images, width).astype(F32), axis=0)

    @pl.when(step == 0)
    def _():
        pooled[...] = sums

    @pl.when(step > 0)
    def _():
        pooled[...] += sums

    @pl.when(step == pl.num_programs(0) - 1)
    def _():
        mean = (pooled[...] / pix).astype(BF16)
        aux_pre = dot(mean, aux_ref[...])
        aux_pre_ref[...] = aux_pre
        head = aux_pre.shape[1]
        part = width // groups
        out = jnp.maximum(aux_pre, 0.0).astype(BF16)
        label = labels_ref[...]
        lane = lax.broadcasted_iota(jnp.int32, (label.shape[0], LANES), 1)
        digits = jnp.where(lane == 0, label // LANES, jnp.where(lane == 1, label % LANES, 0))
        digits = digits.astype(F32).astype(BF16)
        for d in range(groups):
            sent_ref[d, :, :head] = out
            sent_ref[d, :, head : head + part] = mean[:, d * part : (d + 1) * part]
            sent_ref[d, :, head + LANES :] = digits


def forward(acts, first, second, aux, labels, groups, before):
    pix, images, width = acts.shape
    inner, head = first.shape[1], aux.shape[1]
    block = pix // STEPS
    whole = lambda g: (0, 0)
    rows = lambda n: pl.BlockSpec((block * images, n), lambda g: (g, 0))
    return call(
        functools.partial(forward_kernel, groups, pix),
        [
            shape((pix * images, inner), BF16),
            shape((pix * images, width), BF16),
            shape((images, head), F32),
            shape((groups, images, head + 2 * LANES), BF16),
        ],
        limit=58,
        grid=(STEPS,),
        in_specs=[
            pl.BlockSpec((block, images, width), lambda g: (g, 0, 0)),
            pl.BlockSpec(first.shape, whole),
            pl.BlockSpec(second.shape, whole),
            pl.BlockSpec(aux.shape, whole),
            pl.BlockSpec((images, 1), whole),
            *[ANY] * len(before),
        ],
        out_specs=[
            rows(inner),
            rows(width),
            pl.BlockSpec((images, head), whole),
            pl.BlockSpec((groups, images, head + 2 * LANES), lambda g: (0, 0, 0)),
        ],
        scratch_shapes=[pltpu.VMEM((images, width), F32)],
        name="forward",
    )(acts, first, second, aux, labels, *before)


def patch_operands(own_blocks, shared_blocks):
    per_half = STEPS // 2
    own = lambda g, where: (g // per_half, g % per_half, 0, 0)
    shared = lambda g, where: (g // per_half, per_half, 0, 0)
    args = [*own_blocks, *shared_blocks]
    dims = (1, args[0].shape[1] // (per_half + 1)) + args[0].shape[2:]
    specs = [pl.BlockSpec(dims, own)] * len(own_blocks) + [pl.BlockSpec(dims, shared)] * len(shared_blocks)
    return args, specs


def lay_target(step, where_ref, refs, target):
    if len(refs) == 1:
        target[...] = refs[0][...]
        return
    own, shared = refs[:-2], refs[-2:]
    for j, ref in enumerate(own):
        target[:, :, j * LANES : (j + 1) * LANES] = ref[0]
    first, second = shared[0][0].astype(F32), shared[1][0].astype(F32)
    even_first = where_ref[PARITY] == 0
    even = jnp.where(even_first, first, second)
    odd = jnp.where(even_first, second, first)
    turn = lambda v: jnp.concatenate([v[:, :, 64:], v[:, :, :64]], axis=2)
    upper = step % (STEPS // 2) == 1
    low = jnp.where(upper, turn(even), even)
    high = jnp.where(upper, odd, turn(odd))
    lane = lax.broadcasted_iota(jnp.int32, even.shape, 2)
    target[:, :, len(own) * LANES :] = jnp.where(lane < 64, low, high).astype(BF16)


def deal(where_ref, sums, part, keep_ref, send_ref):
    core = where_ref[CORE]
    at = 0
    for value in sums:
        height = value.shape[0]
        for z in range(keep_ref.shape[0]):
            even = value[:, 2 * z * part : (2 * z + 1) * part]
            odd = value[:, (2 * z + 1) * part : (2 * z + 2) * part]
            mine = jnp.where(core == 0, even, odd)
            other = jnp.where(core == 0, odd, even)
            keep_ref[z, at : at + height, :] = mine.astype(BF16)
            send_ref[z, at : at + height, :] = other.astype(BF16)
        at += height


def fetch(source, held, sems, step):
    size = held.shape[0] // STEPS
    copies = [
        pltpu.make_async_copy(source.at[pl.ds(g * size, size)], held.at[pl.ds(g * size, size)], sems.at[g])
        for g in range(STEPS)
    ]

    @pl.when(step == 0)
    def _():
        for copy in copies:
            copy.start()

    for g in range(STEPS):

        @pl.when(step == g)
        def _():
            copies[g].wait()


def early_kernel(groups, scale, n_tiles, n_patch, where_ref, feature_ref, *refs):
    decode_refs, refs = refs[:n_tiles], refs[n_tiles:]
    patch_refs, refs = refs[:n_patch], refs[n_patch:]
    aux_ref, back_ref, keep_ref, send_ref, target, feature, grads, sems = refs
    step = pl.program_id(0)
    size = back_ref.shape[0]
    fetch(feature_ref, feature, sems, step)
    lay_target(step, where_ref, patch_refs, target)
    rows = pl.ds(pl.multiple_of(step * size, size), size)
    decode = jnp.concatenate([ref[...] for ref in decode_refs], axis=1)
    recon = dot(feature[rows], decode)
    grad = ((recon - target[...].reshape(recon.shape).astype(F32)) * scale).astype(BF16)
    grads[rows] = grad
    back_ref[...] = dot(grad, decode, COLS_1)

    @pl.when(step == STEPS - 1)
    def _():
        width = feature.shape[1]
        part = width // groups
        total = dot(grads[...], feature[...], ROWS_0)
        n = total.shape[0]
        deal(where_ref, [total], part, keep_ref, send_ref)
        aux = aux_ref[...].astype(F32)
        images, head = aux.shape
        for c in range(2):
            value = jnp.where(where_ref[CORE] == c, aux, 0.0).astype(BF16)
            for q in range(head // part):
                at = n + (c * (head // part) + q) * images
                for z in range(keep_ref.shape[0]):
                    keep_ref[z, at : at + images, :] = value[:, q * part : (q + 1) * part]
                    send_ref[z, at : at + images, :] = value[:, q * part : (q + 1) * part]


def early_blocks(where, feature, decode, patch_args, patch_specs, aux_grad, images, scale, groups):
    rows, width = feature.shape
    n = EARLY * LANES
    size = rows // STEPS
    part = width // groups
    parts = (groups // 2, n + 2 * aux_grad.size // part, part)
    dealt = pl.BlockSpec(parts, lambda g, where: (0, 0, 0))
    tile = lambda j: pl.BlockSpec((width, LANES), lambda g, where: (0, where[TILES + j]))
    return call(
        functools.partial(early_kernel, groups, scale, EARLY, len(patch_args)),
        [shape((rows, width), F32), shape(parts, BF16), shape(parts, BF16)],
        limit=58,
        flops=6 * rows * width * n,
        moved=rows * (6 * width),
        grid_spec=pltpu.PrefetchScalarGridSpec(
            num_scalar_prefetch=1,
            grid=(STEPS,),
            in_specs=[
                HBM,
                *[tile(j) for j in range(EARLY)],
                *patch_specs,
                pl.BlockSpec(aux_grad.shape, lambda g, where: (0, 0)),
            ],
            out_specs=[pl.BlockSpec((size, width), lambda g, where: (g, 0)), dealt, dealt],
            scratch_shapes=[
                pltpu.VMEM((size // images, images, n), BF16),
                pltpu.VMEM((rows, width), BF16),
                pltpu.VMEM((rows, n), BF16),
                pltpu.SemaphoreType.DMA((STEPS,)),
            ],
        ),
        name="early_blocks",
    )(where, feature, *[decode] * EARLY, *patch_args, aux_grad)


def last_kernel(groups, scale, n_tiles, n_patch, where_ref, feature_ref, hidden_ref, acts_ref, *refs):
    decode_refs, refs = refs[:n_tiles], refs[n_tiles:]
    patch_refs, refs = refs[:n_patch], refs[n_patch:]
    (back_ref, pooled_ref, second_ref, _, keep_ref, send_ref,
     target, feature, hidden, acts, grads, feature_grads, hidden_grads, sems) = refs
    step = pl.program_id(0)
    size, width = back_ref.shape
    fetch(feature_ref, feature, sems.at[0], step)
    fetch(hidden_ref, hidden, sems.at[1], step)
    fetch(acts_ref, acts, sems.at[2], step)
    lay_target(step, where_ref, patch_refs, target)
    rows = pl.ds(pl.multiple_of(step * size, size), size)
    decode = jnp.concatenate([ref[...] for ref in decode_refs], axis=1)
    recon = dot(feature[rows], decode)
    grad = ((recon - target[...].reshape(recon.shape).astype(F32)) * scale).astype(BF16)
    grads[rows] = grad
    images = pooled_ref.shape[0]
    decode_back = back_ref[...] + dot(grad, decode, COLS_1)
    feature_grad = (decode_back.reshape(size // images, images, width) + pooled_ref[...][None]).astype(BF16)
    feature_grad = feature_grad.reshape(size, width)
    feature_grads[rows] = feature_grad
    hidden_back = dot(feature_grad, second_ref[...], COLS_1)
    hidden_grads[rows] = jnp.where(hidden[rows].astype(F32) > 0, hidden_back, 0.0).astype(BF16)

    @pl.when(step == STEPS - 1)
    def _():
        part = width // groups
        total_decode = dot(grads[...], feature[...], ROWS_0)
        total_second = dot(hidden[...], feature_grads[...], ROWS_0)
        total_first = dot(hidden_grads[...], acts[...].reshape(feature.shape), ROWS_0)
        tall = total_second.shape[0] // groups
        second = jnp.concatenate(
            [
                jnp.concatenate(
                    [total_second[d * tall : (d + 1) * tall, q * part : (q + 1) * part] for q in range(groups)], axis=0
                )
                for d in range(groups)
            ],
            axis=1,
        )
        deal(where_ref, [total_decode, second, total_first], part, keep_ref, send_ref)


def last_blocks(
    where, feature, hidden, acts, decode, patch_args, patch_specs, back, pooled, second, before, scale, groups
):
    rows, width = feature.shape
    inner = hidden.shape[1]
    n_tiles = decode.shape[1] // LANES - EARLY
    n = n_tiles * LANES
    size = rows // STEPS
    images = pooled.shape[0]
    parts = (groups // 2, n + 2 * inner, width // groups)
    dealt = pl.BlockSpec(parts, lambda g, where: (0, 0, 0))
    tile = lambda j: pl.BlockSpec((width, LANES), lambda g, where: (0, where[TILES + EARLY + j]))
    whole = lambda g, where: (0, 0)
    return call(
        functools.partial(last_kernel, groups, scale, n_tiles, len(patch_args)),
        [shape(parts, BF16), shape(parts, BF16)],
        limit=58,
        flops=6 * rows * width * (n + inner),
        moved=rows * (8 * width),
        grid_spec=pltpu.PrefetchScalarGridSpec(
            num_scalar_prefetch=1,
            grid=(STEPS,),
            in_specs=[
                HBM,
                HBM,
                HBM,
                *[tile(j) for j in range(n_tiles)],
                *patch_specs,
                pl.BlockSpec((size, width), lambda g, where: (g, 0)),
                pl.BlockSpec(pooled.shape, whole),
                pl.BlockSpec(second.shape, whole),
                ANY,
            ],
            out_specs=[dealt, dealt],
            scratch_shapes=[
                pltpu.VMEM((size // images, images, n), BF16),
                pltpu.VMEM((rows, width), BF16),
                pltpu.VMEM((rows, inner), BF16),
                pltpu.VMEM(acts.shape, BF16),
                pltpu.VMEM((rows, n), BF16),
                pltpu.VMEM((rows, width), BF16),
                pltpu.VMEM((rows, inner), BF16),
                pltpu.SemaphoreType.DMA((3, STEPS)),
            ],
        ),
        name="last_blocks",
    )(where, feature, hidden, acts, *[decode] * n_tiles, *patch_args, back, pooled, second, before)


TOPS, DENOMS = 16, 64


def labels_of(got, head):
    digits = got[:, head + LANES : head + LANES + 2].astype(F32)
    return (digits[:, 0:1] * LANES + digits[:, 1:2]).astype(jnp.int32)


def logits_kernel(where_ref, got_ref, klass_ref, logits_ref, sent_ref):
    groups, images, _ = got_ref.shape
    classes, head = klass_ref.shape
    got = got_ref[...].reshape(groups * images, -1)
    logits = dot(got[:, :head], klass_ref[...], COLS_1)
    logits_ref[...] = logits
    ids = lax.broadcasted_iota(jnp.int32, logits.shape, 1) + where_ref[ME] * classes
    hit = labels_of(got, head) == ids
    top = jnp.max(logits, axis=1, keepdims=True)
    expo = jnp.exp(logits - top)
    denom = jnp.sum(expo, axis=1, keepdims=True)
    own = jnp.sum(jnp.where(hit, expo, 0.0), axis=1, keepdims=True)
    rest = jnp.where(hit, 0.0, expo).astype(BF16)
    onehot = jnp.where(hit, 1.0, 0.0).astype(BF16)
    sent_ref[:, :, :head] = dot(rest, klass_ref[...]).reshape(groups, images, head)
    sent_ref[:, :, head : 2 * head] = dot(onehot, klass_ref[...]).reshape(groups, images, head)
    lane = lax.broadcasted_iota(jnp.int32, (images, LANES), 1)
    cut = lambda value, d: value[d * images : (d + 1) * images]
    common = jnp.zeros((images, LANES), F32)
    for d in range(groups):
        common = jnp.where(lane == TOPS + d, cut(top, d), common)
        common = jnp.where(lane == DENOMS + d, cut(denom, d), common)
    for d in range(groups):
        stats = jnp.where(lane == 1, cut(denom, d), jnp.where(lane == 2, cut(own, d), common))
        sent_ref[d, :, 2 * head :] = jnp.where(lane == 0, cut(top, d), stats)


def class_logits(where, got, klass):
    groups, images, _ = got.shape
    classes, head = klass.shape
    return call(
        logits_kernel,
        [shape((groups * images, classes), F32), shape((groups, images, 2 * head + LANES), F32)],
        limit=16,
        in_specs=[SMEM, VMEM, VMEM],
        name="class_logits",
    )(where, got, klass)


def aux_kernel(pix, norm, got_ref, aux_pre_ref, aux_ref, pooled_ref, grad_ref):
    groups = got_ref.shape[0]
    head = aux_pre_ref.shape[1]
    stats = [got_ref[d, :, 2 * head : 2 * head + 3] for d in range(groups)]
    top = functools.reduce(jnp.maximum, [s[:, 0:1] for s in stats])
    scales = [jnp.exp(s[:, 0:1] - top) for s in stats]
    denom = sum(s[:, 1:2] * f for s, f in zip(stats, scales))
    own = sum(s[:, 2:3] * f for s, f in zip(stats, scales)) / denom
    rest = sum(got_ref[d, :, :head] * scales[d] for d in range(groups)) / (denom * norm)
    row = sum(got_ref[d, :, head : 2 * head] for d in range(groups))
    back = rest + row * ((own - 1.0) / norm).astype(BF16).astype(F32)
    aux_grad = jnp.where(aux_pre_ref[...] > 0, back, 0.0).astype(BF16)
    pooled_ref[...] = dot(aux_grad, aux_ref[...], COLS_1) / pix
    grad_ref[...] = aux_grad


def aux_backward(got, aux_pre, aux, pix, norm):
    images = got.shape[1]
    width, head = aux.shape
    return call(
        functools.partial(aux_kernel, pix, norm),
        [shape((images, width), F32), shape((images, head), BF16)],
        limit=16,
        name="aux_backward",
    )(got, aux_pre, aux)


def class_kernel(norm, n, where_ref, logits_ref, got_ref, stats_ref, grads_ref, class_ref, aux_ref):
    groups, images, _ = got_ref.shape
    head = class_ref.shape[1]
    classes, part = class_ref.shape[0], aux_ref.shape[0]
    got = got_ref[...].reshape(groups * images, -1)
    tops, denoms = [], []
    for d in range(groups):
        top = functools.reduce(jnp.maximum, [stats_ref[e, :, TOPS + d : TOPS + d + 1] for e in range(groups)])
        tops.append(top)
        denoms.append(
            sum(
                stats_ref[e, :, DENOMS + d : DENOMS + d + 1] * jnp.exp(stats_ref[e, :, TOPS + d : TOPS + d + 1] - top)
                for e in range(groups)
            )
        )
    top, denom = jnp.concatenate(tops, axis=0), jnp.concatenate(denoms, axis=0)
    logits = logits_ref[...]
    ids = lax.broadcasted_iota(jnp.int32, logits.shape, 1) + where_ref[ME] * classes
    onehot = jnp.where(labels_of(got, head) == ids, 1.0, 0.0)
    logit_grad = ((jnp.exp(logits - top) / denom - onehot) / norm).astype(BF16)
    class_ref[...] = dot(logit_grad, got[:, :head], ROWS_0)
    total = jnp.zeros(aux_ref.shape, F32)
    for d in range(groups):
        at = n + d % 2 * (head // part) * images
        grad = jnp.concatenate(
            [grads_ref[d // 2, at + q * images : at + (q + 1) * images, :] for q in range(head // part)], axis=1
        )
        pooled = got_ref[d, :, head : head + part]
        total += dot(pooled, grad, ROWS_0).astype(BF16).astype(F32)
    aux_ref[...] = total


def class_backward(where, logits, got, partial, grads, classes, head, norm):
    groups, images, wide = partial.shape
    whole = lambda *dims: pl.BlockSpec(dims, lambda i: (0,) * len(dims))
    part = grads.shape[2]
    return call(
        functools.partial(class_kernel, norm, EARLY * LANES),
        [shape((classes, head), F32), shape((part, head), F32)],
        limit=20,
        flops=2 * groups * images * classes * head,
        moved=4 * classes * head,
        grid=(1,),
        in_specs=[
            SMEM,
            whole(*logits.shape),
            whole(*got.shape),
            pl.BlockSpec((groups, images, LANES), lambda i: (0, 0, wide // LANES - 1)),
            whole(*grads.shape),
        ],
        out_specs=[whole(classes, head), whole(part, head)],
        name="class_backward",
    )(where, logits, got, partial, grads)


def add_cores(keep, send):
    return (keep.astype(F32) + swap(send, "dp", 1).astype(F32)).astype(BF16)


def exchange_chips(parts):
    count = lax.axis_size("dp")
    return exchange(parts, [[z + core for z in range(0, count, 2)] for core in range(2)])


def finish_kernel(inner, n_tiles, where_ref, early_ref, last_ref, first_ref, second_ref, decode_ref):
    chips, _, part = early_ref.shape
    n_last = (n_tiles - EARLY) * LANES
    last = sum(last_ref[z].astype(F32) for z in range(chips))
    first_ref[...] = last[n_last + inner :].T
    tall = second_ref.shape[0]
    for q in range(inner // tall):
        at = n_last + q * tall
        second_ref[:, q * part : (q + 1) * part] = last[at : at + tall]
    early = sum(early_ref[z, : EARLY * LANES].astype(F32) for z in range(chips))
    for j in range(n_tiles):
        value = early[j * LANES : (j + 1) * LANES] if j < EARLY else last[(j - EARLY) * LANES : (j - EARLY + 1) * LANES]
        decode_ref[:, pl.ds(pl.multiple_of(where_ref[TILES + j] * LANES, LANES), LANES)] = value.T


def finish(where, early, last, inner, groups, n_tiles):
    part = early.shape[2]
    return call(
        functools.partial(finish_kernel, inner, n_tiles),
        [shape((part, inner), F32), shape((inner // groups, part * groups), F32), shape((part, n_tiles * LANES), F32)],
        limit=16,
        in_specs=[SMEM, VMEM, VMEM],
        name="finish",
    )(where, early, last)


def local(acts, patches, labels, w_first, w_second, w_decode, w_aux, w_class):
    acts = acts[0].transpose(1, 0, 2)
    pix, images, width = acts.shape
    groups, count = lax.axis_size("dp"), lax.axis_size("section")
    me, section = lax.axis_index("dp"), lax.axis_index("section")
    scale = (groups * images * pix) ** -0.5
    norm = (groups * images) ** 0.5
    first, second, decode, aux, klass = w_first[0], w_second[0], w_decode[0], w_aux[0], w_class[0]
    inner, head = first.shape[1], aux.shape[1]
    n_tiles = decode.shape[1] // LANES
    span = patches.shape[2]
    paired = count == 4 and span == 192

    if paired:
        own_tile = lambda s: 3 * (s >> 1) + 2 * (s & 1)
        shared_tile = lambda s: 3 * (s >> 1) + 1
        tiles = [own_tile(section), own_tile(section ^ 1), own_tile(section ^ 2), shared_tile(section)]
        tiles += [own_tile(section ^ 3), shared_tile(section ^ 2)]
    else:
        tiles = [jnp.int32(j) for j in range(n_tiles)]
    where = jnp.stack([section & 1, me & 1, me, *tiles]).astype(jnp.int32)

    before = []
    if paired:
        packed = pack(where, patches.transpose(0, 2, 1))
        before = [packed]
        near = [swap(packed, "section", 1), swap(packed, "section", 2)]
    hidden, feature, aux_pre, sent = forward(acts, first, second, aux, labels[:, None], groups, before)
    got = exchange(sent)
    if paired:
        packed, got = lax.optimization_barrier((packed, got))
        diagonal = swap(packed, "section", 3)
        early_patches = patch_operands([packed, *near], [packed, near[0]])
        last_patches = patch_operands([diagonal], [near[1], diagonal])
    else:
        target = lax.all_gather(patches, "section", axis=2, tiled=True).transpose(1, 0, 2)
        n_early = EARLY * LANES
        block = lambda n: pl.BlockSpec((pix // STEPS, images, n), lambda g, where: (g, 0, 0))
        early_patches = [target[:, :, :n_early]], [block(n_early)]
        last_patches = [target[:, :, n_early:]], [block(n_tiles * LANES - n_early)]
    logits, partial = class_logits(where, got, klass)
    partial = exchange(partial)
    pooled_grad, aux_grad = aux_backward(partial, aux_pre, aux, pix, norm)
    back, keep, send = early_blocks(where, feature, decode, *early_patches, aux_grad, images, scale, groups)
    chip_early = add_cores(keep, send)
    sum_early = exchange_chips(chip_early)
    keep, send = last_blocks(
        where, feature, hidden, acts, decode, *last_patches, back, pooled_grad, second, chip_early, scale, groups
    )
    sum_last = exchange_chips(add_cores(keep, send))
    grad_class, grad_aux = class_backward(where, logits, got, partial, sum_early, klass.shape[0], head, norm)
    grad_first, grad_second, grad_decode = finish(where, sum_early, sum_last, inner, groups, n_tiles)
    return grad_first[None], grad_second[None], grad_decode[None], grad_aux[None], grad_class[None]


def solution(mesh):
    in_specs = (
        P("section", "dp", None, None),
        P("dp", None, "section"),
        P("dp"),
        P("section", None, None),
        P("section", None, None),
        P("section", None, None),
        P("section", None, None),
        P("section", "dp", None),
    )
    out_specs = (P("section", "dp", None),) * 5
    return jax.shard_map(local, mesh=mesh, in_specs=in_specs, out_specs=out_specs, check_vma=False)
```

```python
import functools

import jax
import jax.numpy as jnp
from jax import lax
from jax.experimental import pallas as pl
from jax.experimental.pallas import tpu as pltpu
from jax.sharding import PartitionSpec as P

F32 = jnp.float32
BF16 = jnp.bfloat16
STEPS = 4
LANES = 128
EARLY = 4
MIB = 1024 * 1024
ROWS_0 = (((0,), (0,)), ((), ()))
COLS_1 = (((1,), (1,)), ((), ()))
PARITY, CORE, ME, TILES = 0, 1, 2, 3


def dot(left, right, dims=(((1,), (0,)), ((), ()))):
    return lax.dot_general(left, right, dims, preferred_element_type=F32)


def call(kernel, out_shape, *, limit, flops=0, moved=0, **kwargs):
    return pl.pallas_call(
        kernel,
        out_shape=out_shape,
        compiler_params=pltpu.CompilerParams(vmem_limit_bytes=limit * MIB),
        cost_estimate=pl.CostEstimate(flops=int(flops), bytes_accessed=int(moved), transcendentals=0),
        **kwargs,
    )


def shape(dims, kind):
    return jax.ShapeDtypeStruct(dims, kind)


SMEM = pl.BlockSpec(memory_space=pltpu.SMEM)
VMEM = pl.BlockSpec(memory_space=pltpu.VMEM)
ANY = pl.BlockSpec(memory_space=pl.ANY)
HBM = pl.BlockSpec(memory_space=pltpu.HBM)


def swap(value, axis, bits):
    count = lax.axis_size(axis)
    return lax.ppermute(value, axis, [(i, i ^ bits) for i in range(count)])


def exchange(value, groups=None):
    return lax.all_to_all(value, "dp", 0, 0, axis_index_groups=groups, tiled=True)


def pack_kernel(where_ref, patches_ref, *refs):
    halves, (turned, own, shared) = refs[:-3], refs[-3:]
    images, span, pix = patches_ref.shape
    padded = turned.shape[1]
    parity = where_ref[PARITY]
    at_own = pl.multiple_of(64 * parity, 64)
    at_shared = pl.multiple_of(128 * (1 - parity), 64)
    unit = lambda n: (
        lax.broadcasted_iota(jnp.int32, (n, n), 0) == lax.broadcasted_iota(jnp.int32, (n, n), 1)
    ).astype(F32).astype(BF16)
    eye = unit(pix)
    for i in range(images):
        turned[i, :pix, :LANES] = dot(eye, patches_ref[i, pl.ds(at_own, LANES), :], COLS_1).astype(BF16)
        turned[i, :pix, LANES:] = dot(eye, patches_ref[i, pl.ds(at_shared, 64), :], COLS_1).astype(BF16)
        turned[i, pix:, :] = jnp.zeros((padded - pix, span), BF16)
    size = 16 * images
    row = lax.broadcasted_iota(jnp.int32, (size, size), 0)
    column = lax.broadcasted_iota(jnp.int32, (size, size), 1)
    order = (row // images == column % 16) & (row % images == column // 16)
    order = order.astype(F32).astype(BF16)
    for b in range(padded // 16):
        rows = turned[:, 16 * b : 16 * b + 16, :].reshape(size, span)
        out = dot(order, rows).astype(BF16)
        own[16 * b : 16 * b + 16] = out[:, :LANES].reshape(16, images, LANES)
        shared[16 * b : 16 * b + 16] = out[:, LANES:].reshape(16, images, 64)
    count = pix // 2
    quarter = count // 2
    for h, half in enumerate(halves):
        base = h * count
        half[:count] = own[base : base + count]
        half[count:] = jnp.concatenate(
            [shared[base : base + quarter], shared[base + quarter : base + count]], axis=2
        )


def pack(where, patches):
    images, span, pix = patches.shape
    padded = -(-pix // 16) * 16
    half = pix // 2
    return call(
        pack_kernel,
        [shape((half + half // 2, images, LANES), BF16)] * 2,
        limit=20,
        in_specs=[SMEM, VMEM],
        scratch_shapes=[
            pltpu.VMEM((images, padded, span), BF16),
            pltpu.VMEM((padded, images, LANES), BF16),
            pltpu.VMEM((padded, images, 64), BF16),
        ],
        name="pack_patches",
    )(where, patches)


def gather_patches(halves):
    x = [swap(half, "section", 1) for half in halves]
    y = [swap(half, "section", 2) for half in halves]
    return [halves, x, y, [swap(y[0], "section", 1), swap(x[1], "section", 2)]]


def forward_kernel(acts_ref, first_ref, second_ref, hidden_ref, feature_ref, pooled_ref):
    step = pl.program_id(0)
    block, images, width = acts_ref.shape
    flat = acts_ref[...].reshape(block * images, width)
    hidden = jnp.maximum(dot(flat, first_ref[...]), 0.0).astype(BF16)
    hidden_ref[...] = hidden
    feature = (flat.astype(F32) + dot(hidden, second_ref[...])).astype(BF16)
    feature_ref[...] = feature
    sums = jnp.sum(feature.reshape(block, images, width).astype(F32), axis=0)

    @pl.when(step == 0)
    def _():
        pooled_ref[...] = sums

    @pl.when(step > 0)
    def _():
        pooled_ref[...] += sums


def forward(acts, first, second):
    pix, images, width = acts.shape
    inner = first.shape[1]
    steps = 7 if pix % 7 == 0 else STEPS
    block = pix // steps
    whole = lambda g: (0, 0)
    rows = lambda n: pl.BlockSpec((block * images, n), lambda g: (g, 0))
    return call(
        forward_kernel,
        [
            shape((pix * images, inner), BF16),
            shape((pix * images, width), BF16),
            shape((images, width), F32),
        ],
        limit=58,
        grid=(steps,),
        in_specs=[
            pl.BlockSpec((block, images, width), lambda g: (g, 0, 0)),
            pl.BlockSpec(first.shape, whole),
            pl.BlockSpec(second.shape, whole),
        ],
        out_specs=[rows(inner), rows(width), pl.BlockSpec((images, width), whole)],
        name="forward",
    )(acts, first, second)


def head_kernel(pix, pooled_ref, aux_ref, labels_ref, *refs):
    aux_pre_ref, sent_ref = refs[-2:]
    groups, images, _ = sent_ref.shape
    width, head = aux_ref.shape
    part = width // groups
    mean = (pooled_ref[...] / pix).astype(BF16)
    aux_pre = dot(mean, aux_ref[...])
    aux_pre_ref[...] = aux_pre
    out = jnp.maximum(aux_pre, 0.0).astype(BF16)
    row = lax.broadcasted_iota(jnp.int32, (images, LANES), 0)
    lane = lax.broadcasted_iota(jnp.int32, (images, LANES), 1)
    digits = jnp.zeros((images, LANES), jnp.int32)
    for i in range(images):
        label = labels_ref[i]
        digits = jnp.where((row == i) & (lane == 0), label // LANES, digits)
        digits = jnp.where((row == i) & (lane == 1), label % LANES, digits)
    digits = digits.astype(F32).astype(BF16)
    for d in range(groups):
        sent_ref[d, :, :head] = out
        sent_ref[d, :, head : head + part] = mean[:, d * part : (d + 1) * part]
        sent_ref[d, :, head + LANES :] = digits


def aux_head(pooled, aux, labels, pix, groups, before):
    images, head = pooled.shape[0], aux.shape[1]
    return call(
        functools.partial(head_kernel, pix),
        [shape((images, head), F32), shape((groups, images, head + 2 * LANES), BF16)],
        limit=16,
        in_specs=[VMEM, VMEM, SMEM, *[ANY] * len(before)],
        name="aux_head",
    )(pooled, aux, labels, *before)


def own_index(h):
    per_half = STEPS // 2
    return lambda g, where: (jnp.clip(g - h * per_half, 0, per_half - 1), 0, 0)


def patch_operands(blocks, own_blocks, shared_blocks):
    args, specs = [], []
    for k in own_blocks:
        for h, half in enumerate(blocks[k]):
            dims = (half.shape[0] // 3,) + half.shape[1:]
            args.append(half)
            specs.append(pl.BlockSpec(dims, own_index(h)))
    for k in shared_blocks:
        for half in blocks[k]:
            dims = (half.shape[0] // 3,) + half.shape[1:]
            args.append(half)
            specs.append(pl.BlockSpec(dims, lambda g, where: (2, 0, 0)))
    return args, specs


def lay_target(step, where_ref, refs, target):
    if len(refs) == 1:
        target[...] = refs[0][...]
        return
    pairs = [refs[j : j + 2] for j in range(0, len(refs), 2)]
    own, shared = pairs[:-2], pairs[-2:]
    per_half = STEPS // 2
    even_first = where_ref[PARITY] == 0
    for h in range(2):

        @pl.when(step // per_half == h)
        def _():
            for j, pair in enumerate(own):
                target[:, :, j * LANES : (j + 1) * LANES] = pair[h][...]

    for g in range(STEPS):

        @pl.when(step == g)
        def _():
            h, side = g // per_half, g % per_half
            mine, other = shared[0][h][...].astype(F32), shared[1][h][...].astype(F32)
            even = jnp.where(even_first, mine, other)
            odd = jnp.where(even_first, other, mine)
            turn = lambda v: jnp.concatenate([v[:, :, 64:], v[:, :, :64]], axis=2)
            lane = lax.broadcasted_iota(jnp.int32, even.shape, 2)
            low = turn(even) if side else even
            high = odd if side else turn(odd)
            target[:, :, len(own) * LANES :] = jnp.where(lane < 64, low, high).astype(BF16)


def deal(where_ref, sums, part, keep_ref, send_ref):
    core = where_ref[CORE]
    at = 0
    for value in sums:
        height = value.shape[0]
        for z in range(keep_ref.shape[0]):
            even = value[:, 2 * z * part : (2 * z + 1) * part]
            odd = value[:, (2 * z + 1) * part : (2 * z + 2) * part]
            mine = jnp.where(core == 0, even, odd)
            other = jnp.where(core == 0, odd, even)
            keep_ref[z, at : at + height, :] = mine.astype(BF16)
            send_ref[z, at : at + height, :] = other.astype(BF16)
        at += height


def fetch(source, held, sems, step):
    size = held.shape[0] // STEPS
    copies = [
        pltpu.make_async_copy(source.at[pl.ds(g * size, size)], held.at[pl.ds(g * size, size)], sems.at[g])
        for g in range(STEPS)
    ]

    @pl.when(step == 0)
    def _():
        for copy in copies:
            copy.start()

    for g in range(STEPS):

        @pl.when(step == g)
        def _():
            copies[g].wait()


def early_kernel(groups, scale, n_tiles, n_patch, where_ref, feature_ref, *refs):
    decode_refs, refs = refs[:n_tiles], refs[n_tiles:]
    patch_refs, refs = refs[:n_patch], refs[n_patch:]
    _, back_ref, keep_ref, send_ref, target, feature, grads, sems = refs
    step = pl.program_id(0)
    size = back_ref.shape[0]
    fetch(feature_ref, feature, sems, step)
    lay_target(step, where_ref, patch_refs, target)
    rows = pl.ds(pl.multiple_of(step * size, size), size)
    decode = jnp.concatenate([ref[...] for ref in decode_refs], axis=1)
    recon = dot(feature[rows], decode)
    grad = ((recon - target[...].reshape(recon.shape).astype(F32)) * scale).astype(BF16)
    grads[rows] = grad
    back_ref[...] = dot(grad, decode, COLS_1)

    @pl.when(step == STEPS - 1)
    def _():
        width = feature.shape[1]
        part = width // groups
        deal(where_ref, [dot(grads[...], feature[...], ROWS_0)], part, keep_ref, send_ref)


def early_blocks(where, feature, decode, patch_args, patch_specs, before, images, scale, groups):
    rows, width = feature.shape
    n = EARLY * LANES
    size = rows // STEPS
    part = width // groups
    parts = (groups // 2, n, part)
    dealt = pl.BlockSpec(parts, lambda g, where: (0, 0, 0))
    tile = lambda j: pl.BlockSpec((width, LANES), lambda g, where: (0, where[TILES + j]))
    return call(
        functools.partial(early_kernel, groups, scale, EARLY, len(patch_args)),
        [shape((rows, width), F32), shape(parts, BF16), shape(parts, BF16)],
        limit=58,
        flops=6 * rows * width * n,
        moved=rows * (6 * width),
        grid_spec=pltpu.PrefetchScalarGridSpec(
            num_scalar_prefetch=1,
            grid=(STEPS,),
            in_specs=[
                HBM,
                *[tile(j) for j in range(EARLY)],
                *patch_specs,
                ANY,
            ],
            out_specs=[pl.BlockSpec((size, width), lambda g, where: (g, 0)), dealt, dealt],
            scratch_shapes=[
                pltpu.VMEM((size // images, images, n), BF16),
                pltpu.VMEM((rows, width), BF16),
                pltpu.VMEM((rows, n), BF16),
                pltpu.SemaphoreType.DMA((STEPS,)),
            ],
        ),
        name="early_blocks",
    )(where, feature, *[decode] * EARLY, *patch_args, before)


def last_kernel(groups, scale, n_tiles, n_patch, where_ref, feature_ref, hidden_ref, *refs):
    decode_refs, refs = refs[:n_tiles], refs[n_tiles:]
    patch_refs, refs = refs[:n_patch], refs[n_patch:]
    (back_ref, pooled_ref, second_ref, _, hidden_grad_ref, keep_ref, send_ref,
     target, feature, hidden, grads, feature_grads, sems) = refs
    step = pl.program_id(0)
    size, width = back_ref.shape
    fetch(feature_ref, feature, sems.at[0], step)
    fetch(hidden_ref, hidden, sems.at[1], step)
    lay_target(step, where_ref, patch_refs, target)
    rows = pl.ds(pl.multiple_of(step * size, size), size)
    decode = jnp.concatenate([ref[...] for ref in decode_refs], axis=1)
    recon = dot(feature[rows], decode)
    grad = ((recon - target[...].reshape(recon.shape).astype(F32)) * scale).astype(BF16)
    grads[rows] = grad
    images = pooled_ref.shape[0]
    decode_back = back_ref[...] + dot(grad, decode, COLS_1)
    feature_grad = (decode_back.reshape(size // images, images, width) + pooled_ref[...][None]).astype(BF16)
    feature_grad = feature_grad.reshape(size, width)
    feature_grads[rows] = feature_grad
    hidden_back = dot(feature_grad, second_ref[...], COLS_1)
    hidden_grad_ref[...] = jnp.where(hidden[rows].astype(F32) > 0, hidden_back, 0.0).astype(BF16)

    @pl.when(step == STEPS - 1)
    def _():
        part = width // groups
        total_decode = dot(grads[...], feature[...], ROWS_0)
        total_second = dot(hidden[...], feature_grads[...], ROWS_0)
        tall = total_second.shape[0] // groups
        second = jnp.concatenate(
            [
                jnp.concatenate(
                    [total_second[d * tall : (d + 1) * tall, q * part : (q + 1) * part] for q in range(groups)], axis=0
                )
                for d in range(groups)
            ],
            axis=1,
        )
        deal(where_ref, [total_decode, second], part, keep_ref, send_ref)


def last_blocks(where, feature, hidden, decode, patch_args, patch_specs, back, pooled, second, before, scale, groups):
    rows, width = feature.shape
    inner = hidden.shape[1]
    n_tiles = decode.shape[1] // LANES - EARLY
    n = n_tiles * LANES
    size = rows // STEPS
    images = pooled.shape[0]
    parts = (groups // 2, n + inner, width // groups)
    dealt = pl.BlockSpec(parts, lambda g, where: (0, 0, 0))
    tile = lambda j: pl.BlockSpec((width, LANES), lambda g, where: (0, where[TILES + EARLY + j]))
    whole = lambda g, where: (0, 0)
    block = lambda m: pl.BlockSpec((size, m), lambda g, where: (g, 0))
    return call(
        functools.partial(last_kernel, groups, scale, n_tiles, len(patch_args)),
        [shape((rows, inner), BF16), shape(parts, BF16), shape(parts, BF16)],
        limit=58,
        grid_spec=pltpu.PrefetchScalarGridSpec(
            num_scalar_prefetch=1,
            grid=(STEPS,),
            in_specs=[
                HBM,
                HBM,
                *[tile(j) for j in range(n_tiles)],
                *patch_specs,
                block(width),
                pl.BlockSpec(pooled.shape, whole),
                pl.BlockSpec(second.shape, whole),
                ANY,
            ],
            out_specs=[block(inner), dealt, dealt],
            scratch_shapes=[
                pltpu.VMEM((size // images, images, n), BF16),
                pltpu.VMEM((rows, width), BF16),
                pltpu.VMEM((rows, inner), BF16),
                pltpu.VMEM((rows, n), BF16),
                pltpu.VMEM((rows, width), BF16),
                pltpu.SemaphoreType.DMA((2, STEPS)),
            ],
        ),
        name="last_blocks",
    )(where, feature, hidden, *[decode] * n_tiles, *patch_args, back, pooled, second, before)


def first_kernel(groups, cuts, where_ref, grads_ref, acts_ref, kept_ref, sent_ref, _, keep_ref, send_ref, grads, acts, sems):
    images = acts.shape[1]
    copies = []
    for c, (a, b) in enumerate(cuts):
        copies.append(
            [
                pltpu.make_async_copy(
                    grads_ref.at[pl.ds(a * images, (b - a) * images)], grads.at[pl.ds(a * images, (b - a) * images)], sems.at[0, c]
                ),
                pltpu.make_async_copy(acts_ref.at[pl.ds(a, b - a)], acts.at[pl.ds(a, b - a)], sems.at[1, c]),
            ]
        )
    for pair in copies:
        for copy in pair:
            copy.start()
    width = acts.shape[2]
    done = kept_ref.shape[1]
    keep_ref[:, :done, :] = kept_ref[...]
    send_ref[:, :done, :] = sent_ref[...]
    total = None
    for pair, (a, b) in zip(copies, cuts):
        for copy in pair:
            copy.wait()
        now = dot(grads[a * images : b * images], acts[a:b].reshape((b - a) * images, width), ROWS_0)
        total = now if total is None else total + now
    deal(where_ref, [total], width // groups, keep_ref.at[:, done:], send_ref.at[:, done:])


def first_grad(where, hidden_grad, acts, keep, send, before, groups):
    pix, images, width = acts.shape
    inner = hidden_grad.shape[1]
    unit = max(256 // images, 1) * 3
    cuts = [(a, min(a + unit, pix)) for a in range(0, pix, unit)]
    if len(cuts) > 1 and 2 * (cuts[-1][1] - cuts[-1][0]) < unit:
        cuts[-2:] = [(cuts[-2][0], pix)]
    parts = (keep.shape[0], keep.shape[1] + inner, keep.shape[2])
    return call(
        functools.partial(first_kernel, groups, cuts),
        [shape(parts, BF16), shape(parts, BF16)],
        limit=58,
        in_specs=[SMEM, HBM, HBM, VMEM, VMEM, ANY],
        scratch_shapes=[
            pltpu.VMEM(hidden_grad.shape, BF16),
            pltpu.VMEM(acts.shape, BF16),
            pltpu.SemaphoreType.DMA((2, len(cuts))),
        ],
        name="first_grad",
    )(where, hidden_grad, acts, keep, send, before)


TOPS, DENOMS = 3, 19
DIGIT = 40


def to_digits(value):
    rest, lanes = value, []
    for _ in range(3):
        digit = rest.astype(BF16).astype(F32)
        lanes.append(digit[:, :DIGIT])
        rest = rest - digit
    lanes.append(jnp.zeros((value.shape[0], LANES - 3 * DIGIT), F32))
    return jnp.concatenate(lanes, axis=1).astype(BF16)


def from_digits(value):
    value = value.astype(F32)
    return sum(value[:, j * DIGIT : (j + 1) * DIGIT] for j in (2, 1, 0))


def labels_of(got, head):
    digits = got[:, head + LANES : head + LANES + 2].astype(F32)
    return (digits[:, 0:1] * LANES + digits[:, 1:2]).astype(jnp.int32)


def logits_kernel(where_ref, got_ref, klass_ref, logits_ref, sent_ref):
    groups, images, _ = got_ref.shape
    classes, head = klass_ref.shape
    got = got_ref[...].reshape(groups * images, -1)
    logits = dot(got[:, :head], klass_ref[...], COLS_1)
    logits_ref[...] = logits
    ids = lax.broadcasted_iota(jnp.int32, logits.shape, 1) + where_ref[ME] * classes
    hit = labels_of(got, head) == ids
    top = jnp.max(logits, axis=1, keepdims=True)
    expo = jnp.exp(logits - top)
    denom = jnp.sum(expo, axis=1, keepdims=True)
    own = jnp.sum(jnp.where(hit, expo, 0.0), axis=1, keepdims=True)
    rest = jnp.where(hit, 0.0, expo).astype(BF16)
    onehot = jnp.where(hit, 1.0, 0.0).astype(BF16)
    sent_ref[:, :, :head] = dot(rest, klass_ref[...]).astype(BF16).reshape(groups, images, head)
    sent_ref[:, :, head : 2 * head] = dot(onehot, klass_ref[...]).astype(BF16).reshape(groups, images, head)
    lane = lax.broadcasted_iota(jnp.int32, (images, LANES), 1)
    cut = lambda value, d: value[d * images : (d + 1) * images]
    common = jnp.zeros((images, LANES), F32)
    for d in range(groups):
        common = jnp.where(lane == TOPS + d, cut(top, d), common)
        common = jnp.where(lane == DENOMS + d, cut(denom, d), common)
    for d in range(groups):
        stats = jnp.where(lane == 1, cut(denom, d), jnp.where(lane == 2, cut(own, d), common))
        sent_ref[d, :, 2 * head :] = to_digits(jnp.where(lane == 0, cut(top, d), stats))


def class_logits(where, got, klass):
    groups, images, _ = got.shape
    classes, head = klass.shape
    return call(
        logits_kernel,
        [shape((groups * images, classes), F32), shape((groups, images, 2 * head + LANES), BF16)],
        limit=16,
        in_specs=[SMEM, VMEM, VMEM],
        name="class_logits",
    )(where, got, klass)


def aux_kernel(pix, norm, got_ref, aux_pre_ref, aux_ref, *refs):
    pooled_ref, grad_ref = refs[-2:]
    groups = got_ref.shape[0]
    head = aux_pre_ref.shape[1]
    stats = [from_digits(got_ref[d, :, 2 * head :]) for d in range(groups)]
    top = functools.reduce(jnp.maximum, [s[:, 0:1] for s in stats])
    scales = [jnp.exp(s[:, 0:1] - top) for s in stats]
    denom = sum(s[:, 1:2] * f for s, f in zip(stats, scales))
    own = sum(s[:, 2:3] * f for s, f in zip(stats, scales)) / denom
    rest = sum(got_ref[d, :, :head].astype(F32) * scales[d] for d in range(groups)) / (denom * norm)
    row = sum(got_ref[d, :, head : 2 * head].astype(F32) for d in range(groups))
    back = rest + row * ((own - 1.0) / norm).astype(BF16).astype(F32)
    aux_grad = jnp.where(aux_pre_ref[...] > 0, back, 0.0).astype(BF16)
    pooled_ref[...] = dot(aux_grad, aux_ref[...], COLS_1) / pix
    images, part = aux_grad.shape[0], grad_ref.shape[1]
    for q in range(head // part):
        grad_ref[q * images : (q + 1) * images, :] = aux_grad[:, q * part : (q + 1) * part]


def aux_backward(got, aux_pre, aux, before, pix, norm):
    groups, images, _ = got.shape
    width, head = aux.shape
    part = width // groups
    return call(
        functools.partial(aux_kernel, pix, norm),
        [shape((images, width), F32), shape((images * head // part, part), BF16)],
        limit=16,
        in_specs=[VMEM, VMEM, VMEM, *[ANY] * len(before)],
        name="aux_backward",
    )(got, aux_pre, aux, *before)


def class_kernel(norm, n, where_ref, logits_ref, got_ref, stats_ref, grads_ref, class_ref, aux_ref):
    groups, images, _ = got_ref.shape
    head = class_ref.shape[1]
    classes, part = class_ref.shape[0], aux_ref.shape[0]
    got = got_ref[...].reshape(groups * images, -1)
    stats = [from_digits(stats_ref[e]) for e in range(groups)]
    tops, denoms = [], []
    for d in range(groups):
        top = functools.reduce(jnp.maximum, [s[:, TOPS + d : TOPS + d + 1] for s in stats])
        tops.append(top)
        denoms.append(sum(s[:, DENOMS + d : DENOMS + d + 1] * jnp.exp(s[:, TOPS + d : TOPS + d + 1] - top) for s in stats))
    top, denom = jnp.concatenate(tops, axis=0), jnp.concatenate(denoms, axis=0)
    logits = logits_ref[...]
    ids = lax.broadcasted_iota(jnp.int32, logits.shape, 1) + where_ref[ME] * classes
    onehot = jnp.where(labels_of(got, head) == ids, 1.0, 0.0)
    logit_grad = ((jnp.exp(logits - top) / denom - onehot) / norm).astype(BF16)
    class_ref[...] = dot(logit_grad, got[:, :head], ROWS_0)
    total = jnp.zeros(aux_ref.shape, F32)
    for d in range(groups):
        at = n + d % 2 * (head // part) * images
        grad = jnp.concatenate(
            [grads_ref[d // 2, at + q * images : at + (q + 1) * images, :] for q in range(head // part)], axis=1
        )
        pooled = got_ref[d, :, head : head + part]
        total += dot(pooled, grad, ROWS_0).astype(BF16).astype(F32)
    aux_ref[...] = total


def class_backward(where, logits, got, partial, grads, classes, head, norm):
    groups, images, wide = partial.shape
    whole = lambda *dims: pl.BlockSpec(dims, lambda i: (0,) * len(dims))
    part = grads.shape[2]
    return call(
        functools.partial(class_kernel, norm, EARLY * LANES),
        [shape((classes, head), F32), shape((part, head), F32)],
        limit=20,
        flops=2 * groups * images * classes * head,
        moved=4 * classes * head,
        grid=(1,),
        in_specs=[
            SMEM,
            whole(*logits.shape),
            whole(*got.shape),
            pl.BlockSpec((groups, images, LANES), lambda i: (0, 0, wide // LANES - 1)),
            whole(*grads.shape),
        ],
        out_specs=[whole(classes, head), whole(part, head)],
        name="class_backward",
    )(where, logits, got, partial, grads)


def chip_kernel(where_ref, keep_ref, got_ref, *refs):
    out_ref = refs[-1]
    n = keep_ref.shape[1]
    out_ref[:, :n, :] = (keep_ref[...].astype(F32) + got_ref[...].astype(F32)).astype(BF16)
    if len(refs) > 1:
        mine, other = refs[0][...].astype(F32), refs[1][...].astype(F32)
        even = where_ref[CORE] == 0
        pair = [jnp.where(even, mine, other).astype(BF16), jnp.where(even, other, mine).astype(BF16)]
        size = mine.shape[0]
        for z in range(out_ref.shape[0]):
            for c in range(2):
                out_ref[z, n + c * size : n + (c + 1) * size, :] = pair[c]


def add_cores(where, keep, send, *extra):
    chips, n, part = keep.shape
    extra = [e for own in extra for e in (own, swap(own, "dp", 1))]
    rows = n + sum(e.shape[0] for e in extra)
    return call(
        chip_kernel,
        shape((chips, rows, part), BF16),
        limit=16,
        in_specs=[SMEM, VMEM, VMEM, *[VMEM] * len(extra)],
        name="add_cores",
    )(where, keep, swap(send, "dp", 1), *extra)


def exchange_chips(parts):
    count = lax.axis_size("dp")
    return exchange(parts, [[z + core for z in range(0, count, 2)] for core in range(2)])


def finish_kernel(inner, n_tiles, where_ref, early_ref, last_ref, first_ref, second_ref, decode_ref):
    chips, _, part = early_ref.shape
    n_last = (n_tiles - EARLY) * LANES
    last = sum(last_ref[z].astype(F32) for z in range(chips))
    first_ref[...] = last[n_last + inner :].T
    tall = second_ref.shape[0]
    for q in range(inner // tall):
        at = n_last + q * tall
        second_ref[:, q * part : (q + 1) * part] = last[at : at + tall]
    early = sum(early_ref[z, : EARLY * LANES].astype(F32) for z in range(chips))
    for j in range(n_tiles):
        value = early[j * LANES : (j + 1) * LANES] if j < EARLY else last[(j - EARLY) * LANES : (j - EARLY + 1) * LANES]
        decode_ref[:, pl.ds(pl.multiple_of(where_ref[TILES + j] * LANES, LANES), LANES)] = value.T


def finish(where, early, last, inner, groups, n_tiles):
    part = early.shape[2]
    return call(
        functools.partial(finish_kernel, inner, n_tiles),
        [shape((part, inner), F32), shape((inner // groups, part * groups), F32), shape((part, n_tiles * LANES), F32)],
        limit=16,
        in_specs=[SMEM, VMEM, VMEM],
        name="finish",
    )(where, early, last)


def local(acts, patches, labels, w_first, w_second, w_decode, w_aux, w_class):
    acts = acts[0].transpose(1, 0, 2)
    pix, images, width = acts.shape
    groups, count = lax.axis_size("dp"), lax.axis_size("section")
    me, section = lax.axis_index("dp"), lax.axis_index("section")
    scale = (groups * images * pix) ** -0.5
    norm = (groups * images) ** 0.5
    first, second, decode, aux, klass = w_first[0], w_second[0], w_decode[0], w_aux[0], w_class[0]
    inner, head = first.shape[1], aux.shape[1]
    n_tiles = decode.shape[1] // LANES
    span = patches.shape[2]
    paired = count == 4 and span == 192

    if paired:
        own_tile = lambda s: 3 * (s >> 1) + 2 * (s & 1)
        shared_tile = lambda s: 3 * (s >> 1) + 1
        tiles = [own_tile(section), own_tile(section ^ 1), own_tile(section ^ 2), shared_tile(section)]
        tiles += [own_tile(section ^ 3), shared_tile(section ^ 2)]
    else:
        tiles = [jnp.int32(j) for j in range(n_tiles)]
    where = jnp.stack([section & 1, me & 1, me, *tiles]).astype(jnp.int32)

    hidden, feature, pooled = forward(acts, first, second)
    if paired:
        blocks = gather_patches(pack(where, patches.transpose(0, 2, 1)))
        before = [blocks[1][0], blocks[2][0]]
        early_patches = patch_operands(blocks, [0, 1, 2], [0, 1])
        last_patches = patch_operands(blocks, [3], [2, 3])
    else:
        target = lax.all_gather(patches, "section", axis=2, tiled=True).transpose(1, 0, 2)
        before = []
        n_early = EARLY * LANES
        block = lambda n: pl.BlockSpec((pix // STEPS, images, n), lambda g, where: (g, 0, 0))
        early_patches = [target[:, :, :n_early]], [block(n_early)]
        last_patches = [target[:, :, n_early:]], [block(n_tiles * LANES - n_early)]
    aux_pre, sent = aux_head(pooled, aux, labels, pix, groups, before)
    got = exchange(sent)
    logits, sent = class_logits(where, got, klass)
    partial = exchange(sent)
    back, keep, send = early_blocks(where, feature, decode, *early_patches, sent, images, scale, groups)
    pooled_grad, aux_grad = aux_backward(partial, aux_pre, aux, last_patches[0][:2], pix, norm)
    chip_early = add_cores(where, keep, send, aux_grad)
    sum_early = exchange_chips(chip_early)
    hidden_grad, keep, send = last_blocks(
        where, feature, hidden, decode, *last_patches, back, pooled_grad, second, chip_early, scale, groups
    )
    keep, send = first_grad(where, hidden_grad, acts, keep, send, sum_early, groups)
    sum_last = exchange_chips(add_cores(where, keep, send))
    grad_class, grad_aux = class_backward(where, logits, got, partial, sum_early, klass.shape[0], head, norm)
    grad_first, grad_second, grad_decode = finish(where, sum_early, sum_last, inner, groups, n_tiles)
    return grad_first[None], grad_second[None], grad_decode[None], grad_aux[None], grad_class[None]


def solution(mesh):
    in_specs = (
        P("section", "dp", None, None),
        P("dp", None, "section"),
        P("dp"),
        P("section", None, None),
        P("section", None, None),
        P("section", None, None),
        P("section", None, None),
        P("section", "dp", None),
    )
    out_specs = (P("section", "dp", None),) * 5
    return jax.shard_map(local, mesh=mesh, in_specs=in_specs, out_specs=out_specs, check_vma=False)
```

```python
import functools

import jax
import jax.numpy as jnp
from jax import lax
from jax.experimental import pallas as pl
from jax.experimental.pallas import tpu as pltpu
from jax.sharding import PartitionSpec as P

F32 = jnp.float32
BF16 = jnp.bfloat16
STEPS = 4
LANES = 128
TILE = 256
MIB = 1024 * 1024
TOKEN = (8, LANES)
ROWS_0 = (((0,), (0,)), ((), ()))
COLS_1 = (((1,), (1,)), ((), ()))
PARITY, CORE, ME, TILES = 0, 1, 2, 3


def dot(left, right, dims=(((1,), (0,)), ((), ()))):
    return lax.dot_general(left, right, dims, preferred_element_type=F32)


def call(kernel, out_shape, *, limit, flops=0, moved=0, **kwargs):
    return pl.pallas_call(
        kernel,
        out_shape=out_shape,
        compiler_params=pltpu.CompilerParams(vmem_limit_bytes=limit * MIB),
        cost_estimate=pl.CostEstimate(flops=int(flops), bytes_accessed=int(moved), transcendentals=0),
        **kwargs,
    )


def shape(dims, kind):
    return jax.ShapeDtypeStruct(dims, kind)


SMEM = pl.BlockSpec(memory_space=pltpu.SMEM)
VMEM = pl.BlockSpec(memory_space=pltpu.VMEM)
ANY = pl.BlockSpec(memory_space=pl.ANY)
HBM = pl.BlockSpec(memory_space=pltpu.HBM)


def swap(value, axis, bits):
    count = lax.axis_size(axis)
    return lax.ppermute(value, axis, [(i, i ^ bits) for i in range(count)])


def exchange(value, groups=None):
    return lax.all_to_all(value, "dp", 0, 0, axis_index_groups=groups, tiled=True)


def pack_kernel(first, where_ref, patches_ref, out_ref, token_ref, turned, own, shared):
    images, span, pix = patches_ref.shape
    padded = turned.shape[1]
    count = out_ref.shape[0] // 3 * 2
    parity = where_ref[PARITY]
    at_own = pl.multiple_of(64 * parity, 64)
    at_shared = pl.multiple_of(128 * (1 - parity), 64)
    row = lax.broadcasted_iota(jnp.int32, (padded, pix), 0)
    column = lax.broadcasted_iota(jnp.int32, (padded, pix), 1)
    pick = ((row < count) & (column == row + first)).astype(F32).astype(BF16)
    for i in range(images):
        turned[i, :, :LANES] = dot(pick, patches_ref[i, pl.ds(at_own, LANES), :], COLS_1).astype(BF16)
        turned[i, :, LANES:] = dot(pick, patches_ref[i, pl.ds(at_shared, 64), :], COLS_1).astype(BF16)
    size = 16 * images
    row = lax.broadcasted_iota(jnp.int32, (size, size), 0)
    column = lax.broadcasted_iota(jnp.int32, (size, size), 1)
    order = (row // images == column % 16) & (row % images == column // 16)
    order = order.astype(F32).astype(BF16)
    for b in range(padded // 16):
        rows = turned[:, 16 * b : 16 * b + 16, :].reshape(size, span)
        out = dot(order, rows).astype(BF16)
        own[16 * b : 16 * b + 16] = out[:, :LANES].reshape(16, images, LANES)
        shared[16 * b : 16 * b + 16] = out[:, LANES:].reshape(16, images, 64)
    out_ref[:count] = own[:count]
    out_ref[count:] = jnp.concatenate([shared[: count // 2], shared[count // 2 : count]], axis=2)
    token_ref[...] = jnp.zeros(token_ref.shape, F32)


def pack(where, patches, h):
    images, span, pix = patches.shape
    half = pix // 2
    padded = -(-half // 16) * 16
    return call(
        functools.partial(pack_kernel, h * half),
        [shape((half + half // 2, images, LANES), BF16), shape(TOKEN, F32)],
        limit=20,
        in_specs=[SMEM, VMEM],
        scratch_shapes=[
            pltpu.VMEM((images, padded, span), BF16),
            pltpu.VMEM((padded, images, LANES), BF16),
            pltpu.VMEM((padded, images, 64), BF16),
        ],
        name="pack_patches",
    )(where, patches)


def after(value, other):
    return lax.optimization_barrier((value, other))[0]


def forward_kernel(acts_ref, first_ref, second_ref, *refs):
    hidden_ref, feature_ref, pooled_ref = refs[-3:]
    step = pl.program_id(0)
    block, images, width = acts_ref.shape
    flat = acts_ref[...].reshape(block * images, width)
    hidden = jnp.maximum(dot(flat, first_ref[...]), 0.0).astype(BF16)
    hidden_ref[...] = hidden

    @pl.when(step == 0)
    def _():
        pooled_ref[...] = jnp.zeros(pooled_ref.shape, F32)

    for at in range(0, width, TILE):
        cut = slice(at, at + TILE)
        feature = (flat[:, cut].astype(F32) + dot(hidden, second_ref[:, cut])).astype(BF16)
        feature_ref[:, cut] = feature
        pooled_ref[:, cut] += jnp.sum(feature.reshape(block, images, TILE).astype(F32), axis=0)


def forward(acts, first, second, before):
    pix, images, width = acts.shape
    inner = first.shape[1]
    block = pix // STEPS
    whole = lambda g: (0, 0)
    rows = lambda n: pl.BlockSpec((block * images, n), lambda g: (g, 0))
    return call(
        forward_kernel,
        [
            shape((pix * images, inner), BF16),
            shape((pix * images, width), BF16),
            shape((images, width), F32),
        ],
        limit=58,
        flops=4 * pix * images * width * inner,
        moved=2 * pix * images * (2 * width + inner),
        grid=(STEPS,),
        in_specs=[
            pl.BlockSpec((block, images, width), lambda g: (g, 0, 0)),
            pl.BlockSpec(first.shape, whole),
            pl.BlockSpec(second.shape, whole),
            *[ANY] * len(before),
        ],
        out_specs=[rows(inner), rows(width), pl.BlockSpec((images, width), whole)],
        name="forward",
    )(acts, first, second, *before)


def head_kernel(pix, pooled_ref, aux_ref, labels_ref, *refs):
    aux_pre_ref, sent_ref = refs[-2:]
    groups, images, _ = sent_ref.shape
    width, head = aux_ref.shape
    part = width // groups
    mean = (pooled_ref[...] / pix).astype(BF16)
    aux_pre = dot(mean, aux_ref[...])
    aux_pre_ref[...] = aux_pre
    out = jnp.maximum(aux_pre, 0.0).astype(BF16)
    row = lax.broadcasted_iota(jnp.int32, (images, LANES), 0)
    lane = lax.broadcasted_iota(jnp.int32, (images, LANES), 1)
    digits = jnp.zeros((images, LANES), jnp.int32)
    for i in range(images):
        label = labels_ref[i]
        digits = jnp.where((row == i) & (lane == 0), label // LANES, digits)
        digits = jnp.where((row == i) & (lane == 1), label % LANES, digits)
    digits = digits.astype(F32).astype(BF16)
    for d in range(groups):
        sent_ref[d, :, :head] = out
        sent_ref[d, :, head : head + part] = mean[:, d * part : (d + 1) * part]
        sent_ref[d, :, head + LANES :] = digits


def aux_head(pooled, aux, labels, pix, groups, before):
    images, head = pooled.shape[0], aux.shape[1]
    return call(
        functools.partial(head_kernel, pix),
        [shape((images, head), F32), shape((groups, images, head + 2 * LANES), BF16)],
        limit=16,
        in_specs=[VMEM, VMEM, SMEM, *[ANY] * len(before)],
        name="aux_head",
    )(pooled, aux, labels, *before)


def recon_kernel(feature_ref, decode_ref, _, recon_ref, token_ref):
    token_ref[...] = jnp.zeros(token_ref.shape, F32)
    feature = feature_ref[...]
    for at in range(0, recon_ref.shape[1], TILE):
        cut = slice(at, at + TILE)
        recon_ref[:, cut] = dot(feature, decode_ref[:, cut])


def reconstruct(feature, decode, before):
    rows, width = feature.shape
    n = decode.shape[1]
    block = lambda m: pl.BlockSpec((rows // STEPS, m), lambda g: (g, 0))
    return call(
        recon_kernel,
        [shape((rows, n), F32), shape(TOKEN, F32)],
        limit=58,
        flops=2 * rows * width * n,
        moved=rows * (2 * width + 4 * n),
        grid=(STEPS,),
        in_specs=[block(width), pl.BlockSpec(decode.shape, lambda g: (0, 0)), ANY],
        out_specs=[block(n), pl.BlockSpec(TOKEN, lambda g: (0, 0))],
        name="reconstruct",
    )(feature, decode, before)


def own_index(h):
    per_half = STEPS // 2
    return lambda g, where: (jnp.clip(g - h * per_half, 0, per_half - 1), 0, 0)


def patch_operands(blocks, own_blocks, shared_blocks):
    args, specs = [], []
    for k in own_blocks:
        for h, half in enumerate(blocks[k]):
            dims = (half.shape[0] // 3,) + half.shape[1:]
            args.append(half)
            specs.append(pl.BlockSpec(dims, own_index(h)))
    for k in shared_blocks:
        for half in blocks[k]:
            dims = (half.shape[0] // 3,) + half.shape[1:]
            args.append(half)
            specs.append(pl.BlockSpec(dims, lambda g, where: (2, 0, 0)))
    return args, specs


def lay_target(step, where_ref, refs, target):
    if len(refs) == 1:
        target[...] = refs[0][...]
        return
    pairs = [refs[j : j + 2] for j in range(0, len(refs), 2)]
    own, shared = pairs[: len(pairs) // 2], pairs[len(pairs) // 2 :]
    per_half = STEPS // 2
    even_first = where_ref[PARITY] == 0
    lanes = lambda j: pl.ds(pl.multiple_of(where_ref[TILES + j] * LANES, LANES), LANES)
    for h in range(2):

        @pl.when(step // per_half == h)
        def _():
            for k, pair in enumerate(own):
                target[:, :, lanes(2 * k)] = pair[h][...]

    turn = lambda v: jnp.concatenate([v[:, :, 64:], v[:, :, :64]], axis=2)
    for g in range(STEPS):

        @pl.when(step == g)
        def _():
            h, side = g // per_half, g % per_half
            for k in range(0, len(shared), 2):
                mine, other = shared[k][h][...].astype(F32), shared[k + 1][h][...].astype(F32)
                even = jnp.where(even_first, mine, other)
                odd = jnp.where(even_first, other, mine)
                lane = lax.broadcasted_iota(jnp.int32, even.shape, 2)
                low = turn(even) if side else even
                high = odd if side else turn(odd)
                target[:, :, lanes(2 * k + 1)] = jnp.where(lane < 64, low, high).astype(BF16)


def deal(where_ref, sums, part, keep_ref, send_ref):
    core = where_ref[CORE]
    at = 0
    for value in sums:
        height = value.shape[0]
        for z in range(keep_ref.shape[0]):
            even = value[:, 2 * z * part : (2 * z + 1) * part]
            odd = value[:, (2 * z + 1) * part : (2 * z + 2) * part]
            mine = jnp.where(core == 0, even, odd)
            other = jnp.where(core == 0, odd, even)
            keep_ref[z, at : at + height, :] = mine.astype(BF16)
            send_ref[z, at : at + height, :] = other.astype(BF16)
        at += height


def fetch(source, held, sems, step):
    size = held.shape[0] // STEPS
    copies = [
        pltpu.make_async_copy(source.at[pl.ds(g * size, size)], held.at[pl.ds(g * size, size)], sems.at[g])
        for g in range(STEPS)
    ]

    @pl.when(step == 0)
    def _():
        for copy in copies:
            copy.start()

    for g in range(STEPS):

        @pl.when(step == g)
        def _():
            copies[g].wait()


def fetch(source, held, sems, step):
    size = held.shape[0] // STEPS
    copies = [
        pltpu.make_async_copy(source.at[pl.ds(g * size, size)], held.at[pl.ds(g * size, size)], sems.at[g])
        for g in range(STEPS)
    ]

    @pl.when(step == 0)
    def _():
        for copy in copies:
            copy.start()

    for g in range(STEPS):

        @pl.when(step == g)
        def _():
            copies[g].wait()


def contract(step, rows, pairs):
    unit = rows // STEPS // TILE * TILE
    for g in range(STEPS):

        @pl.when(step == g)
        def _():
            span = slice(g * unit, rows if g == STEPS - 1 else (g + 1) * unit)
            for total, left, right in pairs:
                now = dot(left[span], right[span], ROWS_0)
                total[...] = now if g == 0 else total[...] + now


def residual_kernel(groups, scale, n_patch, where_ref, feature_ref, recon_ref, *refs):
    patch_refs, refs = refs[:n_patch], refs[n_patch:]
    _, grad_ref, keep_ref, send_ref, target, feature, grads, total, sems = refs
    step = pl.program_id(0)
    rows, width = feature.shape
    size = grad_ref.shape[0]
    fetch(feature_ref, feature, sems, step)
    lay_target(step, where_ref, patch_refs, target)
    grad = ((recon_ref[...] - target[...].reshape(recon_ref.shape).astype(F32)) * scale).astype(BF16)
    grad_ref[...] = grad
    grads[pl.ds(pl.multiple_of(step * size, size), size)] = grad
    contract(step, rows, [(total, grads, feature)])

    @pl.when(step == STEPS - 1)
    def _():
        deal(where_ref, [total], width // groups, keep_ref, send_ref)


def residual(where, feature, recon, patch_args, patch_specs, before, images, scale, groups):
    rows, width = feature.shape
    n = recon.shape[1]
    size = rows // STEPS
    parts = (groups // 2, n, width // groups)
    dealt = pl.BlockSpec(parts, lambda g, where: (0, 0, 0))
    block = pl.BlockSpec((size, n), lambda g, where: (g, 0))
    return call(
        functools.partial(residual_kernel, groups, scale, len(patch_args)),
        [shape((rows, n), BF16), shape(parts, BF16), shape(parts, BF16)],
        limit=58,
        flops=2 * rows * width * n,
        moved=rows * (2 * width + 6 * n),
        grid_spec=pltpu.PrefetchScalarGridSpec(
            num_scalar_prefetch=1,
            grid=(STEPS,),
            in_specs=[HBM, block, *patch_specs, ANY],
            out_specs=[block, dealt, dealt],
            scratch_shapes=[
                pltpu.VMEM((size // images, images, n), BF16),
                pltpu.VMEM((rows, width), BF16),
                pltpu.VMEM((rows, n), BF16),
                pltpu.VMEM((n, width), F32),
                pltpu.SemaphoreType.DMA((STEPS,)),
            ],
        ),
        name="residual",
    )(where, feature, recon, *patch_args, before)


def backward_kernel(
    groups, where_ref, grad_ref, hidden_ref, acts_ref, decode_ref, pooled_ref, second_ref, _,
    keep_ref, send_ref, hidden, acts, feature_grads, hidden_grads, total_second, total_first, sems,
):
    step = pl.program_id(0)
    rows, width = feature_grads.shape
    size = grad_ref.shape[0]
    images = pooled_ref.shape[0]
    fetch(hidden_ref, hidden, sems.at[0], step)
    fetch(acts_ref, acts, sems.at[1], step)
    here = pl.ds(pl.multiple_of(step * size, size), size)
    grad = grad_ref[...]
    for at in range(0, width, TILE):
        cut = slice(at, at + TILE)
        back = dot(grad, decode_ref[cut, :], COLS_1).reshape(size // images, images, TILE)
        feature_grads[here, cut] = (back + pooled_ref[:, cut][None]).astype(BF16).reshape(size, TILE)
    hidden_back = dot(feature_grads[here], second_ref[...], COLS_1)
    hidden_grads[here] = jnp.where(hidden[here].astype(F32) > 0, hidden_back, 0.0).astype(BF16)
    contract(step, rows, [(total_second, hidden, feature_grads), (total_first, hidden_grads, acts)])

    @pl.when(step == STEPS - 1)
    def _():
        part = width // groups
        tall = total_second.shape[0] // groups
        second = jnp.concatenate(
            [
                jnp.concatenate(
                    [total_second[d * tall : (d + 1) * tall, q * part : (q + 1) * part] for q in range(groups)], axis=0
                )
                for d in range(groups)
            ],
            axis=1,
        )
        deal(where_ref, [second, total_first], part, keep_ref, send_ref)


def backward(where, grad, hidden, acts, decode, pooled, second, before, groups):
    rows, width = acts.shape
    inner, n = hidden.shape[1], grad.shape[1]
    size = rows // STEPS
    parts = (groups // 2, 2 * inner, width // groups)
    dealt = pl.BlockSpec(parts, lambda g, where: (0, 0, 0))
    whole = lambda array: pl.BlockSpec(array.shape, lambda g, where: (0, 0))
    return call(
        functools.partial(backward_kernel, groups),
        [shape(parts, BF16), shape(parts, BF16)],
        limit=58,
        flops=2 * rows * width * (n + 3 * inner),
        moved=2 * rows * (width + n + inner),
        grid_spec=pltpu.PrefetchScalarGridSpec(
            num_scalar_prefetch=1,
            grid=(STEPS,),
            in_specs=[
                pl.BlockSpec((size, n), lambda g, where: (g, 0)),
                HBM,
                HBM,
                whole(decode),
                whole(pooled),
                whole(second),
                ANY,
            ],
            out_specs=[dealt, dealt],
            scratch_shapes=[
                pltpu.VMEM((rows, inner), BF16),
                pltpu.VMEM((rows, width), BF16),
                pltpu.VMEM((rows, width), BF16),
                pltpu.VMEM((rows, inner), BF16),
                pltpu.VMEM((inner, width), F32),
                pltpu.VMEM((inner, width), F32),
                pltpu.SemaphoreType.DMA((2, STEPS)),
            ],
        ),
        name="backward",
    )(where, grad, hidden, acts, decode, pooled, second, before)


TOPS, DENOMS = 3, 19
DIGIT = 40


def to_digits(value):
    rest, lanes = value, []
    for _ in range(3):
        digit = rest.astype(BF16).astype(F32)
        lanes.append(digit[:, :DIGIT])
        rest = rest - digit
    lanes.append(jnp.zeros((value.shape[0], LANES - 3 * DIGIT), F32))
    return jnp.concatenate(lanes, axis=1).astype(BF16)


def from_digits(value):
    value = value.astype(F32)
    return sum(value[:, j * DIGIT : (j + 1) * DIGIT] for j in (2, 1, 0))


def labels_of(got, head):
    digits = got[:, head + LANES : head + LANES + 2].astype(F32)
    return (digits[:, 0:1] * LANES + digits[:, 1:2]).astype(jnp.int32)


def logits_kernel(where_ref, got_ref, klass_ref, _, logits_ref, sent_ref):
    groups, images, _ = got_ref.shape
    classes, head = klass_ref.shape
    got = got_ref[...].reshape(groups * images, -1)
    logits = dot(got[:, :head], klass_ref[...], COLS_1)
    logits_ref[...] = logits
    ids = lax.broadcasted_iota(jnp.int32, logits.shape, 1) + where_ref[ME] * classes
    hit = labels_of(got, head) == ids
    top = jnp.max(logits, axis=1, keepdims=True)
    expo = jnp.exp(logits - top)
    denom = jnp.sum(expo, axis=1, keepdims=True)
    own = jnp.sum(jnp.where(hit, expo, 0.0), axis=1, keepdims=True)
    rest = jnp.where(hit, 0.0, expo).astype(BF16)
    onehot = jnp.where(hit, 1.0, 0.0).astype(BF16)
    sent_ref[:, :, :head] = dot(rest, klass_ref[...]).astype(BF16).reshape(groups, images, head)
    sent_ref[:, :, head : 2 * head] = dot(onehot, klass_ref[...]).astype(BF16).reshape(groups, images, head)
    lane = lax.broadcasted_iota(jnp.int32, (images, LANES), 1)
    cut = lambda value, d: value[d * images : (d + 1) * images]
    common = jnp.zeros((images, LANES), F32)
    for d in range(groups):
        common = jnp.where(lane == TOPS + d, cut(top, d), common)
        common = jnp.where(lane == DENOMS + d, cut(denom, d), common)
    for d in range(groups):
        stats = jnp.where(lane == 1, cut(denom, d), jnp.where(lane == 2, cut(own, d), common))
        sent_ref[d, :, 2 * head :] = to_digits(jnp.where(lane == 0, cut(top, d), stats))


def class_logits(where, got, klass, before):
    groups, images, _ = got.shape
    classes, head = klass.shape
    return call(
        logits_kernel,
        [shape((groups * images, classes), F32), shape((groups, images, 2 * head + LANES), BF16)],
        limit=16,
        in_specs=[SMEM, VMEM, VMEM, ANY],
        name="class_logits",
    )(where, got, klass, before)


def aux_kernel(pix, norm, got_ref, aux_pre_ref, aux_ref, pooled_ref, grad_ref):
    groups = got_ref.shape[0]
    head = aux_pre_ref.shape[1]
    stats = [from_digits(got_ref[d, :, 2 * head :]) for d in range(groups)]
    top = functools.reduce(jnp.maximum, [s[:, 0:1] for s in stats])
    scales = [jnp.exp(s[:, 0:1] - top) for s in stats]
    denom = sum(s[:, 1:2] * f for s, f in zip(stats, scales))
    own = sum(s[:, 2:3] * f for s, f in zip(stats, scales)) / denom
    rest = sum(got_ref[d, :, :head].astype(F32) * scales[d] for d in range(groups)) / (denom * norm)
    row = sum(got_ref[d, :, head : 2 * head].astype(F32) for d in range(groups))
    back = rest + row * ((own - 1.0) / norm).astype(BF16).astype(F32)
    aux_grad = jnp.where(aux_pre_ref[...] > 0, back, 0.0).astype(BF16)
    pooled_ref[...] = dot(aux_grad, aux_ref[...], COLS_1) / pix
    images, part = aux_grad.shape[0], grad_ref.shape[1]
    for q in range(head // part):
        grad_ref[q * images : (q + 1) * images, :] = aux_grad[:, q * part : (q + 1) * part]


def aux_backward(got, aux_pre, aux, pix, norm):
    groups, images, _ = got.shape
    width, head = aux.shape
    part = width // groups
    return call(
        functools.partial(aux_kernel, pix, norm),
        [shape((images, width), F32), shape((images * head // part, part), BF16)],
        limit=16,
        name="aux_backward",
    )(got, aux_pre, aux)


def class_kernel(norm, n, where_ref, logits_ref, got_ref, stats_ref, grads_ref, class_ref, aux_ref):
    groups, images, _ = got_ref.shape
    head = class_ref.shape[1]
    classes, part = class_ref.shape[0], aux_ref.shape[0]
    got = got_ref[...].reshape(groups * images, -1)
    stats = [from_digits(stats_ref[e]) for e in range(groups)]
    tops, denoms = [], []
    for d in range(groups):
        top = functools.reduce(jnp.maximum, [s[:, TOPS + d : TOPS + d + 1] for s in stats])
        tops.append(top)
        denoms.append(sum(s[:, DENOMS + d : DENOMS + d + 1] * jnp.exp(s[:, TOPS + d : TOPS + d + 1] - top) for s in stats))
    top, denom = jnp.concatenate(tops, axis=0), jnp.concatenate(denoms, axis=0)
    logits = logits_ref[...]
    ids = lax.broadcasted_iota(jnp.int32, logits.shape, 1) + where_ref[ME] * classes
    onehot = jnp.where(labels_of(got, head) == ids, 1.0, 0.0)
    logit_grad = ((jnp.exp(logits - top) / denom - onehot) / norm).astype(BF16)
    class_ref[...] = dot(logit_grad, got[:, :head], ROWS_0)
    total = jnp.zeros(aux_ref.shape, F32)
    for d in range(groups):
        at = n + d % 2 * (head // part) * images
        grad = jnp.concatenate(
            [grads_ref[d // 2, at + q * images : at + (q + 1) * images, :] for q in range(head // part)], axis=1
        )
        pooled = got_ref[d, :, head : head + part]
        total += dot(pooled, grad, ROWS_0).astype(BF16).astype(F32)
    aux_ref[...] = total


def class_backward(where, logits, got, partial, grads, n_decode, classes, head, norm):
    groups, images, wide = partial.shape
    whole = lambda *dims: pl.BlockSpec(dims, lambda i: (0,) * len(dims))
    part = grads.shape[2]
    return call(
        functools.partial(class_kernel, norm, n_decode),
        [shape((classes, head), F32), shape((part, head), F32)],
        limit=20,
        flops=2 * groups * images * classes * head,
        moved=4 * classes * head,
        grid=(1,),
        in_specs=[
            SMEM,
            whole(*logits.shape),
            whole(*got.shape),
            pl.BlockSpec((groups, images, LANES), lambda i: (0, 0, wide // LANES - 1)),
            whole(*grads.shape),
        ],
        out_specs=[whole(classes, head), whole(part, head)],
        name="class_backward",
    )(where, logits, got, partial, grads)


def chip_kernel(has_extra, where_ref, keep_ref, got_ref, *refs):
    out_ref, token_ref = refs[-2:]
    token_ref[...] = jnp.zeros(token_ref.shape, F32)
    n = keep_ref.shape[1]
    out_ref[:, :n, :] = (keep_ref[...].astype(F32) + got_ref[...].astype(F32)).astype(BF16)
    if has_extra:
        mine, other = refs[0][...].astype(F32), refs[1][...].astype(F32)
        even = where_ref[CORE] == 0
        pair = [jnp.where(even, mine, other).astype(BF16), jnp.where(even, other, mine).astype(BF16)]
        size = mine.shape[0]
        for z in range(out_ref.shape[0]):
            for c in range(2):
                out_ref[z, n + c * size : n + (c + 1) * size, :] = pair[c]


def add_cores(where, keep, send, extra=(), before=()):
    chips, n, part = keep.shape
    extra = [e for own in extra for e in (own, swap(own, "dp", 1))]
    rows = n + sum(e.shape[0] for e in extra)
    return call(
        functools.partial(chip_kernel, len(extra) > 0),
        [shape((chips, rows, part), BF16), shape(TOKEN, F32)],
        limit=16,
        in_specs=[SMEM, VMEM, VMEM, *[VMEM] * len(extra), *[ANY] * len(before)],
        name="add_cores",
    )(where, keep, swap(send, "dp", 1), *extra, *before)


def exchange_chips(parts):
    count = lax.axis_size("dp")
    return exchange(parts, [[z + core for z in range(0, count, 2)] for core in range(2)])


def finish_kernel(inner, early_ref, last_ref, first_ref, second_ref, decode_ref):
    chips, _, part = early_ref.shape
    n = decode_ref.shape[1]
    last = sum(last_ref[z].astype(F32) for z in range(chips))
    first_ref[...] = last[inner:].T
    tall = second_ref.shape[0]
    for q in range(inner // tall):
        second_ref[:, q * part : (q + 1) * part] = last[q * tall : (q + 1) * tall]
    decode_ref[...] = sum(early_ref[z, :n].astype(F32) for z in range(chips)).T


def finish(early, last, inner, groups, n):
    part = early.shape[2]
    return call(
        functools.partial(finish_kernel, inner),
        [shape((part, inner), F32), shape((inner // groups, part * groups), F32), shape((part, n), F32)],
        limit=16,
        name="finish",
    )(early, last)


def local(acts, patches, labels, w_first, w_second, w_decode, w_aux, w_class):
    acts = acts[0].transpose(1, 0, 2)
    pix, images, width = acts.shape
    groups, count = lax.axis_size("dp"), lax.axis_size("section")
    me, section = lax.axis_index("dp"), lax.axis_index("section")
    scale = (groups * images * pix) ** -0.5
    norm = (groups * images) ** 0.5
    first, second, decode, aux, klass = w_first[0], w_second[0], w_decode[0], w_aux[0], w_class[0]
    inner, head = first.shape[1], aux.shape[1]
    n_decode = decode.shape[1]
    rows = pix * images

    paired = count == 4 and patches.shape[2] == 192
    if paired:
        near = [section ^ k for k in range(4)]
        tiles = [t for s in near for t in (3 * (s >> 1) + 2 * (s & 1), 3 * (s >> 1) + 1)]
        where = jnp.stack([section & 1, me & 1, me, *tiles]).astype(jnp.int32)
        turned = patches.transpose(0, 2, 1)
        packed = [pack(where, turned, h) for h in range(2)]
        before_forward = [packed[1][1]]
        halves = [half for half, _ in packed]
        x, y = [swap(halves[0], "section", 1)], [swap(halves[0], "section", 2)]
        before_head = [x[0], y[0]]
    else:
        where = jnp.stack([section & 1, me & 1, me]).astype(jnp.int32)
        before_forward = before_head = []
        target = lax.all_gather(patches, "section", axis=2, tiled=True).transpose(1, 0, 2)

    hidden, feature, pooled = forward(acts, first, second, before_forward)
    aux_pre, sent = aux_head(pooled, aux, labels, pix, groups, before_head)
    got = exchange(sent)
    if paired:
        last = after(halves[1], pooled)
        x.append(swap(last, "section", 1))
        y.append(swap(last, "section", 2))
        diagonal = [swap(after(y[0], aux_pre), "section", 1), swap(after(x[1], aux_pre), "section", 2)]
        blocks = [halves, x, y, diagonal]
        target = patch_operands(blocks, [0, 1, 2, 3], [0, 1, 2, 3])
    else:
        target = [target], [pl.BlockSpec((pix // STEPS, images, n_decode), lambda g, where: (g, 0, 0))]
    recon, token = reconstruct(feature, decode, sent)
    logits, sent = class_logits(where, got, klass, token)
    partial = exchange(sent)
    grad, keep, send = residual(where, feature, recon, *target, sent, images, scale, groups)
    pooled_grad, aux_grad = aux_backward(partial, aux_pre, aux, pix, norm)
    chip_decode, token = add_cores(where, keep, send, [aux_grad])
    sum_decode = exchange_chips(chip_decode)
    keep, send = backward(
        where, grad, hidden, acts.reshape(rows, width), decode, pooled_grad, second, token, groups
    )
    sum_last = exchange_chips(add_cores(where, keep, send, before=[sum_decode])[0])
    grad_class, grad_aux = class_backward(
        where, logits, got, partial, sum_decode, n_decode, klass.shape[0], head, norm
    )
    grad_first, grad_second, grad_decode = finish(sum_decode, sum_last, inner, groups, n_decode)
    return grad_first[None], grad_second[None], grad_decode[None], grad_aux[None], grad_class[None]


def solution(mesh):
    in_specs = (
        P("section", "dp", None, None),
        P("dp", None, "section"),
        P("dp"),
        P("section", None, None),
        P("section", None, None),
        P("section", None, None),
        P("section", None, None),
        P("section", "dp", None),
    )
    out_specs = (P("section", "dp", None),) * 5
    return jax.shard_map(local, mesh=mesh, in_specs=in_specs, out_specs=out_specs, check_vma=False)
```

```python
import functools

import jax
import jax.numpy as jnp
from jax import lax
from jax.experimental import pallas as pl
from jax.experimental.pallas import tpu as pltpu
from jax.sharding import PartitionSpec as P

F32 = jnp.float32
BF16 = jnp.bfloat16
STEPS = 4
LANES = 128
TILE = 256
MIB = 1024 * 1024
ROWS_0 = (((0,), (0,)), ((), ()))
COLS_1 = (((1,), (1,)), ((), ()))
PARITY, CORE, ME, TILES = 0, 1, 2, 3


def dot(left, right, dims=(((1,), (0,)), ((), ()))):
    return lax.dot_general(left, right, dims, preferred_element_type=F32)


def call(kernel, out_shape, *, limit, flops=0, moved=0, **kwargs):
    return pl.pallas_call(
        kernel,
        out_shape=out_shape,
        compiler_params=pltpu.CompilerParams(vmem_limit_bytes=limit * MIB),
        cost_estimate=pl.CostEstimate(flops=int(flops), bytes_accessed=int(moved), transcendentals=0),
        **kwargs,
    )


def shape(dims, kind):
    return jax.ShapeDtypeStruct(dims, kind)


SMEM = pl.BlockSpec(memory_space=pltpu.SMEM)
VMEM = pl.BlockSpec(memory_space=pltpu.VMEM)
HBM = pl.BlockSpec(memory_space=pltpu.HBM)


def swap(value, axis, bits):
    count = lax.axis_size(axis)
    return lax.ppermute(value, axis, [(i, i ^ bits) for i in range(count)])


def exchange(value, groups=None):
    return lax.all_to_all(value, "dp", 0, 0, axis_index_groups=groups, tiled=True)


def pack_kernel(first, where_ref, patches_ref, out_ref, turned, own, shared):
    images, span, pix = patches_ref.shape
    padded = turned.shape[1]
    count = out_ref.shape[0] // 3 * 2
    parity = where_ref[PARITY]
    at_own = pl.multiple_of(64 * parity, 64)
    at_shared = pl.multiple_of(128 * (1 - parity), 64)
    row = lax.broadcasted_iota(jnp.int32, (padded, pix), 0)
    column = lax.broadcasted_iota(jnp.int32, (padded, pix), 1)
    pick = ((row < count) & (column == row + first)).astype(F32).astype(BF16)
    for i in range(images):
        turned[i, :, :LANES] = dot(pick, patches_ref[i, pl.ds(at_own, LANES), :], COLS_1).astype(BF16)
        turned[i, :, LANES:] = dot(pick, patches_ref[i, pl.ds(at_shared, 64), :], COLS_1).astype(BF16)
    size = 16 * images
    row = lax.broadcasted_iota(jnp.int32, (size, size), 0)
    column = lax.broadcasted_iota(jnp.int32, (size, size), 1)
    order = (row // images == column % 16) & (row % images == column // 16)
    order = order.astype(F32).astype(BF16)
    for b in range(padded // 16):
        rows = turned[:, 16 * b : 16 * b + 16, :].reshape(size, span)
        out = dot(order, rows).astype(BF16)
        own[16 * b : 16 * b + 16] = out[:, :LANES].reshape(16, images, LANES)
        shared[16 * b : 16 * b + 16] = out[:, LANES:].reshape(16, images, 64)
    out_ref[:count] = own[:count]
    lower, upper = shared[: count // 2], shared[count // 2 : count]

    @pl.when(parity == 0)
    def _():
        out_ref[count:] = jnp.concatenate([lower, upper], axis=2)

    @pl.when(parity == 1)
    def _():
        out_ref[count:] = jnp.concatenate([upper, lower], axis=2)


def pack(where, patches, h):
    images, span, pix = patches.shape
    half = pix // 2
    padded = -(-half // 16) * 16
    return call(
        functools.partial(pack_kernel, h * half),
        shape((half + half // 2, images, LANES), BF16),
        limit=20,
        in_specs=[SMEM, VMEM],
        scratch_shapes=[
            pltpu.VMEM((images, padded, span), BF16),
            pltpu.VMEM((padded, images, LANES), BF16),
            pltpu.VMEM((padded, images, 64), BF16),
        ],
        name="pack_patches",
    )(where, patches)


def after(value, other):
    return lax.optimization_barrier((value, other))[0]


def forward_kernel(acts_ref, first_ref, second_ref, hidden_ref, feature_ref, pooled_ref):
    step = pl.program_id(0)
    block, images, width = acts_ref.shape
    flat = acts_ref[...].reshape(block * images, width)
    hidden = jnp.maximum(dot(flat, first_ref[...]), 0.0).astype(BF16)
    hidden_ref[...] = hidden

    @pl.when(step == 0)
    def _():
        pooled_ref[...] = jnp.zeros(pooled_ref.shape, F32)

    for at in range(0, width, TILE):
        cut = slice(at, at + TILE)
        feature = (flat[:, cut].astype(F32) + dot(hidden, second_ref[:, cut])).astype(BF16)
        feature_ref[:, cut] = feature
        pooled_ref[:, cut] += jnp.sum(feature.reshape(block, images, TILE).astype(F32), axis=0)


def forward(acts, first, second):
    pix, images, width = acts.shape
    inner = first.shape[1]
    block = pix // STEPS
    whole = lambda g: (0, 0)
    rows = lambda n: pl.BlockSpec((block * images, n), lambda g: (g, 0))
    return call(
        forward_kernel,
        [
            shape((pix * images, inner), BF16),
            shape((pix * images, width), BF16),
            shape((images, width), F32),
        ],
        limit=58,
        flops=4 * pix * images * width * inner,
        moved=2 * pix * images * (2 * width + inner),
        grid=(STEPS,),
        in_specs=[
            pl.BlockSpec((block, images, width), lambda g: (g, 0, 0)),
            pl.BlockSpec(first.shape, whole),
            pl.BlockSpec(second.shape, whole),
        ],
        out_specs=[rows(inner), rows(width), pl.BlockSpec((images, width), whole)],
        name="forward",
    )(acts, first, second)


def head_kernel(pix, pooled_ref, aux_ref, labels_ref, aux_pre_ref, sent_ref):
    groups, images, _ = sent_ref.shape
    width, head = aux_ref.shape
    part = width // groups
    mean = (pooled_ref[...] / pix).astype(BF16)
    aux_pre = dot(mean, aux_ref[...])
    aux_pre_ref[...] = aux_pre
    out = jnp.maximum(aux_pre, 0.0).astype(BF16)
    row = lax.broadcasted_iota(jnp.int32, (images, LANES), 0)
    lane = lax.broadcasted_iota(jnp.int32, (images, LANES), 1)
    digits = jnp.zeros((images, LANES), jnp.int32)
    for i in range(images):
        label = labels_ref[i]
        digits = jnp.where((row == i) & (lane == 0), label // LANES, digits)
        digits = jnp.where((row == i) & (lane == 1), label % LANES, digits)
    digits = digits.astype(F32).astype(BF16)
    for d in range(groups):
        sent_ref[d, :, :head] = out
        sent_ref[d, :, head : head + part] = mean[:, d * part : (d + 1) * part]
        sent_ref[d, :, head + LANES :] = digits


def aux_head(pooled, aux, labels, pix, groups):
    images, head = pooled.shape[0], aux.shape[1]
    return call(
        functools.partial(head_kernel, pix),
        [shape((images, head), F32), shape((groups, images, head + 2 * LANES), BF16)],
        limit=16,
        in_specs=[VMEM, VMEM, SMEM],
        name="aux_head",
    )(pooled, aux, labels)


def recon_kernel(feature_ref, decode_ref, recon_ref):
    feature = feature_ref[...]
    for at in range(0, recon_ref.shape[1], TILE):
        cut = slice(at, at + TILE)
        recon_ref[:, cut] = dot(feature, decode_ref[:, cut])


def reconstruct(feature, decode):
    rows, width = feature.shape
    n = decode.shape[1]
    block = lambda m: pl.BlockSpec((rows // STEPS, m), lambda g: (g, 0))
    return call(
        recon_kernel,
        shape((rows, n), F32),
        limit=57,
        flops=2 * rows * width * n,
        moved=rows * (2 * width + 4 * n),
        grid=(STEPS,),
        in_specs=[block(width), pl.BlockSpec(decode.shape, lambda g: (0, 0))],
        out_specs=block(n),
        name="reconstruct",
    )(feature, decode)


def own_index(h):
    per_half = STEPS // 2
    return lambda g, where: (jnp.clip(g - h * per_half, 0, per_half - 1), 0, 0)


def patch_operands(blocks, own_blocks, shared_blocks):
    args, specs = [], []
    for k in own_blocks:
        for h, half in enumerate(blocks[k]):
            dims = (half.shape[0] // 3,) + half.shape[1:]
            args.append(half)
            specs.append(pl.BlockSpec(dims, own_index(h)))
    for k in shared_blocks:
        for half in blocks[k]:
            dims = (half.shape[0] // 3,) + half.shape[1:]
            args.append(half)
            specs.append(pl.BlockSpec(dims, lambda g, where: (2, 0, 0)))
    return args, specs


def lay_target(step, where_ref, refs, target):
    if len(refs) == 1:
        target[...] = refs[0][...]
        return
    pairs = [refs[j : j + 2] for j in range(0, len(refs), 2)]
    own, shared = pairs[: len(pairs) // 2], pairs[len(pairs) // 2 :]
    per_half = STEPS // 2
    lanes = lambda j: pl.ds(pl.multiple_of(where_ref[TILES + j] * LANES, LANES), LANES)
    for h in range(2):

        @pl.when(step // per_half == h)
        def _():
            for k, pair in enumerate(own):
                target[:, :, lanes(2 * k)] = pair[h][...]

    for g in range(STEPS):
        for parity in range(2):

            @pl.when((step == g) & (where_ref[PARITY] == parity))
            def _():
                h, side = g // per_half, g % per_half
                for k in range(0, len(shared), 2):
                    even, odd = shared[k + parity][h][...].astype(F32), shared[k + 1 - parity][h][...].astype(F32)
                    lane = lax.broadcasted_iota(jnp.int32, even.shape, 2)
                    value = jnp.where((lane < 64) == (side == 0), even, odd)
                    if side:
                        value = jnp.concatenate([value[:, :, 64:], value[:, :, :64]], axis=2)
                    target[:, :, lanes(2 * k + 1)] = value.astype(BF16)


def deal(where_ref, sums, part, keep_ref, send_ref):
    core = where_ref[CORE]
    at = 0
    for value in sums:
        height = value.shape[0]
        for z in range(keep_ref.shape[0]):
            even = value[:, 2 * z * part : (2 * z + 1) * part]
            odd = value[:, (2 * z + 1) * part : (2 * z + 2) * part]
            mine = jnp.where(core == 0, even, odd)
            other = jnp.where(core == 0, odd, even)
            keep_ref[z, at : at + height, :] = mine.astype(BF16)
            send_ref[z, at : at + height, :] = other.astype(BF16)
        at += height


def fetch(source, held, sems, step):
    size = held.shape[0] // STEPS
    copies = [
        pltpu.make_async_copy(source.at[pl.ds(g * size, size)], held.at[pl.ds(g * size, size)], sems.at[g])
        for g in range(STEPS)
    ]

    @pl.when(step == 0)
    def _():
        for copy in copies:
            copy.start()

    for g in range(STEPS):

        @pl.when(step == g)
        def _():
            copies[g].wait()


def fetch(source, held, sems, step):
    size = held.shape[0] // STEPS
    copies = [
        pltpu.make_async_copy(source.at[pl.ds(g * size, size)], held.at[pl.ds(g * size, size)], sems.at[g])
        for g in range(STEPS)
    ]

    @pl.when(step == 0)
    def _():
        for copy in copies:
            copy.start()

    for g in range(STEPS):

        @pl.when(step == g)
        def _():
            copies[g].wait()


def contract(step, rows, pairs):
    unit = rows // STEPS // TILE * TILE
    for g in range(STEPS):

        @pl.when(step == g)
        def _():
            span = slice(g * unit, rows if g == STEPS - 1 else (g + 1) * unit)
            for total, left, right in pairs:
                now = dot(left[span], right[span], ROWS_0)
                total[...] = now if g == 0 else total[...] + now


def residual_kernel(groups, scale, n_patch, where_ref, feature_ref, recon_ref, *refs):
    patch_refs, refs = refs[:n_patch], refs[n_patch:]
    grad_ref, keep_ref, send_ref, target, feature, grads, total, sems = refs
    step = pl.program_id(0)
    rows, width = feature.shape
    size = grad_ref.shape[0]
    fetch(feature_ref, feature, sems, step)
    lay_target(step, where_ref, patch_refs, target)
    grad = ((recon_ref[...] - target[...].reshape(recon_ref.shape).astype(F32)) * scale).astype(BF16)
    grad_ref[...] = grad
    grads[pl.ds(pl.multiple_of(step * size, size), size)] = grad
    contract(step, rows, [(total, grads, feature)])

    @pl.when(step == STEPS - 1)
    def _():
        deal(where_ref, [total], width // groups, keep_ref, send_ref)


def residual(where, feature, recon, patch_args, patch_specs, images, scale, groups):
    rows, width = feature.shape
    n = recon.shape[1]
    size = rows // STEPS
    parts = (groups // 2, n, width // groups)
    dealt = pl.BlockSpec(parts, lambda g, where: (0, 0, 0))
    block = pl.BlockSpec((size, n), lambda g, where: (g, 0))
    return call(
        functools.partial(residual_kernel, groups, scale, len(patch_args)),
        [shape((rows, n), BF16), shape(parts, BF16), shape(parts, BF16)],
        limit=48,
        flops=2 * rows * width * n,
        moved=rows * (2 * width + 6 * n),
        grid_spec=pltpu.PrefetchScalarGridSpec(
            num_scalar_prefetch=1,
            grid=(STEPS,),
            in_specs=[HBM, block, *patch_specs],
            out_specs=[block, dealt, dealt],
            scratch_shapes=[
                pltpu.VMEM((size // images, images, n), BF16),
                pltpu.VMEM((rows, width), BF16),
                pltpu.VMEM((rows, n), BF16),
                pltpu.VMEM((n, width), F32),
                pltpu.SemaphoreType.DMA((STEPS,)),
            ],
        ),
        name="residual",
    )(where, feature, recon, *patch_args)


def backward_kernel(
    groups, where_ref, grad_ref, hidden_ref, acts_ref, decode_ref, pooled_ref, second_ref,
    keep_ref, send_ref, hidden, acts, feature_grads, hidden_grads, total_second, total_first, sems,
):
    step = pl.program_id(0)
    rows, width = feature_grads.shape
    size = grad_ref.shape[0]
    images = pooled_ref.shape[0]
    fetch(hidden_ref, hidden, sems.at[0], step)
    fetch(acts_ref, acts, sems.at[1], step)
    here = pl.ds(pl.multiple_of(step * size, size), size)
    grad = grad_ref[...]
    for at in range(0, width, TILE):
        cut = slice(at, at + TILE)
        back = dot(grad, decode_ref[cut, :], COLS_1).reshape(size // images, images, TILE)
        feature_grads[here, cut] = (back + pooled_ref[:, cut][None]).astype(BF16).reshape(size, TILE)
    hidden_back = dot(feature_grads[here], second_ref[...], COLS_1)
    hidden_grads[here] = jnp.where(hidden[here].astype(F32) > 0, hidden_back, 0.0).astype(BF16)
    contract(step, rows, [(total_second, hidden, feature_grads), (total_first, hidden_grads, acts)])

    @pl.when(step == STEPS - 1)
    def _():
        part = width // groups
        tall = total_second.shape[0] // groups
        second = jnp.concatenate(
            [
                jnp.concatenate(
                    [total_second[d * tall : (d + 1) * tall, q * part : (q + 1) * part] for q in range(groups)], axis=0
                )
                for d in range(groups)
            ],
            axis=1,
        )
        deal(where_ref, [second, total_first], part, keep_ref, send_ref)


def backward(where, grad, hidden, acts, decode, pooled, second, groups):
    rows, width = acts.shape
    inner, n = hidden.shape[1], grad.shape[1]
    size = rows // STEPS
    parts = (groups // 2, 2 * inner, width // groups)
    dealt = pl.BlockSpec(parts, lambda g, where: (0, 0, 0))
    whole = lambda array: pl.BlockSpec(array.shape, lambda g, where: (0, 0))
    return call(
        functools.partial(backward_kernel, groups),
        [shape(parts, BF16), shape(parts, BF16)],
        limit=44,
        flops=2 * rows * width * (n + 3 * inner),
        moved=2 * rows * (width + n + inner),
        grid_spec=pltpu.PrefetchScalarGridSpec(
            num_scalar_prefetch=1,
            grid=(STEPS,),
            in_specs=[
                pl.BlockSpec((size, n), lambda g, where: (g, 0)),
                HBM,
                HBM,
                whole(decode),
                whole(pooled),
                whole(second),
            ],
            out_specs=[dealt, dealt],
            scratch_shapes=[
                pltpu.VMEM((rows, inner), BF16),
                pltpu.VMEM((rows, width), BF16),
                pltpu.VMEM((rows, width), BF16),
                pltpu.VMEM((rows, inner), BF16),
                pltpu.VMEM((inner, width), F32),
                pltpu.VMEM((inner, width), F32),
                pltpu.SemaphoreType.DMA((2, STEPS)),
            ],
        ),
        name="backward",
    )(where, grad, hidden, acts, decode, pooled, second)


TOPS, DENOMS = 3, 19
DIGIT = 40


def to_digits(value):
    rest, lanes = value, []
    for _ in range(3):
        digit = rest.astype(BF16).astype(F32)
        lanes.append(digit[:, :DIGIT])
        rest = rest - digit
    lanes.append(jnp.zeros((value.shape[0], LANES - 3 * DIGIT), F32))
    return jnp.concatenate(lanes, axis=1).astype(BF16)


def from_digits(value):
    value = value.astype(F32)
    return sum(value[:, j * DIGIT : (j + 1) * DIGIT] for j in (2, 1, 0))


def labels_of(got, head):
    digits = got[:, head + LANES : head + LANES + 2].astype(F32)
    return (digits[:, 0:1] * LANES + digits[:, 1:2]).astype(jnp.int32)


def logits_kernel(where_ref, got_ref, klass_ref, logits_ref, sent_ref):
    groups, images, _ = got_ref.shape
    classes, head = klass_ref.shape
    got = got_ref[...].reshape(groups * images, -1)
    logits = dot(got[:, :head], klass_ref[...], COLS_1)
    logits_ref[...] = logits
    ids = lax.broadcasted_iota(jnp.int32, logits.shape, 1) + where_ref[ME] * classes
    hit = labels_of(got, head) == ids
    top = jnp.max(logits, axis=1, keepdims=True)
    expo = jnp.exp(logits - top)
    denom = jnp.sum(expo, axis=1, keepdims=True)
    own = jnp.sum(jnp.where(hit, expo, 0.0), axis=1, keepdims=True)
    rest = jnp.where(hit, 0.0, expo).astype(BF16)
    onehot = jnp.where(hit, 1.0, 0.0).astype(BF16)
    sent_ref[:, :, :head] = dot(rest, klass_ref[...]).astype(BF16).reshape(groups, images, head)
    sent_ref[:, :, head : 2 * head] = dot(onehot, klass_ref[...]).astype(BF16).reshape(groups, images, head)
    lane = lax.broadcasted_iota(jnp.int32, (images, LANES), 1)
    cut = lambda value, d: value[d * images : (d + 1) * images]
    common = jnp.zeros((images, LANES), F32)
    for d in range(groups):
        common = jnp.where(lane == TOPS + d, cut(top, d), common)
        common = jnp.where(lane == DENOMS + d, cut(denom, d), common)
    for d in range(groups):
        stats = jnp.where(lane == 1, cut(denom, d), jnp.where(lane == 2, cut(own, d), common))
        sent_ref[d, :, 2 * head :] = to_digits(jnp.where(lane == 0, cut(top, d), stats))


def class_logits(where, got, klass):
    groups, images, _ = got.shape
    classes, head = klass.shape
    return call(
        logits_kernel,
        [shape((groups * images, classes), F32), shape((groups, images, 2 * head + LANES), BF16)],
        limit=16,
        in_specs=[SMEM, VMEM, VMEM],
        name="class_logits",
    )(where, got, klass)


def aux_kernel(pix, norm, got_ref, aux_pre_ref, aux_ref, pooled_ref, grad_ref):
    groups = got_ref.shape[0]
    head = aux_pre_ref.shape[1]
    stats = [from_digits(got_ref[d, :, 2 * head :]) for d in range(groups)]
    top = functools.reduce(jnp.maximum, [s[:, 0:1] for s in stats])
    scales = [jnp.exp(s[:, 0:1] - top) for s in stats]
    denom = sum(s[:, 1:2] * f for s, f in zip(stats, scales))
    own = sum(s[:, 2:3] * f for s, f in zip(stats, scales)) / denom
    rest = sum(got_ref[d, :, :head].astype(F32) * scales[d] for d in range(groups)) / (denom * norm)
    row = sum(got_ref[d, :, head : 2 * head].astype(F32) for d in range(groups))
    back = rest + row * ((own - 1.0) / norm).astype(BF16).astype(F32)
    aux_grad = jnp.where(aux_pre_ref[...] > 0, back, 0.0).astype(BF16)
    pooled_ref[...] = dot(aux_grad, aux_ref[...], COLS_1) / pix
    images, part = aux_grad.shape[0], grad_ref.shape[1]
    for q in range(head // part):
        grad_ref[q * images : (q + 1) * images, :] = aux_grad[:, q * part : (q + 1) * part]


def aux_backward(got, aux_pre, aux, pix, norm):
    groups, images, _ = got.shape
    width, head = aux.shape
    part = width // groups
    return call(
        functools.partial(aux_kernel, pix, norm),
        [shape((images, width), F32), shape((images * head // part, part), BF16)],
        limit=16,
        flops=2e10,
        name="aux_backward",
    )(got, aux_pre, aux)


def class_kernel(norm, n, where_ref, logits_ref, got_ref, stats_ref, *refs):
    grads_refs, (class_ref, aux_ref) = refs[:-2], refs[-2:]
    groups, images, _ = got_ref.shape
    head = class_ref.shape[1]
    classes, part = class_ref.shape[0], aux_ref.shape[0]
    got = got_ref[...].reshape(groups * images, -1)
    stats = [from_digits(stats_ref[e]) for e in range(groups)]
    tops, denoms = [], []
    for d in range(groups):
        top = functools.reduce(jnp.maximum, [s[:, TOPS + d : TOPS + d + 1] for s in stats])
        tops.append(top)
        denoms.append(sum(s[:, DENOMS + d : DENOMS + d + 1] * jnp.exp(s[:, TOPS + d : TOPS + d + 1] - top) for s in stats))
    top, denom = jnp.concatenate(tops, axis=0), jnp.concatenate(denoms, axis=0)
    logits = logits_ref[...]
    ids = lax.broadcasted_iota(jnp.int32, logits.shape, 1) + where_ref[ME] * classes
    onehot = jnp.where(labels_of(got, head) == ids, 1.0, 0.0)
    logit_grad = ((jnp.exp(logits - top) / denom - onehot) / norm).astype(BF16)
    class_ref[...] = dot(logit_grad, got[:, :head], ROWS_0)
    total = jnp.zeros(aux_ref.shape, F32)
    for d in range(groups):
        k, core = d // 2, d % 2
        at = n + core * (head // part) * images
        grad = jnp.concatenate(
            [grads_refs[k][at + q * images : at + (q + 1) * images, :] for q in range(head // part)], axis=1
        )
        pooled = got_ref[((where_ref[ME] >> 1) ^ k) * 2 + core, :, head : head + part]
        total += dot(pooled, grad, ROWS_0).astype(BF16).astype(F32)
    aux_ref[...] = total


def class_backward(where, logits, got, partial, grads, n_decode, classes, head, norm):
    groups, images, wide = partial.shape
    whole = lambda *dims: pl.BlockSpec(dims, lambda i: (0,) * len(dims))
    part = grads[0].shape[1]
    return call(
        functools.partial(class_kernel, norm, n_decode),
        [shape((classes, head), F32), shape((part, head), F32)],
        limit=20,
        flops=2 * groups * images * classes * head,
        moved=4 * classes * head,
        grid=(1,),
        in_specs=[
            SMEM,
            whole(*logits.shape),
            whole(*got.shape),
            pl.BlockSpec((groups, images, LANES), lambda i: (0, 0, wide // LANES - 1)),
            *[whole(*g.shape) for g in grads],
        ],
        out_specs=[whole(classes, head), whole(part, head)],
        name="class_backward",
    )(where, logits, got, partial, *grads)


def chip_kernel(n_extra, where_ref, keep_ref, got_ref, *refs):
    extra, outs = refs[:n_extra], refs[n_extra:]
    n = keep_ref.shape[1]
    chip = where_ref[ME] >> 1
    for k, out_ref in enumerate(outs):
        out_ref[:n] = (keep_ref[chip ^ k].astype(F32) + got_ref[chip ^ k].astype(F32)).astype(BF16)
    if n_extra:
        mine, other = extra[0][...].astype(F32), extra[1][...].astype(F32)
        even = where_ref[CORE] == 0
        pair = [jnp.where(even, mine, other).astype(BF16), jnp.where(even, other, mine).astype(BF16)]
        size = mine.shape[0]
        for out_ref in outs:
            for c in range(2):
                out_ref[n + c * size : n + (c + 1) * size] = pair[c]


def add_cores(where, keep, send, extra=()):
    chips, n, part = keep.shape
    extra = [e for own in extra for e in (own, swap(own, "dp", 1))]
    rows = n + sum(e.shape[0] for e in extra)
    return call(
        functools.partial(chip_kernel, len(extra)),
        [shape((rows, part), BF16)] * chips,
        limit=16,
        in_specs=[SMEM, VMEM, VMEM, *[VMEM] * len(extra)],
        name="add_cores",
    )(where, keep, swap(send, "dp", 1), *extra)


def exchange_chips(parts):
    return [parts[0]] + [swap(part, "dp", 2 * k) for k, part in enumerate(parts) if k]


def finish_kernel(inner, chips, *refs):
    early, last, (first_ref, second_ref, decode_ref) = refs[:chips], refs[chips : 2 * chips], refs[2 * chips :]
    n = decode_ref.shape[1]
    total = sum(ref[...].astype(F32) for ref in last)
    first_ref[...] = total[inner:].T
    tall, part = second_ref.shape[0], total.shape[1]
    for q in range(inner // tall):
        second_ref[:, q * part : (q + 1) * part] = total[q * tall : (q + 1) * tall]
    decode_ref[...] = sum(ref[:n].astype(F32) for ref in early).T


def finish(early, last, inner, groups, n):
    part = early[0].shape[1]
    return call(
        functools.partial(finish_kernel, inner, len(early)),
        [shape((part, inner), F32), shape((inner // groups, part * groups), F32), shape((part, n), F32)],
        limit=16,
        name="finish",
    )(*early, *last)


def local(acts, patches, labels, w_first, w_second, w_decode, w_aux, w_class):
    acts = acts[0].transpose(1, 0, 2)
    pix, images, width = acts.shape
    groups, count = lax.axis_size("dp"), lax.axis_size("section")
    me, section = lax.axis_index("dp"), lax.axis_index("section")
    scale = (groups * images * pix) ** -0.5
    norm = (groups * images) ** 0.5
    first, second, decode, aux, klass = w_first[0], w_second[0], w_decode[0], w_aux[0], w_class[0]
    inner, head = first.shape[1], aux.shape[1]
    n_decode = decode.shape[1]
    rows = pix * images

    paired = count == 4 and patches.shape[2] == 192
    if paired:
        near = [section ^ k for k in range(4)]
        tiles = [t for s in near for t in (3 * (s >> 1) + 2 * (s & 1), 3 * (s >> 1) + 1)]
        where = jnp.stack([section & 1, me & 1, me, *tiles]).astype(jnp.int32)
        turned = patches.transpose(0, 2, 1)
        halves = [pack(where, turned, h) for h in range(2)]
        x, y = [swap(halves[0], "section", 1)], [swap(halves[0], "section", 2)]
        first = after(first, halves[1])
        labels = after(labels, (x[0], y[0]))
    else:
        where = jnp.stack([section & 1, me & 1, me]).astype(jnp.int32)
        target = lax.all_gather(patches, "section", axis=2, tiled=True).transpose(1, 0, 2)

    hidden, feature, pooled = forward(acts, first, second)
    aux_pre, sent = aux_head(pooled, aux, labels, pix, groups)
    got = exchange(sent)
    recon = reconstruct(after(feature, sent), decode)
    if paired:
        last = after(halves[1], pooled)
        x.append(swap(last, "section", 1))
        y.append(swap(last, "section", 2))
        diagonal = [swap(after(y[0], aux_pre), "section", 1), swap(after(x[1], recon), "section", 2)]
        blocks = [halves, x, y, diagonal]
        target = patch_operands(blocks, [0, 1, 2, 3], [0, 1, 2, 3])
    else:
        target = [target], [pl.BlockSpec((pix // STEPS, images, n_decode), lambda g, where: (g, 0, 0))]
    logits, sent = class_logits(where, after(got, recon), klass)
    partial = exchange(sent)
    grad, keep, send = residual(after(where, sent), feature, recon, *target, images, scale, groups)
    pooled_grad, aux_grad = aux_backward(partial, aux_pre, aux, pix, norm)
    chip_decode = add_cores(where, keep, send, [aux_grad])
    sum_decode = exchange_chips(chip_decode)
    keep, send = backward(
        where, grad, hidden, acts.reshape(rows, width), decode, after(pooled_grad, chip_decode[0]), second, groups
    )
    sum_last = exchange_chips(add_cores(where, keep, after(send, sum_decode)))
    grad_class, grad_aux = class_backward(
        where, logits, got, partial, sum_decode, n_decode, klass.shape[0], head, norm
    )
    grad_first, grad_second, grad_decode = finish(sum_decode, sum_last, inner, groups, n_decode)
    return grad_first[None], grad_second[None], grad_decode[None], grad_aux[None], grad_class[None]


def solution(mesh):
    in_specs = (
        P("section", "dp", None, None),
        P("dp", None, "section"),
        P("dp"),
        P("section", None, None),
        P("section", None, None),
        P("section", None, None),
        P("section", None, None),
        P("section", "dp", None),
    )
    out_specs = (P("section", "dp", None),) * 5
    return jax.shard_map(local, mesh=mesh, in_specs=in_specs, out_specs=out_specs, check_vma=False)
```

```python
import functools

import jax
import jax.numpy as jnp
from jax import lax
from jax.experimental import pallas as pl
from jax.experimental.pallas import tpu as pltpu
from jax.sharding import PartitionSpec as P

F32 = jnp.float32
BF16 = jnp.bfloat16
STEPS = 4
LANES = 128
TILE = 256
MIB = 1024 * 1024
ROWS_0 = (((0,), (0,)), ((), ()))
COLS_1 = (((1,), (1,)), ((), ()))
PARITY, CORE, ME, TILES = 0, 1, 2, 3


def dot(left, right, dims=(((1,), (0,)), ((), ()))):
    return lax.dot_general(left, right, dims, preferred_element_type=F32)


def call(kernel, out_shape, *, limit, flops=0, moved=0, **kwargs):
    return pl.pallas_call(
        kernel,
        out_shape=out_shape,
        compiler_params=pltpu.CompilerParams(vmem_limit_bytes=limit * MIB),
        cost_estimate=pl.CostEstimate(flops=int(flops), bytes_accessed=int(moved), transcendentals=0),
        **kwargs,
    )


def shape(dims, kind):
    return jax.ShapeDtypeStruct(dims, kind)


SMEM = pl.BlockSpec(memory_space=pltpu.SMEM)
VMEM = pl.BlockSpec(memory_space=pltpu.VMEM)
HBM = pl.BlockSpec(memory_space=pltpu.HBM)


def swap(value, axis, bits):
    count = lax.axis_size(axis)
    return lax.ppermute(value, axis, [(i, i ^ bits) for i in range(count)])


def exchange(value, groups=None):
    return lax.all_to_all(value, "dp", 0, 0, axis_index_groups=groups, tiled=True)


def pack_kernel(first, where_ref, patches_ref, out_ref, turned, own, shared):
    images, span, pix = patches_ref.shape
    padded = turned.shape[1]
    count = out_ref.shape[0] // 3 * 2
    parity = where_ref[PARITY]
    at_own = pl.multiple_of(64 * parity, 64)
    at_shared = pl.multiple_of(128 * (1 - parity), 64)
    row = lax.broadcasted_iota(jnp.int32, (padded, pix), 0)
    column = lax.broadcasted_iota(jnp.int32, (padded, pix), 1)
    pick = ((row < count) & (column == row + first)).astype(F32).astype(BF16)
    for i in range(images):
        turned[i, :, :LANES] = dot(pick, patches_ref[i, pl.ds(at_own, LANES), :], COLS_1).astype(BF16)
        turned[i, :, LANES:] = dot(pick, patches_ref[i, pl.ds(at_shared, 64), :], COLS_1).astype(BF16)
    size = 16 * images
    row = lax.broadcasted_iota(jnp.int32, (size, size), 0)
    column = lax.broadcasted_iota(jnp.int32, (size, size), 1)
    order = (row // images == column % 16) & (row % images == column // 16)
    order = order.astype(F32).astype(BF16)
    for b in range(padded // 16):
        rows = turned[:, 16 * b : 16 * b + 16, :].reshape(size, span)
        out = dot(order, rows).astype(BF16)
        own[16 * b : 16 * b + 16] = out[:, :LANES].reshape(16, images, LANES)
        shared[16 * b : 16 * b + 16] = out[:, LANES:].reshape(16, images, 64)
    out_ref[:count] = own[:count]
    lower, upper = shared[: count // 2], shared[count // 2 : count]

    @pl.when(parity == 0)
    def _():
        out_ref[count:] = jnp.concatenate([lower, upper], axis=2)

    @pl.when(parity == 1)
    def _():
        out_ref[count:] = jnp.concatenate([upper, lower], axis=2)


def pack(where, patches, h):
    images, span, pix = patches.shape
    half = pix // 2
    padded = -(-half // 16) * 16
    return call(
        functools.partial(pack_kernel, h * half),
        shape((half + half // 2, images, LANES), BF16),
        limit=20,
        in_specs=[SMEM, VMEM],
        scratch_shapes=[
            pltpu.VMEM((images, padded, span), BF16),
            pltpu.VMEM((padded, images, LANES), BF16),
            pltpu.VMEM((padded, images, 64), BF16),
        ],
        name="pack_patches",
    )(where, patches)


def after(value, other):
    return lax.optimization_barrier((value, other))[0]


def forward_kernel(n_tiles, *refs):
    acts_refs, refs = refs[:n_tiles], refs[n_tiles:]
    first_ref, second_ref, hidden_ref = refs[:3]
    feature_refs, pooled_ref = refs[3:-1], refs[-1]
    step = pl.program_id(0)
    block, images, _ = acts_refs[0].shape
    flat = jnp.concatenate([ref[...].reshape(block * images, TILE) for ref in acts_refs], axis=1)
    hidden = jnp.maximum(dot(flat, first_ref[...]), 0.0).astype(BF16)
    hidden_ref[...] = hidden

    @pl.when(step == 0)
    def _():
        pooled_ref[...] = jnp.zeros(pooled_ref.shape, F32)

    for j, feature_ref in enumerate(feature_refs):
        cut = slice(j * TILE, (j + 1) * TILE)
        feature = (flat[:, cut].astype(F32) + dot(hidden, second_ref[:, cut])).astype(BF16)
        feature_ref[...] = feature
        pooled_ref[:, cut] += jnp.sum(feature.reshape(block, images, TILE).astype(F32), axis=0)


def forward(acts, first, second):
    pix, images, width = acts.shape
    inner = first.shape[1]
    block = pix // STEPS
    whole = lambda g: (0, 0)
    rows = lambda n: pl.BlockSpec((block * images, n), lambda g: (g, 0))
    n_tiles = width // TILE
    column = lambda j: pl.BlockSpec((block, images, TILE), lambda g: (g, 0, j))
    hidden, *feature, pooled = call(
        functools.partial(forward_kernel, n_tiles),
        [
            shape((pix * images, inner), BF16),
            *[shape((pix * images, TILE), BF16)] * n_tiles,
            shape((images, width), F32),
        ],
        limit=58,
        flops=4 * pix * images * width * inner,
        moved=2 * pix * images * (2 * width + inner),
        grid=(STEPS,),
        in_specs=[
            *[column(j) for j in range(n_tiles)],
            pl.BlockSpec(first.shape, whole),
            pl.BlockSpec(second.shape, whole),
        ],
        out_specs=[rows(inner), *[rows(TILE)] * n_tiles, pl.BlockSpec((images, width), whole)],
        name="forward",
    )(*[acts] * n_tiles, first, second)
    return hidden, feature, pooled


def head_kernel(pix, pooled_ref, aux_ref, labels_ref, aux_pre_ref, sent_ref):
    groups, images, _ = sent_ref.shape
    width, head = aux_ref.shape
    part = width // groups
    mean = (pooled_ref[...] / pix).astype(BF16)
    aux_pre = dot(mean, aux_ref[...])
    aux_pre_ref[...] = aux_pre
    out = jnp.maximum(aux_pre, 0.0).astype(BF16)
    row = lax.broadcasted_iota(jnp.int32, (images, LANES), 0)
    lane = lax.broadcasted_iota(jnp.int32, (images, LANES), 1)
    digits = jnp.zeros((images, LANES), jnp.int32)
    for i in range(images):
        label = labels_ref[i]
        digits = jnp.where((row == i) & (lane == 0), label // LANES, digits)
        digits = jnp.where((row == i) & (lane == 1), label % LANES, digits)
    digits = digits.astype(F32).astype(BF16)
    for d in range(groups):
        sent_ref[d, :, :head] = out
        sent_ref[d, :, head : head + part] = mean[:, d * part : (d + 1) * part]
        sent_ref[d, :, head + LANES :] = digits


def aux_head(pooled, aux, labels, pix, groups):
    images, head = pooled.shape[0], aux.shape[1]
    return call(
        functools.partial(head_kernel, pix),
        [shape((images, head), F32), shape((groups, images, head + 2 * LANES), BF16)],
        limit=16,
        in_specs=[VMEM, VMEM, SMEM],
        name="aux_head",
    )(pooled, aux, labels)


def recon_kernel(n_feature, *refs):
    feature_refs, decode_ref, recon_refs = refs[:n_feature], refs[n_feature], refs[n_feature + 1 :]
    feature = jnp.concatenate([ref[...] for ref in feature_refs], axis=1)
    for j, recon_ref in enumerate(recon_refs):
        recon_ref[...] = dot(feature, decode_ref[:, j * TILE : (j + 1) * TILE])


def reconstruct(feature, decode):
    rows = feature[0].shape[0]
    width, n = decode.shape
    block = pl.BlockSpec((rows // STEPS, TILE), lambda g: (g, 0))
    return call(
        functools.partial(recon_kernel, len(feature)),
        [shape((rows, TILE), F32)] * (n // TILE),
        limit=57,
        flops=2 * rows * width * n,
        moved=rows * (2 * width + 4 * n),
        grid=(STEPS,),
        in_specs=[*[block] * len(feature), pl.BlockSpec(decode.shape, lambda g: (0, 0))],
        out_specs=[block] * (n // TILE),
        name="reconstruct",
    )(*feature, decode)


def own_index(h):
    per_half = STEPS // 2
    return lambda g, where: (jnp.clip(g - h * per_half, 0, per_half - 1), 0, 0)


def patch_operands(blocks, own_blocks, shared_blocks):
    args, specs = [], []
    for k in own_blocks:
        for h, half in enumerate(blocks[k]):
            dims = (half.shape[0] // 3,) + half.shape[1:]
            args.append(half)
            specs.append(pl.BlockSpec(dims, own_index(h)))
    for k in shared_blocks:
        for half in blocks[k]:
            dims = (half.shape[0] // 3,) + half.shape[1:]
            args.append(half)
            specs.append(pl.BlockSpec(dims, lambda g, where: (2, 0, 0)))
    return args, specs


def lay_target(step, where_ref, refs, target):
    if len(refs) == 1:
        target[...] = refs[0][...]
        return
    pairs = [refs[j : j + 2] for j in range(0, len(refs), 2)]
    own, shared = pairs[: len(pairs) // 2], pairs[len(pairs) // 2 :]
    per_half = STEPS // 2
    lanes = lambda j: pl.ds(pl.multiple_of(where_ref[TILES + j] * LANES, LANES), LANES)
    for h in range(2):

        @pl.when(step // per_half == h)
        def _():
            for k, pair in enumerate(own):
                target[:, :, lanes(2 * k)] = pair[h][...]

    for g in range(STEPS):
        for parity in range(2):

            @pl.when((step == g) & (where_ref[PARITY] == parity))
            def _():
                h, side = g // per_half, g % per_half
                for k in range(0, len(shared), 2):
                    even, odd = shared[k + parity][h][...].astype(F32), shared[k + 1 - parity][h][...].astype(F32)
                    lane = lax.broadcasted_iota(jnp.int32, even.shape, 2)
                    value = jnp.where((lane < 64) == (side == 0), even, odd)
                    if side:
                        value = jnp.concatenate([value[:, :, 64:], value[:, :, :64]], axis=2)
                    target[:, :, lanes(2 * k + 1)] = value.astype(BF16)


def deal(where_ref, sums, part, keep_ref, send_ref):
    core = where_ref[CORE]
    at = 0
    for value in sums:
        height = value.shape[0]
        for z in range(keep_ref.shape[0]):
            even = value[:, 2 * z * part : (2 * z + 1) * part]
            odd = value[:, (2 * z + 1) * part : (2 * z + 2) * part]
            mine = jnp.where(core == 0, even, odd)
            other = jnp.where(core == 0, odd, even)
            keep_ref[z, at : at + height, :] = mine.astype(BF16)
            send_ref[z, at : at + height, :] = other.astype(BF16)
        at += height


def fetch(sources, held, sems, step):
    size, wide = held.shape[0] // STEPS, sources[0].shape[1]
    copies = [
        [
            pltpu.make_async_copy(
                source.at[pl.ds(g * size, size)], held.at[pl.ds(g * size, size), pl.ds(j * wide, wide)], sems.at[g, j]
            )
            for j, source in enumerate(sources)
        ]
        for g in range(STEPS)
    ]

    @pl.when(step == 0)
    def _():
        for several in copies:
            for copy in several:
                copy.start()

    for g in range(STEPS):

        @pl.when(step == g)
        def _():
            for copy in copies[g]:
                copy.wait()


def contract(step, rows, pairs):
    unit = rows // STEPS // TILE * TILE
    for g in range(STEPS):

        @pl.when(step == g)
        def _():
            span = slice(g * unit, rows if g == STEPS - 1 else (g + 1) * unit)
            for total, left, right in pairs:
                now = dot(left[span], right[span], ROWS_0)
                total[...] = now if g == 0 else total[...] + now


def residual_kernel(groups, scale, n_feature, n_recon, n_patch, where_ref, *refs):
    feature_refs, refs = refs[:n_feature], refs[n_feature:]
    recon_refs, refs = refs[:n_recon], refs[n_recon:]
    patch_refs, refs = refs[:n_patch], refs[n_patch:]
    grad_refs, refs = refs[:n_recon], refs[n_recon:]
    keep_ref, send_ref, target, feature, grads, total, sems = refs
    step = pl.program_id(0)
    rows, width = feature.shape
    size = recon_refs[0].shape[0]
    fetch(feature_refs, feature, sems, step)
    lay_target(step, where_ref, patch_refs, target)
    for j, (recon_ref, grad_ref) in enumerate(zip(recon_refs, grad_refs)):
        cut = slice(j * TILE, (j + 1) * TILE)
        grad = ((recon_ref[...] - target[:, :, cut].reshape(size, TILE).astype(F32)) * scale).astype(BF16)
        grad_ref[...] = grad
        grads[pl.ds(pl.multiple_of(step * size, size), size), cut] = grad
    contract(step, rows, [(total, grads, feature)])

    @pl.when(step == STEPS - 1)
    def _():
        deal(where_ref, [total], width // groups, keep_ref, send_ref)


def residual(where, feature, recon, patch_args, patch_specs, images, scale, groups):
    rows = feature[0].shape[0]
    width, n = len(feature) * TILE, len(recon) * TILE
    size = rows // STEPS
    parts = (groups // 2, n, width // groups)
    dealt = pl.BlockSpec(parts, lambda g, where: (0, 0, 0))
    block = pl.BlockSpec((size, TILE), lambda g, where: (g, 0))
    *grad, keep, send = call(
        functools.partial(residual_kernel, groups, scale, len(feature), len(recon), len(patch_args)),
        [*[shape((rows, TILE), BF16)] * len(recon), shape(parts, BF16), shape(parts, BF16)],
        limit=48,
        flops=2 * rows * width * n,
        moved=rows * (2 * width + 6 * n),
        grid_spec=pltpu.PrefetchScalarGridSpec(
            num_scalar_prefetch=1,
            grid=(STEPS,),
            in_specs=[*[HBM] * len(feature), *[block] * len(recon), *patch_specs],
            out_specs=[*[block] * len(recon), dealt, dealt],
            scratch_shapes=[
                pltpu.VMEM((size // images, images, n), BF16),
                pltpu.VMEM((rows, width), BF16),
                pltpu.VMEM((rows, n), BF16),
                pltpu.VMEM((n, width), F32),
                pltpu.SemaphoreType.DMA((STEPS, len(feature))),
            ],
        ),
        name="residual",
    )(where, *feature, *recon, *patch_args)
    return grad, keep, send


def backward_kernel(groups, n_grad, where_ref, *refs):
    grad_refs, refs = refs[:n_grad], refs[n_grad:]
    (hidden_ref, acts_ref, decode_ref, pooled_ref, second_ref, keep_ref, send_ref,
     hidden, acts, feature_grads, hidden_grads, total_second, total_first, sems) = refs
    step = pl.program_id(0)
    rows, width = feature_grads.shape
    size = grad_refs[0].shape[0]
    images = pooled_ref.shape[0]
    fetch([hidden_ref], hidden, sems.at[0], step)
    fetch([acts_ref], acts, sems.at[1], step)
    here = pl.ds(pl.multiple_of(step * size, size), size)
    grad = jnp.concatenate([ref[...] for ref in grad_refs], axis=1)
    for at in range(0, width, TILE):
        cut = slice(at, at + TILE)
        back = dot(grad, decode_ref[cut, :], COLS_1).reshape(size // images, images, TILE)
        feature_grads[here, cut] = (back + pooled_ref[:, cut][None]).astype(BF16).reshape(size, TILE)
    hidden_back = dot(feature_grads[here], second_ref[...], COLS_1)
    hidden_grads[here] = jnp.where(hidden[here].astype(F32) > 0, hidden_back, 0.0).astype(BF16)
    contract(step, rows, [(total_second, hidden, feature_grads), (total_first, hidden_grads, acts)])

    @pl.when(step == STEPS - 1)
    def _():
        part = width // groups
        tall = total_second.shape[0] // groups
        second = jnp.concatenate(
            [
                jnp.concatenate(
                    [total_second[d * tall : (d + 1) * tall, q * part : (q + 1) * part] for q in range(groups)], axis=0
                )
                for d in range(groups)
            ],
            axis=1,
        )
        deal(where_ref, [second, total_first], part, keep_ref, send_ref)


def backward(where, grad, hidden, acts, decode, pooled, second, groups):
    rows, width = acts.shape
    inner, n = hidden.shape[1], len(grad) * TILE
    size = rows // STEPS
    parts = (groups // 2, 2 * inner, width // groups)
    dealt = pl.BlockSpec(parts, lambda g, where: (0, 0, 0))
    whole = lambda array: pl.BlockSpec(array.shape, lambda g, where: (0, 0))
    return call(
        functools.partial(backward_kernel, groups, len(grad)),
        [shape(parts, BF16), shape(parts, BF16)],
        limit=44,
        flops=2 * rows * width * (n + 3 * inner),
        moved=2 * rows * (width + n + inner),
        grid_spec=pltpu.PrefetchScalarGridSpec(
            num_scalar_prefetch=1,
            grid=(STEPS,),
            in_specs=[
                *[pl.BlockSpec((size, TILE), lambda g, where: (g, 0))] * len(grad),
                HBM,
                HBM,
                whole(decode),
                whole(pooled),
                whole(second),
            ],
            out_specs=[dealt, dealt],
            scratch_shapes=[
                pltpu.VMEM((rows, inner), BF16),
                pltpu.VMEM((rows, width), BF16),
                pltpu.VMEM((rows, width), BF16),
                pltpu.VMEM((rows, inner), BF16),
                pltpu.VMEM((inner, width), F32),
                pltpu.VMEM((inner, width), F32),
                pltpu.SemaphoreType.DMA((2, STEPS, 1)),
            ],
        ),
        name="backward",
    )(where, *grad, hidden, acts, decode, pooled, second)


TOPS, DENOMS = 3, 19
DIGIT = 40


def to_digits(value):
    rest, lanes = value, []
    for _ in range(3):
        digit = rest.astype(BF16).astype(F32)
        lanes.append(digit[:, :DIGIT])
        rest = rest - digit
    lanes.append(jnp.zeros((value.shape[0], LANES - 3 * DIGIT), F32))
    return jnp.concatenate(lanes, axis=1).astype(BF16)


def from_digits(value):
    value = value.astype(F32)
    return sum(value[:, j * DIGIT : (j + 1) * DIGIT] for j in (2, 1, 0))


def labels_of(got, head):
    digits = got[:, head + LANES : head + LANES + 2].astype(F32)
    return (digits[:, 0:1] * LANES + digits[:, 1:2]).astype(jnp.int32)


def logits_kernel(where_ref, got_ref, klass_ref, logits_ref, sent_ref):
    groups, images, _ = got_ref.shape
    classes, head = klass_ref.shape
    got = got_ref[...].reshape(groups * images, -1)
    logits = dot(got[:, :head], klass_ref[...], COLS_1)
    logits_ref[...] = logits
    ids = lax.broadcasted_iota(jnp.int32, logits.shape, 1) + where_ref[ME] * classes
    hit = labels_of(got, head) == ids
    top = jnp.max(logits, axis=1, keepdims=True)
    expo = jnp.exp(logits - top)
    denom = jnp.sum(expo, axis=1, keepdims=True)
    own = jnp.sum(jnp.where(hit, expo, 0.0), axis=1, keepdims=True)
    rest = jnp.where(hit, 0.0, expo).astype(BF16)
    onehot = jnp.where(hit, 1.0, 0.0).astype(BF16)
    sent_ref[:, :, :head] = dot(rest, klass_ref[...]).astype(BF16).reshape(groups, images, head)
    sent_ref[:, :, head : 2 * head] = dot(onehot, klass_ref[...]).astype(BF16).reshape(groups, images, head)
    lane = lax.broadcasted_iota(jnp.int32, (images, LANES), 1)
    cut = lambda value, d: value[d * images : (d + 1) * images]
    common = jnp.zeros((images, LANES), F32)
    for d in range(groups):
        common = jnp.where(lane == TOPS + d, cut(top, d), common)
        common = jnp.where(lane == DENOMS + d, cut(denom, d), common)
    for d in range(groups):
        stats = jnp.where(lane == 1, cut(denom, d), jnp.where(lane == 2, cut(own, d), common))
        sent_ref[d, :, 2 * head :] = to_digits(jnp.where(lane == 0, cut(top, d), stats))


def class_logits(where, got, klass):
    groups, images, _ = got.shape
    classes, head = klass.shape
    return call(
        logits_kernel,
        [shape((groups * images, classes), F32), shape((groups, images, 2 * head + LANES), BF16)],
        limit=16,
        flops=2e10,
        in_specs=[SMEM, VMEM, VMEM],
        name="class_logits",
    )(where, got, klass)


def aux_kernel(pix, norm, got_ref, aux_pre_ref, aux_ref, pooled_ref, grad_ref):
    groups = got_ref.shape[0]
    head = aux_pre_ref.shape[1]
    stats = [from_digits(got_ref[d, :, 2 * head :]) for d in range(groups)]
    top = functools.reduce(jnp.maximum, [s[:, 0:1] for s in stats])
    scales = [jnp.exp(s[:, 0:1] - top) for s in stats]
    denom = sum(s[:, 1:2] * f for s, f in zip(stats, scales))
    own = sum(s[:, 2:3] * f for s, f in zip(stats, scales)) / denom
    rest = sum(got_ref[d, :, :head].astype(F32) * scales[d] for d in range(groups)) / (denom * norm)
    row = sum(got_ref[d, :, head : 2 * head].astype(F32) for d in range(groups))
    back = rest + row * ((own - 1.0) / norm).astype(BF16).astype(F32)
    aux_grad = jnp.where(aux_pre_ref[...] > 0, back, 0.0).astype(BF16)
    pooled_ref[...] = dot(aux_grad, aux_ref[...], COLS_1) / pix
    images, part = aux_grad.shape[0], grad_ref.shape[1]
    for q in range(head // part):
        grad_ref[q * images : (q + 1) * images, :] = aux_grad[:, q * part : (q + 1) * part]


def aux_backward(got, aux_pre, aux, pix, norm):
    groups, images, _ = got.shape
    width, head = aux.shape
    part = width // groups
    return call(
        functools.partial(aux_kernel, pix, norm),
        [shape((images, width), F32), shape((images * head // part, part), BF16)],
        limit=16,
        flops=2e10,
        name="aux_backward",
    )(got, aux_pre, aux)


def class_kernel(norm, n, where_ref, logits_ref, got_ref, stats_ref, *refs):
    grads_refs, (class_ref, aux_ref) = refs[:-2], refs[-2:]
    groups, images, _ = got_ref.shape
    head = class_ref.shape[1]
    classes, part = class_ref.shape[0], aux_ref.shape[0]
    got = got_ref[...].reshape(groups * images, -1)
    stats = [from_digits(stats_ref[e]) for e in range(groups)]
    tops, denoms = [], []
    for d in range(groups):
        top = functools.reduce(jnp.maximum, [s[:, TOPS + d : TOPS + d + 1] for s in stats])
        tops.append(top)
        denoms.append(sum(s[:, DENOMS + d : DENOMS + d + 1] * jnp.exp(s[:, TOPS + d : TOPS + d + 1] - top) for s in stats))
    top, denom = jnp.concatenate(tops, axis=0), jnp.concatenate(denoms, axis=0)
    logits = logits_ref[...]
    ids = lax.broadcasted_iota(jnp.int32, logits.shape, 1) + where_ref[ME] * classes
    onehot = jnp.where(labels_of(got, head) == ids, 1.0, 0.0)
    logit_grad = ((jnp.exp(logits - top) / denom - onehot) / norm).astype(BF16)
    class_ref[...] = dot(logit_grad, got[:, :head], ROWS_0)
    total = jnp.zeros(aux_ref.shape, F32)
    for d in range(groups):
        k, core = d // 2, d % 2
        at = n + core * (head // part) * images
        grad = jnp.concatenate(
            [grads_refs[k][at + q * images : at + (q + 1) * images, :] for q in range(head // part)], axis=1
        )
        pooled = got_ref[((where_ref[ME] >> 1) ^ k) * 2 + core, :, head : head + part]
        total += dot(pooled, grad, ROWS_0).astype(BF16).astype(F32)
    aux_ref[...] = total


def class_backward(where, logits, got, partial, grads, n_decode, classes, head, norm):
    groups, images, wide = partial.shape
    whole = lambda *dims: pl.BlockSpec(dims, lambda i: (0,) * len(dims))
    part = grads[0].shape[1]
    return call(
        functools.partial(class_kernel, norm, n_decode),
        [shape((classes, head), F32), shape((part, head), F32)],
        limit=20,
        flops=2 * groups * images * classes * head,
        moved=4 * classes * head,
        grid=(1,),
        in_specs=[
            SMEM,
            whole(*logits.shape),
            whole(*got.shape),
            pl.BlockSpec((groups, images, LANES), lambda i: (0, 0, wide // LANES - 1)),
            *[whole(*g.shape) for g in grads],
        ],
        out_specs=[whole(classes, head), whole(part, head)],
        name="class_backward",
    )(where, logits, got, partial, *grads)


def chip_kernel(n_extra, where_ref, keep_ref, got_ref, *refs):
    extra, outs = refs[:n_extra], refs[n_extra:]
    n = keep_ref.shape[1]
    chip = where_ref[ME] >> 1
    for k, out_ref in enumerate(outs):
        out_ref[:n] = (keep_ref[chip ^ k].astype(F32) + got_ref[chip ^ k].astype(F32)).astype(BF16)
    if n_extra:
        mine, other = extra[0][...].astype(F32), extra[1][...].astype(F32)
        even = where_ref[CORE] == 0
        pair = [jnp.where(even, mine, other).astype(BF16), jnp.where(even, other, mine).astype(BF16)]
        size = mine.shape[0]
        for out_ref in outs:
            for c in range(2):
                out_ref[n + c * size : n + (c + 1) * size] = pair[c]


def add_cores(where, keep, send, extra=()):
    chips, n, part = keep.shape
    extra = [e for own in extra for e in (own, swap(own, "dp", 1))]
    rows = n + sum(e.shape[0] for e in extra)
    return call(
        functools.partial(chip_kernel, len(extra)),
        [shape((rows, part), BF16)] * chips,
        limit=16,
        in_specs=[SMEM, VMEM, VMEM, *[VMEM] * len(extra)],
        name="add_cores",
    )(where, keep, swap(send, "dp", 1), *extra)


def exchange_chips(parts):
    return [parts[0]] + [swap(part, "dp", 2 * k) for k, part in enumerate(parts) if k]


def finish_kernel(inner, chips, *refs):
    early, last, (first_ref, second_ref, decode_ref) = refs[:chips], refs[chips : 2 * chips], refs[2 * chips :]
    n = decode_ref.shape[1]
    total = sum(ref[...].astype(F32) for ref in last)
    first_ref[...] = total[inner:].T
    tall, part = second_ref.shape[0], total.shape[1]
    for q in range(inner // tall):
        second_ref[:, q * part : (q + 1) * part] = total[q * tall : (q + 1) * tall]
    decode_ref[...] = sum(ref[:n].astype(F32) for ref in early).T


def finish(early, last, inner, groups, n):
    part = early[0].shape[1]
    return call(
        functools.partial(finish_kernel, inner, len(early)),
        [shape((part, inner), F32), shape((inner // groups, part * groups), F32), shape((part, n), F32)],
        limit=16,
        name="finish",
    )(*early, *last)


def local(acts, patches, labels, w_first, w_second, w_decode, w_aux, w_class):
    acts = acts[0].transpose(1, 0, 2)
    pix, images, width = acts.shape
    groups, count = lax.axis_size("dp"), lax.axis_size("section")
    me, section = lax.axis_index("dp"), lax.axis_index("section")
    scale = (groups * images * pix) ** -0.5
    norm = (groups * images) ** 0.5
    first, second, decode, aux, klass = w_first[0], w_second[0], w_decode[0], w_aux[0], w_class[0]
    inner, head = first.shape[1], aux.shape[1]
    n_decode = decode.shape[1]
    rows = pix * images

    paired = count == 4 and patches.shape[2] == 192
    if paired:
        near = [section ^ k for k in range(4)]
        tiles = [t for s in near for t in (3 * (s >> 1) + 2 * (s & 1), 3 * (s >> 1) + 1)]
        where = jnp.stack([section & 1, me & 1, me, *tiles]).astype(jnp.int32)
        turned = patches.transpose(0, 2, 1)
        halves = [pack(where, turned, h) for h in range(2)]
        x, y = [swap(halves[0], "section", 1)], [swap(halves[0], "section", 2)]
        first = after(first, halves[1])
        labels = after(labels, (x[0], y[0]))
    else:
        where = jnp.stack([section & 1, me & 1, me]).astype(jnp.int32)
        target = lax.all_gather(patches, "section", axis=2, tiled=True).transpose(1, 0, 2)

    hidden, feature, pooled = forward(acts, first, second)
    aux_pre, sent = aux_head(pooled, aux, labels, pix, groups)
    got = exchange(sent)
    recon = reconstruct([after(feature[0], sent), *feature[1:]], decode)
    if paired:
        last = after(halves[1], pooled)
        x.append(swap(last, "section", 1))
        y.append(swap(last, "section", 2))
        diagonal = [swap(after(y[0], aux_pre), "section", 1), swap(after(x[1], recon[0]), "section", 2)]
        blocks = [halves, x, y, diagonal]
        target = patch_operands(blocks, [0, 1, 2, 3], [0, 1, 2, 3])
    else:
        target = [target], [pl.BlockSpec((pix // STEPS, images, n_decode), lambda g, where: (g, 0, 0))]
    logits, sent = class_logits(where, after(got, recon[0]), klass)
    partial = exchange(sent)
    grad, keep, send = residual(after(where, sent), feature, recon, *target, images, scale, groups)
    pooled_grad, aux_grad = aux_backward(partial, aux_pre, aux, pix, norm)
    chip_decode = add_cores(where, keep, send, [aux_grad])
    sum_decode = exchange_chips(chip_decode)
    keep, send = backward(
        where, grad, hidden, acts.reshape(rows, width), decode, after(pooled_grad, chip_decode[0]), second, groups
    )
    sum_last = exchange_chips(add_cores(where, keep, after(send, sum_decode)))
    grad_class, grad_aux = class_backward(
        where, logits, got, partial, sum_decode, n_decode, klass.shape[0], head, norm
    )
    grad_first, grad_second, grad_decode = finish(sum_decode, sum_last, inner, groups, n_decode)
    return grad_first[None], grad_second[None], grad_decode[None], grad_aux[None], grad_class[None]


def solution(mesh):
    in_specs = (
        P("section", "dp", None, None),
        P("dp", None, "section"),
        P("dp"),
        P("section", None, None),
        P("section", None, None),
        P("section", None, None),
        P("section", None, None),
        P("section", "dp", None),
    )
    out_specs = (P("section", "dp", None),) * 5
    return jax.shard_map(local, mesh=mesh, in_specs=in_specs, out_specs=out_specs, check_vma=False)
```

```python
import functools

import jax
import jax.numpy as jnp
from jax import lax
from jax.experimental import pallas as pl
from jax.experimental.pallas import tpu as pltpu
from jax.sharding import PartitionSpec as P

F32 = jnp.float32
BF16 = jnp.bfloat16
STEPS = 4
LANES = 128
TILE = 256
MIB = 1024 * 1024
ROWS_0 = (((0,), (0,)), ((), ()))
COLS_1 = (((1,), (1,)), ((), ()))
PARITY, CORE, ME, TILES = 0, 1, 2, 3


def dot(left, right, dims=(((1,), (0,)), ((), ()))):
    return lax.dot_general(left, right, dims, preferred_element_type=F32)


def call(kernel, out_shape, *, limit, flops=0, moved=0, **kwargs):
    return pl.pallas_call(
        kernel,
        out_shape=out_shape,
        compiler_params=pltpu.CompilerParams(vmem_limit_bytes=limit * MIB),
        cost_estimate=pl.CostEstimate(flops=int(flops), bytes_accessed=int(moved), transcendentals=0),
        **kwargs,
    )


def shape(dims, kind):
    return jax.ShapeDtypeStruct(dims, kind)


SMEM = pl.BlockSpec(memory_space=pltpu.SMEM)
VMEM = pl.BlockSpec(memory_space=pltpu.VMEM)
HBM = pl.BlockSpec(memory_space=pltpu.HBM)


def swap(value, axis, bits):
    count = lax.axis_size(axis)
    return lax.ppermute(value, axis, [(i, i ^ bits) for i in range(count)])


def exchange(value, groups=None):
    return lax.all_to_all(value, "dp", 0, 0, axis_index_groups=groups, tiled=True)


def pack_kernel(first, where_ref, patches_ref, out_ref, turned, own, shared):
    images, span, pix = patches_ref.shape
    padded = turned.shape[1]
    count = out_ref.shape[0] // 3 * 2
    parity = where_ref[PARITY]
    at_own = pl.multiple_of(64 * parity, 64)
    at_shared = pl.multiple_of(128 * (1 - parity), 64)
    row = lax.broadcasted_iota(jnp.int32, (padded, pix), 0)
    column = lax.broadcasted_iota(jnp.int32, (padded, pix), 1)
    pick = ((row < count) & (column == row + first)).astype(F32).astype(BF16)
    for i in range(images):
        turned[i, :, :LANES] = dot(pick, patches_ref[i, pl.ds(at_own, LANES), :], COLS_1).astype(BF16)
        turned[i, :, LANES:] = dot(pick, patches_ref[i, pl.ds(at_shared, 64), :], COLS_1).astype(BF16)
    size = 16 * images
    row = lax.broadcasted_iota(jnp.int32, (size, size), 0)
    column = lax.broadcasted_iota(jnp.int32, (size, size), 1)
    order = (row // images == column % 16) & (row % images == column // 16)
    order = order.astype(F32).astype(BF16)
    for b in range(padded // 16):
        rows = turned[:, 16 * b : 16 * b + 16, :].reshape(size, span)
        out = dot(order, rows).astype(BF16)
        own[16 * b : 16 * b + 16] = out[:, :LANES].reshape(16, images, LANES)
        shared[16 * b : 16 * b + 16] = out[:, LANES:].reshape(16, images, 64)
    out_ref[:count] = own[:count]
    lower, upper = shared[: count // 2], shared[count // 2 : count]

    @pl.when(parity == 0)
    def _():
        out_ref[count:] = jnp.concatenate([lower, upper], axis=2)

    @pl.when(parity == 1)
    def _():
        out_ref[count:] = jnp.concatenate([upper, lower], axis=2)


def pack(where, patches, h):
    images, span, pix = patches.shape
    half = pix // 2
    padded = -(-half // 16) * 16
    return call(
        functools.partial(pack_kernel, h * half),
        shape((half + half // 2, images, LANES), BF16),
        limit=20,
        in_specs=[SMEM, VMEM],
        scratch_shapes=[
            pltpu.VMEM((images, padded, span), BF16),
            pltpu.VMEM((padded, images, LANES), BF16),
            pltpu.VMEM((padded, images, 64), BF16),
        ],
        name="pack_patches",
    )(where, patches)


def after(value, other):
    return lax.optimization_barrier((value, other))[0]


def forward_kernel(n_tiles, pix, *refs):
    acts_refs, refs = refs[:n_tiles], refs[n_tiles:]
    first_ref, second_ref, aux_ref, labels_ref, hidden_ref = refs[:5]
    feature_refs, (aux_pre_ref, sent_ref, pooled) = refs[5:-3], refs[-3:]
    step = pl.program_id(0)
    block, images, _ = acts_refs[0].shape
    cut = lambda j: slice(j * TILE, (j + 1) * TILE)
    start = step == 0
    halves = []
    for a, b in ((0, block // 2), (block // 2, block)):
        flat = jnp.concatenate([ref[a:b].reshape((b - a) * images, TILE) for ref in acts_refs], axis=1)
        halves.append((a, b, flat, jnp.maximum(dot(flat, first_ref[...]), 0.0).astype(BF16)))
    for a, b, flat, hidden in halves:
        rows = slice(a * images, b * images)
        hidden_ref[rows] = hidden
        for j, feature_ref in enumerate(feature_refs):
            feature = (flat[:, cut(j)].astype(F32) + dot(hidden, second_ref[:, cut(j)])).astype(BF16)
            feature_ref[rows] = feature
            sums = jnp.sum(feature.reshape(b - a, images, TILE).astype(F32), axis=0)
            pooled[:, cut(j)] = sums + (pooled[:, cut(j)] if a else jnp.where(start, 0.0, pooled[:, cut(j)]))

    @pl.when(step == pl.num_programs(0) - 1)
    def _():
        groups = sent_ref.shape[0]
        width, head = aux_ref.shape
        part = width // groups
        mean = (pooled[...] / pix).astype(BF16)
        aux_pre = dot(mean, aux_ref[...])
        aux_pre_ref[...] = aux_pre
        out = jnp.maximum(aux_pre, 0.0).astype(BF16)
        row = lax.broadcasted_iota(jnp.int32, (images, LANES), 0)
        lane = lax.broadcasted_iota(jnp.int32, (images, LANES), 1)
        digits = jnp.zeros((images, LANES), jnp.int32)
        for i in range(images):
            label = labels_ref[i]
            digits = jnp.where((row == i) & (lane == 0), label // LANES, digits)
            digits = jnp.where((row == i) & (lane == 1), label % LANES, digits)
        digits = digits.astype(F32).astype(BF16)
        for d in range(groups):
            sent_ref[d, :, :head] = out
            sent_ref[d, :, head : head + part] = mean[:, d * part : (d + 1) * part]
            sent_ref[d, :, head + LANES :] = digits


def forward(acts, first, second, aux, labels, groups):
    pix, images, width = acts.shape
    inner, head = first.shape[1], aux.shape[1]
    block = pix // STEPS
    n_tiles = width // TILE
    whole = lambda *dims: pl.BlockSpec(dims, lambda g: (0,) * len(dims))
    rows = lambda n: pl.BlockSpec((block * images, n), lambda g: (g, 0))
    column = lambda j: pl.BlockSpec((block, images, TILE), lambda g: (g, 0, j))
    hidden, *feature, aux_pre, sent = call(
        functools.partial(forward_kernel, n_tiles, pix),
        [
            shape((pix * images, inner), BF16),
            *[shape((pix * images, TILE), BF16)] * n_tiles,
            shape((images, head), F32),
            shape((groups, images, head + 2 * LANES), BF16),
        ],
        limit=58,
        flops=4 * pix * images * width * inner,
        moved=2 * pix * images * (2 * width + inner),
        grid=(STEPS,),
        in_specs=[
            *[column(j) for j in range(n_tiles)],
            whole(*first.shape),
            whole(*second.shape),
            whole(*aux.shape),
            SMEM,
        ],
        out_specs=[
            rows(inner),
            *[rows(TILE)] * n_tiles,
            whole(images, head),
            whole(groups, images, head + 2 * LANES),
        ],
        scratch_shapes=[pltpu.VMEM((images, width), F32)],
        name="forward",
    )(*[acts] * n_tiles, first, second, aux, labels)
    return hidden, feature, aux_pre, sent


def own_index(h):
    per_half = STEPS // 2
    return lambda g, where: (jnp.clip(g - h * per_half, 0, per_half - 1), 0, 0)


def patch_operands(blocks, own_blocks, shared_blocks):
    args, specs = [], []
    for k in own_blocks:
        for h, half in enumerate(blocks[k]):
            dims = (half.shape[0] // 3,) + half.shape[1:]
            args.append(half)
            specs.append(pl.BlockSpec(dims, own_index(h)))
    for k in shared_blocks:
        for half in blocks[k]:
            dims = (half.shape[0] // 3,) + half.shape[1:]
            args.append(half)
            specs.append(pl.BlockSpec(dims, lambda g, where: (2, 0, 0)))
    return args, specs


def lay_target(g, where_ref, refs, target):
    if len(refs) == 1:
        target[...] = refs[0][...]
        return
    pairs = [refs[j : j + 2] for j in range(0, len(refs), 2)]
    own, shared = pairs[: len(pairs) // 2], pairs[len(pairs) // 2 :]
    per_half = STEPS // 2
    h, side = g // per_half, g % per_half
    lanes = lambda j: pl.ds(pl.multiple_of(where_ref[TILES + j] * LANES, LANES), LANES)
    for k, pair in enumerate(own):
        target[:, :, lanes(2 * k)] = pair[h][...]
    for k in range(0, len(shared), 2):
        mine, other = shared[k][h][...].astype(F32), shared[k + 1][h][...].astype(F32)
        lane = lax.broadcasted_iota(jnp.int32, mine.shape, 2)
        value = jnp.where((lane < 64) == ((where_ref[PARITY] == 0) == (side == 0)), mine, other)
        if side:
            value = jnp.concatenate([value[:, :, 64:], value[:, :, :64]], axis=2)
        target[:, :, lanes(2 * k + 1)] = value.astype(BF16)


def deal(where_ref, sums, part, keep_ref, send_ref):
    core = where_ref[CORE]
    at = 0
    for value in sums:
        height = value.shape[0]
        for z in range(keep_ref.shape[0]):
            even = value[:, 2 * z * part : (2 * z + 1) * part]
            odd = value[:, (2 * z + 1) * part : (2 * z + 2) * part]
            mine = jnp.where(core == 0, even, odd)
            other = jnp.where(core == 0, odd, even)
            keep_ref[z, at : at + height, :] = mine.astype(BF16)
            send_ref[z, at : at + height, :] = other.astype(BF16)
        at += height


def copies_of(sources, held, sems):
    size, wide = held.shape[0] // STEPS, sources[0].shape[1]
    return [
        [
            pltpu.make_async_copy(
                source.at[pl.ds(g * size, size)], held.at[pl.ds(g * size, size), pl.ds(j * wide, wide)], sems.at[g, j]
            )
            for j, source in enumerate(sources)
        ]
        for g in range(STEPS)
    ]


def by_step(copies, body):
    step = pl.program_id(0)
    for g in range(STEPS):

        @pl.when(step == g)
        def _():
            if g == 0:
                for h in range(STEPS):
                    for copy in copies[h]:
                        copy.start()
            for copy in copies[g]:
                copy.wait()
            body(g)


def contract(g, rows, pairs):
    unit = rows // STEPS // TILE * TILE
    span = slice(g * unit, rows if g == STEPS - 1 else (g + 1) * unit)
    for total, left, right in pairs:
        now = dot(left[span], right[span], ROWS_0)
        total[...] = now if g == 0 else total[...] + now


def residual_kernel(groups, scale, n_feature, n_tiles, n_patch, where_ref, *refs):
    feature_refs, refs = refs[:n_feature], refs[n_feature:]
    decode_refs, refs = refs[:n_tiles], refs[n_tiles:]
    patch_refs, refs = refs[:n_patch], refs[n_patch:]
    grad_refs, refs = refs[:n_tiles], refs[n_tiles:]
    keep_ref, send_ref, target, feature, grads, total, sems = refs
    rows, width = feature.shape
    size = grad_refs[0].shape[0]

    def body(g):
        here = slice(g * size, (g + 1) * size)
        lay_target(g, where_ref, patch_refs, target)
        if g:
            contract(g - 1, rows, [(total, grads, feature)])
        now = feature[here]
        for j, grad_ref in enumerate(grad_refs):
            cut = slice(j * TILE, (j + 1) * TILE)
            recon = dot(now, decode_refs[j][...])
            grad = ((recon - target[:, :, cut].reshape(size, TILE).astype(F32)) * scale).astype(BF16)
            grad_ref[...] = grad
            grads[here, cut] = grad
        if g == STEPS - 1:
            contract(g, rows, [(total, grads, feature)])
            deal(where_ref, [total], width // groups, keep_ref, send_ref)

    by_step(copies_of(feature_refs, feature, sems), body)


def residual(where, feature, decode, patch_args, patch_specs, images, scale, groups):
    rows = feature[0].shape[0]
    width, n = decode.shape
    size = rows // STEPS
    n_tiles = n // TILE
    parts = (groups // 2, n, width // groups)
    dealt = pl.BlockSpec(parts, lambda g, where: (0, 0, 0))
    block = pl.BlockSpec((size, TILE), lambda g, where: (g, 0))
    column = lambda j: pl.BlockSpec((width, TILE), lambda g, where: (0, j))
    *grad, keep, send = call(
        functools.partial(residual_kernel, groups, scale, len(feature), n_tiles, len(patch_args)),
        [*[shape((rows, TILE), BF16)] * n_tiles, shape(parts, BF16), shape(parts, BF16)],
        limit=58,
        flops=4 * rows * width * n,
        moved=rows * (2 * width + 6 * n),
        grid_spec=pltpu.PrefetchScalarGridSpec(
            num_scalar_prefetch=1,
            grid=(STEPS,),
            in_specs=[*[HBM] * len(feature), *[column(j) for j in range(n_tiles)], *patch_specs],
            out_specs=[*[block] * n_tiles, dealt, dealt],
            scratch_shapes=[
                pltpu.VMEM((size // images, images, n), BF16),
                pltpu.VMEM((rows, width), BF16),
                pltpu.VMEM((rows, n), BF16),
                pltpu.VMEM((n, width), F32),
                pltpu.SemaphoreType.DMA((STEPS, len(feature))),
            ],
        ),
        name="residual",
    )(where, *feature, *[decode] * n_tiles, *patch_args)
    return grad, keep, send


def backward_kernel(groups, n_grad, n_decode, where_ref, *refs):
    grad_refs, refs = refs[:n_grad], refs[n_grad:]
    decode_refs, refs = refs[:n_decode], refs[n_decode:]
    (hidden_ref, acts_ref, pooled_ref, second_ref, keep_ref, send_ref,
     hidden, acts, feature_grads, hidden_grads, total_second, total_first, sems) = refs
    rows, width = feature_grads.shape
    size = grad_refs[0].shape[0]
    images = pooled_ref.shape[0]
    pairs = [(total_second, hidden, feature_grads), (total_first, hidden_grads, acts)]

    def body(g):
        here = slice(g * size, (g + 1) * size)
        if g:
            contract(g - 1, rows, pairs)
        grad = jnp.concatenate([ref[...] for ref in grad_refs], axis=1)
        for j, decode_ref in enumerate(decode_refs):
            cut = slice(j * TILE, (j + 1) * TILE)
            back = dot(grad, decode_ref[...], COLS_1).reshape(size // images, images, TILE)
            feature_grads[here, cut] = (back + pooled_ref[:, cut][None]).astype(BF16).reshape(size, TILE)
        hidden_back = dot(feature_grads[here], second_ref[...], COLS_1)
        hidden_grads[here] = jnp.where(hidden[here].astype(F32) > 0, hidden_back, 0.0).astype(BF16)
        if g == STEPS - 1:
            contract(g, rows, pairs)
            part = width // groups
            tall = total_second.shape[0] // groups
            second = jnp.concatenate(
                [
                    jnp.concatenate(
                        [total_second[d * tall : (d + 1) * tall, q * part : (q + 1) * part] for q in range(groups)], axis=0
                    )
                    for d in range(groups)
                ],
                axis=1,
            )
            deal(where_ref, [second, total_first], part, keep_ref, send_ref)

    copies = zip(copies_of([hidden_ref], hidden, sems.at[0]), copies_of([acts_ref], acts, sems.at[1]))
    by_step([one + other for one, other in copies], body)


def backward(where, grad, hidden, acts, decode, pooled, second, groups):
    rows, width = acts.shape
    inner, n = hidden.shape[1], len(grad) * TILE
    n_decode = width // TILE
    row_block = lambda j: pl.BlockSpec((TILE, n), lambda g, where: (j, 0))
    size = rows // STEPS
    parts = (groups // 2, 2 * inner, width // groups)
    dealt = pl.BlockSpec(parts, lambda g, where: (0, 0, 0))
    whole = lambda array: pl.BlockSpec(array.shape, lambda g, where: (0, 0))
    return call(
        functools.partial(backward_kernel, groups, len(grad), n_decode),
        [shape(parts, BF16), shape(parts, BF16)],
        limit=58,
        flops=2 * rows * width * (n + 3 * inner),
        moved=2 * rows * (width + n + inner),
        grid_spec=pltpu.PrefetchScalarGridSpec(
            num_scalar_prefetch=1,
            grid=(STEPS,),
            in_specs=[
                *[pl.BlockSpec((size, TILE), lambda g, where: (g, 0))] * len(grad),
                *[row_block(j) for j in range(n_decode)],
                HBM,
                HBM,
                whole(pooled),
                whole(second),
            ],
            out_specs=[dealt, dealt],
            scratch_shapes=[
                pltpu.VMEM((rows, inner), BF16),
                pltpu.VMEM((rows, width), BF16),
                pltpu.VMEM((rows, width), BF16),
                pltpu.VMEM((rows, inner), BF16),
                pltpu.VMEM((inner, width), F32),
                pltpu.VMEM((inner, width), F32),
                pltpu.SemaphoreType.DMA((2, STEPS, 1)),
            ],
        ),
        name="backward",
    )(where, *grad, *[decode] * n_decode, hidden, acts, pooled, second)


TOPS, DENOMS = 3, 19
DIGIT = 40


def to_digits(value):
    rest, lanes = value, []
    for _ in range(3):
        digit = rest.astype(BF16).astype(F32)
        lanes.append(digit[:, :DIGIT])
        rest = rest - digit
    lanes.append(jnp.zeros((value.shape[0], LANES - 3 * DIGIT), F32))
    return jnp.concatenate(lanes, axis=1).astype(BF16)


def from_digits(value):
    value = value.astype(F32)
    return sum(value[:, j * DIGIT : (j + 1) * DIGIT] for j in (2, 1, 0))


def labels_of(got, head):
    digits = got[:, head + LANES : head + LANES + 2].astype(F32)
    return (digits[:, 0:1] * LANES + digits[:, 1:2]).astype(jnp.int32)


def logits_kernel(where_ref, got_ref, klass_hbm, sent_ref, klass_ref, logits_ref, sems):
    groups, images, _ = got_ref.shape
    classes, head = klass_ref.shape
    size = classes // sems.shape[0]
    copies = [
        pltpu.make_async_copy(klass_hbm.at[pl.ds(j * size, size)], klass_ref.at[pl.ds(j * size, size)], sems.at[j])
        for j in range(sems.shape[0])
    ]
    for copy in copies:
        copy.start()
    got = got_ref[...].reshape(groups * images, -1)
    for copy in copies:
        copy.wait()
    logits_ref[...] = dot(got[:, :head], klass_ref[...], COLS_1)
    logits = logits_ref[...]
    ids = lax.broadcasted_iota(jnp.int32, logits.shape, 1) + where_ref[ME] * classes
    hit = labels_of(got, head) == ids
    top = jnp.max(logits, axis=1, keepdims=True)
    expo = jnp.exp(logits - top)
    denom = jnp.sum(expo, axis=1, keepdims=True)
    own = jnp.sum(jnp.where(hit, expo, 0.0), axis=1, keepdims=True)
    rest = jnp.where(hit, 0.0, expo).astype(BF16)
    onehot = jnp.where(hit, 1.0, 0.0).astype(BF16)
    sent_ref[:, :, :head] = dot(rest, klass_ref[...]).astype(BF16).reshape(groups, images, head)
    sent_ref[:, :, head : 2 * head] = dot(onehot, klass_ref[...]).astype(BF16).reshape(groups, images, head)
    lane = lax.broadcasted_iota(jnp.int32, (images, LANES), 1)
    cut = lambda value, d: value[d * images : (d + 1) * images]
    common = jnp.zeros((images, LANES), F32)
    for d in range(groups):
        common = jnp.where(lane == TOPS + d, cut(top, d), common)
        common = jnp.where(lane == DENOMS + d, cut(denom, d), common)
    for d in range(groups):
        stats = jnp.where(lane == 1, cut(denom, d), jnp.where(lane == 2, cut(own, d), common))
        sent_ref[d, :, 2 * head :] = to_digits(jnp.where(lane == 0, cut(top, d), stats))


def class_logits(where, got, klass):
    groups, images, _ = got.shape
    classes, head = klass.shape
    return call(
        logits_kernel,
        shape((groups, images, 2 * head + LANES), BF16),
        limit=58,
        flops=2e10,
        in_specs=[SMEM, VMEM, HBM],
        scratch_shapes=[
            pltpu.VMEM(klass.shape, BF16),
            pltpu.VMEM((groups * images, classes), F32),
            pltpu.SemaphoreType.DMA((4,)),
        ],
        name="class_logits",
    )(where, got, klass)


def aux_kernel(pix, norm, got_ref, aux_pre_ref, aux_hbm, pooled_ref, grad_ref, aux_ref, sems):
    size = aux_ref.shape[0] // sems.shape[0]
    copies = [
        pltpu.make_async_copy(aux_hbm.at[pl.ds(j * size, size)], aux_ref.at[pl.ds(j * size, size)], sems.at[j])
        for j in range(sems.shape[0])
    ]
    for copy in copies:
        copy.start()
    groups = got_ref.shape[0]
    head = aux_pre_ref.shape[1]
    stats = [from_digits(got_ref[d, :, 2 * head :]) for d in range(groups)]
    top = functools.reduce(jnp.maximum, [s[:, 0:1] for s in stats])
    scales = [jnp.exp(s[:, 0:1] - top) for s in stats]
    denom = sum(s[:, 1:2] * f for s, f in zip(stats, scales))
    own = sum(s[:, 2:3] * f for s, f in zip(stats, scales)) / denom
    rest = sum(got_ref[d, :, :head].astype(F32) * scales[d] for d in range(groups)) / (denom * norm)
    row = sum(got_ref[d, :, head : 2 * head].astype(F32) for d in range(groups))
    back = rest + row * ((own - 1.0) / norm).astype(BF16).astype(F32)
    aux_grad = jnp.where(aux_pre_ref[...] > 0, back, 0.0).astype(BF16)
    for copy in copies:
        copy.wait()
    pooled_ref[...] = dot(aux_grad, aux_ref[...], COLS_1) / pix
    images, part = aux_grad.shape[0], grad_ref.shape[1]
    for q in range(head // part):
        grad_ref[q * images : (q + 1) * images, :] = aux_grad[:, q * part : (q + 1) * part]


def aux_backward(got, aux_pre, aux, pix, norm):
    groups, images, _ = got.shape
    width, head = aux.shape
    part = width // groups
    return call(
        functools.partial(aux_kernel, pix, norm),
        [shape((images, width), F32), shape((images * head // part, part), BF16)],
        limit=58,
        flops=2e10,
        in_specs=[VMEM, VMEM, HBM],
        scratch_shapes=[pltpu.VMEM(aux.shape, BF16), pltpu.SemaphoreType.DMA((4,))],
        name="aux_backward",
    )(got, aux_pre, aux)


def class_kernel(norm, n, where_ref, klass_ref, got_ref, stats_ref, *refs):
    grads_refs, (class_ref, aux_ref) = refs[:-2], refs[-2:]
    groups, images, _ = got_ref.shape
    head = class_ref.shape[1]
    classes, part = class_ref.shape[0], aux_ref.shape[0]
    got = got_ref[...].reshape(groups * images, -1)
    stats = [from_digits(stats_ref[e]) for e in range(groups)]
    tops, denoms = [], []
    for d in range(groups):
        top = functools.reduce(jnp.maximum, [s[:, TOPS + d : TOPS + d + 1] for s in stats])
        tops.append(top)
        denoms.append(sum(s[:, DENOMS + d : DENOMS + d + 1] * jnp.exp(s[:, TOPS + d : TOPS + d + 1] - top) for s in stats))
    top, denom = jnp.concatenate(tops, axis=0), jnp.concatenate(denoms, axis=0)
    logits = dot(got[:, :head], klass_ref[...], COLS_1)
    ids = lax.broadcasted_iota(jnp.int32, logits.shape, 1) + where_ref[ME] * classes
    onehot = jnp.where(labels_of(got, head) == ids, 1.0, 0.0)
    logit_grad = ((jnp.exp(logits - top) / denom - onehot) / norm).astype(BF16)
    class_ref[...] = dot(logit_grad, got[:, :head], ROWS_0)
    total = jnp.zeros(aux_ref.shape, F32)
    for d in range(groups):
        k, core = d // 2, d % 2
        at = n + core * (head // part) * images
        grad = jnp.concatenate(
            [grads_refs[k][at + q * images : at + (q + 1) * images, :] for q in range(head // part)], axis=1
        )
        pooled = got_ref[((where_ref[ME] >> 1) ^ k) * 2 + core, :, head : head + part]
        total += dot(pooled, grad, ROWS_0).astype(BF16).astype(F32)
    aux_ref[...] = total


def class_backward(where, klass, got, partial, grads, n_decode, norm):
    groups, images, wide = partial.shape
    classes, head = klass.shape
    whole = lambda *dims: pl.BlockSpec(dims, lambda i: (0,) * len(dims))
    part = grads[0].shape[1]
    return call(
        functools.partial(class_kernel, norm, n_decode),
        [shape((classes, head), F32), shape((part, head), F32)],
        limit=20,
        flops=2 * groups * images * classes * head,
        moved=4 * classes * head,
        grid=(1,),
        in_specs=[
            SMEM,
            whole(*klass.shape),
            whole(*got.shape),
            pl.BlockSpec((groups, images, LANES), lambda i: (0, 0, wide // LANES - 1)),
            *[whole(*g.shape) for g in grads],
        ],
        out_specs=[whole(classes, head), whole(part, head)],
        name="class_backward",
    )(where, klass, got, partial, *grads)


def chip_kernel(n_extra, where_ref, keep_ref, got_ref, *refs):
    extra, outs = refs[:n_extra], refs[n_extra:]
    n = keep_ref.shape[1]
    chip = where_ref[ME] >> 1
    for k, out_ref in enumerate(outs):
        out_ref[:n] = (keep_ref[chip ^ k].astype(F32) + got_ref[chip ^ k].astype(F32)).astype(BF16)
    if n_extra:
        mine, other = extra[0][...].astype(F32), extra[1][...].astype(F32)
        even = where_ref[CORE] == 0
        pair = [jnp.where(even, mine, other).astype(BF16), jnp.where(even, other, mine).astype(BF16)]
        size = mine.shape[0]
        for out_ref in outs:
            for c in range(2):
                out_ref[n + c * size : n + (c + 1) * size] = pair[c]


def add_cores(where, keep, send, extra=()):
    chips, n, part = keep.shape
    extra = [e for own in extra for e in (own, swap(own, "dp", 1))]
    rows = n + sum(e.shape[0] for e in extra)
    return call(
        functools.partial(chip_kernel, len(extra)),
        [shape((rows, part), BF16)] * chips,
        limit=16,
        in_specs=[SMEM, VMEM, VMEM, *[VMEM] * len(extra)],
        name="add_cores",
    )(where, keep, swap(send, "dp", 1), *extra)


def exchange_chips(parts):
    return [parts[0]] + [swap(part, "dp", 2 * k) for k, part in enumerate(parts) if k]


def finish_kernel(inner, chips, *refs):
    early, last, (first_ref, second_ref, decode_ref) = refs[:chips], refs[chips : 2 * chips], refs[2 * chips :]
    n = decode_ref.shape[1]
    total = sum(ref[...].astype(F32) for ref in last)
    first_ref[...] = total[inner:].T
    tall, part = second_ref.shape[0], total.shape[1]
    for q in range(inner // tall):
        second_ref[:, q * part : (q + 1) * part] = total[q * tall : (q + 1) * tall]
    decode_ref[...] = sum(ref[:n].astype(F32) for ref in early).T


def finish(early, last, inner, groups, n):
    part = early[0].shape[1]
    return call(
        functools.partial(finish_kernel, inner, len(early)),
        [shape((part, inner), F32), shape((inner // groups, part * groups), F32), shape((part, n), F32)],
        limit=16,
        name="finish",
    )(*early, *last)


def local(acts, patches, labels, w_first, w_second, w_decode, w_aux, w_class):
    acts = acts[0].transpose(1, 0, 2)
    pix, images, width = acts.shape
    groups, count = lax.axis_size("dp"), lax.axis_size("section")
    me, section = lax.axis_index("dp"), lax.axis_index("section")
    scale = (groups * images * pix) ** -0.5
    norm = (groups * images) ** 0.5
    first, second, decode, aux, klass = w_first[0], w_second[0], w_decode[0], w_aux[0], w_class[0]
    inner = first.shape[1]
    n_decode = decode.shape[1]
    rows = pix * images

    paired = count == 4 and patches.shape[2] == 192
    if paired:
        near = [section ^ k for k in range(4)]
        tiles = [t for s in near for t in (3 * (s >> 1) + 2 * (s & 1), 3 * (s >> 1) + 1)]
        where = jnp.stack([section & 1, me & 1, me, *tiles]).astype(jnp.int32)
        turned = patches.transpose(0, 2, 1)
        halves = [pack(where, turned, h) for h in range(2)]
        x = [swap(half, "section", 1) for half in halves]
        y = [swap(half, "section", 2) for half in halves]
        first = after(first, halves[1])
    else:
        where = jnp.stack([section & 1, me & 1, me]).astype(jnp.int32)
        target = lax.all_gather(patches, "section", axis=2, tiled=True).transpose(1, 0, 2)

    hidden, feature, aux_pre, sent = forward(acts, first, second, aux, labels, groups)
    if paired:
        sent = after(sent, (x[0], y[0]))
        diagonal = [swap(after(y[0], aux_pre), "section", 1), swap(after(x[1], aux_pre), "section", 2)]
        target = patch_operands([halves, x, y, diagonal], [0, 1, 2, 3], [0, 1, 2, 3])
    else:
        target = [target], [pl.BlockSpec((pix // STEPS, images, n_decode), lambda g, where: (g, 0, 0))]
    got = exchange(sent)
    sent = class_logits(where, got, klass)
    partial = exchange(sent)
    grad, keep, send = residual(after(where, sent), feature, decode, *target, images, scale, groups)
    pooled_grad, aux_grad = aux_backward(partial, aux_pre, aux, pix, norm)
    chip_decode = add_cores(where, keep, send, [aux_grad])
    sum_decode = exchange_chips(chip_decode)
    keep, send = backward(
        where, grad, hidden, acts.reshape(rows, width), decode, after(pooled_grad, chip_decode[0]), second, groups
    )
    sum_last = exchange_chips(add_cores(where, keep, after(send, sum_decode)))
    grad_class, grad_aux = class_backward(where, klass, got, partial, sum_decode, n_decode, norm)
    grad_first, grad_second, grad_decode = finish(sum_decode, sum_last, inner, groups, n_decode)
    return grad_first[None], grad_second[None], grad_decode[None], grad_aux[None], grad_class[None]


def solution(mesh):
    in_specs = (
        P("section", "dp", None, None),
        P("dp", None, "section"),
        P("dp"),
        P("section", None, None),
        P("section", None, None),
        P("section", None, None),
        P("section", None, None),
        P("section", "dp", None),
    )
    out_specs = (P("section", "dp", None),) * 5
    return jax.shard_map(local, mesh=mesh, in_specs=in_specs, out_specs=out_specs, check_vma=False)
```

```python
import functools

import jax
import jax.numpy as jnp
from jax import lax
from jax.experimental import pallas as pl
from jax.experimental.pallas import tpu as pltpu
from jax.sharding import PartitionSpec as P

F32 = jnp.float32
BF16 = jnp.bfloat16
STEPS = 4
LANES = 128
TILE = 256
MIB = 1024 * 1024
ROWS_0 = (((0,), (0,)), ((), ()))
COLS_1 = (((1,), (1,)), ((), ()))
PARITY, CORE, ME, TILES = 0, 1, 2, 3


def dot(left, right, dims=(((1,), (0,)), ((), ()))):
    return lax.dot_general(left, right, dims, preferred_element_type=F32)


def call(kernel, out_shape, *, limit, flops=0, moved=0, **kwargs):
    return pl.pallas_call(
        kernel,
        out_shape=out_shape,
        compiler_params=pltpu.CompilerParams(vmem_limit_bytes=limit * MIB),
        cost_estimate=pl.CostEstimate(flops=int(flops), bytes_accessed=int(moved), transcendentals=0),
        **kwargs,
    )


def shape(dims, kind):
    return jax.ShapeDtypeStruct(dims, kind)


SMEM = pl.BlockSpec(memory_space=pltpu.SMEM)
VMEM = pl.BlockSpec(memory_space=pltpu.VMEM)
HBM = pl.BlockSpec(memory_space=pltpu.HBM)


def swap(value, axis, bits):
    count = lax.axis_size(axis)
    return lax.ppermute(value, axis, [(i, i ^ bits) for i in range(count)])


def exchange(value, groups=None):
    return lax.all_to_all(value, "dp", 0, 0, axis_index_groups=groups, tiled=True)


def pack_kernel(first, where_ref, *refs):
    patches_refs, (out_ref, turned, own, shared) = refs[:-4], refs[-4:]
    several, span, pix = patches_refs[0].shape
    images = turned.shape[0]
    padded = turned.shape[1]
    count = out_ref.shape[0] // 3 * 2
    parity = where_ref[PARITY]
    at_own = pl.multiple_of(64 * parity, 64)
    at_shared = pl.multiple_of(128 * (1 - parity), 64)
    row = lax.broadcasted_iota(jnp.int32, (padded, pix), 0)
    column = lax.broadcasted_iota(jnp.int32, (padded, pix), 1)
    pick = ((row < count) & (column == row + first)).astype(F32).astype(BF16)
    for i in range(images):
        patches_ref, j = patches_refs[i // several], i % several
        turned[i, :, :LANES] = dot(pick, patches_ref[j, pl.ds(at_own, LANES), :], COLS_1).astype(BF16)
        turned[i, :, LANES:] = dot(pick, patches_ref[j, pl.ds(at_shared, 64), :], COLS_1).astype(BF16)
    size = 16 * images
    row = lax.broadcasted_iota(jnp.int32, (size, size), 0)
    column = lax.broadcasted_iota(jnp.int32, (size, size), 1)
    order = (row // images == column % 16) & (row % images == column // 16)
    order = order.astype(F32).astype(BF16)
    for b in range(padded // 16):
        rows = turned[:, 16 * b : 16 * b + 16, :].reshape(size, span)
        out = dot(order, rows).astype(BF16)
        own[16 * b : 16 * b + 16] = out[:, :LANES].reshape(16, images, LANES)
        shared[16 * b : 16 * b + 16] = out[:, LANES:].reshape(16, images, 64)
    out_ref[:count] = own[:count]
    lower, upper = shared[: count // 2], shared[count // 2 : count]

    @pl.when(parity == 0)
    def _():
        out_ref[count:] = jnp.concatenate([lower, upper], axis=2)

    @pl.when(parity == 1)
    def _():
        out_ref[count:] = jnp.concatenate([upper, lower], axis=2)


def pack(where, patches, h):
    images, span, pix = patches.shape
    half = pix // 2
    padded = -(-half // 16) * 16
    several = images // 4
    lanes = LANES if h == 0 and half <= LANES < pix else pix
    group = lambda j: pl.BlockSpec((several, span, lanes), lambda i: (j, 0, 0))
    dims = (half + half // 2, images, LANES)
    return call(
        functools.partial(pack_kernel, h * half),
        shape(dims, BF16),
        limit=20,
        grid=(1,),
        in_specs=[SMEM, *[group(j) for j in range(4)]],
        out_specs=pl.BlockSpec(dims, lambda i: (0, 0, 0)),
        scratch_shapes=[
            pltpu.VMEM((images, padded, span), BF16),
            pltpu.VMEM((padded, images, LANES), BF16),
            pltpu.VMEM((padded, images, 64), BF16),
        ],
        name="pack_patches",
    )(where, *[patches] * 4)


def after(value, other):
    return lax.optimization_barrier((value, other))[0]


def forward_kernel(n_tiles, pix, *refs):
    acts_refs, refs = refs[:n_tiles], refs[n_tiles:]
    first_ref, second_ref, aux_ref, labels_ref, hidden_ref = refs[:5]
    feature_refs, (aux_pre_ref, sent_ref, pooled) = refs[5:-3], refs[-3:]
    step = pl.program_id(0)
    block, images, _ = acts_refs[0].shape
    cut = lambda j: slice(j * TILE, (j + 1) * TILE)
    start = step == 0
    halves = []
    for a, b in ((0, block // 2), (block // 2, block)):
        flat = jnp.concatenate([ref[a:b].reshape((b - a) * images, TILE) for ref in acts_refs], axis=1)
        halves.append((a, b, flat, jnp.maximum(dot(flat, first_ref[...]), 0.0).astype(BF16)))
    for a, b, flat, hidden in halves:
        rows = slice(a * images, b * images)
        hidden_ref[rows] = hidden
        for j, feature_ref in enumerate(feature_refs):
            feature = (flat[:, cut(j)].astype(F32) + dot(hidden, second_ref[:, cut(j)])).astype(BF16)
            feature_ref[rows] = feature
            sums = jnp.sum(feature.reshape(b - a, images, TILE).astype(F32), axis=0)
            pooled[:, cut(j)] = sums + (pooled[:, cut(j)] if a else jnp.where(start, 0.0, pooled[:, cut(j)]))

    @pl.when(step == pl.num_programs(0) - 1)
    def _():
        groups = sent_ref.shape[0]
        width, head = aux_ref.shape
        part = width // groups
        mean = (pooled[...] / pix).astype(BF16)
        aux_pre = dot(mean, aux_ref[...])
        aux_pre_ref[...] = aux_pre
        out = jnp.maximum(aux_pre, 0.0).astype(BF16)
        row = lax.broadcasted_iota(jnp.int32, (images, LANES), 0)
        lane = lax.broadcasted_iota(jnp.int32, (images, LANES), 1)
        digits = jnp.zeros((images, LANES), jnp.int32)
        for i in range(images):
            label = labels_ref[i]
            digits = jnp.where((row == i) & (lane == 0), label // LANES, digits)
            digits = jnp.where((row == i) & (lane == 1), label % LANES, digits)
        digits = digits.astype(F32).astype(BF16)
        for d in range(groups):
            sent_ref[d, :, :head] = out
            sent_ref[d, :, head : head + part] = mean[:, d * part : (d + 1) * part]
            sent_ref[d, :, head + LANES :] = digits


def forward(acts, first, second, aux, labels, groups):
    pix, images, width = acts.shape
    inner, head = first.shape[1], aux.shape[1]
    block = pix // STEPS
    n_tiles = width // TILE
    whole = lambda *dims: pl.BlockSpec(dims, lambda g: (0,) * len(dims))
    rows = lambda n: pl.BlockSpec((block * images, n), lambda g: (g, 0))
    column = lambda j: pl.BlockSpec((block, images, TILE), lambda g: (g, 0, j))
    hidden, *feature, aux_pre, sent = call(
        functools.partial(forward_kernel, n_tiles, pix),
        [
            shape((pix * images, inner), BF16),
            *[shape((pix * images, TILE), BF16)] * n_tiles,
            shape((images, head), F32),
            shape((groups, images, head + 2 * LANES), BF16),
        ],
        limit=58,
        flops=4 * pix * images * width * inner,
        moved=2 * pix * images * (2 * width + inner),
        grid=(STEPS,),
        in_specs=[
            *[column(j) for j in range(n_tiles)],
            whole(*first.shape),
            whole(*second.shape),
            whole(*aux.shape),
            SMEM,
        ],
        out_specs=[
            rows(inner),
            *[rows(TILE)] * n_tiles,
            whole(images, head),
            whole(groups, images, head + 2 * LANES),
        ],
        scratch_shapes=[pltpu.VMEM((images, width), F32)],
        name="forward",
    )(*[acts] * n_tiles, first, second, aux, labels)
    return hidden, feature, aux_pre, sent


def recon_kernel(n_feature, n_tiles, *refs):
    feature_refs, decode_refs, recon_refs = refs[:n_feature], refs[n_feature : n_feature + n_tiles], refs[n_feature + n_tiles :]
    feature = jnp.concatenate([ref[...] for ref in feature_refs], axis=1)
    for decode_ref, recon_ref in zip(decode_refs, recon_refs):
        recon_ref[...] = dot(feature, decode_ref[...])


def reconstruct(feature, decode, n_tiles):
    rows = feature[0].shape[0]
    width = decode.shape[0]
    block = pl.BlockSpec((rows // STEPS, TILE), lambda g: (g, 0))
    return call(
        functools.partial(recon_kernel, len(feature), n_tiles),
        [shape((rows, TILE), F32)] * n_tiles,
        limit=57,
        flops=2 * rows * width * n_tiles * TILE,
        moved=rows * (2 * width + 4 * n_tiles * TILE),
        grid=(STEPS,),
        in_specs=[*[block] * len(feature), *[pl.BlockSpec((width, TILE), lambda g, j=j: (0, j)) for j in range(n_tiles)]],
        out_specs=[block] * n_tiles,
        name="reconstruct",
    )(*feature, *[decode] * n_tiles)


def own_index(h):
    per_half = STEPS // 2
    return lambda g, where: (jnp.clip(g - h * per_half, 0, per_half - 1), 0, 0)


def patch_operands(blocks, own_blocks, shared_blocks):
    args, specs = [], []
    for k in own_blocks:
        for h, half in enumerate(blocks[k]):
            dims = (half.shape[0] // 3,) + half.shape[1:]
            args.append(half)
            specs.append(pl.BlockSpec(dims, own_index(h)))
    for k in shared_blocks:
        for half in blocks[k]:
            dims = (half.shape[0] // 3,) + half.shape[1:]
            args.append(half)
            specs.append(pl.BlockSpec(dims, lambda g, where: (2, 0, 0)))
    return args, specs


def lay_target(g, where_ref, refs, target):
    if len(refs) == 1:
        target[...] = refs[0][...]
        return
    pairs = [refs[j : j + 2] for j in range(0, len(refs), 2)]
    own, shared = pairs[: len(pairs) // 2], pairs[len(pairs) // 2 :]
    per_half = STEPS // 2
    h, side = g // per_half, g % per_half
    lanes = lambda j: pl.ds(pl.multiple_of(where_ref[TILES + j] * LANES, LANES), LANES)
    for k, pair in enumerate(own):
        target[:, :, lanes(2 * k)] = pair[h][...]
    for k in range(0, len(shared), 2):
        mine, other = shared[k][h][...].astype(F32), shared[k + 1][h][...].astype(F32)
        lane = lax.broadcasted_iota(jnp.int32, mine.shape, 2)
        value = jnp.where((lane < 64) == ((where_ref[PARITY] == 0) == (side == 0)), mine, other)
        if side:
            value = jnp.concatenate([value[:, :, 64:], value[:, :, :64]], axis=2)
        target[:, :, lanes(2 * k + 1)] = value.astype(BF16)


def deal(where_ref, sums, part, keep_ref, send_ref):
    core = where_ref[CORE]
    at = 0
    for value in sums:
        height = value.shape[0]
        for z in range(keep_ref.shape[0]):
            even = value[:, 2 * z * part : (2 * z + 1) * part]
            odd = value[:, (2 * z + 1) * part : (2 * z + 2) * part]
            mine = jnp.where(core == 0, even, odd)
            other = jnp.where(core == 0, odd, even)
            keep_ref[z, at : at + height, :] = mine.astype(BF16)
            send_ref[z, at : at + height, :] = other.astype(BF16)
        at += height


def copies_of(sources, held, sems):
    size, wide = held.shape[0] // STEPS, sources[0].shape[1]
    return [
        [
            pltpu.make_async_copy(
                source.at[pl.ds(g * size, size)], held.at[pl.ds(g * size, size), pl.ds(j * wide, wide)], sems.at[g, j]
            )
            for j, source in enumerate(sources)
        ]
        for g in range(STEPS)
    ]


def by_step(copies, body):
    step = pl.program_id(0)
    for g in range(STEPS):

        @pl.when(step == g)
        def _():
            if g == 0:
                for h in range(STEPS):
                    for copy in copies[h]:
                        copy.start()
            for copy in copies[g]:
                copy.wait()
            body(g)


def contract(g, rows, pairs):
    unit = rows // STEPS // TILE * TILE
    span = slice(g * unit, rows if g == STEPS - 1 else (g + 1) * unit)
    for total, left, right in pairs:
        now = dot(left[span], right[span], ROWS_0)
        total[...] = now if g == 0 else total[...] + now


def residual_kernel(groups, scale, n_feature, n_recon, n_tiles, n_patch, where_ref, *refs):
    feature_refs, refs = refs[:n_feature], refs[n_feature:]
    recon_refs, refs = refs[:n_recon], refs[n_recon:]
    decode_refs, refs = refs[: n_tiles - n_recon], refs[n_tiles - n_recon :]
    patch_refs, refs = refs[:n_patch], refs[n_patch:]
    grad_refs, refs = refs[:n_tiles], refs[n_tiles:]
    keep_ref, send_ref, target, feature, grads, total, sems = refs
    rows, width = feature.shape
    size = grad_refs[0].shape[0]

    def body(g):
        here = slice(g * size, (g + 1) * size)
        lay_target(g, where_ref, patch_refs, target)
        if g:
            contract(g - 1, rows, [(total, grads, feature)])
        now = feature[here]
        for j, grad_ref in enumerate(grad_refs):
            cut = slice(j * TILE, (j + 1) * TILE)
            recon = recon_refs[j][...] if j < n_recon else dot(now, decode_refs[j - n_recon][...])
            grad = ((recon - target[:, :, cut].reshape(size, TILE).astype(F32)) * scale).astype(BF16)
            grad_ref[...] = grad
            grads[here, cut] = grad
        if g == STEPS - 1:
            contract(g, rows, [(total, grads, feature)])
            deal(where_ref, [total], width // groups, keep_ref, send_ref)

    by_step(copies_of(feature_refs, feature, sems), body)


def residual(where, feature, recon, decode, patch_args, patch_specs, images, scale, groups):
    rows = feature[0].shape[0]
    width, n = decode.shape
    size = rows // STEPS
    n_tiles = n // TILE
    parts = (groups // 2, n, width // groups)
    dealt = pl.BlockSpec(parts, lambda g, where: (0, 0, 0))
    block = pl.BlockSpec((size, TILE), lambda g, where: (g, 0))
    column = lambda j: pl.BlockSpec((width, TILE), lambda g, where: (0, j))
    *grad, keep, send = call(
        functools.partial(residual_kernel, groups, scale, len(feature), len(recon), n_tiles, len(patch_args)),
        [*[shape((rows, TILE), BF16)] * n_tiles, shape(parts, BF16), shape(parts, BF16)],
        limit=58,
        flops=2 * rows * width * (2 * n - len(recon) * TILE),
        moved=rows * (2 * width + 6 * n),
        grid_spec=pltpu.PrefetchScalarGridSpec(
            num_scalar_prefetch=1,
            grid=(STEPS,),
            in_specs=[
                *[HBM] * len(feature),
                *[block] * len(recon),
                *[column(j) for j in range(len(recon), n_tiles)],
                *patch_specs,
            ],
            out_specs=[*[block] * n_tiles, dealt, dealt],
            scratch_shapes=[
                pltpu.VMEM((size // images, images, n), BF16),
                pltpu.VMEM((rows, width), BF16),
                pltpu.VMEM((rows, n), BF16),
                pltpu.VMEM((n, width), F32),
                pltpu.SemaphoreType.DMA((STEPS, len(feature))),
            ],
        ),
        name="residual",
    )(where, *feature, *recon, *[decode] * (n_tiles - len(recon)), *patch_args)
    return grad, keep, send


def backward_kernel(groups, n_grad, n_decode, where_ref, *refs):
    grad_refs, refs = refs[:n_grad], refs[n_grad:]
    decode_refs, refs = refs[:n_decode], refs[n_decode:]
    (hidden_ref, acts_ref, aux_grad_ref, aux_ref, second_ref, keep_ref, send_ref,
     hidden, acts, feature_grads, hidden_grads, pooled, total_second, total_first, sems) = refs
    rows, width = feature_grads.shape
    size = grad_refs[0].shape[0]
    images = aux_grad_ref.shape[0]
    pairs = [(total_second, hidden, feature_grads), (total_first, hidden_grads, acts)]

    def body(g):
        here = slice(g * size, (g + 1) * size)
        if g:
            contract(g - 1, rows, pairs)
        else:
            pooled[...] = dot(aux_grad_ref[...], aux_ref[...], COLS_1) / (rows // images)
        grad = jnp.concatenate([ref[...] for ref in grad_refs], axis=1)
        for j, decode_ref in enumerate(decode_refs):
            cut = slice(j * TILE, (j + 1) * TILE)
            back = dot(grad, decode_ref[...], COLS_1).reshape(size // images, images, TILE)
            feature_grads[here, cut] = (back + pooled[:, cut][None]).astype(BF16).reshape(size, TILE)
        hidden_back = dot(feature_grads[here], second_ref[...], COLS_1)
        hidden_grads[here] = jnp.where(hidden[here].astype(F32) > 0, hidden_back, 0.0).astype(BF16)
        if g == STEPS - 1:
            contract(g, rows, pairs)
            part = width // groups
            tall = total_second.shape[0] // groups
            second = jnp.concatenate(
                [
                    jnp.concatenate(
                        [total_second[d * tall : (d + 1) * tall, q * part : (q + 1) * part] for q in range(groups)], axis=0
                    )
                    for d in range(groups)
                ],
                axis=1,
            )
            deal(where_ref, [second, total_first], part, keep_ref, send_ref)

    copies = zip(copies_of([hidden_ref], hidden, sems.at[0]), copies_of([acts_ref], acts, sems.at[1]))
    by_step([one + other for one, other in copies], body)


def backward(where, grad, hidden, acts, decode, aux_grad, aux, second, groups):
    rows, width = acts.shape
    inner, n = hidden.shape[1], len(grad) * TILE
    n_decode = width // TILE
    row_block = lambda j: pl.BlockSpec((TILE, n), lambda g, where: (j, 0))
    size = rows // STEPS
    parts = (groups // 2, 2 * inner, width // groups)
    dealt = pl.BlockSpec(parts, lambda g, where: (0, 0, 0))
    whole = lambda array: pl.BlockSpec(array.shape, lambda g, where: (0, 0))
    return call(
        functools.partial(backward_kernel, groups, len(grad), n_decode),
        [shape(parts, BF16), shape(parts, BF16)],
        limit=44,
        flops=2 * rows * width * (n + 3 * inner),
        moved=2 * rows * (width + n + inner),
        grid_spec=pltpu.PrefetchScalarGridSpec(
            num_scalar_prefetch=1,
            grid=(STEPS,),
            in_specs=[
                *[pl.BlockSpec((size, TILE), lambda g, where: (g, 0))] * len(grad),
                *[row_block(j) for j in range(n_decode)],
                HBM,
                HBM,
                whole(aux_grad),
                whole(aux),
                whole(second),
            ],
            out_specs=[dealt, dealt],
            scratch_shapes=[
                pltpu.VMEM((rows, inner), BF16),
                pltpu.VMEM((rows, width), BF16),
                pltpu.VMEM((rows, width), BF16),
                pltpu.VMEM((rows, inner), BF16),
                pltpu.VMEM((aux_grad.shape[0], width), F32),
                pltpu.VMEM((inner, width), F32),
                pltpu.VMEM((inner, width), F32),
                pltpu.SemaphoreType.DMA((2, STEPS, 1)),
            ],
        ),
        name="backward",
    )(where, *grad, *[decode] * n_decode, hidden, acts, aux_grad, aux, second)


TOPS, DENOMS = 3, 19
DIGIT = 40


def to_digits(value):
    rest, lanes = value, []
    for _ in range(3):
        digit = rest.astype(BF16).astype(F32)
        lanes.append(digit[:, :DIGIT])
        rest = rest - digit
    lanes.append(jnp.zeros((value.shape[0], LANES - 3 * DIGIT), F32))
    return jnp.concatenate(lanes, axis=1).astype(BF16)


def from_digits(value):
    value = value.astype(F32)
    return sum(value[:, j * DIGIT : (j + 1) * DIGIT] for j in (2, 1, 0))


def labels_of(got, head):
    digits = got[:, head + LANES : head + LANES + 2].astype(F32)
    return (digits[:, 0:1] * LANES + digits[:, 1:2]).astype(jnp.int32)


def logits_kernel(where_ref, got_ref, klass_ref, sent_ref, logits_ref):
    groups, images, _ = got_ref.shape
    classes, head = klass_ref.shape
    got = got_ref[...].reshape(groups * images, -1)
    logits_ref[...] = dot(got[:, :head], klass_ref[...], COLS_1)
    logits = logits_ref[...]
    ids = lax.broadcasted_iota(jnp.int32, logits.shape, 1) + where_ref[ME] * classes
    hit = labels_of(got, head) == ids
    top = jnp.max(logits, axis=1, keepdims=True)
    expo = jnp.exp(logits - top)
    denom = jnp.sum(expo, axis=1, keepdims=True)
    own = jnp.sum(jnp.where(hit, expo, 0.0), axis=1, keepdims=True)
    rest = jnp.where(hit, 0.0, expo).astype(BF16)
    onehot = jnp.where(hit, 1.0, 0.0).astype(BF16)
    sent_ref[:, :, :head] = dot(rest, klass_ref[...]).astype(BF16).reshape(groups, images, head)
    sent_ref[:, :, head : 2 * head] = dot(onehot, klass_ref[...]).astype(BF16).reshape(groups, images, head)
    lane = lax.broadcasted_iota(jnp.int32, (images, LANES), 1)
    cut = lambda value, d: value[d * images : (d + 1) * images]
    common = jnp.zeros((images, LANES), F32)
    for d in range(groups):
        common = jnp.where(lane == TOPS + d, cut(top, d), common)
        common = jnp.where(lane == DENOMS + d, cut(denom, d), common)
    for d in range(groups):
        stats = jnp.where(lane == 1, cut(denom, d), jnp.where(lane == 2, cut(own, d), common))
        sent_ref[d, :, 2 * head :] = to_digits(jnp.where(lane == 0, cut(top, d), stats))


def class_logits(where, got, klass):
    groups, images, _ = got.shape
    classes, head = klass.shape
    return call(
        logits_kernel,
        shape((groups, images, 2 * head + LANES), BF16),
        limit=16,
        flops=2e10,
        in_specs=[SMEM, VMEM, VMEM],
        scratch_shapes=[pltpu.VMEM((groups * images, classes), F32)],
        name="class_logits",
    )(where, got, klass)


def aux_kernel(norm, got_ref, aux_pre_ref, grad_ref, cut_ref):
    groups, images, _ = got_ref.shape
    head = aux_pre_ref.shape[1]
    stats = [from_digits(got_ref[d, :, 2 * head :]) for d in range(groups)]
    top = functools.reduce(jnp.maximum, [s[:, 0:1] for s in stats])
    scales = [jnp.exp(s[:, 0:1] - top) for s in stats]
    denom = sum(s[:, 1:2] * f for s, f in zip(stats, scales))
    own = sum(s[:, 2:3] * f for s, f in zip(stats, scales)) / denom
    rest = sum(got_ref[d, :, :head].astype(F32) * scales[d] for d in range(groups)) / (denom * norm)
    row = sum(got_ref[d, :, head : 2 * head].astype(F32) for d in range(groups))
    back = rest + row * ((own - 1.0) / norm).astype(BF16).astype(F32)
    aux_grad = jnp.where(aux_pre_ref[...] > 0, back, 0.0).astype(BF16)
    grad_ref[...] = aux_grad
    part = cut_ref.shape[1]
    for q in range(head // part):
        cut_ref[q * images : (q + 1) * images, :] = aux_grad[:, q * part : (q + 1) * part]


def aux_backward(got, aux_pre, part, norm):
    images, head = aux_pre.shape
    return call(
        functools.partial(aux_kernel, norm),
        [shape((images, head), BF16), shape((images * head // part, part), BF16)],
        limit=16,
        flops=2e10,
        name="aux_backward",
    )(got, aux_pre)


def class_kernel(norm, n, where_ref, klass_ref, got_ref, stats_ref, *refs):
    grads_refs, (class_ref, aux_ref) = refs[:-2], refs[-2:]
    groups, images, _ = got_ref.shape
    head = class_ref.shape[1]
    classes, part = class_ref.shape[0], aux_ref.shape[0]
    got = got_ref[...].reshape(groups * images, -1)
    stats = [from_digits(stats_ref[e]) for e in range(groups)]
    tops, denoms = [], []
    for d in range(groups):
        top = functools.reduce(jnp.maximum, [s[:, TOPS + d : TOPS + d + 1] for s in stats])
        tops.append(top)
        denoms.append(sum(s[:, DENOMS + d : DENOMS + d + 1] * jnp.exp(s[:, TOPS + d : TOPS + d + 1] - top) for s in stats))
    top, denom = jnp.concatenate(tops, axis=0), jnp.concatenate(denoms, axis=0)
    logits = dot(got[:, :head], klass_ref[...], COLS_1)
    ids = lax.broadcasted_iota(jnp.int32, logits.shape, 1) + where_ref[ME] * classes
    onehot = jnp.where(labels_of(got, head) == ids, 1.0, 0.0)
    logit_grad = ((jnp.exp(logits - top) / denom - onehot) / norm).astype(BF16)
    class_ref[...] = dot(logit_grad, got[:, :head], ROWS_0)
    total = jnp.zeros(aux_ref.shape, F32)
    for d in range(groups):
        k, core = d // 2, d % 2
        at = n + core * (head // part) * images
        grad = jnp.concatenate(
            [grads_refs[k][at + q * images : at + (q + 1) * images, :] for q in range(head // part)], axis=1
        )
        pooled = got_ref[((where_ref[ME] >> 1) ^ k) * 2 + core, :, head : head + part]
        total += dot(pooled, grad, ROWS_0).astype(BF16).astype(F32)
    aux_ref[...] = total


def class_backward(where, klass, got, partial, grads, n_decode, norm):
    groups, images, wide = partial.shape
    classes, head = klass.shape
    whole = lambda *dims: pl.BlockSpec(dims, lambda i: (0,) * len(dims))
    part = grads[0].shape[1]
    return call(
        functools.partial(class_kernel, norm, n_decode),
        [shape((classes, head), F32), shape((part, head), F32)],
        limit=20,
        flops=2 * groups * images * classes * head,
        moved=4 * classes * head,
        grid=(1,),
        in_specs=[
            SMEM,
            whole(*klass.shape),
            whole(*got.shape),
            pl.BlockSpec((groups, images, LANES), lambda i: (0, 0, wide // LANES - 1)),
            *[whole(*g.shape) for g in grads],
        ],
        out_specs=[whole(classes, head), whole(part, head)],
        name="class_backward",
    )(where, klass, got, partial, *grads)


def chip_kernel(n_extra, where_ref, keep_ref, got_ref, *refs):
    extra, outs = refs[:n_extra], refs[n_extra:]
    n = keep_ref.shape[1]
    chip = where_ref[ME] >> 1
    for k, out_ref in enumerate(outs):
        out_ref[:n] = (keep_ref[chip ^ k].astype(F32) + got_ref[chip ^ k].astype(F32)).astype(BF16)
    if n_extra:
        mine, other = extra[0][...].astype(F32), extra[1][...].astype(F32)
        even = where_ref[CORE] == 0
        pair = [jnp.where(even, mine, other).astype(BF16), jnp.where(even, other, mine).astype(BF16)]
        size = mine.shape[0]
        for out_ref in outs:
            for c in range(2):
                out_ref[n + c * size : n + (c + 1) * size] = pair[c]


def add_cores(where, keep, send, extra=()):
    chips, n, part = keep.shape
    extra = [e for own in extra for e in (own, swap(own, "dp", 1))]
    rows = n + sum(e.shape[0] for e in extra)
    return call(
        functools.partial(chip_kernel, len(extra)),
        [shape((rows, part), BF16)] * chips,
        limit=16,
        in_specs=[SMEM, VMEM, VMEM, *[VMEM] * len(extra)],
        name="add_cores",
    )(where, keep, swap(send, "dp", 1), *extra)


def exchange_chips(parts):
    return [parts[0]] + [swap(part, "dp", 2 * k) for k, part in enumerate(parts) if k]


def finish_kernel(inner, chips, *refs):
    early, last, (first_ref, second_ref, decode_ref) = refs[:chips], refs[chips : 2 * chips], refs[2 * chips :]
    n = decode_ref.shape[1]
    total = sum(ref[...].astype(F32) for ref in last)
    first_ref[...] = total[inner:].T
    tall, part = second_ref.shape[0], total.shape[1]
    for q in range(inner // tall):
        second_ref[:, q * part : (q + 1) * part] = total[q * tall : (q + 1) * tall]
    decode_ref[...] = sum(ref[:n].astype(F32) for ref in early).T


def finish(early, last, inner, groups, n):
    part = early[0].shape[1]
    return call(
        functools.partial(finish_kernel, inner, len(early)),
        [shape((part, inner), F32), shape((inner // groups, part * groups), F32), shape((part, n), F32)],
        limit=16,
        name="finish",
    )(*early, *last)


def local(acts, patches, labels, w_first, w_second, w_decode, w_aux, w_class):
    acts = acts[0].transpose(1, 0, 2)
    pix, images, width = acts.shape
    groups, count = lax.axis_size("dp"), lax.axis_size("section")
    me, section = lax.axis_index("dp"), lax.axis_index("section")
    scale = (groups * images * pix) ** -0.5
    norm = (groups * images) ** 0.5
    first, second, decode, aux, klass = w_first[0], w_second[0], w_decode[0], w_aux[0], w_class[0]
    inner = first.shape[1]
    n_decode = decode.shape[1]
    rows = pix * images

    paired = count == 4 and patches.shape[2] == 192
    if paired:
        near = [section ^ k for k in range(4)]
        tiles = [t for s in near for t in (3 * (s >> 1) + 2 * (s & 1), 3 * (s >> 1) + 1)]
        where = jnp.stack([section & 1, me & 1, me, *tiles]).astype(jnp.int32)
        turned = patches.transpose(0, 2, 1)
        halves = [pack(where, turned, h) for h in range(2)]
        x, y = [swap(halves[0], "section", 1)], [swap(halves[1], "section", 2)]
        first = after(first, halves[1])
    else:
        where = jnp.stack([section & 1, me & 1, me]).astype(jnp.int32)
        target = lax.all_gather(patches, "section", axis=2, tiled=True).transpose(1, 0, 2)

    hidden, feature, aux_pre, sent = forward(acts, first, second, aux, labels, groups)
    if paired:
        sent = after(sent, (x[0], y[0]))
        diagonal = [swap(after(x[0], aux_pre), "section", 2), swap(after(y[0], aux_pre), "section", 1)]
        x.append(swap(after(halves[1], aux_pre), "section", 1))
        y.insert(0, swap(after(halves[0], aux_pre), "section", 2))
        target = patch_operands([halves, x, y, diagonal], [0, 1, 2, 3], [0, 1, 2, 3])
    else:
        target = [target], [pl.BlockSpec((pix // STEPS, images, n_decode), lambda g, where: (g, 0, 0))]
    got = exchange(sent)
    recon = reconstruct([after(feature[0], sent), *feature[1:]], decode, 1)
    sent = class_logits(where, after(got, recon[0]), klass)
    partial = exchange(sent)
    grad, keep, send = residual(after(where, sent), feature, recon, decode, *target, images, scale, groups)
    aux_grad, aux_cut = aux_backward(partial, aux_pre, width // groups, norm)
    chip_decode = add_cores(where, keep, send, [aux_cut])
    sum_decode = exchange_chips(chip_decode)
    keep, send = backward(
        where, grad, hidden, acts.reshape(rows, width), decode, after(aux_grad, chip_decode[0]), aux, second, groups
    )
    sum_last = exchange_chips(add_cores(where, keep, after(send, sum_decode)))
    grad_class, grad_aux = class_backward(where, klass, got, partial, sum_decode, n_decode, norm)
    grad_first, grad_second, grad_decode = finish(sum_decode, sum_last, inner, groups, n_decode)
    return grad_first[None], grad_second[None], grad_decode[None], grad_aux[None], grad_class[None]


def solution(mesh):
    in_specs = (
        P("section", "dp", None, None),
        P("dp", None, "section"),
        P("dp"),
        P("section", None, None),
        P("section", None, None),
        P("section", None, None),
        P("section", None, None),
        P("section", "dp", None),
    )
    out_specs = (P("section", "dp", None),) * 5
    return jax.shard_map(local, mesh=mesh, in_specs=in_specs, out_specs=out_specs, check_vma=False)
```

```python
import functools

import jax
import jax.numpy as jnp
from jax import lax
from jax.experimental import pallas as pl
from jax.experimental.pallas import tpu as pltpu
from jax.sharding import PartitionSpec as P

F32 = jnp.float32
BF16 = jnp.bfloat16
STEPS = 4
LANES = 128
TILE = 256
MIB = 1024 * 1024
ROWS_0 = (((0,), (0,)), ((), ()))
COLS_1 = (((1,), (1,)), ((), ()))
PARITY, CORE, ME, TILES = 0, 1, 2, 3


def dot(left, right, dims=(((1,), (0,)), ((), ()))):
    return lax.dot_general(left, right, dims, preferred_element_type=F32)


def call(kernel, out_shape, *, limit, flops=0, moved=0, **kwargs):
    return pl.pallas_call(
        kernel,
        out_shape=out_shape,
        compiler_params=pltpu.CompilerParams(vmem_limit_bytes=limit * MIB),
        cost_estimate=pl.CostEstimate(flops=int(flops), bytes_accessed=int(moved), transcendentals=0),
        **kwargs,
    )


def shape(dims, kind):
    return jax.ShapeDtypeStruct(dims, kind)


SMEM = pl.BlockSpec(memory_space=pltpu.SMEM)
VMEM = pl.BlockSpec(memory_space=pltpu.VMEM)
HBM = pl.BlockSpec(memory_space=pltpu.HBM)


def swap(value, axis, bits):
    count = lax.axis_size(axis)
    return lax.ppermute(value, axis, [(i, i ^ bits) for i in range(count)])


def exchange(value, groups=None):
    return lax.all_to_all(value, "dp", 0, 0, axis_index_groups=groups, tiled=True)


def pack_kernel(first, where_ref, *refs):
    patches_refs, (out_ref, turned, own, shared) = refs[:-4], refs[-4:]
    several, span, pix = patches_refs[0].shape
    images = turned.shape[0]
    padded = turned.shape[1]
    count = out_ref.shape[0] // 3 * 2
    parity = where_ref[PARITY]
    at_own = pl.multiple_of(64 * parity, 64)
    at_shared = pl.multiple_of(128 * (1 - parity), 64)
    row = lax.broadcasted_iota(jnp.int32, (padded, pix), 0)
    column = lax.broadcasted_iota(jnp.int32, (padded, pix), 1)
    pick = ((row < count) & (column == row + first)).astype(F32).astype(BF16)
    for i in range(images):
        patches_ref, j = patches_refs[i // several], i % several
        turned[i, :, :LANES] = dot(pick, patches_ref[j, pl.ds(at_own, LANES), :], COLS_1).astype(BF16)
        turned[i, :, LANES:] = dot(pick, patches_ref[j, pl.ds(at_shared, 64), :], COLS_1).astype(BF16)
    size = 16 * images
    row = lax.broadcasted_iota(jnp.int32, (size, size), 0)
    column = lax.broadcasted_iota(jnp.int32, (size, size), 1)
    order = (row // images == column % 16) & (row % images == column // 16)
    order = order.astype(F32).astype(BF16)
    for b in range(padded // 16):
        rows = turned[:, 16 * b : 16 * b + 16, :].reshape(size, span)
        out = dot(order, rows).astype(BF16)
        own[16 * b : 16 * b + 16] = out[:, :LANES].reshape(16, images, LANES)
        shared[16 * b : 16 * b + 16] = out[:, LANES:].reshape(16, images, 64)
    out_ref[:count] = own[:count]
    lower, upper = shared[: count // 2], shared[count // 2 : count]

    @pl.when(parity == 0)
    def _():
        out_ref[count:] = jnp.concatenate([lower, upper], axis=2)

    @pl.when(parity == 1)
    def _():
        out_ref[count:] = jnp.concatenate([upper, lower], axis=2)


def pack(where, patches, h):
    images, span, pix = patches.shape
    half = pix // 2
    padded = -(-half // 16) * 16
    several = images // 4
    lanes = LANES if h == 0 and half <= LANES < pix else pix
    group = lambda j: pl.BlockSpec((several, span, lanes), lambda i: (j, 0, 0))
    dims = (half + half // 2, images, LANES)
    return call(
        functools.partial(pack_kernel, h * half),
        shape(dims, BF16),
        limit=20,
        grid=(1,),
        in_specs=[SMEM, *[group(j) for j in range(4)]],
        out_specs=pl.BlockSpec(dims, lambda i: (0, 0, 0)),
        scratch_shapes=[
            pltpu.VMEM((images, padded, span), BF16),
            pltpu.VMEM((padded, images, LANES), BF16),
            pltpu.VMEM((padded, images, 64), BF16),
        ],
        name="pack_patches",
    )(where, *[patches] * 4)


def after(value, other):
    return lax.optimization_barrier((value, other))[0]


def forward_kernel(n_tiles, pix, *refs):
    acts_refs, refs = refs[:n_tiles], refs[n_tiles:]
    first_ref, second_ref, aux_ref, labels_ref, hidden_ref = refs[:5]
    feature_refs, (aux_pre_ref, sent_ref, pooled) = refs[5:-3], refs[-3:]
    step = pl.program_id(0)
    block, images, _ = acts_refs[0].shape
    cut = lambda j: slice(j * TILE, (j + 1) * TILE)
    start = step == 0
    halves = []
    for a, b in ((0, block // 2), (block // 2, block)):
        flat = jnp.concatenate([ref[a:b].reshape((b - a) * images, TILE) for ref in acts_refs], axis=1)
        halves.append((a, b, flat, jnp.maximum(dot(flat, first_ref[...]), 0.0).astype(BF16)))
    for a, b, flat, hidden in halves:
        rows = slice(a * images, b * images)
        hidden_ref[rows] = hidden
        for j, feature_ref in enumerate(feature_refs):
            feature = (flat[:, cut(j)].astype(F32) + dot(hidden, second_ref[:, cut(j)])).astype(BF16)
            feature_ref[rows] = feature
            sums = jnp.sum(feature.reshape(b - a, images, TILE).astype(F32), axis=0)
            pooled[:, cut(j)] = sums + (pooled[:, cut(j)] if a else jnp.where(start, 0.0, pooled[:, cut(j)]))

    @pl.when(step == pl.num_programs(0) - 1)
    def _():
        groups = sent_ref.shape[0]
        width, head = aux_ref.shape
        part = width // groups
        mean = (pooled[...] / pix).astype(BF16)
        aux_pre = dot(mean, aux_ref[...])
        aux_pre_ref[...] = aux_pre
        out = jnp.maximum(aux_pre, 0.0).astype(BF16)
        row = lax.broadcasted_iota(jnp.int32, (images, LANES), 0)
        lane = lax.broadcasted_iota(jnp.int32, (images, LANES), 1)
        digits = jnp.zeros((images, LANES), jnp.int32)
        for i in range(images):
            label = labels_ref[i]
            digits = jnp.where((row == i) & (lane == 0), label // LANES, digits)
            digits = jnp.where((row == i) & (lane == 1), label % LANES, digits)
        digits = digits.astype(F32).astype(BF16)
        for d in range(groups):
            sent_ref[d, :, :head] = out
            sent_ref[d, :, head : head + part] = mean[:, d * part : (d + 1) * part]
            sent_ref[d, :, head + LANES :] = digits


def forward(acts, first, second, aux, labels, groups):
    pix, images, width = acts.shape
    inner, head = first.shape[1], aux.shape[1]
    block = pix // STEPS
    n_tiles = width // TILE
    whole = lambda *dims: pl.BlockSpec(dims, lambda g: (0,) * len(dims))
    rows = lambda n: pl.BlockSpec((block * images, n), lambda g: (g, 0))
    column = lambda j: pl.BlockSpec((block, images, TILE), lambda g: (g, 0, j))
    hidden, *feature, aux_pre, sent = call(
        functools.partial(forward_kernel, n_tiles, pix),
        [
            shape((pix * images, inner), BF16),
            *[shape((pix * images, TILE), BF16)] * n_tiles,
            shape((images, head), F32),
            shape((groups, images, head + 2 * LANES), BF16),
        ],
        limit=58,
        grid=(STEPS,),
        in_specs=[
            *[column(j) for j in range(n_tiles)],
            whole(*first.shape),
            whole(*second.shape),
            whole(*aux.shape),
            SMEM,
        ],
        out_specs=[
            rows(inner),
            *[rows(TILE)] * n_tiles,
            whole(images, head),
            whole(groups, images, head + 2 * LANES),
        ],
        scratch_shapes=[pltpu.VMEM((images, width), F32)],
        name="forward",
    )(*[acts] * n_tiles, first, second, aux, labels)
    return hidden, feature, aux_pre, sent


def own_index(h):
    per_half = STEPS // 2
    return lambda g, where: (jnp.clip(g - h * per_half, 0, per_half - 1), 0, 0)


def patch_operands(blocks, own_blocks, shared_blocks):
    args, specs = [], []
    for k in own_blocks:
        for h, half in enumerate(blocks[k]):
            dims = (half.shape[0] // 3,) + half.shape[1:]
            args.append(half)
            specs.append(pl.BlockSpec(dims, own_index(h)))
    for k in shared_blocks:
        for half in blocks[k]:
            dims = (half.shape[0] // 3,) + half.shape[1:]
            args.append(half)
            specs.append(pl.BlockSpec(dims, lambda g, where: (2, 0, 0)))
    return args, specs


def lay_target(g, where_ref, refs, target):
    if len(refs) == 1:
        target[...] = refs[0][...]
        return
    pairs = [refs[j : j + 2] for j in range(0, len(refs), 2)]
    own, shared = pairs[: len(pairs) // 2], pairs[len(pairs) // 2 :]
    per_half = STEPS // 2
    h, side = g // per_half, g % per_half
    lanes = lambda j: pl.ds(pl.multiple_of(where_ref[TILES + j] * LANES, LANES), LANES)
    for k, pair in enumerate(own):
        target[:, :, lanes(2 * k)] = pair[h][...]
    for k in range(0, len(shared), 2):
        mine, other = shared[k][h][...].astype(F32), shared[k + 1][h][...].astype(F32)
        lane = lax.broadcasted_iota(jnp.int32, mine.shape, 2)
        value = jnp.where((lane < 64) == ((where_ref[PARITY] == 0) == (side == 0)), mine, other)
        if side:
            value = jnp.concatenate([value[:, :, 64:], value[:, :, :64]], axis=2)
        target[:, :, lanes(2 * k + 1)] = value.astype(BF16)


def deal(where_ref, sums, part, keep_ref, send_ref):
    core = where_ref[CORE]
    at = 0
    for value in sums:
        height = value.shape[0]
        for z in range(keep_ref.shape[0]):
            even = value[:, 2 * z * part : (2 * z + 1) * part]
            odd = value[:, (2 * z + 1) * part : (2 * z + 2) * part]
            mine = jnp.where(core == 0, even, odd)
            other = jnp.where(core == 0, odd, even)
            keep_ref[z, at : at + height, :] = mine.astype(BF16)
            send_ref[z, at : at + height, :] = other.astype(BF16)
        at += height


def copies_of(sources, held, sems):
    size, wide = held.shape[0] // STEPS, sources[0].shape[1]
    return [
        [
            pltpu.make_async_copy(
                source.at[pl.ds(g * size, size)], held.at[pl.ds(g * size, size), pl.ds(j * wide, wide)], sems.at[g, j]
            )
            for j, source in enumerate(sources)
        ]
        for g in range(STEPS)
    ]


def by_step(copies, body):
    step = pl.program_id(0)
    for g in range(STEPS):

        @pl.when(step == g)
        def _():
            if g == 0:
                for h in range(STEPS):
                    for copy in copies[h]:
                        copy.start()
            for copy in copies[g]:
                copy.wait()
            body(g)


def contract(g, rows, pairs):
    unit = rows // STEPS // TILE * TILE
    span = slice(g * unit, rows if g == STEPS - 1 else (g + 1) * unit)
    for total, left, right in pairs:
        now = dot(left[span], right[span], ROWS_0)
        total[...] = now if g == 0 else total[...] + now


def residual_kernel(groups, scale, n_feature, n_tiles, n_patch, where_ref, *refs):
    feature_refs, refs = refs[:n_feature], refs[n_feature:]
    decode_refs, refs = refs[:n_tiles], refs[n_tiles:]
    patch_refs, refs = refs[:n_patch], refs[n_patch:]
    grad_refs, refs = refs[:n_tiles], refs[n_tiles:]
    keep_ref, send_ref, target, feature, grads, total, sems = refs
    rows, width = feature.shape
    size = grad_refs[0].shape[0]

    def body(g):
        here = slice(g * size, (g + 1) * size)
        lay_target(g, where_ref, patch_refs, target)
        if g:
            contract(g - 1, rows, [(total, grads, feature)])
        now = feature[here]
        for j, grad_ref in enumerate(grad_refs):
            cut = slice(j * TILE, (j + 1) * TILE)
            recon = sum(dot(now[:, k : k + TILE], decode_refs[j][k : k + TILE]) for k in range(0, width, TILE))
            grad = ((recon - target[:, :, cut].reshape(size, TILE).astype(F32)) * scale).astype(BF16)
            grad_ref[...] = grad
            grads[here, cut] = grad
        if g == STEPS - 1:
            contract(g, rows, [(total, grads, feature)])
            deal(where_ref, [total], width // groups, keep_ref, send_ref)

    by_step(copies_of(feature_refs, feature, sems), body)


def residual(where, feature, decode, patch_args, patch_specs, images, scale, groups):
    rows = feature[0].shape[0]
    width, n = decode.shape
    size = rows // STEPS
    n_tiles = n // TILE
    parts = (groups // 2, n, width // groups)
    dealt = pl.BlockSpec(parts, lambda g, where: (0, 0, 0))
    block = pl.BlockSpec((size, TILE), lambda g, where: (g, 0))
    column = lambda j: pl.BlockSpec((width, TILE), lambda g, where: (0, j))
    *grad, keep, send = call(
        functools.partial(residual_kernel, groups, scale, len(feature), n_tiles, len(patch_args)),
        [*[shape((rows, TILE), BF16)] * n_tiles, shape(parts, BF16), shape(parts, BF16)],
        limit=58,
        flops=4 * rows * width * n,
        moved=rows * (2 * width + 6 * n),
        grid_spec=pltpu.PrefetchScalarGridSpec(
            num_scalar_prefetch=1,
            grid=(STEPS,),
            in_specs=[
                *[HBM] * len(feature),
                *[column(j) for j in range(n_tiles)],
                *patch_specs,
            ],
            out_specs=[*[block] * n_tiles, dealt, dealt],
            scratch_shapes=[
                pltpu.VMEM((size // images, images, n), BF16),
                pltpu.VMEM((rows, width), BF16),
                pltpu.VMEM((rows, n), BF16),
                pltpu.VMEM((n, width), F32),
                pltpu.SemaphoreType.DMA((STEPS, len(feature))),
            ],
        ),
        name="residual",
    )(where, *feature, *[decode] * n_tiles, *patch_args)
    return grad, keep, send


def backward_kernel(groups, n_grad, n_decode, where_ref, *refs):
    grad_refs, refs = refs[:n_grad], refs[n_grad:]
    decode_refs, refs = refs[:n_decode], refs[n_decode:]
    (hidden_ref, acts_ref, aux_grad_ref, aux_ref, second_ref, keep_ref, send_ref,
     hidden, acts, feature_grads, hidden_grads, pooled, total_second, total_first, sems) = refs
    rows, width = feature_grads.shape
    size = grad_refs[0].shape[0]
    images = aux_grad_ref.shape[0]
    pairs = [(total_second, hidden, feature_grads), (total_first, hidden_grads, acts)]

    def body(g):
        here = slice(g * size, (g + 1) * size)
        if g:
            contract(g - 1, rows, pairs)
        else:
            pooled[...] = dot(aux_grad_ref[...], aux_ref[...], COLS_1) / (rows // images)
        grad = jnp.concatenate([ref[...] for ref in grad_refs], axis=1)
        for j, decode_ref in enumerate(decode_refs):
            cut = slice(j * TILE, (j + 1) * TILE)
            back = dot(grad, decode_ref[...], COLS_1).reshape(size // images, images, TILE)
            feature_grads[here, cut] = (back + pooled[:, cut][None]).astype(BF16).reshape(size, TILE)
        hidden_back = dot(feature_grads[here], second_ref[...], COLS_1)
        hidden_grads[here] = jnp.where(hidden[here].astype(F32) > 0, hidden_back, 0.0).astype(BF16)
        if g == STEPS - 1:
            contract(g, rows, pairs)
            part = width // groups
            tall = total_second.shape[0] // groups
            second = jnp.concatenate(
                [
                    jnp.concatenate(
                        [total_second[d * tall : (d + 1) * tall, q * part : (q + 1) * part] for q in range(groups)], axis=0
                    )
                    for d in range(groups)
                ],
                axis=1,
            )
            deal(where_ref, [second, total_first], part, keep_ref, send_ref)

    copies = zip(copies_of([hidden_ref], hidden, sems.at[0]), copies_of([acts_ref], acts, sems.at[1]))
    by_step([one + other for one, other in copies], body)


def backward(where, grad, hidden, acts, decode, aux_grad, aux, second, groups):
    rows, width = acts.shape
    inner, n = hidden.shape[1], len(grad) * TILE
    n_decode = width // TILE
    row_block = lambda j: pl.BlockSpec((TILE, n), lambda g, where: (j, 0))
    size = rows // STEPS
    parts = (groups // 2, 2 * inner, width // groups)
    dealt = pl.BlockSpec(parts, lambda g, where: (0, 0, 0))
    whole = lambda array: pl.BlockSpec(array.shape, lambda g, where: (0, 0))
    return call(
        functools.partial(backward_kernel, groups, len(grad), n_decode),
        [shape(parts, BF16), shape(parts, BF16)],
        limit=44,
        flops=2 * rows * width * (n + 3 * inner),
        moved=2 * rows * (width + n + inner),
        grid_spec=pltpu.PrefetchScalarGridSpec(
            num_scalar_prefetch=1,
            grid=(STEPS,),
            in_specs=[
                *[pl.BlockSpec((size, TILE), lambda g, where: (g, 0))] * len(grad),
                *[row_block(j) for j in range(n_decode)],
                HBM,
                HBM,
                whole(aux_grad),
                whole(aux),
                whole(second),
            ],
            out_specs=[dealt, dealt],
            scratch_shapes=[
                pltpu.VMEM((rows, inner), BF16),
                pltpu.VMEM((rows, width), BF16),
                pltpu.VMEM((rows, width), BF16),
                pltpu.VMEM((rows, inner), BF16),
                pltpu.VMEM((aux_grad.shape[0], width), F32),
                pltpu.VMEM((inner, width), F32),
                pltpu.VMEM((inner, width), F32),
                pltpu.SemaphoreType.DMA((2, STEPS, 1)),
            ],
        ),
        name="backward",
    )(where, *grad, *[decode] * n_decode, hidden, acts, aux_grad, aux, second)


TOPS, DENOMS = 3, 19
DIGIT = 40


def to_digits(value):
    rest, lanes = value, []
    for _ in range(3):
        digit = rest.astype(BF16).astype(F32)
        lanes.append(digit[:, :DIGIT])
        rest = rest - digit
    lanes.append(jnp.zeros((value.shape[0], LANES - 3 * DIGIT), F32))
    return jnp.concatenate(lanes, axis=1).astype(BF16)


def from_digits(value):
    value = value.astype(F32)
    return sum(value[:, j * DIGIT : (j + 1) * DIGIT] for j in (2, 1, 0))


def labels_of(got, head):
    digits = got[:, head + LANES : head + LANES + 2].astype(F32)
    return (digits[:, 0:1] * LANES + digits[:, 1:2]).astype(jnp.int32)


def logits_kernel(where_ref, got_ref, klass_ref, sent_ref, logits_ref):
    groups, images, _ = got_ref.shape
    classes, head = klass_ref.shape
    got = got_ref[...].reshape(groups * images, -1)
    logits_ref[...] = dot(got[:, :head], klass_ref[...], COLS_1)
    logits = logits_ref[...]
    ids = lax.broadcasted_iota(jnp.int32, logits.shape, 1) + where_ref[ME] * classes
    hit = labels_of(got, head) == ids
    top = jnp.max(logits, axis=1, keepdims=True)
    expo = jnp.exp(logits - top)
    denom = jnp.sum(expo, axis=1, keepdims=True)
    own = jnp.sum(jnp.where(hit, expo, 0.0), axis=1, keepdims=True)
    rest = jnp.where(hit, 0.0, expo).astype(BF16)
    onehot = jnp.where(hit, 1.0, 0.0).astype(BF16)
    sent_ref[:, :, :head] = dot(rest, klass_ref[...]).astype(BF16).reshape(groups, images, head)
    sent_ref[:, :, head : 2 * head] = dot(onehot, klass_ref[...]).astype(BF16).reshape(groups, images, head)
    lane = lax.broadcasted_iota(jnp.int32, (images, LANES), 1)
    cut = lambda value, d: value[d * images : (d + 1) * images]
    common = jnp.zeros((images, LANES), F32)
    for d in range(groups):
        common = jnp.where(lane == TOPS + d, cut(top, d), common)
        common = jnp.where(lane == DENOMS + d, cut(denom, d), common)
    for d in range(groups):
        stats = jnp.where(lane == 1, cut(denom, d), jnp.where(lane == 2, cut(own, d), common))
        sent_ref[d, :, 2 * head :] = to_digits(jnp.where(lane == 0, cut(top, d), stats))


def class_logits(where, got, klass):
    groups, images, _ = got.shape
    classes, head = klass.shape
    return call(
        logits_kernel,
        shape((groups, images, 2 * head + LANES), BF16),
        limit=16,
        in_specs=[SMEM, VMEM, VMEM],
        scratch_shapes=[pltpu.VMEM((groups * images, classes), F32)],
        name="class_logits",
    )(where, got, klass)


def aux_kernel(norm, got_ref, aux_pre_ref, grad_ref, cut_ref):
    groups, images, _ = got_ref.shape
    head = aux_pre_ref.shape[1]
    stats = [from_digits(got_ref[d, :, 2 * head :]) for d in range(groups)]
    top = functools.reduce(jnp.maximum, [s[:, 0:1] for s in stats])
    scales = [jnp.exp(s[:, 0:1] - top) for s in stats]
    denom = sum(s[:, 1:2] * f for s, f in zip(stats, scales))
    own = sum(s[:, 2:3] * f for s, f in zip(stats, scales)) / denom
    rest = sum(got_ref[d, :, :head].astype(F32) * scales[d] for d in range(groups)) / (denom * norm)
    row = sum(got_ref[d, :, head : 2 * head].astype(F32) for d in range(groups))
    back = rest + row * ((own - 1.0) / norm).astype(BF16).astype(F32)
    aux_grad = jnp.where(aux_pre_ref[...] > 0, back, 0.0).astype(BF16)
    grad_ref[...] = aux_grad
    part = cut_ref.shape[1]
    for q in range(head // part):
        cut_ref[q * images : (q + 1) * images, :] = aux_grad[:, q * part : (q + 1) * part]


def aux_backward(got, aux_pre, part, norm):
    images, head = aux_pre.shape
    return call(
        functools.partial(aux_kernel, norm),
        [shape((images, head), BF16), shape((images * head // part, part), BF16)],
        limit=16,
        flops=2e10,
        name="aux_backward",
    )(got, aux_pre)


def class_kernel(norm, where_ref, klass_ref, got_ref, stats_ref, mine_ref, other_ref, class_ref, aux_ref):
    groups, images, _ = got_ref.shape
    head = class_ref.shape[1]
    classes, part = class_ref.shape[0], aux_ref.shape[0]
    got = got_ref[...].reshape(groups * images, -1)
    stats = [from_digits(stats_ref[e]) for e in range(groups)]
    tops, denoms = [], []
    for d in range(groups):
        top = functools.reduce(jnp.maximum, [s[:, TOPS + d : TOPS + d + 1] for s in stats])
        tops.append(top)
        denoms.append(sum(s[:, DENOMS + d : DENOMS + d + 1] * jnp.exp(s[:, TOPS + d : TOPS + d + 1] - top) for s in stats))
    top, denom = jnp.concatenate(tops, axis=0), jnp.concatenate(denoms, axis=0)
    logits = dot(got[:, :head], klass_ref[...], COLS_1)
    ids = lax.broadcasted_iota(jnp.int32, logits.shape, 1) + where_ref[ME] * classes
    onehot = jnp.where(labels_of(got, head) == ids, 1.0, 0.0)
    logit_grad = ((jnp.exp(logits - top) / denom - onehot) / norm).astype(BF16)
    class_ref[...] = dot(logit_grad, got[:, :head], ROWS_0)
    total = jnp.zeros(aux_ref.shape, F32)
    for d in range(groups):
        k, ref = d // 2, other_ref if d % 2 else mine_ref
        grad = jnp.concatenate([ref[k, q * images : (q + 1) * images] for q in range(head // part)], axis=1)
        pooled = got_ref[where_ref[ME] ^ d, :, head : head + part]
        total += dot(pooled, grad, ROWS_0).astype(BF16).astype(F32)
    aux_ref[...] = total


def class_backward(where, klass, got, partial, mine, other, norm):
    groups, images, wide = partial.shape
    classes, head = klass.shape
    whole = lambda *dims: pl.BlockSpec(dims, lambda i: (0,) * len(dims))
    part = mine.shape[2]
    return call(
        functools.partial(class_kernel, norm),
        [shape((classes, head), F32), shape((part, head), F32)],
        limit=20,
        flops=2 * groups * images * classes * head,
        moved=4 * classes * head,
        grid=(1,),
        in_specs=[
            SMEM,
            whole(*klass.shape),
            whole(*got.shape),
            pl.BlockSpec((groups, images, LANES), lambda i: (0, 0, wide // LANES - 1)),
            whole(*mine.shape),
            whole(*other.shape),
        ],
        out_specs=[whole(classes, head), whole(part, head)],
        name="class_backward",
    )(where, klass, got, partial, mine, other)


def chip_kernel(chips, below, collect, where_ref, keep_ref, got_ref, *refs):
    refs, outs = refs[: below + collect], refs[below + collect :]
    n = keep_ref.shape[1]
    chip = where_ref[ME] >> 1
    for k in range(chips):
        outs[k][:n] = (keep_ref[chip ^ k].astype(F32) + got_ref[chip ^ k].astype(F32)).astype(BF16)
        for ref in refs[:below]:
            outs[k][n:] = ref[...]
    if collect:
        size = outs[-1].shape[1]
        for k, ref in enumerate(refs[below:]):
            outs[-1][k] = ref[ref.shape[0] - size :]


def add_cores(where, keep, send, below=(), collect=(), size=0):
    chips, n, part = keep.shape
    rows = n + sum(e.shape[0] for e in below)
    outs = [shape((rows, part), BF16)] * chips
    if collect:
        outs.append(shape((len(collect), size, part), BF16))
    outs = call(
        functools.partial(chip_kernel, chips, len(below), len(collect)),
        outs,
        limit=16,
        in_specs=[SMEM, VMEM, VMEM, *[VMEM] * (len(below) + len(collect))],
        name="add_cores",
    )(where, keep, swap(send, "dp", 1), *below, *collect)
    return (outs[:chips], outs[chips]) if collect else outs


def exchange_chips(parts):
    return [parts[0]] + [swap(part, "dp", 2 * k) for k, part in enumerate(parts) if k]


def finish_kernel(inner, chips, *refs):
    early, last, (first_ref, second_ref, decode_ref) = refs[:chips], refs[chips : 2 * chips], refs[2 * chips :]
    n = decode_ref.shape[1]
    total = sum(ref[...].astype(F32) for ref in last)
    first_ref[...] = total[inner:].T
    tall, part = second_ref.shape[0], total.shape[1]
    for q in range(inner // tall):
        second_ref[:, q * part : (q + 1) * part] = total[q * tall : (q + 1) * tall]
    decode_ref[...] = sum(ref[:n].astype(F32) for ref in early).T


def finish(early, last, inner, groups, n):
    part = early[0].shape[1]
    return call(
        functools.partial(finish_kernel, inner, len(early)),
        [shape((part, inner), F32), shape((inner // groups, part * groups), F32), shape((part, n), F32)],
        limit=16,
        name="finish",
    )(*early, *last)


def local(acts, patches, labels, w_first, w_second, w_decode, w_aux, w_class):
    acts = acts[0].transpose(1, 0, 2)
    pix, images, width = acts.shape
    groups, count = lax.axis_size("dp"), lax.axis_size("section")
    me, section = lax.axis_index("dp"), lax.axis_index("section")
    scale = (groups * images * pix) ** -0.5
    norm = (groups * images) ** 0.5
    first, second, decode, aux, klass = w_first[0], w_second[0], w_decode[0], w_aux[0], w_class[0]
    inner = first.shape[1]
    n_decode = decode.shape[1]
    rows = pix * images

    paired = count == 4 and patches.shape[2] == 192
    if paired:
        near = [section ^ k for k in range(4)]
        tiles = [t for s in near for t in (3 * (s >> 1) + 2 * (s & 1), 3 * (s >> 1) + 1)]
        where = jnp.stack([section & 1, me & 1, me, *tiles]).astype(jnp.int32)
        turned = patches.transpose(0, 2, 1)
        halves = [pack(where, turned, h) for h in range(2)]
        x, y = [swap(halves[0], "section", 1)], [swap(halves[1], "section", 2)]
        first = after(first, halves[1])
    else:
        where = jnp.stack([section & 1, me & 1, me]).astype(jnp.int32)
        target = lax.all_gather(patches, "section", axis=2, tiled=True).transpose(1, 0, 2)

    hidden, feature, aux_pre, sent = forward(acts, first, second, aux, labels, groups)
    if paired:
        sent = after(sent, x[0])
        diagonal = [swap(after(x[0], aux_pre), "section", 2), swap(after(y[0], aux_pre), "section", 1)]
        x.append(swap(halves[1], "section", 1))
        y.insert(0, swap(halves[0], "section", 2))
        target = patch_operands([halves, x, y, diagonal], [0, 1, 2, 3], [0, 1, 2, 3])
    else:
        target = [target], [pl.BlockSpec((pix // STEPS, images, n_decode), lambda g, where: (g, 0, 0))]
    got = exchange(sent)
    sent = class_logits(where, got, klass)
    partial = exchange(sent)
    grad, keep, send = residual(after(where, sent), feature, decode, *target, images, scale, groups)
    aux_grad, aux_cut = aux_backward(partial, aux_pre, width // groups, norm)
    chip_decode = add_cores(where, keep, send, [aux_cut])
    sum_decode = exchange_chips(chip_decode)
    keep, send = backward(
        where, grad, hidden, acts.reshape(rows, width), decode, after(aux_grad, chip_decode[0]), aux, second, groups
    )
    chip_last, mine = add_cores(where, keep, after(send, sum_decode), collect=sum_decode, size=aux_cut.shape[0])
    sum_last = exchange_chips(chip_last)
    grad_class, grad_aux = class_backward(where, klass, got, partial, mine, swap(mine, "dp", 1), norm)
    grad_first, grad_second, grad_decode = finish(sum_decode, sum_last, inner, groups, n_decode)
    return grad_first[None], grad_second[None], grad_decode[None], grad_aux[None], grad_class[None]


def solution(mesh):
    in_specs = (
        P("section", "dp", None, None),
        P("dp", None, "section"),
        P("dp"),
        P("section", None, None),
        P("section", None, None),
        P("section", None, None),
        P("section", None, None),
        P("section", "dp", None),
    )
    out_specs = (P("section", "dp", None),) * 5
    return jax.shard_map(local, mesh=mesh, in_specs=in_specs, out_specs=out_specs, check_vma=False)
```

```python
import functools

import jax
import jax.numpy as jnp
from jax import lax
from jax.experimental import pallas as pl
from jax.experimental.pallas import tpu as pltpu
from jax.sharding import PartitionSpec as P

F32 = jnp.float32
BF16 = jnp.bfloat16
STEPS = 4
LANES = 128
TILE = 256
MIB = 1024 * 1024
ROWS_0 = (((0,), (0,)), ((), ()))
COLS_1 = (((1,), (1,)), ((), ()))
PARITY, CORE, ME, TILES = 0, 1, 2, 3


def dot(left, right, dims=(((1,), (0,)), ((), ()))):
    return lax.dot_general(left, right, dims, preferred_element_type=F32)


def call(kernel, out_shape, *, limit, flops=0, moved=0, **kwargs):
    return pl.pallas_call(
        kernel,
        out_shape=out_shape,
        compiler_params=pltpu.CompilerParams(vmem_limit_bytes=limit * MIB),
        cost_estimate=pl.CostEstimate(flops=int(flops), bytes_accessed=int(moved), transcendentals=0),
        **kwargs,
    )


def shape(dims, kind):
    return jax.ShapeDtypeStruct(dims, kind)


SMEM = pl.BlockSpec(memory_space=pltpu.SMEM)
VMEM = pl.BlockSpec(memory_space=pltpu.VMEM)
HBM = pl.BlockSpec(memory_space=pltpu.HBM)


def swap(value, axis, bits):
    count = lax.axis_size(axis)
    return lax.ppermute(value, axis, [(i, i ^ bits) for i in range(count)])


def exchange(value, groups=None):
    return lax.all_to_all(value, "dp", 0, 0, axis_index_groups=groups, tiled=True)


def pack_kernel(first, where_ref, *refs):
    patches_refs, (out_ref, turned, own, shared) = refs[:-4], refs[-4:]
    several, span, pix = patches_refs[0].shape
    images = turned.shape[0]
    padded = turned.shape[1]
    count = out_ref.shape[0] // 3 * 2
    parity = where_ref[PARITY]
    at_own = pl.multiple_of(64 * parity, 64)
    at_shared = pl.multiple_of(128 * (1 - parity), 64)
    row = lax.broadcasted_iota(jnp.int32, (padded, pix), 0)
    column = lax.broadcasted_iota(jnp.int32, (padded, pix), 1)
    pick = ((row < count) & (column == row + first)).astype(F32).astype(BF16)
    for i in range(images):
        patches_ref, j = patches_refs[i // several], i % several
        turned[i, :, :LANES] = dot(pick, patches_ref[j, pl.ds(at_own, LANES), :], COLS_1).astype(BF16)
        turned[i, :, LANES:] = dot(pick, patches_ref[j, pl.ds(at_shared, 64), :], COLS_1).astype(BF16)
    size = 16 * images
    row = lax.broadcasted_iota(jnp.int32, (size, size), 0)
    column = lax.broadcasted_iota(jnp.int32, (size, size), 1)
    order = (row // images == column % 16) & (row % images == column // 16)
    order = order.astype(F32).astype(BF16)
    for b in range(padded // 16):
        rows = turned[:, 16 * b : 16 * b + 16, :].reshape(size, span)
        out = dot(order, rows).astype(BF16)
        own[16 * b : 16 * b + 16] = out[:, :LANES].reshape(16, images, LANES)
        shared[16 * b : 16 * b + 16] = out[:, LANES:].reshape(16, images, 64)
    out_ref[:count] = own[:count]
    lower, upper = shared[: count // 2], shared[count // 2 : count]

    @pl.when(parity == 0)
    def _():
        out_ref[count:] = jnp.concatenate([lower, upper], axis=2)

    @pl.when(parity == 1)
    def _():
        out_ref[count:] = jnp.concatenate([upper, lower], axis=2)


def pack(where, patches, h):
    images, span, pix = patches.shape
    half = pix // 2
    padded = -(-half // 16) * 16
    several = images // 4
    lanes = LANES if h == 0 and half <= LANES < pix else pix
    group = lambda j: pl.BlockSpec((several, span, lanes), lambda i: (j, 0, 0))
    dims = (half + half // 2, images, LANES)
    return call(
        functools.partial(pack_kernel, h * half),
        shape(dims, BF16),
        limit=20,
        grid=(1,),
        in_specs=[SMEM, *[group(j) for j in range(4)]],
        out_specs=pl.BlockSpec(dims, lambda i: (0, 0, 0)),
        scratch_shapes=[
            pltpu.VMEM((images, padded, span), BF16),
            pltpu.VMEM((padded, images, LANES), BF16),
            pltpu.VMEM((padded, images, 64), BF16),
        ],
        name="pack_patches",
    )(where, *[patches] * 4)


def after(value, other):
    return lax.optimization_barrier((value, other))[0]


def forward_kernel(n_tiles, pix, *refs):
    acts_refs, refs = refs[:n_tiles], refs[n_tiles:]
    first_ref, second_ref, aux_ref, labels_ref, hidden_ref = refs[:5]
    feature_refs, (aux_pre_ref, sent_ref, pooled) = refs[5:-3], refs[-3:]
    step = pl.program_id(0)
    block, images, _ = acts_refs[0].shape
    cut = lambda j: slice(j * TILE, (j + 1) * TILE)
    start = step == 0
    halves = []
    for a, b in ((0, block // 2), (block // 2, block)):
        flat = jnp.concatenate([ref[a:b].reshape((b - a) * images, TILE) for ref in acts_refs], axis=1)
        halves.append((a, b, flat, jnp.maximum(dot(flat, first_ref[...]), 0.0).astype(BF16)))
    for a, b, flat, hidden in halves:
        rows = slice(a * images, b * images)
        hidden_ref[rows] = hidden
        for j, feature_ref in enumerate(feature_refs):
            feature = (flat[:, cut(j)].astype(F32) + dot(hidden, second_ref[:, cut(j)])).astype(BF16)
            feature_ref[rows] = feature
            sums = jnp.sum(feature.reshape(b - a, images, TILE).astype(F32), axis=0)
            pooled[:, cut(j)] = sums + (pooled[:, cut(j)] if a else jnp.where(start, 0.0, pooled[:, cut(j)]))

    @pl.when(step == pl.num_programs(0) - 1)
    def _():
        groups = sent_ref.shape[0]
        width, head = aux_ref.shape
        part = width // groups
        mean = (pooled[...] / pix).astype(BF16)
        aux_pre = dot(mean, aux_ref[...])
        aux_pre_ref[...] = aux_pre
        out = jnp.maximum(aux_pre, 0.0).astype(BF16)
        row = lax.broadcasted_iota(jnp.int32, (images, LANES), 0)
        lane = lax.broadcasted_iota(jnp.int32, (images, LANES), 1)
        digits = jnp.zeros((images, LANES), jnp.int32)
        for i in range(images):
            label = labels_ref[i]
            digits = jnp.where((row == i) & (lane == 0), label // LANES, digits)
            digits = jnp.where((row == i) & (lane == 1), label % LANES, digits)
        digits = digits.astype(F32).astype(BF16)
        for d in range(groups):
            sent_ref[d, :, :head] = out
            sent_ref[d, :, head : head + part] = mean[:, d * part : (d + 1) * part]
            sent_ref[d, :, head + LANES :] = digits


def forward(acts, first, second, aux, labels, groups):
    pix, images, width = acts.shape
    inner, head = first.shape[1], aux.shape[1]
    block = pix // STEPS
    n_tiles = width // TILE
    whole = lambda *dims: pl.BlockSpec(dims, lambda g: (0,) * len(dims))
    rows = lambda n: pl.BlockSpec((block * images, n), lambda g: (g, 0))
    column = lambda j: pl.BlockSpec((block, images, TILE), lambda g: (g, 0, j))
    hidden, *feature, aux_pre, sent = call(
        functools.partial(forward_kernel, n_tiles, pix),
        [
            shape((pix * images, inner), BF16),
            *[shape((pix * images, TILE), BF16)] * n_tiles,
            shape((images, head), F32),
            shape((groups, images, head + 2 * LANES), BF16),
        ],
        limit=58,
        grid=(STEPS,),
        in_specs=[
            *[column(j) for j in range(n_tiles)],
            whole(*first.shape),
            whole(*second.shape),
            whole(*aux.shape),
            SMEM,
        ],
        out_specs=[
            rows(inner),
            *[rows(TILE)] * n_tiles,
            whole(images, head),
            whole(groups, images, head + 2 * LANES),
        ],
        scratch_shapes=[pltpu.VMEM((images, width), F32)],
        name="forward",
    )(*[acts] * n_tiles, first, second, aux, labels)
    return hidden, feature, aux_pre, sent


def own_index(h):
    per_half = STEPS // 2
    return lambda g, where: (jnp.clip(g - h * per_half, 0, per_half - 1), 0, 0)


def patch_operands(blocks, own_blocks, shared_blocks):
    args, specs = [], []
    for k in own_blocks:
        for h, half in enumerate(blocks[k]):
            dims = (half.shape[0] // 3,) + half.shape[1:]
            args.append(half)
            specs.append(pl.BlockSpec(dims, own_index(h)))
    for k in shared_blocks:
        for half in blocks[k]:
            dims = (half.shape[0] // 3,) + half.shape[1:]
            args.append(half)
            specs.append(pl.BlockSpec(dims, lambda g, where: (2, 0, 0)))
    return args, specs


def lay_target(g, where_ref, refs, target):
    if len(refs) == 1:
        target[...] = refs[0][...]
        return
    pairs = [refs[j : j + 2] for j in range(0, len(refs), 2)]
    own, shared = pairs[: len(pairs) // 2], pairs[len(pairs) // 2 :]
    per_half = STEPS // 2
    h, side = g // per_half, g % per_half
    lanes = lambda j: pl.ds(pl.multiple_of(where_ref[TILES + j] * LANES, LANES), LANES)
    for k, pair in enumerate(own):
        target[:, :, lanes(2 * k)] = pair[h][...]
    for k in range(0, len(shared), 2):
        mine, other = shared[k][h][...].astype(F32), shared[k + 1][h][...].astype(F32)
        lane = lax.broadcasted_iota(jnp.int32, mine.shape, 2)
        value = jnp.where((lane < 64) == ((where_ref[PARITY] == 0) == (side == 0)), mine, other)
        if side:
            value = jnp.concatenate([value[:, :, 64:], value[:, :, :64]], axis=2)
        target[:, :, lanes(2 * k + 1)] = value.astype(BF16)


def deal(where_ref, sums, part, keep_ref, send_ref):
    core = where_ref[CORE]
    at = 0
    for value in sums:
        height = value.shape[0]
        for z in range(keep_ref.shape[0]):
            even = value[:, 2 * z * part : (2 * z + 1) * part]
            odd = value[:, (2 * z + 1) * part : (2 * z + 2) * part]
            mine = jnp.where(core == 0, even, odd)
            other = jnp.where(core == 0, odd, even)
            keep_ref[z, at : at + height, :] = mine.astype(BF16)
            send_ref[z, at : at + height, :] = other.astype(BF16)
        at += height


def copies_of(sources, held, sems):
    size, wide = held.shape[0] // STEPS, sources[0].shape[1]
    return [
        [
            pltpu.make_async_copy(
                source.at[pl.ds(g * size, size)], held.at[pl.ds(g * size, size), pl.ds(j * wide, wide)], sems.at[g, j]
            )
            for j, source in enumerate(sources)
        ]
        for g in range(STEPS)
    ]


def by_step(copies, body):
    step = pl.program_id(0)
    for g in range(STEPS):

        @pl.when(step == g)
        def _():
            if g == 0:
                for h in range(STEPS):
                    for copy in copies[h]:
                        copy.start()
            for copy in copies[g]:
                copy.wait()
            body(g)


def contract(g, rows, pairs):
    unit = rows // STEPS // TILE * TILE
    span = slice(g * unit, rows if g == STEPS - 1 else (g + 1) * unit)
    for total, left, right in pairs:
        now = dot(left[span], right[span], ROWS_0)
        total[...] = now if g == 0 else total[...] + now


def residual_kernel(groups, scale, n_feature, n_tiles, n_patch, where_ref, *refs):
    feature_refs, refs = refs[:n_feature], refs[n_feature:]
    decode_refs, refs = refs[:n_tiles], refs[n_tiles:]
    patch_refs, refs = refs[:n_patch], refs[n_patch:]
    grad_refs, refs = refs[:n_tiles], refs[n_tiles:]
    keep_ref, send_ref, target, feature, grads, total, sems = refs
    rows, width = feature.shape
    size = grad_refs[0].shape[0]

    def body(g):
        here = slice(g * size, (g + 1) * size)
        lay_target(g, where_ref, patch_refs, target)
        if g:
            contract(g - 1, rows, [(total, grads, feature)])
        now = feature[here]
        for j, grad_ref in enumerate(grad_refs):
            cut = slice(j * TILE, (j + 1) * TILE)
            recon = sum(dot(now[:, k : k + TILE], decode_refs[j][k : k + TILE]) for k in range(0, width, TILE))
            grad = ((recon - target[:, :, cut].reshape(size, TILE).astype(F32)) * scale).astype(BF16)
            grad_ref[...] = grad
            grads[here, cut] = grad
        if g == STEPS - 1:
            contract(g, rows, [(total, grads, feature)])
            deal(where_ref, [total], width // groups, keep_ref, send_ref)

    by_step(copies_of(feature_refs, feature, sems), body)


def residual(where, feature, decode, patch_args, patch_specs, images, scale, groups):
    rows = feature[0].shape[0]
    width, n = decode.shape
    size = rows // STEPS
    n_tiles = n // TILE
    parts = (groups // 2, n, width // groups)
    dealt = pl.BlockSpec(parts, lambda g, where: (0, 0, 0))
    block = pl.BlockSpec((size, TILE), lambda g, where: (g, 0))
    column = lambda j: pl.BlockSpec((width, TILE), lambda g, where: (0, j))
    *grad, keep, send = call(
        functools.partial(residual_kernel, groups, scale, len(feature), n_tiles, len(patch_args)),
        [*[shape((rows, TILE), BF16)] * n_tiles, shape(parts, BF16), shape(parts, BF16)],
        limit=44,
        flops=4 * rows * width * n,
        moved=rows * (2 * width + 6 * n),
        grid_spec=pltpu.PrefetchScalarGridSpec(
            num_scalar_prefetch=1,
            grid=(STEPS,),
            in_specs=[
                *[HBM] * len(feature),
                *[column(j) for j in range(n_tiles)],
                *patch_specs,
            ],
            out_specs=[*[block] * n_tiles, dealt, dealt],
            scratch_shapes=[
                pltpu.VMEM((size // images, images, n), BF16),
                pltpu.VMEM((rows, width), BF16),
                pltpu.VMEM((rows, n), BF16),
                pltpu.VMEM((n, width), F32),
                pltpu.SemaphoreType.DMA((STEPS, len(feature))),
            ],
        ),
        name="residual",
    )(where, *feature, *[decode] * n_tiles, *patch_args)
    return grad, keep, send


def backward_kernel(groups, n_grad, n_decode, where_ref, *refs):
    grad_refs, refs = refs[:n_grad], refs[n_grad:]
    decode_refs, refs = refs[:n_decode], refs[n_decode:]
    (hidden_ref, acts_ref, aux_grad_ref, aux_ref, second_ref, keep_ref, send_ref,
     hidden, acts, feature_grads, hidden_grads, pooled, total_second, total_first, sems) = refs
    rows, width = feature_grads.shape
    size = grad_refs[0].shape[0]
    images = aux_grad_ref.shape[0]
    pairs = [(total_second, hidden, feature_grads), (total_first, hidden_grads, acts)]

    def body(g):
        here = slice(g * size, (g + 1) * size)
        if g:
            contract(g - 1, rows, pairs)
        else:
            pooled[...] = dot(aux_grad_ref[...], aux_ref[...], COLS_1) / (rows // images)
        grad = jnp.concatenate([ref[...] for ref in grad_refs], axis=1)
        for j, decode_ref in enumerate(decode_refs):
            cut = slice(j * TILE, (j + 1) * TILE)
            back = dot(grad, decode_ref[...], COLS_1).reshape(size // images, images, TILE)
            feature_grads[here, cut] = (back + pooled[:, cut][None]).astype(BF16).reshape(size, TILE)
        hidden_back = dot(feature_grads[here], second_ref[...], COLS_1)
        hidden_grads[here] = jnp.where(hidden[here].astype(F32) > 0, hidden_back, 0.0).astype(BF16)
        if g == STEPS - 1:
            contract(g, rows, pairs)
            part = width // groups
            tall = total_second.shape[0] // groups
            second = jnp.concatenate(
                [
                    jnp.concatenate(
                        [total_second[d * tall : (d + 1) * tall, q * part : (q + 1) * part] for q in range(groups)], axis=0
                    )
                    for d in range(groups)
                ],
                axis=1,
            )
            deal(where_ref, [second, total_first], part, keep_ref, send_ref)

    copies = zip(copies_of([hidden_ref], hidden, sems.at[0]), copies_of([acts_ref], acts, sems.at[1]))
    by_step([one + other for one, other in copies], body)


def backward(where, grad, hidden, acts, decode, aux_grad, aux, second, groups):
    rows, width = acts.shape
    inner, n = hidden.shape[1], len(grad) * TILE
    n_decode = width // TILE
    row_block = lambda j: pl.BlockSpec((TILE, n), lambda g, where: (j, 0))
    size = rows // STEPS
    parts = (groups // 2, 2 * inner, width // groups)
    dealt = pl.BlockSpec(parts, lambda g, where: (0, 0, 0))
    whole = lambda array: pl.BlockSpec(array.shape, lambda g, where: (0, 0))
    return call(
        functools.partial(backward_kernel, groups, len(grad), n_decode),
        [shape(parts, BF16), shape(parts, BF16)],
        limit=44,
        flops=2 * rows * width * (n + 3 * inner),
        moved=2 * rows * (width + n + inner),
        grid_spec=pltpu.PrefetchScalarGridSpec(
            num_scalar_prefetch=1,
            grid=(STEPS,),
            in_specs=[
                *[pl.BlockSpec((size, TILE), lambda g, where: (g, 0))] * len(grad),
                *[row_block(j) for j in range(n_decode)],
                HBM,
                HBM,
                whole(aux_grad),
                whole(aux),
                whole(second),
            ],
            out_specs=[dealt, dealt],
            scratch_shapes=[
                pltpu.VMEM((rows, inner), BF16),
                pltpu.VMEM((rows, width), BF16),
                pltpu.VMEM((rows, width), BF16),
                pltpu.VMEM((rows, inner), BF16),
                pltpu.VMEM((aux_grad.shape[0], width), F32),
                pltpu.VMEM((inner, width), F32),
                pltpu.VMEM((inner, width), F32),
                pltpu.SemaphoreType.DMA((2, STEPS, 1)),
            ],
        ),
        name="backward",
    )(where, *grad, *[decode] * n_decode, hidden, acts, aux_grad, aux, second)


TOPS, DENOMS = 3, 19
DIGIT = 40


def to_digits(value):
    rest, lanes = value, []
    for _ in range(3):
        digit = rest.astype(BF16).astype(F32)
        lanes.append(digit[:, :DIGIT])
        rest = rest - digit
    lanes.append(jnp.zeros((value.shape[0], LANES - 3 * DIGIT), F32))
    return jnp.concatenate(lanes, axis=1).astype(BF16)


def from_digits(value):
    value = value.astype(F32)
    return sum(value[:, j * DIGIT : (j + 1) * DIGIT] for j in (2, 1, 0))


def labels_of(got, head):
    digits = got[:, head + LANES : head + LANES + 2].astype(F32)
    return (digits[:, 0:1] * LANES + digits[:, 1:2]).astype(jnp.int32)


def logits_kernel(where_ref, got_ref, klass_ref, sent_ref, logits_ref):
    groups, images, _ = got_ref.shape
    classes, head = klass_ref.shape
    got = got_ref[...].reshape(groups * images, -1)
    logits_ref[...] = dot(got[:, :head], klass_ref[...], COLS_1)
    logits = logits_ref[...]
    ids = lax.broadcasted_iota(jnp.int32, logits.shape, 1) + where_ref[ME] * classes
    hit = labels_of(got, head) == ids
    top = jnp.max(logits, axis=1, keepdims=True)
    expo = jnp.exp(logits - top)
    denom = jnp.sum(expo, axis=1, keepdims=True)
    own = jnp.sum(jnp.where(hit, expo, 0.0), axis=1, keepdims=True)
    rest = jnp.where(hit, 0.0, expo).astype(BF16)
    onehot = jnp.where(hit, 1.0, 0.0).astype(BF16)
    sent_ref[:, :, :head] = dot(rest, klass_ref[...]).astype(BF16).reshape(groups, images, head)
    sent_ref[:, :, head : 2 * head] = dot(onehot, klass_ref[...]).astype(BF16).reshape(groups, images, head)
    lane = lax.broadcasted_iota(jnp.int32, (images, LANES), 1)
    cut = lambda value, d: value[d * images : (d + 1) * images]
    common = jnp.zeros((images, LANES), F32)
    for d in range(groups):
        common = jnp.where(lane == TOPS + d, cut(top, d), common)
        common = jnp.where(lane == DENOMS + d, cut(denom, d), common)
    for d in range(groups):
        stats = jnp.where(lane == 1, cut(denom, d), jnp.where(lane == 2, cut(own, d), common))
        sent_ref[d, :, 2 * head :] = to_digits(jnp.where(lane == 0, cut(top, d), stats))


def class_logits(where, got, klass):
    groups, images, _ = got.shape
    classes, head = klass.shape
    return call(
        logits_kernel,
        shape((groups, images, 2 * head + LANES), BF16),
        limit=16,
        in_specs=[SMEM, VMEM, VMEM],
        scratch_shapes=[pltpu.VMEM((groups * images, classes), F32)],
        name="class_logits",
    )(where, got, klass)


def aux_kernel(norm, got_ref, aux_pre_ref, grad_ref, cut_ref):
    groups, images, _ = got_ref.shape
    head = aux_pre_ref.shape[1]
    stats = [from_digits(got_ref[d, :, 2 * head :]) for d in range(groups)]
    top = functools.reduce(jnp.maximum, [s[:, 0:1] for s in stats])
    scales = [jnp.exp(s[:, 0:1] - top) for s in stats]
    denom = sum(s[:, 1:2] * f for s, f in zip(stats, scales))
    own = sum(s[:, 2:3] * f for s, f in zip(stats, scales)) / denom
    rest = sum(got_ref[d, :, :head].astype(F32) * scales[d] for d in range(groups)) / (denom * norm)
    row = sum(got_ref[d, :, head : 2 * head].astype(F32) for d in range(groups))
    back = rest + row * ((own - 1.0) / norm).astype(BF16).astype(F32)
    aux_grad = jnp.where(aux_pre_ref[...] > 0, back, 0.0).astype(BF16)
    grad_ref[...] = aux_grad
    part = cut_ref.shape[1]
    for q in range(head // part):
        cut_ref[q * images : (q + 1) * images, :] = aux_grad[:, q * part : (q + 1) * part]


def aux_backward(got, aux_pre, part, norm):
    images, head = aux_pre.shape
    return call(
        functools.partial(aux_kernel, norm),
        [shape((images, head), BF16), shape((images * head // part, part), BF16)],
        limit=16,
        flops=2e10,
        name="aux_backward",
    )(got, aux_pre)


def class_kernel(norm, where_ref, klass_ref, got_ref, stats_ref, mine_ref, other_ref, class_ref, aux_ref):
    groups, images, _ = got_ref.shape
    head = class_ref.shape[1]
    classes, part = class_ref.shape[0], aux_ref.shape[0]
    got = got_ref[...].reshape(groups * images, -1)
    stats = [from_digits(stats_ref[e]) for e in range(groups)]
    tops, denoms = [], []
    for d in range(groups):
        top = functools.reduce(jnp.maximum, [s[:, TOPS + d : TOPS + d + 1] for s in stats])
        tops.append(top)
        denoms.append(sum(s[:, DENOMS + d : DENOMS + d + 1] * jnp.exp(s[:, TOPS + d : TOPS + d + 1] - top) for s in stats))
    top, denom = jnp.concatenate(tops, axis=0), jnp.concatenate(denoms, axis=0)
    logits = dot(got[:, :head], klass_ref[...], COLS_1)
    ids = lax.broadcasted_iota(jnp.int32, logits.shape, 1) + where_ref[ME] * classes
    onehot = jnp.where(labels_of(got, head) == ids, 1.0, 0.0)
    logit_grad = ((jnp.exp(logits - top) / denom - onehot) / norm).astype(BF16)
    class_ref[...] = dot(logit_grad, got[:, :head], ROWS_0)
    total = jnp.zeros(aux_ref.shape, F32)
    for d in range(groups):
        k, ref = d // 2, other_ref if d % 2 else mine_ref
        grad = jnp.concatenate([ref[k, q * images : (q + 1) * images] for q in range(head // part)], axis=1)
        pooled = got_ref[where_ref[ME] ^ d, :, head : head + part]
        total += dot(pooled, grad, ROWS_0).astype(BF16).astype(F32)
    aux_ref[...] = total


def class_backward(where, klass, got, partial, mine, other, norm):
    groups, images, wide = partial.shape
    classes, head = klass.shape
    whole = lambda *dims: pl.BlockSpec(dims, lambda i: (0,) * len(dims))
    part = mine.shape[2]
    return call(
        functools.partial(class_kernel, norm),
        [shape((classes, head), F32), shape((part, head), F32)],
        limit=20,
        flops=2 * groups * images * classes * head,
        moved=4 * classes * head,
        grid=(1,),
        in_specs=[
            SMEM,
            whole(*klass.shape),
            whole(*got.shape),
            pl.BlockSpec((groups, images, LANES), lambda i: (0, 0, wide // LANES - 1)),
            whole(*mine.shape),
            whole(*other.shape),
        ],
        out_specs=[whole(classes, head), whole(part, head)],
        name="class_backward",
    )(where, klass, got, partial, mine, other)


def chip_kernel(chips, below, collect, where_ref, keep_ref, got_ref, *refs):
    refs, outs = refs[: below + collect], refs[below + collect :]
    n = keep_ref.shape[1]
    chip = where_ref[ME] >> 1
    for k in range(chips):
        outs[k][:n] = (keep_ref[chip ^ k].astype(F32) + got_ref[chip ^ k].astype(F32)).astype(BF16)
        for ref in refs[:below]:
            outs[k][n:] = ref[...]
    if collect:
        size = outs[-1].shape[1]
        for k, ref in enumerate(refs[below:]):
            outs[-1][k] = ref[ref.shape[0] - size :]


def add_cores(where, keep, send, below=(), collect=(), size=0):
    chips, n, part = keep.shape
    rows = n + sum(e.shape[0] for e in below)
    outs = [shape((rows, part), BF16)] * chips
    if collect:
        outs.append(shape((len(collect), size, part), BF16))
    outs = call(
        functools.partial(chip_kernel, chips, len(below), len(collect)),
        outs,
        limit=16,
        in_specs=[SMEM, VMEM, VMEM, *[VMEM] * (len(below) + len(collect))],
        name="add_cores",
    )(where, keep, swap(send, "dp", 1), *below, *collect)
    return (outs[:chips], outs[chips]) if collect else outs


def exchange_chips(parts):
    got = {k: swap(parts[k], "dp", 2 * k) for k in reversed(range(1, len(parts)))}
    return [parts[0]] + [got[k] for k in range(1, len(parts))]


def finish_kernel(inner, chips, *refs):
    early, last, (first_ref, second_ref, decode_ref) = refs[:chips], refs[chips : 2 * chips], refs[2 * chips :]
    n = decode_ref.shape[1]
    total = sum(ref[...].astype(F32) for ref in last)
    first_ref[...] = total[inner:].T
    tall, part = second_ref.shape[0], total.shape[1]
    for q in range(inner // tall):
        second_ref[:, q * part : (q + 1) * part] = total[q * tall : (q + 1) * tall]
    decode_ref[...] = sum(ref[:n].astype(F32) for ref in early).T


def finish(early, last, inner, groups, n):
    part = early[0].shape[1]
    return call(
        functools.partial(finish_kernel, inner, len(early)),
        [shape((part, inner), F32), shape((inner // groups, part * groups), F32), shape((part, n), F32)],
        limit=16,
        name="finish",
    )(*early, *last)


def local(acts, patches, labels, w_first, w_second, w_decode, w_aux, w_class):
    acts = acts[0].transpose(1, 0, 2)
    pix, images, width = acts.shape
    groups, count = lax.axis_size("dp"), lax.axis_size("section")
    me, section = lax.axis_index("dp"), lax.axis_index("section")
    scale = (groups * images * pix) ** -0.5
    norm = (groups * images) ** 0.5
    first, second, decode, aux, klass = w_first[0], w_second[0], w_decode[0], w_aux[0], w_class[0]
    inner = first.shape[1]
    n_decode = decode.shape[1]
    rows = pix * images

    paired = count == 4 and patches.shape[2] == 192
    if paired:
        near = [section ^ k for k in range(4)]
        tiles = [t for s in near for t in (3 * (s >> 1) + 2 * (s & 1), 3 * (s >> 1) + 1)]
        where = jnp.stack([section & 1, me & 1, me, *tiles]).astype(jnp.int32)
        turned = patches.transpose(0, 2, 1)
        halves = [pack(where, turned, h) for h in range(2)]
        x, y = [swap(halves[0], "section", 1)], [swap(halves[1], "section", 2)]
        first = after(first, halves[1])
    else:
        where = jnp.stack([section & 1, me & 1, me]).astype(jnp.int32)
        target = lax.all_gather(patches, "section", axis=2, tiled=True).transpose(1, 0, 2)

    hidden, feature, aux_pre, sent = forward(acts, first, second, aux, labels, groups)
    if paired:
        sent = after(sent, x[0])
    got = exchange(sent)
    if paired:
        diagonal = [swap(after(x[0], got), "section", 2), swap(after(y[0], got), "section", 1)]
        x.append(swap(halves[1], "section", 1))
        y.insert(0, swap(halves[0], "section", 2))
        target = patch_operands([halves, x, y, diagonal], [0, 1, 2, 3], [0, 1, 2, 3])
    else:
        target = [target], [pl.BlockSpec((pix // STEPS, images, n_decode), lambda g, where: (g, 0, 0))]
    sent = class_logits(where, got, klass)
    partial = exchange(sent)
    grad, keep, send = residual(after(where, sent), feature, decode, *target, images, scale, groups)
    aux_grad, aux_cut = aux_backward(partial, aux_pre, width // groups, norm)
    chip_decode = add_cores(where, keep, send, [aux_cut])
    sum_decode = exchange_chips(chip_decode)
    keep, send = backward(
        where, grad, hidden, acts.reshape(rows, width), decode, after(aux_grad, chip_decode[0]), aux, second, groups
    )
    chip_last, mine = add_cores(where, keep, after(send, sum_decode), collect=sum_decode, size=aux_cut.shape[0])
    sum_last = exchange_chips(chip_last)
    grad_class, grad_aux = class_backward(where, klass, got, partial, mine, swap(mine, "dp", 1), norm)
    grad_first, grad_second, grad_decode = finish(sum_decode, sum_last, inner, groups, n_decode)
    return grad_first[None], grad_second[None], grad_decode[None], grad_aux[None], grad_class[None]


def solution(mesh):
    in_specs = (
        P("section", "dp", None, None),
        P("dp", None, "section"),
        P("dp"),
        P("section", None, None),
        P("section", None, None),
        P("section", None, None),
        P("section", None, None),
        P("section", "dp", None),
    )
    out_specs = (P("section", "dp", None),) * 5
    return jax.shard_map(local, mesh=mesh, in_specs=in_specs, out_specs=out_specs, check_vma=False)
```

```python
import functools

import jax
import jax.numpy as jnp
from jax import lax
from jax.experimental import pallas as pl
from jax.experimental.pallas import tpu as pltpu
from jax.sharding import PartitionSpec as P

F32 = jnp.float32
BF16 = jnp.bfloat16
STEPS = 4
LANES = 128
TILE = 256
MIB = 1024 * 1024
ROWS_0 = (((0,), (0,)), ((), ()))
COLS_1 = (((1,), (1,)), ((), ()))
PARITY, CORE, ME, TILES = 0, 1, 2, 3


def dot(left, right, dims=(((1,), (0,)), ((), ()))):
    return lax.dot_general(left, right, dims, preferred_element_type=F32)


def call(kernel, out_shape, *, limit, flops=0, moved=0, **kwargs):
    return pl.pallas_call(
        kernel,
        out_shape=out_shape,
        compiler_params=pltpu.CompilerParams(vmem_limit_bytes=limit * MIB),
        cost_estimate=pl.CostEstimate(flops=int(flops), bytes_accessed=int(moved), transcendentals=0),
        **kwargs,
    )


def shape(dims, kind):
    return jax.ShapeDtypeStruct(dims, kind)


SMEM = pl.BlockSpec(memory_space=pltpu.SMEM)
VMEM = pl.BlockSpec(memory_space=pltpu.VMEM)
HBM = pl.BlockSpec(memory_space=pltpu.HBM)


def swap(value, axis, bits):
    count = lax.axis_size(axis)
    return lax.ppermute(value, axis, [(i, i ^ bits) for i in range(count)])


def exchange(value, groups=None):
    return lax.all_to_all(value, "dp", 0, 0, axis_index_groups=groups, tiled=True)


def pack_kernel(first, where_ref, *refs):
    patches_refs, (out_ref, turned, own, shared) = refs[:-4], refs[-4:]
    several, span, pix = patches_refs[0].shape
    images = turned.shape[0]
    padded = turned.shape[1]
    count = out_ref.shape[0] // 3 * 2
    parity = where_ref[PARITY]
    at_own = pl.multiple_of(64 * parity, 64)
    at_shared = pl.multiple_of(128 * (1 - parity), 64)
    row = lax.broadcasted_iota(jnp.int32, (padded, pix), 0)
    column = lax.broadcasted_iota(jnp.int32, (padded, pix), 1)
    pick = ((row < count) & (column == row + first)).astype(F32).astype(BF16)
    for i in range(images):
        patches_ref, j = patches_refs[i // several], i % several
        turned[i, :, :LANES] = dot(pick, patches_ref[j, pl.ds(at_own, LANES), :], COLS_1).astype(BF16)
        turned[i, :, LANES:] = dot(pick, patches_ref[j, pl.ds(at_shared, 64), :], COLS_1).astype(BF16)
    size = 16 * images
    row = lax.broadcasted_iota(jnp.int32, (size, size), 0)
    column = lax.broadcasted_iota(jnp.int32, (size, size), 1)
    order = (row // images == column % 16) & (row % images == column // 16)
    order = order.astype(F32).astype(BF16)
    for b in range(padded // 16):
        rows = turned[:, 16 * b : 16 * b + 16, :].reshape(size, span)
        out = dot(order, rows).astype(BF16)
        own[16 * b : 16 * b + 16] = out[:, :LANES].reshape(16, images, LANES)
        shared[16 * b : 16 * b + 16] = out[:, LANES:].reshape(16, images, 64)
    out_ref[:count] = own[:count]
    lower, upper = shared[: count // 2], shared[count // 2 : count]

    @pl.when(parity == 0)
    def _():
        out_ref[count:] = jnp.concatenate([lower, upper], axis=2)

    @pl.when(parity == 1)
    def _():
        out_ref[count:] = jnp.concatenate([upper, lower], axis=2)


def pack(where, patches, h):
    images, span, pix = patches.shape
    half = pix // 2
    padded = -(-half // 16) * 16
    several = images // 4
    lanes = LANES if h == 0 and half <= LANES < pix else pix
    group = lambda j: pl.BlockSpec((several, span, lanes), lambda i: (j, 0, 0))
    dims = (half + half // 2, images, LANES)
    return call(
        functools.partial(pack_kernel, h * half),
        shape(dims, BF16),
        limit=20,
        grid=(1,),
        in_specs=[SMEM, *[group(j) for j in range(4)]],
        out_specs=pl.BlockSpec(dims, lambda i: (0, 0, 0)),
        scratch_shapes=[
            pltpu.VMEM((images, padded, span), BF16),
            pltpu.VMEM((padded, images, LANES), BF16),
            pltpu.VMEM((padded, images, 64), BF16),
        ],
        name="pack_patches",
    )(where, *[patches] * 4)


def after(value, other):
    return lax.optimization_barrier((value, other))[0]


def forward_kernel(n_tiles, pix, *refs):
    acts_refs, refs = refs[:n_tiles], refs[n_tiles:]
    first_ref, second_ref, aux_ref, labels_ref, hidden_ref = refs[:5]
    feature_refs, (aux_pre_ref, sent_ref, pooled) = refs[5:-3], refs[-3:]
    step = pl.program_id(0)
    block, images, _ = acts_refs[0].shape
    cut = lambda j: slice(j * TILE, (j + 1) * TILE)
    start = step == 0
    halves = []
    for a, b in ((0, block // 2), (block // 2, block)):
        flat = jnp.concatenate([ref[a:b].reshape((b - a) * images, TILE) for ref in acts_refs], axis=1)
        halves.append((a, b, flat, jnp.maximum(dot(flat, first_ref[...]), 0.0).astype(BF16)))
    for a, b, flat, hidden in halves:
        rows = slice(a * images, b * images)
        hidden_ref[rows] = hidden
        for j, feature_ref in enumerate(feature_refs):
            feature = (flat[:, cut(j)].astype(F32) + dot(hidden, second_ref[:, cut(j)])).astype(BF16)
            feature_ref[rows] = feature
            sums = jnp.sum(feature.reshape(b - a, images, TILE).astype(F32), axis=0)
            pooled[:, cut(j)] = sums + (pooled[:, cut(j)] if a else jnp.where(start, 0.0, pooled[:, cut(j)]))

    @pl.when(step == pl.num_programs(0) - 1)
    def _():
        groups = sent_ref.shape[0]
        width, head = aux_ref.shape
        part = width // groups
        mean = (pooled[...] / pix).astype(BF16)
        aux_pre = dot(mean, aux_ref[...])
        aux_pre_ref[...] = aux_pre
        out = jnp.maximum(aux_pre, 0.0).astype(BF16)
        row = lax.broadcasted_iota(jnp.int32, (images, LANES), 0)
        lane = lax.broadcasted_iota(jnp.int32, (images, LANES), 1)
        digits = jnp.zeros((images, LANES), jnp.int32)
        for i in range(images):
            label = labels_ref[i]
            digits = jnp.where((row == i) & (lane == 0), label // LANES, digits)
            digits = jnp.where((row == i) & (lane == 1), label % LANES, digits)
        digits = digits.astype(F32).astype(BF16)
        for d in range(groups):
            sent_ref[d, :, :head] = out
            sent_ref[d, :, head : head + part] = mean[:, d * part : (d + 1) * part]
            sent_ref[d, :, head + LANES :] = digits


def forward(acts, first, second, aux, labels, groups):
    pix, images, width = acts.shape
    inner, head = first.shape[1], aux.shape[1]
    block = pix // STEPS
    n_tiles = width // TILE
    whole = lambda *dims: pl.BlockSpec(dims, lambda g: (0,) * len(dims))
    rows = lambda n: pl.BlockSpec((block * images, n), lambda g: (g, 0))
    column = lambda j: pl.BlockSpec((block, images, TILE), lambda g: (g, 0, j))
    hidden, *feature, aux_pre, sent = call(
        functools.partial(forward_kernel, n_tiles, pix),
        [
            shape((pix * images, inner), BF16),
            *[shape((pix * images, TILE), BF16)] * n_tiles,
            shape((images, head), F32),
            shape((groups, images, head + 2 * LANES), BF16),
        ],
        limit=58,
        grid=(STEPS,),
        in_specs=[
            *[column(j) for j in range(n_tiles)],
            whole(*first.shape),
            whole(*second.shape),
            whole(*aux.shape),
            SMEM,
        ],
        out_specs=[
            rows(inner),
            *[rows(TILE)] * n_tiles,
            whole(images, head),
            whole(groups, images, head + 2 * LANES),
        ],
        scratch_shapes=[pltpu.VMEM((images, width), F32)],
        name="forward",
    )(*[acts] * n_tiles, first, second, aux, labels)
    return hidden, feature, aux_pre, sent


def own_index(h):
    per_half = STEPS // 2
    return lambda g, where: (jnp.clip(g - h * per_half, 0, per_half - 1), 0, 0)


def patch_operands(blocks, own_blocks, shared_blocks):
    args, specs = [], []
    for k in own_blocks:
        for h, half in enumerate(blocks[k]):
            dims = (half.shape[0] // 3,) + half.shape[1:]
            args.append(half)
            specs.append(pl.BlockSpec(dims, own_index(h)))
    for k in shared_blocks:
        for half in blocks[k]:
            dims = (half.shape[0] // 3,) + half.shape[1:]
            args.append(half)
            specs.append(pl.BlockSpec(dims, lambda g, where: (2, 0, 0)))
    return args, specs


def lay_target(g, where_ref, refs, target):
    if len(refs) == 1:
        target[...] = refs[0][...]
        return
    pairs = [refs[j : j + 2] for j in range(0, len(refs), 2)]
    own, shared = pairs[: len(pairs) // 2], pairs[len(pairs) // 2 :]
    per_half = STEPS // 2
    h, side = g // per_half, g % per_half
    lanes = lambda j: pl.ds(pl.multiple_of(where_ref[TILES + j] * LANES, LANES), LANES)
    for k, pair in enumerate(own):
        target[:, :, lanes(2 * k)] = pair[h][...]
    for k in range(0, len(shared), 2):
        mine, other = shared[k][h][...].astype(F32), shared[k + 1][h][...].astype(F32)
        lane = lax.broadcasted_iota(jnp.int32, mine.shape, 2)
        value = jnp.where((lane < 64) == ((where_ref[PARITY] == 0) == (side == 0)), mine, other)
        if side:
            value = jnp.concatenate([value[:, :, 64:], value[:, :, :64]], axis=2)
        target[:, :, lanes(2 * k + 1)] = value.astype(BF16)


def deal(where_ref, sums, part, keep_ref, send_ref):
    core = where_ref[CORE]
    at = 0
    for value in sums:
        height = value.shape[0]
        for z in range(keep_ref.shape[0]):
            even = value[:, 2 * z * part : (2 * z + 1) * part]
            odd = value[:, (2 * z + 1) * part : (2 * z + 2) * part]
            mine = jnp.where(core == 0, even, odd)
            other = jnp.where(core == 0, odd, even)
            keep_ref[z, at : at + height, :] = mine.astype(BF16)
            send_ref[z, at : at + height, :] = other.astype(BF16)
        at += height


def copies_of(sources, held, sems):
    size, wide = held.shape[0] // STEPS, sources[0].shape[1]
    return [
        [
            pltpu.make_async_copy(
                source.at[pl.ds(g * size, size)], held.at[pl.ds(g * size, size), pl.ds(j * wide, wide)], sems.at[g, j]
            )
            for j, source in enumerate(sources)
        ]
        for g in range(STEPS)
    ]


def by_step(copies, body):
    step = pl.program_id(0)
    for g in range(STEPS):

        @pl.when(step == g)
        def _():
            if g == 0:
                for h in range(STEPS):
                    for copy in copies[h]:
                        copy.start()
            for copy in copies[g]:
                copy.wait()
            body(g)


def contract(g, rows, pairs):
    middle = rows // STEPS * 2 // TILE * TILE
    span = slice(0, middle) if g == 2 else slice(middle, rows)
    for total, left, right in pairs:
        now = dot(left[span], right[span], ROWS_0)
        total[...] = now if g == 2 else total[...] + now


def residual_kernel(groups, scale, n_feature, n_tiles, n_patch, where_ref, *refs):
    feature_refs, refs = refs[:n_feature], refs[n_feature:]
    decode_refs, refs = refs[:n_tiles], refs[n_tiles:]
    patch_refs, refs = refs[:n_patch], refs[n_patch:]
    grad_refs, refs = refs[:n_tiles], refs[n_tiles:]
    keep_ref, send_ref, target, feature, grads, total, sems = refs
    rows, width = feature.shape
    size = grad_refs[0].shape[0]

    def body(g):
        here = slice(g * size, (g + 1) * size)
        lay_target(g, where_ref, patch_refs, target)
        if g == 2:
            contract(g, rows, [(total, grads, feature)])
        now = feature[here]
        for j, grad_ref in enumerate(grad_refs):
            cut = slice(j * TILE, (j + 1) * TILE)
            recon = sum(dot(now[:, k : k + TILE], decode_refs[j][k : k + TILE]) for k in range(0, width, TILE))
            grad = ((recon - target[:, :, cut].reshape(size, TILE).astype(F32)) * scale).astype(BF16)
            grad_ref[...] = grad
            grads[here, cut] = grad
        if g == STEPS - 1:
            contract(g, rows, [(total, grads, feature)])
            deal(where_ref, [total], width // groups, keep_ref, send_ref)

    by_step(copies_of(feature_refs, feature, sems), body)


def residual(where, feature, decode, patch_args, patch_specs, images, scale, groups):
    rows = feature[0].shape[0]
    width, n = decode.shape
    size = rows // STEPS
    n_tiles = n // TILE
    parts = (groups // 2, n, width // groups)
    dealt = pl.BlockSpec(parts, lambda g, where: (0, 0, 0))
    block = pl.BlockSpec((size, TILE), lambda g, where: (g, 0))
    column = lambda j: pl.BlockSpec((width, TILE), lambda g, where: (0, j))
    *grad, keep, send = call(
        functools.partial(residual_kernel, groups, scale, len(feature), n_tiles, len(patch_args)),
        [*[shape((rows, TILE), BF16)] * n_tiles, shape(parts, BF16), shape(parts, BF16)],
        limit=58,
        flops=4 * rows * width * n,
        moved=rows * (2 * width + 6 * n),
        grid_spec=pltpu.PrefetchScalarGridSpec(
            num_scalar_prefetch=1,
            grid=(STEPS,),
            in_specs=[
                *[HBM] * len(feature),
                *[column(j) for j in range(n_tiles)],
                *patch_specs,
            ],
            out_specs=[*[block] * n_tiles, dealt, dealt],
            scratch_shapes=[
                pltpu.VMEM((size // images, images, n), BF16),
                pltpu.VMEM((rows, width), BF16),
                pltpu.VMEM((rows, n), BF16),
                pltpu.VMEM((n, width), F32),
                pltpu.SemaphoreType.DMA((STEPS, len(feature))),
            ],
        ),
        name="residual",
    )(where, *feature, *[decode] * n_tiles, *patch_args)
    return grad, keep, send


def backward_kernel(groups, n_grad, n_decode, where_ref, *refs):
    grad_refs, refs = refs[:n_grad], refs[n_grad:]
    decode_refs, refs = refs[:n_decode], refs[n_decode:]
    (hidden_ref, acts_ref, aux_grad_ref, aux_ref, second_ref, keep_ref, send_ref,
     hidden, acts, feature_grads, hidden_grads, pooled, total_second, total_first, sems) = refs
    rows, width = feature_grads.shape
    size = grad_refs[0].shape[0]
    images = aux_grad_ref.shape[0]
    pairs = [(total_second, hidden, feature_grads), (total_first, hidden_grads, acts)]

    def body(g):
        here = slice(g * size, (g + 1) * size)
        if g == 2:
            contract(g, rows, pairs)
        if g == 0:
            pooled[...] = dot(aux_grad_ref[...], aux_ref[...], COLS_1) / (rows // images)
        grad = jnp.concatenate([ref[...] for ref in grad_refs], axis=1)
        for j, decode_ref in enumerate(decode_refs):
            cut = slice(j * TILE, (j + 1) * TILE)
            back = dot(grad, decode_ref[...], COLS_1).reshape(size // images, images, TILE)
            feature_grads[here, cut] = (back + pooled[:, cut][None]).astype(BF16).reshape(size, TILE)
        hidden_back = dot(feature_grads[here], second_ref[...], COLS_1)
        hidden_grads[here] = jnp.where(hidden[here].astype(F32) > 0, hidden_back, 0.0).astype(BF16)
        if g == STEPS - 1:
            contract(g, rows, pairs)
            part = width // groups
            tall = total_second.shape[0] // groups
            second = jnp.concatenate(
                [
                    jnp.concatenate(
                        [total_second[d * tall : (d + 1) * tall, q * part : (q + 1) * part] for q in range(groups)], axis=0
                    )
                    for d in range(groups)
                ],
                axis=1,
            )
            deal(where_ref, [second, total_first], part, keep_ref, send_ref)

    copies = zip(copies_of([hidden_ref], hidden, sems.at[0]), copies_of([acts_ref], acts, sems.at[1]))
    by_step([one + other for one, other in copies], body)


def backward(where, grad, hidden, acts, decode, aux_grad, aux, second, groups):
    rows, width = acts.shape
    inner, n = hidden.shape[1], len(grad) * TILE
    n_decode = width // TILE
    row_block = lambda j: pl.BlockSpec((TILE, n), lambda g, where: (j, 0))
    size = rows // STEPS
    parts = (groups // 2, 2 * inner, width // groups)
    dealt = pl.BlockSpec(parts, lambda g, where: (0, 0, 0))
    whole = lambda array: pl.BlockSpec(array.shape, lambda g, where: (0, 0))
    return call(
        functools.partial(backward_kernel, groups, len(grad), n_decode),
        [shape(parts, BF16), shape(parts, BF16)],
        limit=44,
        flops=2 * rows * width * (n + 3 * inner),
        moved=2 * rows * (width + n + inner),
        grid_spec=pltpu.PrefetchScalarGridSpec(
            num_scalar_prefetch=1,
            grid=(STEPS,),
            in_specs=[
                *[pl.BlockSpec((size, TILE), lambda g, where: (g, 0))] * len(grad),
                *[row_block(j) for j in range(n_decode)],
                HBM,
                HBM,
                whole(aux_grad),
                whole(aux),
                whole(second),
            ],
            out_specs=[dealt, dealt],
            scratch_shapes=[
                pltpu.VMEM((rows, inner), BF16),
                pltpu.VMEM((rows, width), BF16),
                pltpu.VMEM((rows, width), BF16),
                pltpu.VMEM((rows, inner), BF16),
                pltpu.VMEM((aux_grad.shape[0], width), F32),
                pltpu.VMEM((inner, width), F32),
                pltpu.VMEM((inner, width), F32),
                pltpu.SemaphoreType.DMA((2, STEPS, 1)),
            ],
        ),
        name="backward",
    )(where, *grad, *[decode] * n_decode, hidden, acts, aux_grad, aux, second)


TOPS, DENOMS = 3, 19
DIGIT = 40


def to_digits(value):
    rest, lanes = value, []
    for _ in range(3):
        digit = rest.astype(BF16).astype(F32)
        lanes.append(digit[:, :DIGIT])
        rest = rest - digit
    lanes.append(jnp.zeros((value.shape[0], LANES - 3 * DIGIT), F32))
    return jnp.concatenate(lanes, axis=1).astype(BF16)


def from_digits(value):
    value = value.astype(F32)
    return sum(value[:, j * DIGIT : (j + 1) * DIGIT] for j in (2, 1, 0))


def labels_of(got, head):
    digits = got[:, head + LANES : head + LANES + 2].astype(F32)
    return (digits[:, 0:1] * LANES + digits[:, 1:2]).astype(jnp.int32)


def logits_kernel(where_ref, got_ref, klass_ref, sent_ref, logits_ref):
    groups, images, _ = got_ref.shape
    classes, head = klass_ref.shape
    got = got_ref[...].reshape(groups * images, -1)
    logits_ref[...] = dot(got[:, :head], klass_ref[...], COLS_1)
    logits = logits_ref[...]
    ids = lax.broadcasted_iota(jnp.int32, logits.shape, 1) + where_ref[ME] * classes
    hit = labels_of(got, head) == ids
    top = jnp.max(logits, axis=1, keepdims=True)
    expo = jnp.exp(logits - top)
    denom = jnp.sum(expo, axis=1, keepdims=True)
    own = jnp.sum(jnp.where(hit, expo, 0.0), axis=1, keepdims=True)
    rest = jnp.where(hit, 0.0, expo).astype(BF16)
    onehot = jnp.where(hit, 1.0, 0.0).astype(BF16)
    sent_ref[:, :, :head] = dot(rest, klass_ref[...]).astype(BF16).reshape(groups, images, head)
    sent_ref[:, :, head : 2 * head] = dot(onehot, klass_ref[...]).astype(BF16).reshape(groups, images, head)
    lane = lax.broadcasted_iota(jnp.int32, (images, LANES), 1)
    cut = lambda value, d: value[d * images : (d + 1) * images]
    common = jnp.zeros((images, LANES), F32)
    for d in range(groups):
        common = jnp.where(lane == TOPS + d, cut(top, d), common)
        common = jnp.where(lane == DENOMS + d, cut(denom, d), common)
    for d in range(groups):
        stats = jnp.where(lane == 1, cut(denom, d), jnp.where(lane == 2, cut(own, d), common))
        sent_ref[d, :, 2 * head :] = to_digits(jnp.where(lane == 0, cut(top, d), stats))


def class_logits(where, got, klass):
    groups, images, _ = got.shape
    classes, head = klass.shape
    return call(
        logits_kernel,
        shape((groups, images, 2 * head + LANES), BF16),
        limit=16,
        in_specs=[SMEM, VMEM, VMEM],
        scratch_shapes=[pltpu.VMEM((groups * images, classes), F32)],
        name="class_logits",
    )(where, got, klass)


def aux_kernel(norm, got_ref, aux_pre_ref, grad_ref, cut_ref):
    groups, images, _ = got_ref.shape
    head = aux_pre_ref.shape[1]
    stats = [from_digits(got_ref[d, :, 2 * head :]) for d in range(groups)]
    top = functools.reduce(jnp.maximum, [s[:, 0:1] for s in stats])
    scales = [jnp.exp(s[:, 0:1] - top) for s in stats]
    denom = sum(s[:, 1:2] * f for s, f in zip(stats, scales))
    own = sum(s[:, 2:3] * f for s, f in zip(stats, scales)) / denom
    rest = sum(got_ref[d, :, :head].astype(F32) * scales[d] for d in range(groups)) / (denom * norm)
    row = sum(got_ref[d, :, head : 2 * head].astype(F32) for d in range(groups))
    back = rest + row * ((own - 1.0) / norm).astype(BF16).astype(F32)
    aux_grad = jnp.where(aux_pre_ref[...] > 0, back, 0.0).astype(BF16)
    grad_ref[...] = aux_grad
    part = cut_ref.shape[1]
    for q in range(head // part):
        cut_ref[q * images : (q + 1) * images, :] = aux_grad[:, q * part : (q + 1) * part]


def aux_backward(got, aux_pre, part, norm):
    images, head = aux_pre.shape
    return call(
        functools.partial(aux_kernel, norm),
        [shape((images, head), BF16), shape((images * head // part, part), BF16)],
        limit=16,
        flops=2e10,
        name="aux_backward",
    )(got, aux_pre)


def class_kernel(norm, where_ref, klass_ref, got_ref, stats_ref, mine_ref, other_ref, class_ref, aux_ref):
    groups, images, _ = got_ref.shape
    head = class_ref.shape[1]
    classes, part = class_ref.shape[0], aux_ref.shape[0]
    got = got_ref[...].reshape(groups * images, -1)
    stats = [from_digits(stats_ref[e]) for e in range(groups)]
    tops, denoms = [], []
    for d in range(groups):
        top = functools.reduce(jnp.maximum, [s[:, TOPS + d : TOPS + d + 1] for s in stats])
        tops.append(top)
        denoms.append(sum(s[:, DENOMS + d : DENOMS + d + 1] * jnp.exp(s[:, TOPS + d : TOPS + d + 1] - top) for s in stats))
    top, denom = jnp.concatenate(tops, axis=0), jnp.concatenate(denoms, axis=0)
    logits = dot(got[:, :head], klass_ref[...], COLS_1)
    ids = lax.broadcasted_iota(jnp.int32, logits.shape, 1) + where_ref[ME] * classes
    onehot = jnp.where(labels_of(got, head) == ids, 1.0, 0.0)
    logit_grad = ((jnp.exp(logits - top) / denom - onehot) / norm).astype(BF16)
    class_ref[...] = dot(logit_grad, got[:, :head], ROWS_0)
    total = jnp.zeros(aux_ref.shape, F32)
    for d in range(groups):
        k, ref = d // 2, other_ref if d % 2 else mine_ref
        grad = jnp.concatenate([ref[k, q * images : (q + 1) * images] for q in range(head // part)], axis=1)
        pooled = got_ref[where_ref[ME] ^ d, :, head : head + part]
        total += dot(pooled, grad, ROWS_0).astype(BF16).astype(F32)
    aux_ref[...] = total


def class_backward(where, klass, got, partial, mine, other, norm):
    groups, images, wide = partial.shape
    classes, head = klass.shape
    whole = lambda *dims: pl.BlockSpec(dims, lambda i: (0,) * len(dims))
    part = mine.shape[2]
    return call(
        functools.partial(class_kernel, norm),
        [shape((classes, head), F32), shape((part, head), F32)],
        limit=20,
        flops=2 * groups * images * classes * head,
        moved=4 * classes * head,
        grid=(1,),
        in_specs=[
            SMEM,
            whole(*klass.shape),
            whole(*got.shape),
            pl.BlockSpec((groups, images, LANES), lambda i: (0, 0, wide // LANES - 1)),
            whole(*mine.shape),
            whole(*other.shape),
        ],
        out_specs=[whole(classes, head), whole(part, head)],
        name="class_backward",
    )(where, klass, got, partial, mine, other)


def chip_kernel(chips, below, collect, where_ref, keep_ref, got_ref, *refs):
    refs, outs = refs[: below + collect], refs[below + collect :]
    n = keep_ref.shape[1]
    chip = where_ref[ME] >> 1
    for k in range(chips):
        outs[k][:n] = (keep_ref[chip ^ k].astype(F32) + got_ref[chip ^ k].astype(F32)).astype(BF16)
        for ref in refs[:below]:
            outs[k][n:] = ref[...]
    if collect:
        size = outs[-1].shape[1]
        for k, ref in enumerate(refs[below:]):
            outs[-1][k] = ref[ref.shape[0] - size :]


def add_cores(where, keep, send, below=(), collect=(), size=0):
    chips, n, part = keep.shape
    rows = n + sum(e.shape[0] for e in below)
    outs = [shape((rows, part), BF16)] * chips
    if collect:
        outs.append(shape((len(collect), size, part), BF16))
    outs = call(
        functools.partial(chip_kernel, chips, len(below), len(collect)),
        outs,
        limit=16,
        in_specs=[SMEM, VMEM, VMEM, *[VMEM] * (len(below) + len(collect))],
        name="add_cores",
    )(where, keep, swap(send, "dp", 1), *below, *collect)
    return (outs[:chips], outs[chips]) if collect else outs


def exchange_chips(parts):
    got = {k: swap(parts[k], "dp", 2 * k) for k in reversed(range(1, len(parts)))}
    return [parts[0]] + [got[k] for k in range(1, len(parts))]


def finish_kernel(inner, chips, *refs):
    early, last, (first_ref, second_ref, decode_ref) = refs[:chips], refs[chips : 2 * chips], refs[2 * chips :]
    n = decode_ref.shape[1]
    total = sum(ref[...].astype(F32) for ref in last)
    first_ref[...] = total[inner:].T
    tall, part = second_ref.shape[0], total.shape[1]
    for q in range(inner // tall):
        second_ref[:, q * part : (q + 1) * part] = total[q * tall : (q + 1) * tall]
    decode_ref[...] = sum(ref[:n].astype(F32) for ref in early).T


def finish(early, last, inner, groups, n):
    part = early[0].shape[1]
    return call(
        functools.partial(finish_kernel, inner, len(early)),
        [shape((part, inner), F32), shape((inner // groups, part * groups), F32), shape((part, n), F32)],
        limit=16,
        name="finish",
    )(*early, *last)


def local(acts, patches, labels, w_first, w_second, w_decode, w_aux, w_class):
    acts = acts[0].transpose(1, 0, 2)
    pix, images, width = acts.shape
    groups, count = lax.axis_size("dp"), lax.axis_size("section")
    me, section = lax.axis_index("dp"), lax.axis_index("section")
    scale = (groups * images * pix) ** -0.5
    norm = (groups * images) ** 0.5
    first, second, decode, aux, klass = w_first[0], w_second[0], w_decode[0], w_aux[0], w_class[0]
    inner = first.shape[1]
    n_decode = decode.shape[1]
    rows = pix * images

    paired = count == 4 and patches.shape[2] == 192
    if paired:
        near = [section ^ k for k in range(4)]
        tiles = [t for s in near for t in (3 * (s >> 1) + 2 * (s & 1), 3 * (s >> 1) + 1)]
        where = jnp.stack([section & 1, me & 1, me, *tiles]).astype(jnp.int32)
        turned = patches.transpose(0, 2, 1)
        halves = [pack(where, turned, h) for h in range(2)]
        x, y = [swap(halves[0], "section", 1)], [swap(halves[1], "section", 2)]
        first = after(first, halves[1])
    else:
        where = jnp.stack([section & 1, me & 1, me]).astype(jnp.int32)
        target = lax.all_gather(patches, "section", axis=2, tiled=True).transpose(1, 0, 2)

    hidden, feature, aux_pre, sent = forward(acts, first, second, aux, labels, groups)
    if paired:
        sent = after(sent, x[0])
    got = exchange(sent)
    if paired:
        x.append(swap(halves[1], "section", 1))
        y.insert(0, swap(halves[0], "section", 2))
        ready = (got, x[1], y[0])
        diagonal = [swap(after(x[0], ready), "section", 2), swap(after(y[1], ready), "section", 1)]
        target = patch_operands([halves, x, y, diagonal], [0, 1, 2, 3], [0, 1, 2, 3])
    else:
        target = [target], [pl.BlockSpec((pix // STEPS, images, n_decode), lambda g, where: (g, 0, 0))]
    sent = class_logits(where, got, klass)
    partial = exchange(sent)
    grad, keep, send = residual(after(where, sent), feature, decode, *target, images, scale, groups)
    aux_grad, aux_cut = aux_backward(partial, aux_pre, width // groups, norm)
    chip_decode = add_cores(where, keep, send, [aux_cut])
    sum_decode = exchange_chips(chip_decode)
    keep, send = backward(
        where, grad, hidden, acts.reshape(rows, width), decode, after(aux_grad, chip_decode[0]), aux, second, groups
    )
    chip_last, mine = add_cores(where, keep, after(send, sum_decode), collect=sum_decode, size=aux_cut.shape[0])
    sum_last = exchange_chips(chip_last)
    grad_class, grad_aux = class_backward(where, klass, got, partial, mine, swap(mine, "dp", 1), norm)
    grad_first, grad_second, grad_decode = finish(sum_decode, sum_last, inner, groups, n_decode)
    return grad_first[None], grad_second[None], grad_decode[None], grad_aux[None], grad_class[None]


def solution(mesh):
    in_specs = (
        P("section", "dp", None, None),
        P("dp", None, "section"),
        P("dp"),
        P("section", None, None),
        P("section", None, None),
        P("section", None, None),
        P("section", None, None),
        P("section", "dp", None),
    )
    out_specs = (P("section", "dp", None),) * 5
    return jax.shard_map(local, mesh=mesh, in_specs=in_specs, out_specs=out_specs, check_vma=False)
```

```python
import functools

import jax
import jax.numpy as jnp
from jax import lax
from jax.experimental import pallas as pl
from jax.experimental.pallas import tpu as pltpu
from jax.sharding import PartitionSpec as P

F32 = jnp.float32
BF16 = jnp.bfloat16
STEPS = 4
LANES = 128
TILE = 256
MIB = 1024 * 1024
ROWS_0 = (((0,), (0,)), ((), ()))
COLS_1 = (((1,), (1,)), ((), ()))
PARITY, CORE, ME, TILES = 0, 1, 2, 3


def dot(left, right, dims=(((1,), (0,)), ((), ()))):
    return lax.dot_general(left, right, dims, preferred_element_type=F32)


def call(kernel, out_shape, *, limit, flops=0, moved=0, **kwargs):
    return pl.pallas_call(
        kernel,
        out_shape=out_shape,
        compiler_params=pltpu.CompilerParams(vmem_limit_bytes=limit * MIB),
        cost_estimate=pl.CostEstimate(flops=int(flops), bytes_accessed=int(moved), transcendentals=0),
        **kwargs,
    )


def shape(dims, kind):
    return jax.ShapeDtypeStruct(dims, kind)


SMEM = pl.BlockSpec(memory_space=pltpu.SMEM)
VMEM = pl.BlockSpec(memory_space=pltpu.VMEM)
HBM = pl.BlockSpec(memory_space=pltpu.HBM)


def swap(value, axis, bits):
    count = lax.axis_size(axis)
    return lax.ppermute(value, axis, [(i, i ^ bits) for i in range(count)])


def exchange(value, groups=None):
    return lax.all_to_all(value, "dp", 0, 0, axis_index_groups=groups, tiled=True)


def pack_kernel(first, where_ref, *refs):
    patches_refs, (out_ref, turned, own, shared) = refs[:-4], refs[-4:]
    several, span, pix = patches_refs[0].shape
    images = turned.shape[0]
    padded = turned.shape[1]
    count = out_ref.shape[0] // 3 * 2
    parity = where_ref[PARITY]
    at_own = pl.multiple_of(64 * parity, 64)
    at_shared = pl.multiple_of(128 * (1 - parity), 64)
    row = lax.broadcasted_iota(jnp.int32, (padded, pix), 0)
    column = lax.broadcasted_iota(jnp.int32, (padded, pix), 1)
    pick = ((row < count) & (column == row + first)).astype(F32).astype(BF16)
    for i in range(images):
        patches_ref, j = patches_refs[i // several], i % several
        turned[i, :, :LANES] = dot(pick, patches_ref[j, pl.ds(at_own, LANES), :], COLS_1).astype(BF16)
        turned[i, :, LANES:] = dot(pick, patches_ref[j, pl.ds(at_shared, 64), :], COLS_1).astype(BF16)
    size = 16 * images
    row = lax.broadcasted_iota(jnp.int32, (size, size), 0)
    column = lax.broadcasted_iota(jnp.int32, (size, size), 1)
    order = (row // images == column % 16) & (row % images == column // 16)
    order = order.astype(F32).astype(BF16)
    for b in range(padded // 16):
        rows = turned[:, 16 * b : 16 * b + 16, :].reshape(size, span)
        out = dot(order, rows).astype(BF16)
        own[16 * b : 16 * b + 16] = out[:, :LANES].reshape(16, images, LANES)
        shared[16 * b : 16 * b + 16] = out[:, LANES:].reshape(16, images, 64)
    out_ref[:count] = own[:count]
    lower, upper = shared[: count // 2], shared[count // 2 : count]

    @pl.when(parity == 0)
    def _():
        out_ref[count:] = jnp.concatenate([lower, upper], axis=2)

    @pl.when(parity == 1)
    def _():
        out_ref[count:] = jnp.concatenate([upper, lower], axis=2)


def pack(where, patches, h):
    images, span, pix = patches.shape
    half = pix // 2
    padded = -(-half // 16) * 16
    several = images // 4
    lanes = LANES if h == 0 and half <= LANES < pix else pix
    group = lambda j: pl.BlockSpec((several, span, lanes), lambda i: (j, 0, 0))
    dims = (half + half // 2, images, LANES)
    return call(
        functools.partial(pack_kernel, h * half),
        shape(dims, BF16),
        limit=20,
        grid=(1,),
        in_specs=[SMEM, *[group(j) for j in range(4)]],
        out_specs=pl.BlockSpec(dims, lambda i: (0, 0, 0)),
        scratch_shapes=[
            pltpu.VMEM((images, padded, span), BF16),
            pltpu.VMEM((padded, images, LANES), BF16),
            pltpu.VMEM((padded, images, 64), BF16),
        ],
        name="pack_patches",
    )(where, *[patches] * 4)


def after(value, other):
    return lax.optimization_barrier((value, other))[0]


def forward_kernel(n_tiles, pix, *refs):
    acts_refs, refs = refs[:n_tiles], refs[n_tiles:]
    first_ref, second_ref, aux_ref, labels_ref, hidden_ref = refs[:5]
    feature_refs, (aux_pre_ref, sent_ref, pooled) = refs[5:-3], refs[-3:]
    step = pl.program_id(0)
    block, images, _ = acts_refs[0].shape
    cut = lambda j: slice(j * TILE, (j + 1) * TILE)
    start = step == 0
    halves = []
    for a, b in ((0, block // 2), (block // 2, block)):
        flat = jnp.concatenate([ref[a:b].reshape((b - a) * images, TILE) for ref in acts_refs], axis=1)
        halves.append((a, b, flat, jnp.maximum(dot(flat, first_ref[...]), 0.0).astype(BF16)))
    for a, b, flat, hidden in halves:
        rows = slice(a * images, b * images)
        hidden_ref[rows] = hidden
        for j, feature_ref in enumerate(feature_refs):
            feature = (flat[:, cut(j)].astype(F32) + dot(hidden, second_ref[:, cut(j)])).astype(BF16)
            feature_ref[rows] = feature
            sums = jnp.sum(feature.reshape(b - a, images, TILE).astype(F32), axis=0)
            pooled[:, cut(j)] = sums + (pooled[:, cut(j)] if a else jnp.where(start, 0.0, pooled[:, cut(j)]))

    @pl.when(step == pl.num_programs(0) - 1)
    def _():
        groups = sent_ref.shape[0]
        width, head = aux_ref.shape
        part = width // groups
        mean = (pooled[...] / pix).astype(BF16)
        aux_pre = dot(mean, aux_ref[...])
        aux_pre_ref[...] = aux_pre
        out = jnp.maximum(aux_pre, 0.0).astype(BF16)
        row = lax.broadcasted_iota(jnp.int32, (images, LANES), 0)
        lane = lax.broadcasted_iota(jnp.int32, (images, LANES), 1)
        digits = jnp.zeros((images, LANES), jnp.int32)
        for i in range(images):
            label = labels_ref[i]
            digits = jnp.where((row == i) & (lane == 0), label // LANES, digits)
            digits = jnp.where((row == i) & (lane == 1), label % LANES, digits)
        digits = digits.astype(F32).astype(BF16)
        for d in range(groups):
            sent_ref[d, :, :head] = out
            sent_ref[d, :, head : head + part] = mean[:, d * part : (d + 1) * part]
            sent_ref[d, :, head + LANES :] = digits


def forward(acts, first, second, aux, labels, groups):
    pix, images, width = acts.shape
    inner, head = first.shape[1], aux.shape[1]
    block = pix // STEPS
    n_tiles = width // TILE
    whole = lambda *dims: pl.BlockSpec(dims, lambda g: (0,) * len(dims))
    rows = lambda n: pl.BlockSpec((block * images, n), lambda g: (g, 0))
    column = lambda j: pl.BlockSpec((block, images, TILE), lambda g: (g, 0, j))
    hidden, *feature, aux_pre, sent = call(
        functools.partial(forward_kernel, n_tiles, pix),
        [
            shape((pix * images, inner), BF16),
            *[shape((pix * images, TILE), BF16)] * n_tiles,
            shape((images, head), F32),
            shape((groups, images, head + 2 * LANES), BF16),
        ],
        limit=53,
        grid=(STEPS,),
        in_specs=[
            *[column(j) for j in range(n_tiles)],
            whole(*first.shape),
            whole(*second.shape),
            whole(*aux.shape),
            SMEM,
        ],
        out_specs=[
            rows(inner),
            *[rows(TILE)] * n_tiles,
            whole(images, head),
            whole(groups, images, head + 2 * LANES),
        ],
        scratch_shapes=[pltpu.VMEM((images, width), F32)],
        name="forward",
    )(*[acts] * n_tiles, first, second, aux, labels)
    return hidden, feature, aux_pre, sent


def own_index(h):
    per_half = STEPS // 2
    return lambda g, where: (jnp.clip(g - h * per_half, 0, per_half - 1), 0, 0)


def patch_operands(blocks, own_blocks, shared_blocks):
    args, specs = [], []
    for k in own_blocks:
        for h, half in enumerate(blocks[k]):
            dims = (half.shape[0] // 3,) + half.shape[1:]
            args.append(half)
            specs.append(pl.BlockSpec(dims, own_index(h)))
    for k in shared_blocks:
        for half in blocks[k]:
            dims = (half.shape[0] // 3,) + half.shape[1:]
            args.append(half)
            specs.append(pl.BlockSpec(dims, lambda g, where: (2, 0, 0)))
    return args, specs


def lay_target(g, where_ref, refs, target):
    if len(refs) == 1:
        target[...] = refs[0][...]
        return
    pairs = [refs[j : j + 2] for j in range(0, len(refs), 2)]
    own, shared = pairs[: len(pairs) // 2], pairs[len(pairs) // 2 :]
    per_half = STEPS // 2
    h, side = g // per_half, g % per_half
    lanes = lambda j: pl.ds(pl.multiple_of(where_ref[TILES + j] * LANES, LANES), LANES)
    for k, pair in enumerate(own):
        target[:, :, lanes(2 * k)] = pair[h][...]
    for k in range(0, len(shared), 2):
        mine, other = shared[k][h][...].astype(F32), shared[k + 1][h][...].astype(F32)
        lane = lax.broadcasted_iota(jnp.int32, mine.shape, 2)
        value = jnp.where((lane < 64) == ((where_ref[PARITY] == 0) == (side == 0)), mine, other)
        if side:
            value = jnp.concatenate([value[:, :, 64:], value[:, :, :64]], axis=2)
        target[:, :, lanes(2 * k + 1)] = value.astype(BF16)


def deal(where_ref, sums, part, keep_ref, send_ref):
    core = where_ref[CORE]
    at = 0
    for value in sums:
        height = value.shape[0]
        for z in range(keep_ref.shape[0]):
            even = value[:, 2 * z * part : (2 * z + 1) * part]
            odd = value[:, (2 * z + 1) * part : (2 * z + 2) * part]
            mine = jnp.where(core == 0, even, odd)
            other = jnp.where(core == 0, odd, even)
            keep_ref[z, at : at + height, :] = mine.astype(BF16)
            send_ref[z, at : at + height, :] = other.astype(BF16)
        at += height


def copies_of(sources, held, sems):
    size, wide = held.shape[0] // STEPS, sources[0].shape[1]
    return [
        [
            pltpu.make_async_copy(
                source.at[pl.ds(g * size, size)], held.at[pl.ds(g * size, size), pl.ds(j * wide, wide)], sems.at[g, j]
            )
            for j, source in enumerate(sources)
        ]
        for g in range(STEPS)
    ]


def by_step(copies, body):
    step = pl.program_id(0)
    for g in range(STEPS):

        @pl.when(step == g)
        def _():
            if g == 0:
                for h in range(STEPS):
                    for copy in copies[h]:
                        copy.start()
            for copy in copies[g]:
                copy.wait()
            body(g)


def contract(g, rows, pairs):
    middle = rows // STEPS * 2 // TILE * TILE
    span = slice(0, middle) if g == 2 else slice(middle, rows)
    for total, left, right in pairs:
        now = dot(left[span], right[span], ROWS_0)
        total[...] = now if g == 2 else total[...] + now


def residual_kernel(groups, scale, n_feature, n_tiles, n_patch, where_ref, *refs):
    feature_refs, refs = refs[:n_feature], refs[n_feature:]
    decode_refs, refs = refs[:n_tiles], refs[n_tiles:]
    patch_refs, refs = refs[:n_patch], refs[n_patch:]
    grad_refs, refs = refs[:n_tiles], refs[n_tiles:]
    keep_ref, send_ref, target, feature, grads, total, sems = refs
    rows, width = feature.shape
    size = grad_refs[0].shape[0]

    def body(g):
        here = slice(g * size, (g + 1) * size)
        lay_target(g, where_ref, patch_refs, target)
        if g == 2:
            contract(g, rows, [(total, grads, feature)])
        now = feature[here]
        for j, grad_ref in enumerate(grad_refs):
            cut = slice(j * TILE, (j + 1) * TILE)
            recon = sum(dot(now[:, k : k + TILE], decode_refs[j][k : k + TILE]) for k in range(0, width, TILE))
            grad = ((recon - target[:, :, cut].reshape(size, TILE).astype(F32)) * scale).astype(BF16)
            grad_ref[...] = grad
            grads[here, cut] = grad
        if g == STEPS - 1:
            contract(g, rows, [(total, grads, feature)])
            deal(where_ref, [total], width // groups, keep_ref, send_ref)

    by_step(copies_of(feature_refs, feature, sems), body)


def residual(where, feature, decode, patch_args, patch_specs, images, scale, groups):
    rows = feature[0].shape[0]
    width, n = decode.shape
    size = rows // STEPS
    n_tiles = n // TILE
    parts = (groups // 2, n, width // groups)
    dealt = pl.BlockSpec(parts, lambda g, where: (0, 0, 0))
    block = pl.BlockSpec((size, TILE), lambda g, where: (g, 0))
    column = lambda j: pl.BlockSpec((width, TILE), lambda g, where: (0, j))
    *grad, keep, send = call(
        functools.partial(residual_kernel, groups, scale, len(feature), n_tiles, len(patch_args)),
        [*[shape((rows, TILE), BF16)] * n_tiles, shape(parts, BF16), shape(parts, BF16)],
        limit=42,
        flops=4 * rows * width * n,
        moved=rows * (2 * width + 6 * n),
        grid_spec=pltpu.PrefetchScalarGridSpec(
            num_scalar_prefetch=1,
            grid=(STEPS,),
            in_specs=[
                *[HBM] * len(feature),
                *[column(j) for j in range(n_tiles)],
                *patch_specs,
            ],
            out_specs=[*[block] * n_tiles, dealt, dealt],
            scratch_shapes=[
                pltpu.VMEM((size // images, images, n), BF16),
                pltpu.VMEM((rows, width), BF16),
                pltpu.VMEM((rows, n), BF16),
                pltpu.VMEM((n, width), F32),
                pltpu.SemaphoreType.DMA((STEPS, len(feature))),
            ],
        ),
        name="residual",
    )(where, *feature, *[decode] * n_tiles, *patch_args)
    return grad, keep, send


def backward_kernel(groups, n_grad, n_decode, where_ref, *refs):
    grad_refs, refs = refs[:n_grad], refs[n_grad:]
    decode_refs, refs = refs[:n_decode], refs[n_decode:]
    (hidden_ref, acts_ref, aux_grad_ref, aux_ref, second_ref, keep_ref, send_ref,
     hidden, acts, feature_grads, hidden_grads, pooled, total_second, total_first, sems) = refs
    rows, width = feature_grads.shape
    size = grad_refs[0].shape[0]
    images = aux_grad_ref.shape[0]
    pairs = [(total_second, hidden, feature_grads), (total_first, hidden_grads, acts)]

    def body(g):
        here = slice(g * size, (g + 1) * size)
        if g == 2:
            contract(g, rows, pairs)
        if g == 0:
            pooled[...] = dot(aux_grad_ref[...], aux_ref[...], COLS_1) / (rows // images)
        grad = jnp.concatenate([ref[...] for ref in grad_refs], axis=1)
        for j, decode_ref in enumerate(decode_refs):
            cut = slice(j * TILE, (j + 1) * TILE)
            back = dot(grad, decode_ref[...], COLS_1).reshape(size // images, images, TILE)
            feature_grads[here, cut] = (back + pooled[:, cut][None]).astype(BF16).reshape(size, TILE)
        hidden_back = dot(feature_grads[here], second_ref[...], COLS_1)
        hidden_grads[here] = jnp.where(hidden[here].astype(F32) > 0, hidden_back, 0.0).astype(BF16)
        if g == STEPS - 1:
            contract(g, rows, pairs)
            part = width // groups
            tall = total_second.shape[0] // groups
            second = jnp.concatenate(
                [
                    jnp.concatenate(
                        [total_second[d * tall : (d + 1) * tall, q * part : (q + 1) * part] for q in range(groups)], axis=0
                    )
                    for d in range(groups)
                ],
                axis=1,
            )
            deal(where_ref, [second, total_first], part, keep_ref, send_ref)

    copies = zip(copies_of([hidden_ref], hidden, sems.at[0]), copies_of([acts_ref], acts, sems.at[1]))
    by_step([one + other for one, other in copies], body)


def backward(where, grad, hidden, acts, decode, aux_grad, aux, second, groups):
    rows, width = acts.shape
    inner, n = hidden.shape[1], len(grad) * TILE
    n_decode = width // TILE
    row_block = lambda j: pl.BlockSpec((TILE, n), lambda g, where: (j, 0))
    size = rows // STEPS
    parts = (groups // 2, 2 * inner, width // groups)
    dealt = pl.BlockSpec(parts, lambda g, where: (0, 0, 0))
    whole = lambda array: pl.BlockSpec(array.shape, lambda g, where: (0, 0))
    return call(
        functools.partial(backward_kernel, groups, len(grad), n_decode),
        [shape(parts, BF16), shape(parts, BF16)],
        limit=44,
        flops=2 * rows * width * (n + 3 * inner),
        moved=2 * rows * (width + n + inner),
        grid_spec=pltpu.PrefetchScalarGridSpec(
            num_scalar_prefetch=1,
            grid=(STEPS,),
            in_specs=[
                *[pl.BlockSpec((size, TILE), lambda g, where: (g, 0))] * len(grad),
                *[row_block(j) for j in range(n_decode)],
                HBM,
                HBM,
                whole(aux_grad),
                whole(aux),
                whole(second),
            ],
            out_specs=[dealt, dealt],
            scratch_shapes=[
                pltpu.VMEM((rows, inner), BF16),
                pltpu.VMEM((rows, width), BF16),
                pltpu.VMEM((rows, width), BF16),
                pltpu.VMEM((rows, inner), BF16),
                pltpu.VMEM((aux_grad.shape[0], width), F32),
                pltpu.VMEM((inner, width), F32),
                pltpu.VMEM((inner, width), F32),
                pltpu.SemaphoreType.DMA((2, STEPS, 1)),
            ],
        ),
        name="backward",
    )(where, *grad, *[decode] * n_decode, hidden, acts, aux_grad, aux, second)


TOPS, DENOMS = 3, 19
DIGIT = 40


def to_digits(value):
    rest, lanes = value, []
    for _ in range(3):
        digit = rest.astype(BF16).astype(F32)
        lanes.append(digit[:, :DIGIT])
        rest = rest - digit
    lanes.append(jnp.zeros((value.shape[0], LANES - 3 * DIGIT), F32))
    return jnp.concatenate(lanes, axis=1).astype(BF16)


def from_digits(value):
    value = value.astype(F32)
    return sum(value[:, j * DIGIT : (j + 1) * DIGIT] for j in (2, 1, 0))


def labels_of(got, head):
    digits = got[:, head + LANES : head + LANES + 2].astype(F32)
    return (digits[:, 0:1] * LANES + digits[:, 1:2]).astype(jnp.int32)


def logits_kernel(where_ref, got_ref, klass_ref, sent_ref, logits_ref):
    groups, images, _ = got_ref.shape
    classes, head = klass_ref.shape
    got = got_ref[...].reshape(groups * images, -1)
    logits_ref[...] = dot(got[:, :head], klass_ref[...], COLS_1)
    logits = logits_ref[...]
    ids = lax.broadcasted_iota(jnp.int32, logits.shape, 1) + where_ref[ME] * classes
    hit = labels_of(got, head) == ids
    top = jnp.max(logits, axis=1, keepdims=True)
    expo = jnp.exp(logits - top)
    denom = jnp.sum(expo, axis=1, keepdims=True)
    own = jnp.sum(jnp.where(hit, expo, 0.0), axis=1, keepdims=True)
    rest = jnp.where(hit, 0.0, expo).astype(BF16)
    onehot = jnp.where(hit, 1.0, 0.0).astype(BF16)
    sent_ref[:, :, :head] = dot(rest, klass_ref[...]).astype(BF16).reshape(groups, images, head)
    sent_ref[:, :, head : 2 * head] = dot(onehot, klass_ref[...]).astype(BF16).reshape(groups, images, head)
    lane = lax.broadcasted_iota(jnp.int32, (images, LANES), 1)
    cut = lambda value, d: value[d * images : (d + 1) * images]
    common = jnp.zeros((images, LANES), F32)
    for d in range(groups):
        common = jnp.where(lane == TOPS + d, cut(top, d), common)
        common = jnp.where(lane == DENOMS + d, cut(denom, d), common)
    for d in range(groups):
        stats = jnp.where(lane == 1, cut(denom, d), jnp.where(lane == 2, cut(own, d), common))
        sent_ref[d, :, 2 * head :] = to_digits(jnp.where(lane == 0, cut(top, d), stats))


def class_logits(where, got, klass):
    groups, images, _ = got.shape
    classes, head = klass.shape
    return call(
        logits_kernel,
        shape((groups, images, 2 * head + LANES), BF16),
        limit=16,
        in_specs=[SMEM, VMEM, VMEM],
        scratch_shapes=[pltpu.VMEM((groups * images, classes), F32)],
        name="class_logits",
    )(where, got, klass)


def aux_kernel(norm, got_ref, aux_pre_ref, grad_ref, cut_ref):
    groups, images, _ = got_ref.shape
    head = aux_pre_ref.shape[1]
    stats = [from_digits(got_ref[d, :, 2 * head :]) for d in range(groups)]
    top = functools.reduce(jnp.maximum, [s[:, 0:1] for s in stats])
    scales = [jnp.exp(s[:, 0:1] - top) for s in stats]
    denom = sum(s[:, 1:2] * f for s, f in zip(stats, scales))
    own = sum(s[:, 2:3] * f for s, f in zip(stats, scales)) / denom
    rest = sum(got_ref[d, :, :head].astype(F32) * scales[d] for d in range(groups)) / (denom * norm)
    row = sum(got_ref[d, :, head : 2 * head].astype(F32) for d in range(groups))
    back = rest + row * ((own - 1.0) / norm).astype(BF16).astype(F32)
    aux_grad = jnp.where(aux_pre_ref[...] > 0, back, 0.0).astype(BF16)
    grad_ref[...] = aux_grad
    part = cut_ref.shape[1]
    for q in range(head // part):
        cut_ref[q * images : (q + 1) * images, :] = aux_grad[:, q * part : (q + 1) * part]


def aux_backward(got, aux_pre, part, norm):
    images, head = aux_pre.shape
    return call(
        functools.partial(aux_kernel, norm),
        [shape((images, head), BF16), shape((images * head // part, part), BF16)],
        limit=16,
        flops=2e10,
        name="aux_backward",
    )(got, aux_pre)


def class_kernel(norm, where_ref, klass_ref, got_ref, stats_ref, mine_ref, other_ref, class_ref, aux_ref):
    groups, images, _ = got_ref.shape
    head = class_ref.shape[1]
    classes, part = class_ref.shape[0], aux_ref.shape[0]
    got = got_ref[...].reshape(groups * images, -1)
    stats = [from_digits(stats_ref[e]) for e in range(groups)]
    tops, denoms = [], []
    for d in range(groups):
        top = functools.reduce(jnp.maximum, [s[:, TOPS + d : TOPS + d + 1] for s in stats])
        tops.append(top)
        denoms.append(sum(s[:, DENOMS + d : DENOMS + d + 1] * jnp.exp(s[:, TOPS + d : TOPS + d + 1] - top) for s in stats))
    top, denom = jnp.concatenate(tops, axis=0), jnp.concatenate(denoms, axis=0)
    logits = dot(got[:, :head], klass_ref[...], COLS_1)
    ids = lax.broadcasted_iota(jnp.int32, logits.shape, 1) + where_ref[ME] * classes
    onehot = jnp.where(labels_of(got, head) == ids, 1.0, 0.0)
    logit_grad = ((jnp.exp(logits - top) / denom - onehot) / norm).astype(BF16)
    class_ref[...] = dot(logit_grad, got[:, :head], ROWS_0)
    total = jnp.zeros(aux_ref.shape, F32)
    for d in range(groups):
        k, ref = d // 2, other_ref if d % 2 else mine_ref
        grad = jnp.concatenate([ref[k, q * images : (q + 1) * images] for q in range(head // part)], axis=1)
        pooled = got_ref[where_ref[ME] ^ d, :, head : head + part]
        total += dot(pooled, grad, ROWS_0).astype(BF16).astype(F32)
    aux_ref[...] = total


def class_backward(where, klass, got, partial, mine, other, norm):
    groups, images, wide = partial.shape
    classes, head = klass.shape
    whole = lambda *dims: pl.BlockSpec(dims, lambda i: (0,) * len(dims))
    part = mine.shape[2]
    return call(
        functools.partial(class_kernel, norm),
        [shape((classes, head), F32), shape((part, head), F32)],
        limit=20,
        flops=2 * groups * images * classes * head,
        moved=4 * classes * head,
        grid=(1,),
        in_specs=[
            SMEM,
            whole(*klass.shape),
            whole(*got.shape),
            pl.BlockSpec((groups, images, LANES), lambda i: (0, 0, wide // LANES - 1)),
            whole(*mine.shape),
            whole(*other.shape),
        ],
        out_specs=[whole(classes, head), whole(part, head)],
        name="class_backward",
    )(where, klass, got, partial, mine, other)


def chip_kernel(chips, below, collect, where_ref, keep_ref, got_ref, *refs):
    refs, outs = refs[: below + collect], refs[below + collect :]
    n = keep_ref.shape[1]
    chip = where_ref[ME] >> 1
    for k in range(chips):
        outs[k][:n] = (keep_ref[chip ^ k].astype(F32) + got_ref[chip ^ k].astype(F32)).astype(BF16)
        for ref in refs[:below]:
            outs[k][n:] = ref[...]
    if collect:
        size = outs[-1].shape[1]
        for k, ref in enumerate(refs[below:]):
            outs[-1][k] = ref[ref.shape[0] - size :]


def add_cores(where, keep, send, below=(), collect=(), size=0):
    chips, n, part = keep.shape
    rows = n + sum(e.shape[0] for e in below)
    outs = [shape((rows, part), BF16)] * chips
    if collect:
        outs.append(shape((len(collect), size, part), BF16))
    outs = call(
        functools.partial(chip_kernel, chips, len(below), len(collect)),
        outs,
        limit=16,
        in_specs=[SMEM, VMEM, VMEM, *[VMEM] * (len(below) + len(collect))],
        name="add_cores",
    )(where, keep, swap(send, "dp", 1), *below, *collect)
    return (outs[:chips], outs[chips]) if collect else outs


def exchange_chips(parts):
    got = {k: swap(parts[k], "dp", 2 * k) for k in reversed(range(1, len(parts)))}
    return [parts[0]] + [got[k] for k in range(1, len(parts))]


def finish_kernel(inner, chips, *refs):
    early, last, (first_ref, second_ref, decode_ref) = refs[:chips], refs[chips : 2 * chips], refs[2 * chips :]
    n = decode_ref.shape[1]
    total = sum(ref[...].astype(F32) for ref in last)
    first_ref[...] = total[inner:].T
    tall, part = second_ref.shape[0], total.shape[1]
    for q in range(inner // tall):
        second_ref[:, q * part : (q + 1) * part] = total[q * tall : (q + 1) * tall]
    decode_ref[...] = sum(ref[:n].astype(F32) for ref in early).T


def finish(early, last, inner, groups, n):
    part = early[0].shape[1]
    return call(
        functools.partial(finish_kernel, inner, len(early)),
        [shape((part, inner), F32), shape((inner // groups, part * groups), F32), shape((part, n), F32)],
        limit=16,
        name="finish",
    )(*early, *last)


def local(acts, patches, labels, w_first, w_second, w_decode, w_aux, w_class):
    acts = acts[0].transpose(1, 0, 2)
    pix, images, width = acts.shape
    groups, count = lax.axis_size("dp"), lax.axis_size("section")
    me, section = lax.axis_index("dp"), lax.axis_index("section")
    scale = (groups * images * pix) ** -0.5
    norm = (groups * images) ** 0.5
    first, second, decode, aux, klass = w_first[0], w_second[0], w_decode[0], w_aux[0], w_class[0]
    inner = first.shape[1]
    n_decode = decode.shape[1]
    rows = pix * images

    paired = count == 4 and patches.shape[2] == 192
    if paired:
        near = [section ^ k for k in range(4)]
        tiles = [t for s in near for t in (3 * (s >> 1) + 2 * (s & 1), 3 * (s >> 1) + 1)]
        where = jnp.stack([section & 1, me & 1, me, *tiles]).astype(jnp.int32)
        turned = patches.transpose(0, 2, 1)
        halves = [pack(where, turned, h) for h in range(2)]
        x, y = [swap(halves[0], "section", 1)], [swap(halves[1], "section", 2)]
        first = after(first, halves[1])
    else:
        where = jnp.stack([section & 1, me & 1, me]).astype(jnp.int32)
        target = lax.all_gather(patches, "section", axis=2, tiled=True).transpose(1, 0, 2)

    hidden, feature, aux_pre, sent = forward(acts, first, second, aux, labels, groups)
    if paired:
        sent = after(sent, x[0])
    got = exchange(sent)
    if paired:
        x.append(swap(halves[1], "section", 1))
        y.insert(0, swap(halves[0], "section", 2))
        diagonal = [swap(after(x[0], aux_pre), "section", 2), swap(after(y[1], aux_pre), "section", 1)]
        target = patch_operands([halves, x, y, diagonal], [0, 1, 2, 3], [0, 1, 2, 3])
    else:
        target = [target], [pl.BlockSpec((pix // STEPS, images, n_decode), lambda g, where: (g, 0, 0))]
    sent = class_logits(where, got, klass)
    partial = exchange(sent)
    grad, keep, send = residual(after(where, sent), feature, decode, *target, images, scale, groups)
    aux_grad, aux_cut = aux_backward(partial, aux_pre, width // groups, norm)
    chip_decode = add_cores(where, keep, send, [aux_cut])
    sum_decode = exchange_chips(chip_decode)
    keep, send = backward(
        where, grad, hidden, acts.reshape(rows, width), decode, after(aux_grad, chip_decode[0]), aux, second, groups
    )
    chip_last, mine = add_cores(where, keep, after(send, sum_decode), collect=sum_decode, size=aux_cut.shape[0])
    sum_last = exchange_chips(chip_last)
    grad_class, grad_aux = class_backward(where, klass, got, partial, mine, swap(mine, "dp", 1), norm)
    grad_first, grad_second, grad_decode = finish(sum_decode, sum_last, inner, groups, n_decode)
    return grad_first[None], grad_second[None], grad_decode[None], grad_aux[None], grad_class[None]


def solution(mesh):
    in_specs = (
        P("section", "dp", None, None),
        P("dp", None, "section"),
        P("dp"),
        P("section", None, None),
        P("section", None, None),
        P("section", None, None),
        P("section", None, None),
        P("section", "dp", None),
    )
    out_specs = (P("section", "dp", None),) * 5
    return jax.shard_map(local, mesh=mesh, in_specs=in_specs, out_specs=out_specs, check_vma=False)
```

```python
import functools

import jax
import jax.numpy as jnp
from jax import lax
from jax.experimental import pallas as pl
from jax.experimental.pallas import tpu as pltpu
from jax.sharding import PartitionSpec as P

F32 = jnp.float32
BF16 = jnp.bfloat16
STEPS = 4
LANES = 128
TILE = 256
MIB = 1024 * 1024
ROWS_0 = (((0,), (0,)), ((), ()))
COLS_1 = (((1,), (1,)), ((), ()))
PARITY, CORE, ME, TILES = 0, 1, 2, 3


def dot(left, right, dims=(((1,), (0,)), ((), ()))):
    return lax.dot_general(left, right, dims, preferred_element_type=F32)


def call(kernel, out_shape, *, limit, flops=0, moved=0, **kwargs):
    return pl.pallas_call(
        kernel,
        out_shape=out_shape,
        compiler_params=pltpu.CompilerParams(vmem_limit_bytes=limit * MIB),
        cost_estimate=pl.CostEstimate(flops=int(flops), bytes_accessed=int(moved), transcendentals=0),
        **kwargs,
    )


def shape(dims, kind):
    return jax.ShapeDtypeStruct(dims, kind)


SMEM = pl.BlockSpec(memory_space=pltpu.SMEM)
VMEM = pl.BlockSpec(memory_space=pltpu.VMEM)
HBM = pl.BlockSpec(memory_space=pltpu.HBM)


def swap(value, axis, bits):
    count = lax.axis_size(axis)
    return lax.ppermute(value, axis, [(i, i ^ bits) for i in range(count)])


def exchange(value, groups=None):
    return lax.all_to_all(value, "dp", 0, 0, axis_index_groups=groups, tiled=True)


def pack_kernel(first, where_ref, *refs):
    patches_refs, (out_ref, turned, own, shared) = refs[:-4], refs[-4:]
    several, span, pix = patches_refs[0].shape
    images = turned.shape[0]
    padded = turned.shape[1]
    count = out_ref.shape[0] // 3 * 2
    parity = where_ref[PARITY]
    at_own = pl.multiple_of(64 * parity, 64)
    at_shared = pl.multiple_of(128 * (1 - parity), 64)
    row = lax.broadcasted_iota(jnp.int32, (padded, pix), 0)
    column = lax.broadcasted_iota(jnp.int32, (padded, pix), 1)
    pick = ((row < count) & (column == row + first)).astype(F32).astype(BF16)
    for i in range(images):
        patches_ref, j = patches_refs[i // several], i % several
        turned[i, :, :LANES] = dot(pick, patches_ref[j, pl.ds(at_own, LANES), :], COLS_1).astype(BF16)
        turned[i, :, LANES:] = dot(pick, patches_ref[j, pl.ds(at_shared, 64), :], COLS_1).astype(BF16)
    size = 16 * images
    row = lax.broadcasted_iota(jnp.int32, (size, size), 0)
    column = lax.broadcasted_iota(jnp.int32, (size, size), 1)
    order = (row // images == column % 16) & (row % images == column // 16)
    order = order.astype(F32).astype(BF16)
    for b in range(padded // 16):
        rows = turned[:, 16 * b : 16 * b + 16, :].reshape(size, span)
        out = dot(order, rows).astype(BF16)
        own[16 * b : 16 * b + 16] = out[:, :LANES].reshape(16, images, LANES)
        shared[16 * b : 16 * b + 16] = out[:, LANES:].reshape(16, images, 64)
    out_ref[:count] = own[:count]
    lower, upper = shared[: count // 2], shared[count // 2 : count]

    @pl.when(parity == 0)
    def _():
        out_ref[count:] = jnp.concatenate([lower, upper], axis=2)

    @pl.when(parity == 1)
    def _():
        out_ref[count:] = jnp.concatenate([upper, lower], axis=2)


def pack(where, patches, h):
    images, span, pix = patches.shape
    half = pix // 2
    padded = -(-half // 16) * 16
    several = images // 4
    lanes = LANES if h == 0 and half <= LANES < pix else pix
    group = lambda j: pl.BlockSpec((several, span, lanes), lambda i: (j, 0, 0))
    dims = (half + half // 2, images, LANES)
    return call(
        functools.partial(pack_kernel, h * half),
        shape(dims, BF16),
        limit=20,
        grid=(1,),
        in_specs=[SMEM, *[group(j) for j in range(4)]],
        out_specs=pl.BlockSpec(dims, lambda i: (0, 0, 0)),
        scratch_shapes=[
            pltpu.VMEM((images, padded, span), BF16),
            pltpu.VMEM((padded, images, LANES), BF16),
            pltpu.VMEM((padded, images, 64), BF16),
        ],
        name="pack_patches",
    )(where, *[patches] * 4)


def after(value, other):
    return lax.optimization_barrier((value, other))[0]


def forward_kernel(n_tiles, pix, *refs):
    acts_refs, refs = refs[:n_tiles], refs[n_tiles:]
    first_ref, second_ref, aux_ref, labels_ref, hidden_ref = refs[:5]
    feature_refs, (aux_pre_ref, sent_ref, pooled) = refs[5:-3], refs[-3:]
    step = pl.program_id(0)
    block, images, _ = acts_refs[0].shape
    cut = lambda j: slice(j * TILE, (j + 1) * TILE)
    start = step == 0
    halves = []
    for a, b in ((0, block // 2), (block // 2, block)):
        flat = jnp.concatenate([ref[a:b].reshape((b - a) * images, TILE) for ref in acts_refs], axis=1)
        halves.append((a, b, flat, jnp.maximum(dot(flat, first_ref[...]), 0.0).astype(BF16)))
    for a, b, flat, hidden in halves:
        rows = slice(a * images, b * images)
        hidden_ref[rows] = hidden
        for j, feature_ref in enumerate(feature_refs):
            feature = (flat[:, cut(j)].astype(F32) + dot(hidden, second_ref[:, cut(j)])).astype(BF16)
            feature_ref[rows] = feature
            sums = jnp.sum(feature.reshape(b - a, images, TILE).astype(F32), axis=0)
            pooled[:, cut(j)] = sums + (pooled[:, cut(j)] if a else jnp.where(start, 0.0, pooled[:, cut(j)]))

    @pl.when(step == pl.num_programs(0) - 1)
    def _():
        groups = sent_ref.shape[0]
        width, head = aux_ref.shape
        part = width // groups
        mean = (pooled[...] / pix).astype(BF16)
        aux_pre = dot(mean, aux_ref[...])
        aux_pre_ref[...] = aux_pre
        out = jnp.maximum(aux_pre, 0.0).astype(BF16)
        row = lax.broadcasted_iota(jnp.int32, (images, LANES), 0)
        lane = lax.broadcasted_iota(jnp.int32, (images, LANES), 1)
        digits = jnp.zeros((images, LANES), jnp.int32)
        for i in range(images):
            label = labels_ref[i]
            digits = jnp.where((row == i) & (lane == 0), label // LANES, digits)
            digits = jnp.where((row == i) & (lane == 1), label % LANES, digits)
        digits = digits.astype(F32).astype(BF16)
        for d in range(groups):
            sent_ref[d, :, :head] = out
            sent_ref[d, :, head : head + part] = mean[:, d * part : (d + 1) * part]
            sent_ref[d, :, head + LANES :] = digits


def forward(acts, first, second, aux, labels, groups):
    pix, images, width = acts.shape
    inner, head = first.shape[1], aux.shape[1]
    block = pix // STEPS
    n_tiles = width // TILE
    whole = lambda *dims: pl.BlockSpec(dims, lambda g: (0,) * len(dims))
    rows = lambda n: pl.BlockSpec((block * images, n), lambda g: (g, 0))
    column = lambda j: pl.BlockSpec((block, images, TILE), lambda g: (g, 0, j))
    hidden, *feature, aux_pre, sent = call(
        functools.partial(forward_kernel, n_tiles, pix),
        [
            shape((pix * images, inner), BF16),
            *[shape((pix * images, TILE), BF16)] * n_tiles,
            shape((images, head), F32),
            shape((groups, images, head + 2 * LANES), BF16),
        ],
        limit=58,
        grid=(STEPS,),
        in_specs=[
            *[column(j) for j in range(n_tiles)],
            whole(*first.shape),
            whole(*second.shape),
            whole(*aux.shape),
            SMEM,
        ],
        out_specs=[
            rows(inner),
            *[rows(TILE)] * n_tiles,
            whole(images, head),
            whole(groups, images, head + 2 * LANES),
        ],
        scratch_shapes=[pltpu.VMEM((images, width), F32)],
        name="forward",
    )(*[acts] * n_tiles, first, second, aux, labels)
    return hidden, feature, aux_pre, sent


def recon_kernel(n_feature, n_tiles, *refs):
    feature_refs, decode_refs, recon_refs = refs[:n_feature], refs[n_feature : n_feature + n_tiles], refs[n_feature + n_tiles :]
    feature = jnp.concatenate([ref[...] for ref in feature_refs], axis=1)
    for decode_ref, recon_ref in zip(decode_refs, recon_refs):
        recon_ref[...] = dot(feature, decode_ref[...])


def reconstruct(feature, decode, n_tiles):
    rows = feature[0].shape[0]
    width = decode.shape[0]
    block = pl.BlockSpec((rows // STEPS, TILE), lambda g: (g, 0))
    return call(
        functools.partial(recon_kernel, len(feature), n_tiles),
        [shape((rows, TILE), F32)] * n_tiles,
        limit=57,
        grid=(STEPS,),
        in_specs=[*[block] * len(feature), *[pl.BlockSpec((width, TILE), lambda g, j=j: (0, j)) for j in range(n_tiles)]],
        out_specs=[block] * n_tiles,
        name="reconstruct",
    )(*feature, *[decode] * n_tiles)


def own_index(h):
    per_half = STEPS // 2
    return lambda g, where: (jnp.clip(g - h * per_half, 0, per_half - 1), 0, 0)


def patch_operands(blocks, own_blocks, shared_blocks):
    args, specs = [], []
    for k in own_blocks:
        for h, half in enumerate(blocks[k]):
            dims = (half.shape[0] // 3,) + half.shape[1:]
            args.append(half)
            specs.append(pl.BlockSpec(dims, own_index(h)))
    for k in shared_blocks:
        for half in blocks[k]:
            dims = (half.shape[0] // 3,) + half.shape[1:]
            args.append(half)
            specs.append(pl.BlockSpec(dims, lambda g, where: (2, 0, 0)))
    return args, specs


def lay_target(g, where_ref, refs, target):
    if len(refs) == 1:
        target[...] = refs[0][...]
        return
    pairs = [refs[j : j + 2] for j in range(0, len(refs), 2)]
    own, shared = pairs[: len(pairs) // 2], pairs[len(pairs) // 2 :]
    per_half = STEPS // 2
    h, side = g // per_half, g % per_half
    lanes = lambda j: pl.ds(pl.multiple_of(where_ref[TILES + j] * LANES, LANES), LANES)
    for k, pair in enumerate(own):
        target[:, :, lanes(2 * k)] = pair[h][...]
    for k in range(0, len(shared), 2):
        mine, other = shared[k][h][...].astype(F32), shared[k + 1][h][...].astype(F32)
        lane = lax.broadcasted_iota(jnp.int32, mine.shape, 2)
        value = jnp.where((lane < 64) == ((where_ref[PARITY] == 0) == (side == 0)), mine, other)
        if side:
            value = jnp.concatenate([value[:, :, 64:], value[:, :, :64]], axis=2)
        target[:, :, lanes(2 * k + 1)] = value.astype(BF16)


def deal(where_ref, sums, part, keep_ref, send_ref):
    core = where_ref[CORE]
    at = 0
    for value in sums:
        height = value.shape[0]
        for z in range(keep_ref.shape[0]):
            even = value[:, 2 * z * part : (2 * z + 1) * part]
            odd = value[:, (2 * z + 1) * part : (2 * z + 2) * part]
            mine = jnp.where(core == 0, even, odd)
            other = jnp.where(core == 0, odd, even)
            keep_ref[z, at : at + height, :] = mine.astype(BF16)
            send_ref[z, at : at + height, :] = other.astype(BF16)
        at += height


def copies_of(sources, held, sems):
    size, wide = held.shape[0] // STEPS, sources[0].shape[1]
    return [
        [
            pltpu.make_async_copy(
                source.at[pl.ds(g * size, size)], held.at[pl.ds(g * size, size), pl.ds(j * wide, wide)], sems.at[g, j]
            )
            for j, source in enumerate(sources)
        ]
        for g in range(STEPS)
    ]


def by_step(copies, body):
    step = pl.program_id(0)
    for g in range(STEPS):

        @pl.when(step == g)
        def _():
            if g == 0:
                for h in range(STEPS):
                    for copy in copies[h]:
                        copy.start()
            for copy in copies[g]:
                copy.wait()
            body(g)


def contract(g, rows, pairs):
    unit = rows // STEPS // TILE * TILE
    span = slice(g * unit, rows if g == STEPS - 1 else (g + 1) * unit)
    for total, left, right in pairs:
        now = dot(left[span], right[span], ROWS_0)
        total[...] = now if g == 0 else total[...] + now


def residual_kernel(groups, scale, n_feature, n_tiles, n_patch, where_ref, *refs):
    feature_refs, refs = refs[:n_feature], refs[n_feature:]
    recon_refs, refs = refs[:n_tiles], refs[n_tiles:]
    patch_refs, refs = refs[:n_patch], refs[n_patch:]
    grad_refs, refs = refs[:n_tiles], refs[n_tiles:]
    keep_ref, send_ref, target, feature, grads, total, sems = refs
    rows, width = feature.shape
    size = grad_refs[0].shape[0]

    def body(g):
        here = slice(g * size, (g + 1) * size)
        lay_target(g, where_ref, patch_refs, target)
        if g:
            contract(g - 1, rows, [(total, grads, feature)])
        for j, grad_ref in enumerate(grad_refs):
            cut = slice(j * TILE, (j + 1) * TILE)
            grad = ((recon_refs[j][...] - target[:, :, cut].reshape(size, TILE).astype(F32)) * scale).astype(BF16)
            grad_ref[...] = grad
            grads[here, cut] = grad
        if g == STEPS - 1:
            contract(g, rows, [(total, grads, feature)])
            deal(where_ref, [total], width // groups, keep_ref, send_ref)

    by_step(copies_of(feature_refs, feature, sems), body)


def residual(where, feature, recon, patch_args, patch_specs, images, scale, groups):
    rows = feature[0].shape[0]
    n_tiles = len(recon)
    width, n = len(feature) * TILE, n_tiles * TILE
    size = rows // STEPS
    parts = (groups // 2, n, width // groups)
    dealt = pl.BlockSpec(parts, lambda g, where: (0, 0, 0))
    block = pl.BlockSpec((size, TILE), lambda g, where: (g, 0))
    *grad, keep, send = call(
        functools.partial(residual_kernel, groups, scale, len(feature), n_tiles, len(patch_args)),
        [*[shape((rows, TILE), BF16)] * n_tiles, shape(parts, BF16), shape(parts, BF16)],
        limit=58,
        flops=2 * rows * width * n,
        moved=rows * (2 * width + 6 * n),
        grid_spec=pltpu.PrefetchScalarGridSpec(
            num_scalar_prefetch=1,
            grid=(STEPS,),
            in_specs=[
                *[HBM] * len(feature),
                *[block] * n_tiles,
                *patch_specs,
            ],
            out_specs=[*[block] * n_tiles, dealt, dealt],
            scratch_shapes=[
                pltpu.VMEM((size // images, images, n), BF16),
                pltpu.VMEM((rows, width), BF16),
                pltpu.VMEM((rows, n), BF16),
                pltpu.VMEM((n, width), F32),
                pltpu.SemaphoreType.DMA((STEPS, len(feature))),
            ],
        ),
        name="residual",
    )(where, *feature, *recon, *patch_args)
    return grad, keep, send


def backward_kernel(groups, n_grad, n_decode, where_ref, *refs):
    grad_refs, refs = refs[:n_grad], refs[n_grad:]
    decode_refs, refs = refs[:n_decode], refs[n_decode:]
    (hidden_ref, acts_ref, aux_grad_ref, aux_ref, second_ref, keep_ref, send_ref,
     hidden, acts, feature_grads, hidden_grads, pooled, total_second, total_first, sems) = refs
    rows, width = feature_grads.shape
    size = grad_refs[0].shape[0]
    images = aux_grad_ref.shape[0]
    pairs = [(total_second, hidden, feature_grads), (total_first, hidden_grads, acts)]

    def body(g):
        here = slice(g * size, (g + 1) * size)
        if g:
            contract(g - 1, rows, pairs)
        else:
            pooled[...] = dot(aux_grad_ref[...], aux_ref[...], COLS_1) / (rows // images)
        grad = jnp.concatenate([ref[...] for ref in grad_refs], axis=1)
        for j, decode_ref in enumerate(decode_refs):
            cut = slice(j * TILE, (j + 1) * TILE)
            back = dot(grad, decode_ref[...], COLS_1).reshape(size // images, images, TILE)
            feature_grads[here, cut] = (back + pooled[:, cut][None]).astype(BF16).reshape(size, TILE)
        hidden_back = dot(feature_grads[here], second_ref[...], COLS_1)
        hidden_grads[here] = jnp.where(hidden[here].astype(F32) > 0, hidden_back, 0.0).astype(BF16)
        if g == STEPS - 1:
            contract(g, rows, pairs)
            part = width // groups
            tall = total_second.shape[0] // groups
            second = jnp.concatenate(
                [
                    jnp.concatenate(
                        [total_second[d * tall : (d + 1) * tall, q * part : (q + 1) * part] for q in range(groups)], axis=0
                    )
                    for d in range(groups)
                ],
                axis=1,
            )
            deal(where_ref, [second, total_first], part, keep_ref, send_ref)

    copies = zip(copies_of([hidden_ref], hidden, sems.at[0]), copies_of([acts_ref], acts, sems.at[1]))
    by_step([one + other for one, other in copies], body)


def backward(where, grad, hidden, acts, decode, aux_grad, aux, second, groups):
    rows, width = acts.shape
    inner, n = hidden.shape[1], len(grad) * TILE
    n_decode = width // TILE
    row_block = lambda j: pl.BlockSpec((TILE, n), lambda g, where: (j, 0))
    size = rows // STEPS
    parts = (groups // 2, 2 * inner, width // groups)
    dealt = pl.BlockSpec(parts, lambda g, where: (0, 0, 0))
    whole = lambda array: pl.BlockSpec(array.shape, lambda g, where: (0, 0))
    return call(
        functools.partial(backward_kernel, groups, len(grad), n_decode),
        [shape(parts, BF16), shape(parts, BF16)],
        limit=44,
        flops=2 * rows * width * (n + 3 * inner),
        moved=2 * rows * (width + n + inner),
        grid_spec=pltpu.PrefetchScalarGridSpec(
            num_scalar_prefetch=1,
            grid=(STEPS,),
            in_specs=[
                *[pl.BlockSpec((size, TILE), lambda g, where: (g, 0))] * len(grad),
                *[row_block(j) for j in range(n_decode)],
                HBM,
                HBM,
                whole(aux_grad),
                whole(aux),
                whole(second),
            ],
            out_specs=[dealt, dealt],
            scratch_shapes=[
                pltpu.VMEM((rows, inner), BF16),
                pltpu.VMEM((rows, width), BF16),
                pltpu.VMEM((rows, width), BF16),
                pltpu.VMEM((rows, inner), BF16),
                pltpu.VMEM((aux_grad.shape[0], width), F32),
                pltpu.VMEM((inner, width), F32),
                pltpu.VMEM((inner, width), F32),
                pltpu.SemaphoreType.DMA((2, STEPS, 1)),
            ],
        ),
        name="backward",
    )(where, *grad, *[decode] * n_decode, hidden, acts, aux_grad, aux, second)


TOPS, DENOMS = 3, 19
DIGIT = 40


def to_digits(value):
    rest, lanes = value, []
    for _ in range(3):
        digit = rest.astype(BF16).astype(F32)
        lanes.append(digit[:, :DIGIT])
        rest = rest - digit
    lanes.append(jnp.zeros((value.shape[0], LANES - 3 * DIGIT), F32))
    return jnp.concatenate(lanes, axis=1).astype(BF16)


def from_digits(value):
    value = value.astype(F32)
    return sum(value[:, j * DIGIT : (j + 1) * DIGIT] for j in (2, 1, 0))


def labels_of(got, head):
    digits = got[:, head + LANES : head + LANES + 2].astype(F32)
    return (digits[:, 0:1] * LANES + digits[:, 1:2]).astype(jnp.int32)


def logits_kernel(where_ref, got_ref, klass_ref, sent_ref, logits_ref):
    groups, images, _ = got_ref.shape
    classes, head = klass_ref.shape
    got = got_ref[...].reshape(groups * images, -1)
    logits_ref[...] = dot(got[:, :head], klass_ref[...], COLS_1)
    logits = logits_ref[...]
    ids = lax.broadcasted_iota(jnp.int32, logits.shape, 1) + where_ref[ME] * classes
    hit = labels_of(got, head) == ids
    top = jnp.max(logits, axis=1, keepdims=True)
    expo = jnp.exp(logits - top)
    denom = jnp.sum(expo, axis=1, keepdims=True)
    own = jnp.sum(jnp.where(hit, expo, 0.0), axis=1, keepdims=True)
    rest = jnp.where(hit, 0.0, expo).astype(BF16)
    onehot = jnp.where(hit, 1.0, 0.0).astype(BF16)
    sent_ref[:, :, :head] = dot(rest, klass_ref[...]).astype(BF16).reshape(groups, images, head)
    sent_ref[:, :, head : 2 * head] = dot(onehot, klass_ref[...]).astype(BF16).reshape(groups, images, head)
    lane = lax.broadcasted_iota(jnp.int32, (images, LANES), 1)
    cut = lambda value, d: value[d * images : (d + 1) * images]
    common = jnp.zeros((images, LANES), F32)
    for d in range(groups):
        common = jnp.where(lane == TOPS + d, cut(top, d), common)
        common = jnp.where(lane == DENOMS + d, cut(denom, d), common)
    for d in range(groups):
        stats = jnp.where(lane == 1, cut(denom, d), jnp.where(lane == 2, cut(own, d), common))
        sent_ref[d, :, 2 * head :] = to_digits(jnp.where(lane == 0, cut(top, d), stats))


def class_logits(where, got, klass):
    groups, images, _ = got.shape
    classes, head = klass.shape
    return call(
        logits_kernel,
        shape((groups, images, 2 * head + LANES), BF16),
        limit=16,
        in_specs=[SMEM, VMEM, VMEM],
        scratch_shapes=[pltpu.VMEM((groups * images, classes), F32)],
        name="class_logits",
    )(where, got, klass)


def aux_kernel(norm, got_ref, aux_pre_ref, grad_ref, cut_ref):
    groups, images, _ = got_ref.shape
    head = aux_pre_ref.shape[1]
    stats = [from_digits(got_ref[d, :, 2 * head :]) for d in range(groups)]
    top = functools.reduce(jnp.maximum, [s[:, 0:1] for s in stats])
    scales = [jnp.exp(s[:, 0:1] - top) for s in stats]
    denom = sum(s[:, 1:2] * f for s, f in zip(stats, scales))
    own = sum(s[:, 2:3] * f for s, f in zip(stats, scales)) / denom
    rest = sum(got_ref[d, :, :head].astype(F32) * scales[d] for d in range(groups)) / (denom * norm)
    row = sum(got_ref[d, :, head : 2 * head].astype(F32) for d in range(groups))
    back = rest + row * ((own - 1.0) / norm).astype(BF16).astype(F32)
    aux_grad = jnp.where(aux_pre_ref[...] > 0, back, 0.0).astype(BF16)
    grad_ref[...] = aux_grad
    part = cut_ref.shape[1]
    for q in range(head // part):
        cut_ref[q * images : (q + 1) * images, :] = aux_grad[:, q * part : (q + 1) * part]


def aux_backward(got, aux_pre, part, norm):
    images, head = aux_pre.shape
    return call(
        functools.partial(aux_kernel, norm),
        [shape((images, head), BF16), shape((images * head // part, part), BF16)],
        limit=16,
        flops=2e10,
        name="aux_backward",
    )(got, aux_pre)


def class_kernel(norm, where_ref, klass_ref, got_ref, stats_ref, mine_ref, other_ref, class_ref, aux_ref):
    groups, images, _ = got_ref.shape
    head = class_ref.shape[1]
    classes, part = class_ref.shape[0], aux_ref.shape[0]
    got = got_ref[...].reshape(groups * images, -1)
    stats = [from_digits(stats_ref[e]) for e in range(groups)]
    tops, denoms = [], []
    for d in range(groups):
        top = functools.reduce(jnp.maximum, [s[:, TOPS + d : TOPS + d + 1] for s in stats])
        tops.append(top)
        denoms.append(sum(s[:, DENOMS + d : DENOMS + d + 1] * jnp.exp(s[:, TOPS + d : TOPS + d + 1] - top) for s in stats))
    top, denom = jnp.concatenate(tops, axis=0), jnp.concatenate(denoms, axis=0)
    logits = dot(got[:, :head], klass_ref[...], COLS_1)
    ids = lax.broadcasted_iota(jnp.int32, logits.shape, 1) + where_ref[ME] * classes
    onehot = jnp.where(labels_of(got, head) == ids, 1.0, 0.0)
    logit_grad = ((jnp.exp(logits - top) / denom - onehot) / norm).astype(BF16)
    class_ref[...] = dot(logit_grad, got[:, :head], ROWS_0)
    total = jnp.zeros(aux_ref.shape, F32)
    for d in range(groups):
        k, ref = d // 2, other_ref if d % 2 else mine_ref
        grad = jnp.concatenate([ref[k, q * images : (q + 1) * images] for q in range(head // part)], axis=1)
        pooled = got_ref[where_ref[ME] ^ d, :, head : head + part]
        total += dot(pooled, grad, ROWS_0).astype(BF16).astype(F32)
    aux_ref[...] = total


def class_backward(where, klass, got, partial, mine, other, norm):
    groups, images, wide = partial.shape
    classes, head = klass.shape
    whole = lambda *dims: pl.BlockSpec(dims, lambda i: (0,) * len(dims))
    part = mine.shape[2]
    return call(
        functools.partial(class_kernel, norm),
        [shape((classes, head), F32), shape((part, head), F32)],
        limit=20,
        flops=2 * groups * images * classes * head,
        moved=4 * classes * head,
        grid=(1,),
        in_specs=[
            SMEM,
            whole(*klass.shape),
            whole(*got.shape),
            pl.BlockSpec((groups, images, LANES), lambda i: (0, 0, wide // LANES - 1)),
            whole(*mine.shape),
            whole(*other.shape),
        ],
        out_specs=[whole(classes, head), whole(part, head)],
        name="class_backward",
    )(where, klass, got, partial, mine, other)


def chip_kernel(chips, below, collect, where_ref, keep_ref, got_ref, *refs):
    refs, outs = refs[: below + collect], refs[below + collect :]
    n = keep_ref.shape[1]
    chip = where_ref[ME] >> 1
    for k in range(chips):
        outs[k][:n] = (keep_ref[chip ^ k].astype(F32) + got_ref[chip ^ k].astype(F32)).astype(BF16)
        for ref in refs[:below]:
            outs[k][n:] = ref[...]
    if collect:
        size = outs[-1].shape[1]
        for k, ref in enumerate(refs[below:]):
            outs[-1][k] = ref[ref.shape[0] - size :]


def add_cores(where, keep, send, below=(), collect=(), size=0):
    chips, n, part = keep.shape
    rows = n + sum(e.shape[0] for e in below)
    outs = [shape((rows, part), BF16)] * chips
    if collect:
        outs.append(shape((len(collect), size, part), BF16))
    outs = call(
        functools.partial(chip_kernel, chips, len(below), len(collect)),
        outs,
        limit=16,
        in_specs=[SMEM, VMEM, VMEM, *[VMEM] * (len(below) + len(collect))],
        name="add_cores",
    )(where, keep, swap(send, "dp", 1), *below, *collect)
    return (outs[:chips], outs[chips]) if collect else outs


def exchange_chips(parts):
    return [parts[0]] + [swap(part, "dp", 2 * k) for k, part in enumerate(parts) if k]


def finish_kernel(inner, chips, *refs):
    early, last, (first_ref, second_ref, decode_ref) = refs[:chips], refs[chips : 2 * chips], refs[2 * chips :]
    n = decode_ref.shape[1]
    total = sum(ref[...].astype(F32) for ref in last)
    first_ref[...] = total[inner:].T
    tall, part = second_ref.shape[0], total.shape[1]
    for q in range(inner // tall):
        second_ref[:, q * part : (q + 1) * part] = total[q * tall : (q + 1) * tall]
    decode_ref[...] = sum(ref[:n].astype(F32) for ref in early).T


def finish(early, last, inner, groups, n):
    part = early[0].shape[1]
    return call(
        functools.partial(finish_kernel, inner, len(early)),
        [shape((part, inner), F32), shape((inner // groups, part * groups), F32), shape((part, n), F32)],
        limit=16,
        name="finish",
    )(*early, *last)


def local(acts, patches, labels, w_first, w_second, w_decode, w_aux, w_class):
    acts = acts[0].transpose(1, 0, 2)
    pix, images, width = acts.shape
    groups, count = lax.axis_size("dp"), lax.axis_size("section")
    me, section = lax.axis_index("dp"), lax.axis_index("section")
    scale = (groups * images * pix) ** -0.5
    norm = (groups * images) ** 0.5
    first, second, decode, aux, klass = w_first[0], w_second[0], w_decode[0], w_aux[0], w_class[0]
    inner = first.shape[1]
    n_decode = decode.shape[1]
    rows = pix * images

    paired = count == 4 and patches.shape[2] == 192
    if paired:
        near = [section ^ k for k in range(4)]
        tiles = [t for s in near for t in (3 * (s >> 1) + 2 * (s & 1), 3 * (s >> 1) + 1)]
        where = jnp.stack([section & 1, me & 1, me, *tiles]).astype(jnp.int32)
        turned = patches.transpose(0, 2, 1)
        halves = [pack(where, turned, h) for h in range(2)]
        x, y = [swap(halves[0], "section", 1)], [swap(halves[1], "section", 2)]
        first = after(first, halves[1])
    else:
        where = jnp.stack([section & 1, me & 1, me]).astype(jnp.int32)
        target = lax.all_gather(patches, "section", axis=2, tiled=True).transpose(1, 0, 2)

    hidden, feature, aux_pre, sent = forward(acts, first, second, aux, labels, groups)
    if paired:
        sent = after(sent, x[0])
        diagonal = [swap(after(x[0], aux_pre), "section", 2), swap(after(y[0], aux_pre), "section", 1)]
        x.append(swap(halves[1], "section", 1))
        y.insert(0, swap(halves[0], "section", 2))
        target = patch_operands([halves, x, y, diagonal], [0, 1, 2, 3], [0, 1, 2, 3])
    else:
        target = [target], [pl.BlockSpec((pix // STEPS, images, n_decode), lambda g, where: (g, 0, 0))]
    got = exchange(sent)
    recon = reconstruct([after(feature[0], sent), *feature[1:]], decode, n_decode // TILE)
    sent = class_logits(where, after(got, recon[0]), klass)
    partial = exchange(sent)
    grad, keep, send = residual(after(where, sent), feature, recon, *target, images, scale, groups)
    aux_grad, aux_cut = aux_backward(partial, aux_pre, width // groups, norm)
    chip_decode = add_cores(where, keep, send, [aux_cut])
    sum_decode = exchange_chips(chip_decode)
    keep, send = backward(
        where, grad, hidden, acts.reshape(rows, width), decode, after(aux_grad, chip_decode[0]), aux, second, groups
    )
    chip_last, mine = add_cores(where, keep, after(send, sum_decode), collect=sum_decode, size=aux_cut.shape[0])
    sum_last = exchange_chips(chip_last)
    grad_class, grad_aux = class_backward(where, klass, got, partial, mine, swap(mine, "dp", 1), norm)
    grad_first, grad_second, grad_decode = finish(sum_decode, sum_last, inner, groups, n_decode)
    return grad_first[None], grad_second[None], grad_decode[None], grad_aux[None], grad_class[None]


def solution(mesh):
    in_specs = (
        P("section", "dp", None, None),
        P("dp", None, "section"),
        P("dp"),
        P("section", None, None),
        P("section", None, None),
        P("section", None, None),
        P("section", None, None),
        P("section", "dp", None),
    )
    out_specs = (P("section", "dp", None),) * 5
    return jax.shard_map(local, mesh=mesh, in_specs=in_specs, out_specs=out_specs, check_vma=False)
```

```python
import functools

import jax
import jax.numpy as jnp
from jax import lax
from jax.experimental import pallas as pl
from jax.experimental.pallas import tpu as pltpu
from jax.sharding import PartitionSpec as P

F32 = jnp.float32
BF16 = jnp.bfloat16
STEPS = 4
LANES = 128
TILE = 256
MIB = 1024 * 1024
ROWS_0 = (((0,), (0,)), ((), ()))
COLS_1 = (((1,), (1,)), ((), ()))
PARITY, CORE, ME, TILES = 0, 1, 2, 3


def dot(left, right, dims=(((1,), (0,)), ((), ()))):
    return lax.dot_general(left, right, dims, preferred_element_type=F32)


def call(kernel, out_shape, *, limit, flops=0, moved=0, **kwargs):
    return pl.pallas_call(
        kernel,
        out_shape=out_shape,
        compiler_params=pltpu.CompilerParams(vmem_limit_bytes=limit * MIB),
        cost_estimate=pl.CostEstimate(flops=int(flops), bytes_accessed=int(moved), transcendentals=0),
        **kwargs,
    )


def shape(dims, kind):
    return jax.ShapeDtypeStruct(dims, kind)


SMEM = pl.BlockSpec(memory_space=pltpu.SMEM)
VMEM = pl.BlockSpec(memory_space=pltpu.VMEM)
HBM = pl.BlockSpec(memory_space=pltpu.HBM)


def swap(value, axis, bits):
    count = lax.axis_size(axis)
    return lax.ppermute(value, axis, [(i, i ^ bits) for i in range(count)])


def exchange(value, groups=None):
    return lax.all_to_all(value, "dp", 0, 0, axis_index_groups=groups, tiled=True)


def pack_kernel(first, where_ref, *refs):
    patches_refs, (out_ref, turned, own, shared) = refs[:-4], refs[-4:]
    several, span, pix = patches_refs[0].shape
    images = turned.shape[0]
    padded = turned.shape[1]
    count = out_ref.shape[0] // 3 * 2
    parity = where_ref[PARITY]
    at_own = pl.multiple_of(64 * parity, 64)
    at_shared = pl.multiple_of(128 * (1 - parity), 64)
    row = lax.broadcasted_iota(jnp.int32, (padded, pix), 0)
    column = lax.broadcasted_iota(jnp.int32, (padded, pix), 1)
    pick = ((row < count) & (column == row + first)).astype(F32).astype(BF16)
    for i in range(images):
        patches_ref, j = patches_refs[i // several], i % several
        turned[i, :, :LANES] = dot(pick, patches_ref[j, pl.ds(at_own, LANES), :], COLS_1).astype(BF16)
        turned[i, :, LANES:] = dot(pick, patches_ref[j, pl.ds(at_shared, 64), :], COLS_1).astype(BF16)
    size = 16 * images
    row = lax.broadcasted_iota(jnp.int32, (size, size), 0)
    column = lax.broadcasted_iota(jnp.int32, (size, size), 1)
    order = (row // images == column % 16) & (row % images == column // 16)
    order = order.astype(F32).astype(BF16)
    for b in range(padded // 16):
        rows = turned[:, 16 * b : 16 * b + 16, :].reshape(size, span)
        out = dot(order, rows).astype(BF16)
        own[16 * b : 16 * b + 16] = out[:, :LANES].reshape(16, images, LANES)
        shared[16 * b : 16 * b + 16] = out[:, LANES:].reshape(16, images, 64)
    out_ref[:count] = own[:count]
    lower, upper = shared[: count // 2], shared[count // 2 : count]

    @pl.when(parity == 0)
    def _():
        out_ref[count:] = jnp.concatenate([lower, upper], axis=2)

    @pl.when(parity == 1)
    def _():
        out_ref[count:] = jnp.concatenate([upper, lower], axis=2)


def pack(where, patches, h):
    images, span, pix = patches.shape
    half = pix // 2
    padded = -(-half // 16) * 16
    several = images // 4
    lanes = LANES if h == 0 and half <= LANES < pix else pix
    group = lambda j: pl.BlockSpec((several, span, lanes), lambda i: (j, 0, 0))
    dims = (half + half // 2, images, LANES)
    return call(
        functools.partial(pack_kernel, h * half),
        shape(dims, BF16),
        limit=20,
        grid=(1,),
        in_specs=[SMEM, *[group(j) for j in range(4)]],
        out_specs=pl.BlockSpec(dims, lambda i: (0, 0, 0)),
        scratch_shapes=[
            pltpu.VMEM((images, padded, span), BF16),
            pltpu.VMEM((padded, images, LANES), BF16),
            pltpu.VMEM((padded, images, 64), BF16),
        ],
        name="pack_patches",
    )(where, *[patches] * 4)


def after(value, other):
    return lax.optimization_barrier((value, other))[0]


def forward_kernel(n_tiles, pix, *refs):
    acts_refs, refs = refs[:n_tiles], refs[n_tiles:]
    first_ref, second_ref, aux_ref, labels_ref, hidden_ref = refs[:5]
    feature_refs, (aux_pre_ref, sent_ref, pooled) = refs[5:-3], refs[-3:]
    step = pl.program_id(0)
    block, images, _ = acts_refs[0].shape
    cut = lambda j: slice(j * TILE, (j + 1) * TILE)
    start = step == 0
    halves = []
    for a, b in ((0, block // 2), (block // 2, block)):
        flat = jnp.concatenate([ref[a:b].reshape((b - a) * images, TILE) for ref in acts_refs], axis=1)
        halves.append((a, b, flat, jnp.maximum(dot(flat, first_ref[...]), 0.0).astype(BF16)))
    for a, b, flat, hidden in halves:
        rows = slice(a * images, b * images)
        hidden_ref[rows] = hidden
        for j, feature_ref in enumerate(feature_refs):
            feature = (flat[:, cut(j)].astype(F32) + dot(hidden, second_ref[:, cut(j)])).astype(BF16)
            feature_ref[rows] = feature
            sums = jnp.sum(feature.reshape(b - a, images, TILE).astype(F32), axis=0)
            pooled[:, cut(j)] = sums + (pooled[:, cut(j)] if a else jnp.where(start, 0.0, pooled[:, cut(j)]))

    @pl.when(step == pl.num_programs(0) - 1)
    def _():
        groups = sent_ref.shape[0]
        width, head = aux_ref.shape
        part = width // groups
        mean = (pooled[...] / pix).astype(BF16)
        aux_pre = dot(mean, aux_ref[...])
        aux_pre_ref[...] = aux_pre
        out = jnp.maximum(aux_pre, 0.0).astype(BF16)
        row = lax.broadcasted_iota(jnp.int32, (images, LANES), 0)
        lane = lax.broadcasted_iota(jnp.int32, (images, LANES), 1)
        digits = jnp.zeros((images, LANES), jnp.int32)
        for i in range(images):
            label = labels_ref[i]
            digits = jnp.where((row == i) & (lane == 0), label // LANES, digits)
            digits = jnp.where((row == i) & (lane == 1), label % LANES, digits)
        digits = digits.astype(F32).astype(BF16)
        for d in range(groups):
            sent_ref[d, :, :head] = out
            sent_ref[d, :, head : head + part] = mean[:, d * part : (d + 1) * part]
            sent_ref[d, :, head + LANES :] = digits


def forward(acts, first, second, aux, labels, groups):
    pix, images, width = acts.shape
    inner, head = first.shape[1], aux.shape[1]
    block = pix // STEPS
    n_tiles = width // TILE
    whole = lambda *dims: pl.BlockSpec(dims, lambda g: (0,) * len(dims))
    rows = lambda n: pl.BlockSpec((block * images, n), lambda g: (g, 0))
    column = lambda j: pl.BlockSpec((block, images, TILE), lambda g: (g, 0, j))
    hidden, *feature, aux_pre, sent = call(
        functools.partial(forward_kernel, n_tiles, pix),
        [
            shape((pix * images, inner), BF16),
            *[shape((pix * images, TILE), BF16)] * n_tiles,
            shape((images, head), F32),
            shape((groups, images, head + 2 * LANES), BF16),
        ],
        limit=58,
        grid=(STEPS,),
        in_specs=[
            *[column(j) for j in range(n_tiles)],
            whole(*first.shape),
            whole(*second.shape),
            whole(*aux.shape),
            SMEM,
        ],
        out_specs=[
            rows(inner),
            *[rows(TILE)] * n_tiles,
            whole(images, head),
            whole(groups, images, head + 2 * LANES),
        ],
        scratch_shapes=[pltpu.VMEM((images, width), F32)],
        name="forward",
    )(*[acts] * n_tiles, first, second, aux, labels)
    return hidden, feature, aux_pre, sent


def recon_kernel(n_feature, n_tiles, *refs):
    feature_refs, decode_refs, recon_refs = refs[:n_feature], refs[n_feature : n_feature + n_tiles], refs[n_feature + n_tiles :]
    feature = jnp.concatenate([ref[...] for ref in feature_refs], axis=1)
    for decode_ref, recon_ref in zip(decode_refs, recon_refs):
        recon_ref[...] = dot(feature, decode_ref[...])


def reconstruct(feature, decode, n_tiles):
    rows = feature[0].shape[0]
    width = decode.shape[0]
    block = pl.BlockSpec((rows // STEPS, TILE), lambda g: (g, 0))
    return call(
        functools.partial(recon_kernel, len(feature), n_tiles),
        [shape((rows, TILE), F32)] * n_tiles,
        limit=57,
        grid=(STEPS,),
        in_specs=[*[block] * len(feature), *[pl.BlockSpec((width, TILE), lambda g, j=j: (0, j)) for j in range(n_tiles)]],
        out_specs=[block] * n_tiles,
        name="reconstruct",
    )(*feature, *[decode] * n_tiles)


def own_index(h):
    per_half = STEPS // 2
    return lambda g, where: (jnp.clip(g - h * per_half, 0, per_half - 1), 0, 0)


def patch_operands(blocks, own_blocks, shared_blocks):
    args, specs = [], []
    for k in own_blocks:
        for h, half in enumerate(blocks[k]):
            dims = (half.shape[0] // 3,) + half.shape[1:]
            args.append(half)
            specs.append(pl.BlockSpec(dims, own_index(h)))
    for k in shared_blocks:
        for half in blocks[k]:
            dims = (half.shape[0] // 3,) + half.shape[1:]
            args.append(half)
            specs.append(pl.BlockSpec(dims, lambda g, where: (2, 0, 0)))
    return args, specs


def lay_target(g, where_ref, refs, target):
    if len(refs) == 1:
        target[...] = refs[0][...]
        return
    pairs = [refs[j : j + 2] for j in range(0, len(refs), 2)]
    own, shared = pairs[: len(pairs) // 2], pairs[len(pairs) // 2 :]
    per_half = STEPS // 2
    h, side = g // per_half, g % per_half
    lanes = lambda j: pl.ds(pl.multiple_of(where_ref[TILES + j] * LANES, LANES), LANES)
    for k, pair in enumerate(own):
        target[:, :, lanes(2 * k)] = pair[h][...]
    for k in range(0, len(shared), 2):
        mine, other = shared[k][h][...].astype(F32), shared[k + 1][h][...].astype(F32)
        lane = lax.broadcasted_iota(jnp.int32, mine.shape, 2)
        value = jnp.where((lane < 64) == ((where_ref[PARITY] == 0) == (side == 0)), mine, other)
        if side:
            value = jnp.concatenate([value[:, :, 64:], value[:, :, :64]], axis=2)
        target[:, :, lanes(2 * k + 1)] = value.astype(BF16)


def deal(where_ref, sums, part, keep_ref, send_ref):
    core = where_ref[CORE]
    at = 0
    for value in sums:
        height = value.shape[0]
        for z in range(keep_ref.shape[0]):
            even = value[:, 2 * z * part : (2 * z + 1) * part]
            odd = value[:, (2 * z + 1) * part : (2 * z + 2) * part]
            mine = jnp.where(core == 0, even, odd)
            other = jnp.where(core == 0, odd, even)
            keep_ref[z, at : at + height, :] = mine.astype(BF16)
            send_ref[z, at : at + height, :] = other.astype(BF16)
        at += height


def copies_of(sources, held, sems):
    size, wide = held.shape[0] // STEPS, sources[0].shape[1]
    return [
        [
            pltpu.make_async_copy(
                source.at[pl.ds(g * size, size)], held.at[pl.ds(g * size, size), pl.ds(j * wide, wide)], sems.at[g, j]
            )
            for j, source in enumerate(sources)
        ]
        for g in range(STEPS)
    ]


def by_step(copies, body):
    step = pl.program_id(0)
    for g in range(STEPS):

        @pl.when(step == g)
        def _():
            if g == 0:
                for h in range(STEPS):
                    for copy in copies[h]:
                        copy.start()
            for copy in copies[g]:
                copy.wait()
            body(g)


def contract(g, rows, pairs):
    unit = rows // STEPS // TILE * TILE
    span = slice(g * unit, rows if g == STEPS - 1 else (g + 1) * unit)
    for total, left, right in pairs:
        now = dot(left[span], right[span], ROWS_0)
        total[...] = now if g == 0 else total[...] + now


def residual_kernel(groups, scale, n_feature, n_tiles, n_patch, where_ref, *refs):
    feature_refs, refs = refs[:n_feature], refs[n_feature:]
    recon_refs, refs = refs[:n_tiles], refs[n_tiles:]
    patch_refs, refs = refs[:n_patch], refs[n_patch:]
    grad_refs, refs = refs[:n_tiles], refs[n_tiles:]
    keep_ref, send_ref, target, feature, grads, total, sems = refs
    rows, width = feature.shape
    size = grad_refs[0].shape[0]

    def body(g):
        here = slice(g * size, (g + 1) * size)
        lay_target(g, where_ref, patch_refs, target)
        for j, grad_ref in enumerate(grad_refs):
            cut = slice(j * TILE, (j + 1) * TILE)
            grad = ((recon_refs[j][...] - target[:, :, cut].reshape(size, TILE).astype(F32)) * scale).astype(BF16)
            grad_ref[...] = grad
            grads[here, cut] = grad
        contract(g, rows, [(total, grads, feature)])
        if g == STEPS - 1:
            deal(where_ref, [total], width // groups, keep_ref, send_ref)

    by_step(copies_of(feature_refs, feature, sems), body)


def residual(where, feature, recon, patch_args, patch_specs, images, scale, groups):
    rows = feature[0].shape[0]
    n_tiles = len(recon)
    width, n = len(feature) * TILE, n_tiles * TILE
    size = rows // STEPS
    parts = (groups // 2, n, width // groups)
    dealt = pl.BlockSpec(parts, lambda g, where: (0, 0, 0))
    block = pl.BlockSpec((size, TILE), lambda g, where: (g, 0))
    *grad, keep, send = call(
        functools.partial(residual_kernel, groups, scale, len(feature), n_tiles, len(patch_args)),
        [*[shape((rows, TILE), BF16)] * n_tiles, shape(parts, BF16), shape(parts, BF16)],
        limit=58,
        flops=2 * rows * width * n,
        moved=rows * (2 * width + 6 * n),
        grid_spec=pltpu.PrefetchScalarGridSpec(
            num_scalar_prefetch=1,
            grid=(STEPS,),
            in_specs=[
                *[HBM] * len(feature),
                *[block] * n_tiles,
                *patch_specs,
            ],
            out_specs=[*[block] * n_tiles, dealt, dealt],
            scratch_shapes=[
                pltpu.VMEM((size // images, images, n), BF16),
                pltpu.VMEM((rows, width), BF16),
                pltpu.VMEM((rows, n), BF16),
                pltpu.VMEM((n, width), F32),
                pltpu.SemaphoreType.DMA((STEPS, len(feature))),
            ],
        ),
        name="residual",
    )(where, *feature, *recon, *patch_args)
    return grad, keep, send


def backward_kernel(groups, n_grad, n_decode, where_ref, *refs):
    grad_refs, refs = refs[:n_grad], refs[n_grad:]
    decode_refs, refs = refs[:n_decode], refs[n_decode:]
    (hidden_ref, acts_ref, aux_grad_ref, aux_ref, second_ref, keep_ref, send_ref,
     hidden, acts, feature_grads, hidden_grads, pooled, total_second, total_first, sems) = refs
    rows, width = feature_grads.shape
    size = grad_refs[0].shape[0]
    images = aux_grad_ref.shape[0]
    pairs = [(total_second, hidden, feature_grads), (total_first, hidden_grads, acts)]

    def body(g):
        here = slice(g * size, (g + 1) * size)
        if g:
            contract(g - 1, rows, pairs)
        else:
            pooled[...] = dot(aux_grad_ref[...], aux_ref[...], COLS_1) / (rows // images)
        grad = jnp.concatenate([ref[...] for ref in grad_refs], axis=1)
        for j, decode_ref in enumerate(decode_refs):
            cut = slice(j * TILE, (j + 1) * TILE)
            back = dot(grad, decode_ref[...], COLS_1).reshape(size // images, images, TILE)
            feature_grads[here, cut] = (back + pooled[:, cut][None]).astype(BF16).reshape(size, TILE)
        hidden_back = dot(feature_grads[here], second_ref[...], COLS_1)
        hidden_grads[here] = jnp.where(hidden[here].astype(F32) > 0, hidden_back, 0.0).astype(BF16)
        if g == STEPS - 1:
            contract(g, rows, pairs)
            part = width // groups
            tall = total_second.shape[0] // groups
            second = jnp.concatenate(
                [
                    jnp.concatenate(
                        [total_second[d * tall : (d + 1) * tall, q * part : (q + 1) * part] for q in range(groups)], axis=0
                    )
                    for d in range(groups)
                ],
                axis=1,
            )
            deal(where_ref, [second, total_first], part, keep_ref, send_ref)

    copies = zip(copies_of([hidden_ref], hidden, sems.at[0]), copies_of([acts_ref], acts, sems.at[1]))
    by_step([one + other for one, other in copies], body)


def backward(where, grad, hidden, acts, decode, aux_grad, aux, second, groups):
    rows, width = acts.shape
    inner, n = hidden.shape[1], len(grad) * TILE
    n_decode = width // TILE
    row_block = lambda j: pl.BlockSpec((TILE, n), lambda g, where: (j, 0))
    size = rows // STEPS
    parts = (groups // 2, 2 * inner, width // groups)
    dealt = pl.BlockSpec(parts, lambda g, where: (0, 0, 0))
    whole = lambda array: pl.BlockSpec(array.shape, lambda g, where: (0, 0))
    return call(
        functools.partial(backward_kernel, groups, len(grad), n_decode),
        [shape(parts, BF16), shape(parts, BF16)],
        limit=44,
        flops=2 * rows * width * (n + 3 * inner),
        moved=2 * rows * (width + n + inner),
        grid_spec=pltpu.PrefetchScalarGridSpec(
            num_scalar_prefetch=1,
            grid=(STEPS,),
            in_specs=[
                *[pl.BlockSpec((size, TILE), lambda g, where: (g, 0))] * len(grad),
                *[row_block(j) for j in range(n_decode)],
                HBM,
                HBM,
                whole(aux_grad),
                whole(aux),
                whole(second),
            ],
            out_specs=[dealt, dealt],
            scratch_shapes=[
                pltpu.VMEM((rows, inner), BF16),
                pltpu.VMEM((rows, width), BF16),
                pltpu.VMEM((rows, width), BF16),
                pltpu.VMEM((rows, inner), BF16),
                pltpu.VMEM((aux_grad.shape[0], width), F32),
                pltpu.VMEM((inner, width), F32),
                pltpu.VMEM((inner, width), F32),
                pltpu.SemaphoreType.DMA((2, STEPS, 1)),
            ],
        ),
        name="backward",
    )(where, *grad, *[decode] * n_decode, hidden, acts, aux_grad, aux, second)


TOPS, DENOMS = 3, 19
DIGIT = 40


def to_digits(value):
    rest, lanes = value, []
    for _ in range(3):
        digit = rest.astype(BF16).astype(F32)
        lanes.append(digit[:, :DIGIT])
        rest = rest - digit
    lanes.append(jnp.zeros((value.shape[0], LANES - 3 * DIGIT), F32))
    return jnp.concatenate(lanes, axis=1).astype(BF16)


def from_digits(value):
    value = value.astype(F32)
    return sum(value[:, j * DIGIT : (j + 1) * DIGIT] for j in (2, 1, 0))


def labels_of(got, head):
    digits = got[:, head + LANES : head + LANES + 2].astype(F32)
    return (digits[:, 0:1] * LANES + digits[:, 1:2]).astype(jnp.int32)


def logits_kernel(where_ref, got_ref, klass_ref, sent_ref, logits_ref):
    groups, images, _ = got_ref.shape
    classes, head = klass_ref.shape
    got = got_ref[...].reshape(groups * images, -1)
    logits_ref[...] = dot(got[:, :head], klass_ref[...], COLS_1)
    logits = logits_ref[...]
    ids = lax.broadcasted_iota(jnp.int32, logits.shape, 1) + where_ref[ME] * classes
    hit = labels_of(got, head) == ids
    top = jnp.max(logits, axis=1, keepdims=True)
    expo = jnp.exp(logits - top)
    denom = jnp.sum(expo, axis=1, keepdims=True)
    own = jnp.sum(jnp.where(hit, expo, 0.0), axis=1, keepdims=True)
    rest = jnp.where(hit, 0.0, expo).astype(BF16)
    onehot = jnp.where(hit, 1.0, 0.0).astype(BF16)
    sent_ref[:, :, :head] = dot(rest, klass_ref[...]).astype(BF16).reshape(groups, images, head)
    sent_ref[:, :, head : 2 * head] = dot(onehot, klass_ref[...]).astype(BF16).reshape(groups, images, head)
    lane = lax.broadcasted_iota(jnp.int32, (images, LANES), 1)
    cut = lambda value, d: value[d * images : (d + 1) * images]
    common = jnp.zeros((images, LANES), F32)
    for d in range(groups):
        common = jnp.where(lane == TOPS + d, cut(top, d), common)
        common = jnp.where(lane == DENOMS + d, cut(denom, d), common)
    for d in range(groups):
        stats = jnp.where(lane == 1, cut(denom, d), jnp.where(lane == 2, cut(own, d), common))
        sent_ref[d, :, 2 * head :] = to_digits(jnp.where(lane == 0, cut(top, d), stats))


def class_logits(where, got, klass):
    groups, images, _ = got.shape
    classes, head = klass.shape
    return call(
        logits_kernel,
        shape((groups, images, 2 * head + LANES), BF16),
        limit=16,
        in_specs=[SMEM, VMEM, VMEM],
        scratch_shapes=[pltpu.VMEM((groups * images, classes), F32)],
        name="class_logits",
    )(where, got, klass)


def aux_kernel(norm, got_ref, aux_pre_ref, grad_ref, cut_ref):
    groups, images, _ = got_ref.shape
    head = aux_pre_ref.shape[1]
    stats = [from_digits(got_ref[d, :, 2 * head :]) for d in range(groups)]
    top = functools.reduce(jnp.maximum, [s[:, 0:1] for s in stats])
    scales = [jnp.exp(s[:, 0:1] - top) for s in stats]
    denom = sum(s[:, 1:2] * f for s, f in zip(stats, scales))
    own = sum(s[:, 2:3] * f for s, f in zip(stats, scales)) / denom
    rest = sum(got_ref[d, :, :head].astype(F32) * scales[d] for d in range(groups)) / (denom * norm)
    row = sum(got_ref[d, :, head : 2 * head].astype(F32) for d in range(groups))
    back = rest + row * ((own - 1.0) / norm).astype(BF16).astype(F32)
    aux_grad = jnp.where(aux_pre_ref[...] > 0, back, 0.0).astype(BF16)
    grad_ref[...] = aux_grad
    part = cut_ref.shape[1]
    for q in range(head // part):
        cut_ref[q * images : (q + 1) * images, :] = aux_grad[:, q * part : (q + 1) * part]


def aux_backward(got, aux_pre, part, norm):
    images, head = aux_pre.shape
    return call(
        functools.partial(aux_kernel, norm),
        [shape((images, head), BF16), shape((images * head // part, part), BF16)],
        limit=16,
        flops=2e10,
        name="aux_backward",
    )(got, aux_pre)


def class_kernel(norm, where_ref, klass_ref, got_ref, stats_ref, mine_ref, other_ref, class_ref, aux_ref):
    groups, images, _ = got_ref.shape
    head = class_ref.shape[1]
    classes, part = class_ref.shape[0], aux_ref.shape[0]
    got = got_ref[...].reshape(groups * images, -1)
    stats = [from_digits(stats_ref[e]) for e in range(groups)]
    tops, denoms = [], []
    for d in range(groups):
        top = functools.reduce(jnp.maximum, [s[:, TOPS + d : TOPS + d + 1] for s in stats])
        tops.append(top)
        denoms.append(sum(s[:, DENOMS + d : DENOMS + d + 1] * jnp.exp(s[:, TOPS + d : TOPS + d + 1] - top) for s in stats))
    top, denom = jnp.concatenate(tops, axis=0), jnp.concatenate(denoms, axis=0)
    logits = dot(got[:, :head], klass_ref[...], COLS_1)
    ids = lax.broadcasted_iota(jnp.int32, logits.shape, 1) + where_ref[ME] * classes
    onehot = jnp.where(labels_of(got, head) == ids, 1.0, 0.0)
    logit_grad = ((jnp.exp(logits - top) / denom - onehot) / norm).astype(BF16)
    class_ref[...] = dot(logit_grad, got[:, :head], ROWS_0)
    total = jnp.zeros(aux_ref.shape, F32)
    for d in range(groups):
        k, ref = d // 2, other_ref if d % 2 else mine_ref
        grad = jnp.concatenate([ref[k, q * images : (q + 1) * images] for q in range(head // part)], axis=1)
        pooled = got_ref[where_ref[ME] ^ d, :, head : head + part]
        total += dot(pooled, grad, ROWS_0).astype(BF16).astype(F32)
    aux_ref[...] = total


def class_backward(where, klass, got, partial, mine, other, norm):
    groups, images, wide = partial.shape
    classes, head = klass.shape
    whole = lambda *dims: pl.BlockSpec(dims, lambda i: (0,) * len(dims))
    part = mine.shape[2]
    return call(
        functools.partial(class_kernel, norm),
        [shape((classes, head), F32), shape((part, head), F32)],
        limit=20,
        flops=2 * groups * images * classes * head,
        moved=4 * classes * head,
        grid=(1,),
        in_specs=[
            SMEM,
            whole(*klass.shape),
            whole(*got.shape),
            pl.BlockSpec((groups, images, LANES), lambda i: (0, 0, wide // LANES - 1)),
            whole(*mine.shape),
            whole(*other.shape),
        ],
        out_specs=[whole(classes, head), whole(part, head)],
        name="class_backward",
    )(where, klass, got, partial, mine, other)


def chip_kernel(chips, below, collect, where_ref, keep_ref, got_ref, *refs):
    refs, outs = refs[: below + collect], refs[below + collect :]
    n = keep_ref.shape[1]
    chip = where_ref[ME] >> 1
    for k in range(chips):
        outs[k][:n] = (keep_ref[chip ^ k].astype(F32) + got_ref[chip ^ k].astype(F32)).astype(BF16)
        for ref in refs[:below]:
            outs[k][n:] = ref[...]
    if collect:
        size = outs[-1].shape[1]
        for k, ref in enumerate(refs[below:]):
            outs[-1][k] = ref[ref.shape[0] - size :]


def add_cores(where, keep, send, below=(), collect=(), size=0):
    chips, n, part = keep.shape
    rows = n + sum(e.shape[0] for e in below)
    outs = [shape((rows, part), BF16)] * chips
    if collect:
        outs.append(shape((len(collect), size, part), BF16))
    outs = call(
        functools.partial(chip_kernel, chips, len(below), len(collect)),
        outs,
        limit=16,
        in_specs=[SMEM, VMEM, VMEM, *[VMEM] * (len(below) + len(collect))],
        name="add_cores",
    )(where, keep, swap(send, "dp", 1), *below, *collect)
    return (outs[:chips], outs[chips]) if collect else outs


def exchange_chips(parts):
    return [parts[0]] + [swap(part, "dp", 2 * k) for k, part in enumerate(parts) if k]


def finish_kernel(inner, chips, *refs):
    early, last, (first_ref, second_ref, decode_ref) = refs[:chips], refs[chips : 2 * chips], refs[2 * chips :]
    n = decode_ref.shape[1]
    total = sum(ref[...].astype(F32) for ref in last)
    first_ref[...] = total[inner:].T
    tall, part = second_ref.shape[0], total.shape[1]
    for q in range(inner // tall):
        second_ref[:, q * part : (q + 1) * part] = total[q * tall : (q + 1) * tall]
    decode_ref[...] = sum(ref[:n].astype(F32) for ref in early).T


def finish(early, last, inner, groups, n):
    part = early[0].shape[1]
    return call(
        functools.partial(finish_kernel, inner, len(early)),
        [shape((part, inner), F32), shape((inner // groups, part * groups), F32), shape((part, n), F32)],
        limit=16,
        name="finish",
    )(*early, *last)


def local(acts, patches, labels, w_first, w_second, w_decode, w_aux, w_class):
    acts = acts[0].transpose(1, 0, 2)
    pix, images, width = acts.shape
    groups, count = lax.axis_size("dp"), lax.axis_size("section")
    me, section = lax.axis_index("dp"), lax.axis_index("section")
    scale = (groups * images * pix) ** -0.5
    norm = (groups * images) ** 0.5
    first, second, decode, aux, klass = w_first[0], w_second[0], w_decode[0], w_aux[0], w_class[0]
    inner = first.shape[1]
    n_decode = decode.shape[1]
    rows = pix * images

    paired = count == 4 and patches.shape[2] == 192
    if paired:
        near = [section ^ k for k in range(4)]
        tiles = [t for s in near for t in (3 * (s >> 1) + 2 * (s & 1), 3 * (s >> 1) + 1)]
        where = jnp.stack([section & 1, me & 1, me, *tiles]).astype(jnp.int32)
        turned = patches.transpose(0, 2, 1)
        halves = [pack(where, turned, h) for h in range(2)]
        x, y = [swap(halves[0], "section", 1)], [swap(halves[1], "section", 2)]
        first = after(first, halves[1])
    else:
        where = jnp.stack([section & 1, me & 1, me]).astype(jnp.int32)
        target = lax.all_gather(patches, "section", axis=2, tiled=True).transpose(1, 0, 2)

    hidden, feature, aux_pre, sent = forward(acts, first, second, aux, labels, groups)
    if paired:
        sent = after(sent, x[0])
        diagonal = [swap(after(x[0], aux_pre), "section", 2), swap(after(y[0], aux_pre), "section", 1)]
        x.append(swap(halves[1], "section", 1))
        y.insert(0, swap(halves[0], "section", 2))
        target = patch_operands([halves, x, y, diagonal], [0, 1, 2, 3], [0, 1, 2, 3])
    else:
        target = [target], [pl.BlockSpec((pix // STEPS, images, n_decode), lambda g, where: (g, 0, 0))]
    got = exchange(sent)
    recon = reconstruct([after(feature[0], sent), *feature[1:]], decode, n_decode // TILE)
    sent = class_logits(where, after(got, recon[0]), klass)
    partial = exchange(sent)
    grad, keep, send = residual(after(where, sent), feature, recon, *target, images, scale, groups)
    aux_grad, aux_cut = aux_backward(partial, aux_pre, width // groups, norm)
    chip_decode = add_cores(where, keep, send, [aux_cut])
    sum_decode = exchange_chips(chip_decode)
    keep, send = backward(
        where, grad, hidden, acts.reshape(rows, width), decode, after(aux_grad, chip_decode[0]), aux, second, groups
    )
    chip_last, mine = add_cores(where, keep, after(send, sum_decode), collect=sum_decode, size=aux_cut.shape[0])
    sum_last = exchange_chips(chip_last)
    grad_class, grad_aux = class_backward(where, klass, got, partial, mine, swap(mine, "dp", 1), norm)
    grad_first, grad_second, grad_decode = finish(sum_decode, sum_last, inner, groups, n_decode)
    return grad_first[None], grad_second[None], grad_decode[None], grad_aux[None], grad_class[None]


def solution(mesh):
    in_specs = (
        P("section", "dp", None, None),
        P("dp", None, "section"),
        P("dp"),
        P("section", None, None),
        P("section", None, None),
        P("section", None, None),
        P("section", None, None),
        P("section", "dp", None),
    )
    out_specs = (P("section", "dp", None),) * 5
    return jax.shard_map(local, mesh=mesh, in_specs=in_specs, out_specs=out_specs, check_vma=False)
```

```python
import functools

import jax
import jax.numpy as jnp
from jax import lax
from jax.experimental import pallas as pl
from jax.experimental.pallas import tpu as pltpu
from jax.sharding import PartitionSpec as P

F32 = jnp.float32
BF16 = jnp.bfloat16
STEPS = 4
LANES = 128
TILE = 256
MIB = 1024 * 1024
ROWS_0 = (((0,), (0,)), ((), ()))
COLS_1 = (((1,), (1,)), ((), ()))
PARITY, CORE, ME, TILES = 0, 1, 2, 3


def dot(left, right, dims=(((1,), (0,)), ((), ()))):
    return lax.dot_general(left, right, dims, preferred_element_type=F32)


def call(kernel, out_shape, *, limit, flops=0, moved=0, **kwargs):
    return pl.pallas_call(
        kernel,
        out_shape=out_shape,
        compiler_params=pltpu.CompilerParams(vmem_limit_bytes=limit * MIB),
        cost_estimate=pl.CostEstimate(flops=int(flops), bytes_accessed=int(moved), transcendentals=0),
        **kwargs,
    )


def shape(dims, kind):
    return jax.ShapeDtypeStruct(dims, kind)


SMEM = pl.BlockSpec(memory_space=pltpu.SMEM)
VMEM = pl.BlockSpec(memory_space=pltpu.VMEM)
HBM = pl.BlockSpec(memory_space=pltpu.HBM)


def swap(value, axis, bits):
    count = lax.axis_size(axis)
    return lax.ppermute(value, axis, [(i, i ^ bits) for i in range(count)])


def exchange(value, groups=None):
    return lax.all_to_all(value, "dp", 0, 0, axis_index_groups=groups, tiled=True)


def pack_kernel(first, where_ref, *refs):
    patches_refs, (out_ref, turned, mixed) = refs[:-3], refs[-3:]
    several, span, pix = patches_refs[0].shape
    images, padded, _ = turned.shape
    count = out_ref.shape[0] // 3 * 2
    quarter = count // 2
    row = lax.broadcasted_iota(jnp.int32, (padded, pix), 0)
    column = lax.broadcasted_iota(jnp.int32, (padded, pix), 1)
    pick = ((row < count) & (column == row + first)).astype(F32).astype(BF16)
    for i in range(images):
        turned[i] = dot(pick, patches_refs[i // several][i % several], COLS_1).astype(BF16)
    size = 16 * images
    row = lax.broadcasted_iota(jnp.int32, (size, size), 0)
    column = lax.broadcasted_iota(jnp.int32, (size, size), 1)
    order = (row // images == column % 16) & (row % images == column // 16)
    order = order.astype(F32).astype(BF16)
    for b in range(padded // 16):
        rows = turned[:, 16 * b : 16 * b + 16, :].reshape(size, span)
        mixed[16 * b : 16 * b + 16] = dot(order, rows).astype(BF16).reshape(16, images, span)

    @pl.when(where_ref[PARITY] == 0)
    def _():
        out_ref[:count] = mixed[:count, :, :LANES]
        out_ref[count:] = jnp.concatenate([mixed[:quarter, :, LANES:], mixed[quarter:count, :, LANES:]], axis=2)

    @pl.when(where_ref[PARITY] == 1)
    def _():
        out_ref[:count] = mixed[:count, :, 64:]
        out_ref[count:] = jnp.concatenate([mixed[quarter:count, :, :64], mixed[:quarter, :, :64]], axis=2)


def pack(where, patches, h):
    images, span, pix = patches.shape
    half = pix // 2
    padded = -(-half // 16) * 16
    several = images // 4
    lanes = LANES if h == 0 and half <= LANES < pix else pix
    group = lambda j: pl.BlockSpec((several, span, lanes), lambda i: (j, 0, 0))
    dims = (half + half // 2, images, LANES)
    return call(
        functools.partial(pack_kernel, h * half),
        shape(dims, BF16),
        limit=20,
        grid=(1,),
        in_specs=[SMEM, *[group(j) for j in range(4)]],
        out_specs=pl.BlockSpec(dims, lambda i: (0, 0, 0)),
        scratch_shapes=[
            pltpu.VMEM((images, padded, span), BF16),
            pltpu.VMEM((padded, images, span), BF16),
        ],
        name="pack_patches",
    )(where, *[patches] * 4)


def after(value, other):
    return lax.optimization_barrier((value, other))[0]


def forward_kernel(n_tiles, pix, *refs):
    acts_refs, refs = refs[:n_tiles], refs[n_tiles:]
    first_ref, second_ref, aux_ref, labels_ref, hidden_ref = refs[:5]
    feature_refs, (aux_pre_ref, sent_ref, pooled) = refs[5:-3], refs[-3:]
    step = pl.program_id(0)
    block, images, _ = acts_refs[0].shape
    cut = lambda j: slice(j * TILE, (j + 1) * TILE)
    start = step == 0
    halves = []
    for a, b in ((0, block // 2), (block // 2, block)):
        flat = jnp.concatenate([ref[a:b].reshape((b - a) * images, TILE) for ref in acts_refs], axis=1)
        halves.append((a, b, flat, jnp.maximum(dot(flat, first_ref[...]), 0.0).astype(BF16)))
    for a, b, flat, hidden in halves:
        rows = slice(a * images, b * images)
        hidden_ref[rows] = hidden
        for j, feature_ref in enumerate(feature_refs):
            feature = (flat[:, cut(j)].astype(F32) + dot(hidden, second_ref[:, cut(j)])).astype(BF16)
            feature_ref[rows] = feature
            sums = jnp.sum(feature.reshape(b - a, images, TILE).astype(F32), axis=0)
            pooled[:, cut(j)] = sums + (pooled[:, cut(j)] if a else jnp.where(start, 0.0, pooled[:, cut(j)]))

    @pl.when(step == pl.num_programs(0) - 1)
    def _():
        groups = sent_ref.shape[0]
        width, head = aux_ref.shape
        part = width // groups
        mean = (pooled[...] / pix).astype(BF16)
        aux_pre = dot(mean, aux_ref[...])
        aux_pre_ref[...] = aux_pre
        out = jnp.maximum(aux_pre, 0.0).astype(BF16)
        row = lax.broadcasted_iota(jnp.int32, (images, LANES), 0)
        lane = lax.broadcasted_iota(jnp.int32, (images, LANES), 1)
        digits = jnp.zeros((images, LANES), jnp.int32)
        for i in range(images):
            label = labels_ref[i]
            digits = jnp.where((row == i) & (lane == 0), label // LANES, digits)
            digits = jnp.where((row == i) & (lane == 1), label % LANES, digits)
        digits = digits.astype(F32).astype(BF16)
        for d in range(groups):
            sent_ref[d, :, :head] = out
            sent_ref[d, :, head : head + part] = mean[:, d * part : (d + 1) * part]
            sent_ref[d, :, head + LANES :] = digits


def forward(acts, first, second, aux, labels, groups):
    pix, images, width = acts.shape
    inner, head = first.shape[1], aux.shape[1]
    block = pix // STEPS
    n_tiles = width // TILE
    whole = lambda *dims: pl.BlockSpec(dims, lambda g: (0,) * len(dims))
    rows = lambda n: pl.BlockSpec((block * images, n), lambda g: (g, 0))
    column = lambda j: pl.BlockSpec((block, images, TILE), lambda g: (g, 0, j))
    hidden, *feature, aux_pre, sent = call(
        functools.partial(forward_kernel, n_tiles, pix),
        [
            shape((pix * images, inner), BF16),
            *[shape((pix * images, TILE), BF16)] * n_tiles,
            shape((images, head), F32),
            shape((groups, images, head + 2 * LANES), BF16),
        ],
        limit=58,
        grid=(STEPS,),
        in_specs=[
            *[column(j) for j in range(n_tiles)],
            whole(*first.shape),
            whole(*second.shape),
            whole(*aux.shape),
            SMEM,
        ],
        out_specs=[
            rows(inner),
            *[rows(TILE)] * n_tiles,
            whole(images, head),
            whole(groups, images, head + 2 * LANES),
        ],
        scratch_shapes=[pltpu.VMEM((images, width), F32)],
        name="forward",
    )(*[acts] * n_tiles, first, second, aux, labels)
    return hidden, feature, aux_pre, sent


def recon_kernel(n_feature, n_tiles, *refs):
    feature_refs, decode_refs, recon_refs = refs[:n_feature], refs[n_feature : n_feature + n_tiles], refs[n_feature + n_tiles :]
    feature = jnp.concatenate([ref[...] for ref in feature_refs], axis=1)
    for decode_ref, recon_ref in zip(decode_refs, recon_refs):
        recon_ref[...] = dot(feature, decode_ref[...])


def reconstruct(feature, decode, n_tiles):
    rows = feature[0].shape[0]
    width = decode.shape[0]
    block = pl.BlockSpec((rows // STEPS, TILE), lambda g: (g, 0))
    return call(
        functools.partial(recon_kernel, len(feature), n_tiles),
        [shape((rows, TILE), F32)] * n_tiles,
        limit=57,
        grid=(STEPS,),
        in_specs=[*[block] * len(feature), *[pl.BlockSpec((width, TILE), lambda g, j=j: (0, j)) for j in range(n_tiles)]],
        out_specs=[block] * n_tiles,
        name="reconstruct",
    )(*feature, *[decode] * n_tiles)


def own_index(h):
    per_half = STEPS // 2
    return lambda g, where: (jnp.clip(g - h * per_half, 0, per_half - 1), 0, 0)


def patch_operands(blocks, own_blocks, shared_blocks):
    args, specs = [], []
    for k in own_blocks:
        for h, half in enumerate(blocks[k]):
            dims = (half.shape[0] // 3,) + half.shape[1:]
            args.append(half)
            specs.append(pl.BlockSpec(dims, own_index(h)))
    for k in shared_blocks:
        for half in blocks[k]:
            dims = (half.shape[0] // 3,) + half.shape[1:]
            args.append(half)
            specs.append(pl.BlockSpec(dims, lambda g, where: (2, 0, 0)))
    return args, specs


def lay_target(g, where_ref, refs, target):
    if len(refs) == 1:
        target[...] = refs[0][...]
        return
    pairs = [refs[j : j + 2] for j in range(0, len(refs), 2)]
    own, shared = pairs[: len(pairs) // 2], pairs[len(pairs) // 2 :]
    per_half = STEPS // 2
    h, side = g // per_half, g % per_half
    lanes = lambda j: pl.ds(pl.multiple_of(where_ref[TILES + j] * LANES, LANES), LANES)
    for k, pair in enumerate(own):
        target[:, :, lanes(2 * k)] = pair[h][...]
    for k in range(0, len(shared), 2):
        mine, other = shared[k][h][...].astype(F32), shared[k + 1][h][...].astype(F32)
        lane = lax.broadcasted_iota(jnp.int32, mine.shape, 2)
        value = jnp.where((lane < 64) == ((where_ref[PARITY] == 0) == (side == 0)), mine, other)
        if side:
            value = jnp.concatenate([value[:, :, 64:], value[:, :, :64]], axis=2)
        target[:, :, lanes(2 * k + 1)] = value.astype(BF16)


def deal(where_ref, sums, part, keep_ref, send_ref):
    core = where_ref[CORE]
    at = 0
    for value in sums:
        height = value.shape[0]
        for z in range(keep_ref.shape[0]):
            even = value[:, 2 * z * part : (2 * z + 1) * part]
            odd = value[:, (2 * z + 1) * part : (2 * z + 2) * part]
            mine = jnp.where(core == 0, even, odd)
            other = jnp.where(core == 0, odd, even)
            keep_ref[z, at : at + height, :] = mine.astype(BF16)
            send_ref[z, at : at + height, :] = other.astype(BF16)
        at += height


def copies_of(sources, held, sems):
    size, wide = held.shape[0] // STEPS, sources[0].shape[1]
    return [
        [
            pltpu.make_async_copy(
                source.at[pl.ds(g * size, size)], held.at[pl.ds(g * size, size), pl.ds(j * wide, wide)], sems.at[g, j]
            )
            for j, source in enumerate(sources)
        ]
        for g in range(STEPS)
    ]


def by_step(copies, body):
    step = pl.program_id(0)
    for g in range(STEPS):

        @pl.when(step == g)
        def _():
            if g == 0:
                for h in range(STEPS):
                    for copy in copies[h]:
                        copy.start()
            for copy in copies[g]:
                copy.wait()
            body(g)


def contract(g, rows, pairs):
    unit = rows // STEPS // TILE * TILE
    span = slice(g * unit, rows if g == STEPS - 1 else (g + 1) * unit)
    for total, left, right in pairs:
        now = dot(left[span], right[span], ROWS_0)
        total[...] = now if g == 0 else total[...] + now


def residual_kernel(groups, scale, n_feature, n_tiles, n_patch, where_ref, *refs):
    feature_refs, refs = refs[:n_feature], refs[n_feature:]
    recon_refs, refs = refs[:n_tiles], refs[n_tiles:]
    patch_refs, refs = refs[:n_patch], refs[n_patch:]
    grad_refs, refs = refs[:n_tiles], refs[n_tiles:]
    keep_ref, send_ref, target, feature, grads, total, sems = refs
    rows, width = feature.shape
    size = grad_refs[0].shape[0]

    def body(g):
        here = slice(g * size, (g + 1) * size)
        lay_target(g, where_ref, patch_refs, target)
        for j, grad_ref in enumerate(grad_refs):
            cut = slice(j * TILE, (j + 1) * TILE)
            grad = ((recon_refs[j][...] - target[:, :, cut].reshape(size, TILE).astype(F32)) * scale).astype(BF16)
            grad_ref[...] = grad
            grads[here, cut] = grad
        contract(g, rows, [(total, grads, feature)])
        if g == STEPS - 1:
            deal(where_ref, [total], width // groups, keep_ref, send_ref)

    by_step(copies_of(feature_refs, feature, sems), body)


def residual(where, feature, recon, patch_args, patch_specs, images, scale, groups):
    rows = feature[0].shape[0]
    n_tiles = len(recon)
    width, n = len(feature) * TILE, n_tiles * TILE
    size = rows // STEPS
    parts = (groups // 2, n, width // groups)
    dealt = pl.BlockSpec(parts, lambda g, where: (0, 0, 0))
    block = pl.BlockSpec((size, TILE), lambda g, where: (g, 0))
    *grad, keep, send = call(
        functools.partial(residual_kernel, groups, scale, len(feature), n_tiles, len(patch_args)),
        [*[shape((rows, TILE), BF16)] * n_tiles, shape(parts, BF16), shape(parts, BF16)],
        limit=58,
        flops=2 * rows * width * n,
        moved=rows * (2 * width + 6 * n),
        grid_spec=pltpu.PrefetchScalarGridSpec(
            num_scalar_prefetch=1,
            grid=(STEPS,),
            in_specs=[
                *[HBM] * len(feature),
                *[block] * n_tiles,
                *patch_specs,
            ],
            out_specs=[*[block] * n_tiles, dealt, dealt],
            scratch_shapes=[
                pltpu.VMEM((size // images, images, n), BF16),
                pltpu.VMEM((rows, width), BF16),
                pltpu.VMEM((rows, n), BF16),
                pltpu.VMEM((n, width), F32),
                pltpu.SemaphoreType.DMA((STEPS, len(feature))),
            ],
        ),
        name="residual",
    )(where, *feature, *recon, *patch_args)
    return grad, keep, send


def backward_kernel(groups, n_grad, n_decode, where_ref, *refs):
    grad_refs, refs = refs[:n_grad], refs[n_grad:]
    decode_refs, refs = refs[:n_decode], refs[n_decode:]
    (hidden_ref, acts_ref, aux_grad_ref, aux_ref, second_ref, keep_ref, send_ref,
     hidden, acts, feature_grads, hidden_grads, pooled, total_second, total_first, sems) = refs
    rows, width = feature_grads.shape
    size = grad_refs[0].shape[0]
    images = aux_grad_ref.shape[0]
    pairs = [(total_second, hidden, feature_grads), (total_first, hidden_grads, acts)]

    def body(g):
        here = slice(g * size, (g + 1) * size)
        if g:
            contract(g - 1, rows, pairs)
        else:
            pooled[...] = dot(aux_grad_ref[...], aux_ref[...], COLS_1) / (rows // images)
        grad = jnp.concatenate([ref[...] for ref in grad_refs], axis=1)
        for j, decode_ref in enumerate(decode_refs):
            cut = slice(j * TILE, (j + 1) * TILE)
            back = dot(grad, decode_ref[...], COLS_1).reshape(size // images, images, TILE)
            feature_grads[here, cut] = (back + pooled[:, cut][None]).astype(BF16).reshape(size, TILE)
        hidden_back = dot(feature_grads[here], second_ref[...], COLS_1)
        hidden_grads[here] = jnp.where(hidden[here].astype(F32) > 0, hidden_back, 0.0).astype(BF16)
        if g == STEPS - 1:
            contract(g, rows, pairs)
            part = width // groups
            tall = total_second.shape[0] // groups
            second = jnp.concatenate(
                [
                    jnp.concatenate(
                        [total_second[d * tall : (d + 1) * tall, q * part : (q + 1) * part] for q in range(groups)], axis=0
                    )
                    for d in range(groups)
                ],
                axis=1,
            )
            deal(where_ref, [second, total_first], part, keep_ref, send_ref)

    copies = zip(copies_of([hidden_ref], hidden, sems.at[0]), copies_of([acts_ref], acts, sems.at[1]))
    by_step([one + other for one, other in copies], body)


def backward(where, grad, hidden, acts, decode, aux_grad, aux, second, groups):
    rows, width = acts.shape
    inner, n = hidden.shape[1], len(grad) * TILE
    n_decode = width // TILE
    row_block = lambda j: pl.BlockSpec((TILE, n), lambda g, where: (j, 0))
    size = rows // STEPS
    parts = (groups // 2, 2 * inner, width // groups)
    dealt = pl.BlockSpec(parts, lambda g, where: (0, 0, 0))
    whole = lambda array: pl.BlockSpec(array.shape, lambda g, where: (0, 0))
    return call(
        functools.partial(backward_kernel, groups, len(grad), n_decode),
        [shape(parts, BF16), shape(parts, BF16)],
        limit=44,
        flops=2 * rows * width * (n + 3 * inner),
        moved=2 * rows * (width + n + inner),
        grid_spec=pltpu.PrefetchScalarGridSpec(
            num_scalar_prefetch=1,
            grid=(STEPS,),
            in_specs=[
                *[pl.BlockSpec((size, TILE), lambda g, where: (g, 0))] * len(grad),
                *[row_block(j) for j in range(n_decode)],
                HBM,
                HBM,
                whole(aux_grad),
                whole(aux),
                whole(second),
            ],
            out_specs=[dealt, dealt],
            scratch_shapes=[
                pltpu.VMEM((rows, inner), BF16),
                pltpu.VMEM((rows, width), BF16),
                pltpu.VMEM((rows, width), BF16),
                pltpu.VMEM((rows, inner), BF16),
                pltpu.VMEM((aux_grad.shape[0], width), F32),
                pltpu.VMEM((inner, width), F32),
                pltpu.VMEM((inner, width), F32),
                pltpu.SemaphoreType.DMA((2, STEPS, 1)),
            ],
        ),
        name="backward",
    )(where, *grad, *[decode] * n_decode, hidden, acts, aux_grad, aux, second)


TOPS, DENOMS = 3, 19
DIGIT = 40


def to_digits(value):
    rest, lanes = value, []
    for _ in range(3):
        digit = rest.astype(BF16).astype(F32)
        lanes.append(digit[:, :DIGIT])
        rest = rest - digit
    lanes.append(jnp.zeros((value.shape[0], LANES - 3 * DIGIT), F32))
    return jnp.concatenate(lanes, axis=1).astype(BF16)


def from_digits(value):
    value = value.astype(F32)
    return sum(value[:, j * DIGIT : (j + 1) * DIGIT] for j in (2, 1, 0))


def labels_of(got, head):
    digits = got[:, head + LANES : head + LANES + 2].astype(F32)
    return (digits[:, 0:1] * LANES + digits[:, 1:2]).astype(jnp.int32)


def logits_kernel(where_ref, got_ref, klass_ref, sent_ref, logits_ref):
    groups, images, _ = got_ref.shape
    classes, head = klass_ref.shape
    got = got_ref[...].reshape(groups * images, -1)
    logits_ref[...] = dot(got[:, :head], klass_ref[...], COLS_1)
    logits = logits_ref[...]
    ids = lax.broadcasted_iota(jnp.int32, logits.shape, 1) + where_ref[ME] * classes
    hit = labels_of(got, head) == ids
    top = jnp.max(logits, axis=1, keepdims=True)
    expo = jnp.exp(logits - top)
    denom = jnp.sum(expo, axis=1, keepdims=True)
    own = jnp.sum(jnp.where(hit, expo, 0.0), axis=1, keepdims=True)
    rest = jnp.where(hit, 0.0, expo).astype(BF16)
    onehot = jnp.where(hit, 1.0, 0.0).astype(BF16)
    sent_ref[:, :, :head] = dot(rest, klass_ref[...]).astype(BF16).reshape(groups, images, head)
    sent_ref[:, :, head : 2 * head] = dot(onehot, klass_ref[...]).astype(BF16).reshape(groups, images, head)
    lane = lax.broadcasted_iota(jnp.int32, (images, LANES), 1)
    cut = lambda value, d: value[d * images : (d + 1) * images]
    common = jnp.zeros((images, LANES), F32)
    for d in range(groups):
        common = jnp.where(lane == TOPS + d, cut(top, d), common)
        common = jnp.where(lane == DENOMS + d, cut(denom, d), common)
    for d in range(groups):
        stats = jnp.where(lane == 1, cut(denom, d), jnp.where(lane == 2, cut(own, d), common))
        sent_ref[d, :, 2 * head :] = to_digits(jnp.where(lane == 0, cut(top, d), stats))


def class_logits(where, got, klass):
    groups, images, _ = got.shape
    classes, head = klass.shape
    return call(
        logits_kernel,
        shape((groups, images, 2 * head + LANES), BF16),
        limit=16,
        in_specs=[SMEM, VMEM, VMEM],
        scratch_shapes=[pltpu.VMEM((groups * images, classes), F32)],
        name="class_logits",
    )(where, got, klass)


def aux_kernel(norm, got_ref, aux_pre_ref, grad_ref, cut_ref):
    groups, images, _ = got_ref.shape
    head = aux_pre_ref.shape[1]
    stats = [from_digits(got_ref[d, :, 2 * head :]) for d in range(groups)]
    top = functools.reduce(jnp.maximum, [s[:, 0:1] for s in stats])
    scales = [jnp.exp(s[:, 0:1] - top) for s in stats]
    denom = sum(s[:, 1:2] * f for s, f in zip(stats, scales))
    own = sum(s[:, 2:3] * f for s, f in zip(stats, scales)) / denom
    rest = sum(got_ref[d, :, :head].astype(F32) * scales[d] for d in range(groups)) / (denom * norm)
    row = sum(got_ref[d, :, head : 2 * head].astype(F32) for d in range(groups))
    back = rest + row * ((own - 1.0) / norm).astype(BF16).astype(F32)
    aux_grad = jnp.where(aux_pre_ref[...] > 0, back, 0.0).astype(BF16)
    grad_ref[...] = aux_grad
    part = cut_ref.shape[1]
    for q in range(head // part):
        cut_ref[q * images : (q + 1) * images, :] = aux_grad[:, q * part : (q + 1) * part]


def aux_backward(got, aux_pre, part, norm):
    images, head = aux_pre.shape
    return call(
        functools.partial(aux_kernel, norm),
        [shape((images, head), BF16), shape((images * head // part, part), BF16)],
        limit=16,
        flops=2e10,
        name="aux_backward",
    )(got, aux_pre)


def class_kernel(norm, where_ref, klass_ref, got_ref, stats_ref, mine_ref, other_ref, class_ref, aux_ref):
    groups, images, _ = got_ref.shape
    head = class_ref.shape[1]
    classes, part = class_ref.shape[0], aux_ref.shape[0]
    got = got_ref[...].reshape(groups * images, -1)
    stats = [from_digits(stats_ref[e]) for e in range(groups)]
    tops, denoms = [], []
    for d in range(groups):
        top = functools.reduce(jnp.maximum, [s[:, TOPS + d : TOPS + d + 1] for s in stats])
        tops.append(top)
        denoms.append(sum(s[:, DENOMS + d : DENOMS + d + 1] * jnp.exp(s[:, TOPS + d : TOPS + d + 1] - top) for s in stats))
    top, denom = jnp.concatenate(tops, axis=0), jnp.concatenate(denoms, axis=0)
    logits = dot(got[:, :head], klass_ref[...], COLS_1)
    ids = lax.broadcasted_iota(jnp.int32, logits.shape, 1) + where_ref[ME] * classes
    onehot = jnp.where(labels_of(got, head) == ids, 1.0, 0.0)
    logit_grad = ((jnp.exp(logits - top) / denom - onehot) / norm).astype(BF16)
    class_ref[...] = dot(logit_grad, got[:, :head], ROWS_0)
    total = jnp.zeros(aux_ref.shape, F32)
    for d in range(groups):
        k, ref = d // 2, other_ref if d % 2 else mine_ref
        grad = jnp.concatenate([ref[k, q * images : (q + 1) * images] for q in range(head // part)], axis=1)
        pooled = got_ref[where_ref[ME] ^ d, :, head : head + part]
        total += dot(pooled, grad, ROWS_0).astype(BF16).astype(F32)
    aux_ref[...] = total


def class_backward(where, klass, got, partial, mine, other, norm):
    groups, images, wide = partial.shape
    classes, head = klass.shape
    whole = lambda *dims: pl.BlockSpec(dims, lambda i: (0,) * len(dims))
    part = mine.shape[2]
    return call(
        functools.partial(class_kernel, norm),
        [shape((classes, head), F32), shape((part, head), F32)],
        limit=20,
        flops=2 * groups * images * classes * head,
        moved=4 * classes * head,
        grid=(1,),
        in_specs=[
            SMEM,
            whole(*klass.shape),
            whole(*got.shape),
            pl.BlockSpec((groups, images, LANES), lambda i: (0, 0, wide // LANES - 1)),
            whole(*mine.shape),
            whole(*other.shape),
        ],
        out_specs=[whole(classes, head), whole(part, head)],
        name="class_backward",
    )(where, klass, got, partial, mine, other)


def chip_kernel(chips, below, collect, where_ref, keep_ref, got_ref, *refs):
    refs, outs = refs[: below + collect], refs[below + collect :]
    n = keep_ref.shape[1]
    chip = where_ref[ME] >> 1
    for k in range(chips):
        outs[k][:n] = (keep_ref[chip ^ k].astype(F32) + got_ref[chip ^ k].astype(F32)).astype(BF16)
        for ref in refs[:below]:
            outs[k][n:] = ref[...]
    if collect:
        size = outs[-1].shape[1]
        for k, ref in enumerate(refs[below:]):
            outs[-1][k] = ref[ref.shape[0] - size :]


def add_cores(where, keep, send, below=(), collect=(), size=0):
    chips, n, part = keep.shape
    rows = n + sum(e.shape[0] for e in below)
    outs = [shape((rows, part), BF16)] * chips
    if collect:
        outs.append(shape((len(collect), size, part), BF16))
    outs = call(
        functools.partial(chip_kernel, chips, len(below), len(collect)),
        outs,
        limit=16,
        in_specs=[SMEM, VMEM, VMEM, *[VMEM] * (len(below) + len(collect))],
        name="add_cores",
    )(where, keep, swap(send, "dp", 1), *below, *collect)
    return (outs[:chips], outs[chips]) if collect else outs


def exchange_chips(parts):
    return [parts[0]] + [swap(part, "dp", 2 * k) for k, part in enumerate(parts) if k]


def finish_kernel(inner, chips, *refs):
    early, last, (first_ref, second_ref, decode_ref) = refs[:chips], refs[chips : 2 * chips], refs[2 * chips :]
    n = decode_ref.shape[1]
    total = sum(ref[...].astype(F32) for ref in last)
    first_ref[...] = total[inner:].T
    tall, part = second_ref.shape[0], total.shape[1]
    for q in range(inner // tall):
        second_ref[:, q * part : (q + 1) * part] = total[q * tall : (q + 1) * tall]
    decode_ref[...] = sum(ref[:n].astype(F32) for ref in early).T


def finish(early, last, inner, groups, n):
    part = early[0].shape[1]
    return call(
        functools.partial(finish_kernel, inner, len(early)),
        [shape((part, inner), F32), shape((inner // groups, part * groups), F32), shape((part, n), F32)],
        limit=16,
        name="finish",
    )(*early, *last)


def local(acts, patches, labels, w_first, w_second, w_decode, w_aux, w_class):
    acts = acts[0].transpose(1, 0, 2)
    pix, images, width = acts.shape
    groups, count = lax.axis_size("dp"), lax.axis_size("section")
    me, section = lax.axis_index("dp"), lax.axis_index("section")
    scale = (groups * images * pix) ** -0.5
    norm = (groups * images) ** 0.5
    first, second, decode, aux, klass = w_first[0], w_second[0], w_decode[0], w_aux[0], w_class[0]
    inner = first.shape[1]
    n_decode = decode.shape[1]
    rows = pix * images

    paired = count == 4 and patches.shape[2] == 192
    if paired:
        near = [section ^ k for k in range(4)]
        tiles = [t for s in near for t in (3 * (s >> 1) + 2 * (s & 1), 3 * (s >> 1) + 1)]
        where = jnp.stack([section & 1, me & 1, me, *tiles]).astype(jnp.int32)
        turned = patches.transpose(0, 2, 1)
        halves = [pack(where, turned, h) for h in range(2)]
        x, y = [swap(halves[0], "section", 1)], [swap(halves[1], "section", 2)]
        first = after(first, halves[1])
    else:
        where = jnp.stack([section & 1, me & 1, me]).astype(jnp.int32)
        target = lax.all_gather(patches, "section", axis=2, tiled=True).transpose(1, 0, 2)

    hidden, feature, aux_pre, sent = forward(acts, first, second, aux, labels, groups)
    if paired:
        sent = after(sent, x[0])
        diagonal = [swap(after(x[0], aux_pre), "section", 2), swap(after(y[0], aux_pre), "section", 1)]
        x.append(swap(halves[1], "section", 1))
        y.insert(0, swap(halves[0], "section", 2))
        target = patch_operands([halves, x, y, diagonal], [0, 1, 2, 3], [0, 1, 2, 3])
    else:
        target = [target], [pl.BlockSpec((pix // STEPS, images, n_decode), lambda g, where: (g, 0, 0))]
    got = exchange(sent)
    recon = reconstruct([after(feature[0], sent), *feature[1:]], decode, n_decode // TILE)
    sent = class_logits(where, after(got, recon[0]), klass)
    partial = exchange(sent)
    grad, keep, send = residual(after(where, sent), feature, recon, *target, images, scale, groups)
    aux_grad, aux_cut = aux_backward(partial, aux_pre, width // groups, norm)
    chip_decode = add_cores(where, keep, send, [aux_cut])
    sum_decode = exchange_chips(chip_decode)
    keep, send = backward(
        where, grad, hidden, acts.reshape(rows, width), decode, after(aux_grad, chip_decode[0]), aux, second, groups
    )
    chip_last, mine = add_cores(where, keep, after(send, sum_decode), collect=sum_decode, size=aux_cut.shape[0])
    sum_last = exchange_chips(chip_last)
    grad_class, grad_aux = class_backward(where, klass, got, partial, mine, swap(mine, "dp", 1), norm)
    grad_first, grad_second, grad_decode = finish(sum_decode, sum_last, inner, groups, n_decode)
    return grad_first[None], grad_second[None], grad_decode[None], grad_aux[None], grad_class[None]


def solution(mesh):
    in_specs = (
        P("section", "dp", None, None),
        P("dp", None, "section"),
        P("dp"),
        P("section", None, None),
        P("section", None, None),
        P("section", None, None),
        P("section", None, None),
        P("section", "dp", None),
    )
    out_specs = (P("section", "dp", None),) * 5
    return jax.shard_map(local, mesh=mesh, in_specs=in_specs, out_specs=out_specs, check_vma=False)
```

```python
import functools

import jax
import jax.numpy as jnp
from jax import lax
from jax.experimental import pallas as pl
from jax.experimental.pallas import tpu as pltpu
from jax.sharding import PartitionSpec as P

F32 = jnp.float32
BF16 = jnp.bfloat16
STEPS = 4
LANES = 128
TILE = 256
MIB = 1024 * 1024
ROWS_0 = (((0,), (0,)), ((), ()))
COLS_1 = (((1,), (1,)), ((), ()))
PARITY, CORE, ME, TILES = 0, 1, 2, 3


def dot(left, right, dims=(((1,), (0,)), ((), ()))):
    return lax.dot_general(left, right, dims, preferred_element_type=F32)


def call(kernel, out_shape, *, limit, flops=0, moved=0, **kwargs):
    return pl.pallas_call(
        kernel,
        out_shape=out_shape,
        compiler_params=pltpu.CompilerParams(vmem_limit_bytes=limit * MIB),
        cost_estimate=pl.CostEstimate(flops=int(flops), bytes_accessed=int(moved), transcendentals=0),
        **kwargs,
    )


def shape(dims, kind):
    return jax.ShapeDtypeStruct(dims, kind)


SMEM = pl.BlockSpec(memory_space=pltpu.SMEM)
VMEM = pl.BlockSpec(memory_space=pltpu.VMEM)
HBM = pl.BlockSpec(memory_space=pltpu.HBM)


def swap(value, axis, bits):
    count = lax.axis_size(axis)
    return lax.ppermute(value, axis, [(i, i ^ bits) for i in range(count)])


def exchange(value, groups=None):
    return lax.all_to_all(value, "dp", 0, 0, axis_index_groups=groups, tiled=True)


def pack_kernel(first, where_ref, *refs):
    patches_refs, (out_ref, turned, mixed) = refs[:-3], refs[-3:]
    several, span, pix = patches_refs[0].shape
    images, padded, _ = turned.shape
    count = out_ref.shape[0] // 3 * 2
    quarter = count // 2
    row = lax.broadcasted_iota(jnp.int32, (padded, pix), 0)
    column = lax.broadcasted_iota(jnp.int32, (padded, pix), 1)
    pick = ((row < count) & (column == row + first)).astype(F32).astype(BF16)
    for i in range(images):
        turned[i] = dot(pick, patches_refs[i // several][i % several], COLS_1).astype(BF16)
    size = 16 * images
    row = lax.broadcasted_iota(jnp.int32, (size, size), 0)
    column = lax.broadcasted_iota(jnp.int32, (size, size), 1)
    order = (row // images == column % 16) & (row % images == column // 16)
    order = order.astype(F32).astype(BF16)
    for b in range(padded // 16):
        rows = turned[:, 16 * b : 16 * b + 16, :].reshape(size, span)
        mixed[16 * b : 16 * b + 16] = dot(order, rows).astype(BF16).reshape(16, images, span)

    @pl.when(where_ref[PARITY] == 0)
    def _():
        out_ref[:count] = mixed[:count, :, :LANES]
        out_ref[count:] = jnp.concatenate([mixed[:quarter, :, LANES:], mixed[quarter:count, :, LANES:]], axis=2)

    @pl.when(where_ref[PARITY] == 1)
    def _():
        out_ref[:count] = mixed[:count, :, 64:]
        out_ref[count:] = jnp.concatenate([mixed[quarter:count, :, :64], mixed[:quarter, :, :64]], axis=2)


def pack(where, patches, h):
    images, span, pix = patches.shape
    half = pix // 2
    padded = -(-half // 16) * 16
    several = images // 4
    lanes = LANES if h == 0 and half <= LANES < pix else pix
    group = lambda j: pl.BlockSpec((several, span, lanes), lambda i: (j, 0, 0))
    dims = (half + half // 2, images, LANES)
    return call(
        functools.partial(pack_kernel, h * half),
        shape(dims, BF16),
        limit=20,
        grid=(1,),
        in_specs=[SMEM, *[group(j) for j in range(4)]],
        out_specs=pl.BlockSpec(dims, lambda i: (0, 0, 0)),
        scratch_shapes=[
            pltpu.VMEM((images, padded, span), BF16),
            pltpu.VMEM((padded, images, span), BF16),
        ],
        name="pack_patches",
    )(where, *[patches] * 4)


def after(value, other):
    return lax.optimization_barrier((value, other))[0]


def forward_kernel(n_tiles, pix, *refs):
    acts_refs, refs = refs[:n_tiles], refs[n_tiles:]
    first_ref, second_ref, aux_ref, labels_ref, hidden_ref = refs[:5]
    feature_refs, (aux_pre_ref, sent_ref, pooled) = refs[5:-3], refs[-3:]
    step = pl.program_id(0)
    block, images, _ = acts_refs[0].shape
    cut = lambda j: slice(j * TILE, (j + 1) * TILE)
    start = step == 0
    halves = []
    for a, b in ((0, block // 2), (block // 2, block)):
        flat = jnp.concatenate([ref[a:b].reshape((b - a) * images, TILE) for ref in acts_refs], axis=1)
        halves.append((a, b, flat, jnp.maximum(dot(flat, first_ref[...]), 0.0).astype(BF16)))
    for a, b, flat, hidden in halves:
        rows = slice(a * images, b * images)
        hidden_ref[rows] = hidden
        for j, feature_ref in enumerate(feature_refs):
            feature = (flat[:, cut(j)].astype(F32) + dot(hidden, second_ref[:, cut(j)])).astype(BF16)
            feature_ref[rows] = feature
            sums = jnp.sum(feature.reshape(b - a, images, TILE).astype(F32), axis=0)
            pooled[:, cut(j)] = sums + (pooled[:, cut(j)] if a else jnp.where(start, 0.0, pooled[:, cut(j)]))

    @pl.when(step == pl.num_programs(0) - 1)
    def _():
        groups = sent_ref.shape[0]
        width, head = aux_ref.shape
        part = width // groups
        mean = (pooled[...] / pix).astype(BF16)
        aux_pre = dot(mean, aux_ref[...])
        aux_pre_ref[...] = aux_pre
        out = jnp.maximum(aux_pre, 0.0).astype(BF16)
        row = lax.broadcasted_iota(jnp.int32, (images, LANES), 0)
        lane = lax.broadcasted_iota(jnp.int32, (images, LANES), 1)
        digits = jnp.zeros((images, LANES), jnp.int32)
        for i in range(images):
            label = labels_ref[i]
            digits = jnp.where((row == i) & (lane == 0), label // LANES, digits)
            digits = jnp.where((row == i) & (lane == 1), label % LANES, digits)
        digits = digits.astype(F32).astype(BF16)
        for d in range(groups):
            sent_ref[d, :, :head] = out
            sent_ref[d, :, head : head + part] = mean[:, d * part : (d + 1) * part]
            sent_ref[d, :, head + LANES :] = digits


def forward(acts, first, second, aux, labels, groups):
    pix, images, width = acts.shape
    inner, head = first.shape[1], aux.shape[1]
    block = pix // STEPS
    n_tiles = width // TILE
    whole = lambda *dims: pl.BlockSpec(dims, lambda g: (0,) * len(dims))
    rows = lambda n: pl.BlockSpec((block * images, n), lambda g: (g, 0))
    column = lambda j: pl.BlockSpec((block, images, TILE), lambda g: (g, 0, j))
    hidden, *feature, aux_pre, sent = call(
        functools.partial(forward_kernel, n_tiles, pix),
        [
            shape((pix * images, inner), BF16),
            *[shape((pix * images, TILE), BF16)] * n_tiles,
            shape((images, head), F32),
            shape((groups, images, head + 2 * LANES), BF16),
        ],
        limit=58,
        grid=(STEPS,),
        in_specs=[
            *[column(j) for j in range(n_tiles)],
            whole(*first.shape),
            whole(*second.shape),
            whole(*aux.shape),
            SMEM,
        ],
        out_specs=[
            rows(inner),
            *[rows(TILE)] * n_tiles,
            whole(images, head),
            whole(groups, images, head + 2 * LANES),
        ],
        scratch_shapes=[pltpu.VMEM((images, width), F32)],
        name="forward",
    )(*[acts] * n_tiles, first, second, aux, labels)
    return hidden, feature, aux_pre, sent


def recon_kernel(n_feature, n_tiles, *refs):
    feature_refs, decode_refs, recon_refs = refs[:n_feature], refs[n_feature : n_feature + n_tiles], refs[n_feature + n_tiles :]
    feature = jnp.concatenate([ref[...] for ref in feature_refs], axis=1)
    for decode_ref, recon_ref in zip(decode_refs, recon_refs):
        recon_ref[...] = dot(feature, decode_ref[...])


def reconstruct(feature, decode, n_tiles):
    rows = feature[0].shape[0]
    width = decode.shape[0]
    block = pl.BlockSpec((rows // STEPS, TILE), lambda g: (g, 0))
    return call(
        functools.partial(recon_kernel, len(feature), n_tiles),
        [shape((rows, TILE), F32)] * n_tiles,
        limit=57,
        grid=(STEPS,),
        in_specs=[*[block] * len(feature), *[pl.BlockSpec((width, TILE), lambda g, j=j: (0, j)) for j in range(n_tiles)]],
        out_specs=[block] * n_tiles,
        name="reconstruct",
    )(*feature, *[decode] * n_tiles)


def own_index(h):
    per_half = STEPS // 2
    return lambda g, where: (jnp.clip(g - h * per_half, 0, per_half - 1), 0, 0)


def patch_operands(blocks, own_blocks, shared_blocks):
    args, specs = [], []
    for k in own_blocks:
        for h, half in enumerate(blocks[k]):
            dims = (half.shape[0] // 3,) + half.shape[1:]
            args.append(half)
            specs.append(pl.BlockSpec(dims, own_index(h)))
    for k in shared_blocks:
        for half in blocks[k]:
            dims = (half.shape[0] // 3,) + half.shape[1:]
            args.append(half)
            specs.append(pl.BlockSpec(dims, lambda g, where: (2, 0, 0)))
    return args, specs


def lay_target(g, where_ref, refs, target):
    if len(refs) == 1:
        target[...] = refs[0][...]
        return
    pairs = [refs[j : j + 2] for j in range(0, len(refs), 2)]
    own, shared = pairs[: len(pairs) // 2], pairs[len(pairs) // 2 :]
    per_half = STEPS // 2
    h, side = g // per_half, g % per_half
    lanes = lambda j: pl.ds(pl.multiple_of(where_ref[TILES + j] * LANES, LANES), LANES)
    for k, pair in enumerate(own):
        target[:, :, lanes(2 * k)] = pair[h][...]
    for k in range(0, len(shared), 2):
        mine, other = shared[k][h][...].astype(F32), shared[k + 1][h][...].astype(F32)
        lane = lax.broadcasted_iota(jnp.int32, mine.shape, 2)
        value = jnp.where((lane < 64) == ((where_ref[PARITY] == 0) == (side == 0)), mine, other)
        if side:
            value = jnp.concatenate([value[:, :, 64:], value[:, :, :64]], axis=2)
        target[:, :, lanes(2 * k + 1)] = value.astype(BF16)


def deal(where_ref, sums, part, keep_ref, send_ref):
    core = where_ref[CORE]
    at = 0
    for value in sums:
        height = value.shape[0]
        for z in range(keep_ref.shape[0]):
            even = value[:, 2 * z * part : (2 * z + 1) * part]
            odd = value[:, (2 * z + 1) * part : (2 * z + 2) * part]
            mine = jnp.where(core == 0, even, odd)
            other = jnp.where(core == 0, odd, even)
            keep_ref[z, at : at + height, :] = mine.astype(BF16)
            send_ref[z, at : at + height, :] = other.astype(BF16)
        at += height


def copies_of(sources, held, sems):
    size, wide = held.shape[0] // STEPS, sources[0].shape[1]
    return [
        [
            pltpu.make_async_copy(
                source.at[pl.ds(g * size, size)], held.at[pl.ds(g * size, size), pl.ds(j * wide, wide)], sems.at[g, j]
            )
            for j, source in enumerate(sources)
        ]
        for g in range(STEPS)
    ]


def by_step(copies, body):
    step = pl.program_id(0)
    for g in range(STEPS):

        @pl.when(step == g)
        def _():
            if g == 0:
                for h in range(STEPS):
                    for copy in copies[h]:
                        copy.start()
            for copy in copies[g]:
                copy.wait()
            body(g)


def contract(g, rows, pairs):
    unit = rows // STEPS // TILE * TILE
    span = slice(g * unit, rows if g == STEPS - 1 else (g + 1) * unit)
    for total, left, right in pairs:
        now = dot(left[span], right[span], ROWS_0)
        total[...] = now if g == 0 else total[...] + now


def residual_kernel(groups, scale, n_feature, n_tiles, n_patch, where_ref, *refs):
    feature_refs, refs = refs[:n_feature], refs[n_feature:]
    recon_refs, refs = refs[:n_tiles], refs[n_tiles:]
    patch_refs, refs = refs[:n_patch], refs[n_patch:]
    grad_refs, refs = refs[:n_tiles], refs[n_tiles:]
    keep_ref, send_ref, target, feature, grads, total, sems = refs
    rows, width = feature.shape
    size = grad_refs[0].shape[0]

    def body(g):
        here = slice(g * size, (g + 1) * size)
        lay_target(g, where_ref, patch_refs, target)
        for j, grad_ref in enumerate(grad_refs):
            cut = slice(j * TILE, (j + 1) * TILE)
            grad = ((recon_refs[j][...] - target[:, :, cut].reshape(size, TILE).astype(F32)) * scale).astype(BF16)
            grad_ref[...] = grad
            grads[here, cut] = grad
        contract(g, rows, [(total, grads, feature)])
        if g == STEPS - 1:
            deal(where_ref, [total], width // groups, keep_ref, send_ref)

    by_step(copies_of(feature_refs, feature, sems), body)


def residual(where, feature, recon, patch_args, patch_specs, images, scale, groups):
    rows = feature[0].shape[0]
    n_tiles = len(recon)
    width, n = len(feature) * TILE, n_tiles * TILE
    size = rows // STEPS
    parts = (groups // 2, n, width // groups)
    dealt = pl.BlockSpec(parts, lambda g, where: (0, 0, 0))
    block = pl.BlockSpec((size, TILE), lambda g, where: (g, 0))
    *grad, keep, send = call(
        functools.partial(residual_kernel, groups, scale, len(feature), n_tiles, len(patch_args)),
        [*[shape((rows, TILE), BF16)] * n_tiles, shape(parts, BF16), shape(parts, BF16)],
        limit=58,
        flops=2 * rows * width * n,
        moved=rows * (2 * width + 6 * n),
        grid_spec=pltpu.PrefetchScalarGridSpec(
            num_scalar_prefetch=1,
            grid=(STEPS,),
            in_specs=[
                *[HBM] * len(feature),
                *[block] * n_tiles,
                *patch_specs,
            ],
            out_specs=[*[block] * n_tiles, dealt, dealt],
            scratch_shapes=[
                pltpu.VMEM((size // images, images, n), BF16),
                pltpu.VMEM((rows, width), BF16),
                pltpu.VMEM((rows, n), BF16),
                pltpu.VMEM((n, width), F32),
                pltpu.SemaphoreType.DMA((STEPS, len(feature))),
            ],
        ),
        name="residual",
    )(where, *feature, *recon, *patch_args)
    return grad, keep, send


def backward_kernel(groups, n_grad, n_decode, where_ref, *refs):
    grad_refs, refs = refs[:n_grad], refs[n_grad:]
    decode_refs, refs = refs[:n_decode], refs[n_decode:]
    (hidden_ref, acts_ref, aux_grad_ref, aux_ref, second_ref, keep_ref, send_ref,
     hidden, acts, feature_grads, hidden_grads, pooled, total_second, total_first, sems) = refs
    rows, width = feature_grads.shape
    size = grad_refs[0].shape[0]
    images = aux_grad_ref.shape[0]
    pairs = [(total_second, hidden, feature_grads), (total_first, hidden_grads, acts)]

    def body(g):
        here = slice(g * size, (g + 1) * size)
        if g == 0:
            pooled[...] = dot(aux_grad_ref[...], aux_ref[...], COLS_1) / (rows // images)
        grad = jnp.concatenate([ref[...] for ref in grad_refs], axis=1)
        for j, decode_ref in enumerate(decode_refs):
            cut = slice(j * TILE, (j + 1) * TILE)
            back = dot(grad, decode_ref[...], COLS_1).reshape(size // images, images, TILE)
            feature_grads[here, cut] = (back + pooled[:, cut][None]).astype(BF16).reshape(size, TILE)
        hidden_back = dot(feature_grads[here], second_ref[...], COLS_1)
        hidden_grads[here] = jnp.where(hidden[here].astype(F32) > 0, hidden_back, 0.0).astype(BF16)
        contract(g, rows, pairs)
        if g == STEPS - 1:
            part = width // groups
            tall = total_second.shape[0] // groups
            second = jnp.concatenate(
                [
                    jnp.concatenate(
                        [total_second[d * tall : (d + 1) * tall, q * part : (q + 1) * part] for q in range(groups)], axis=0
                    )
                    for d in range(groups)
                ],
                axis=1,
            )
            deal(where_ref, [second, total_first], part, keep_ref, send_ref)

    copies = zip(copies_of([hidden_ref], hidden, sems.at[0]), copies_of([acts_ref], acts, sems.at[1]))
    by_step([one + other for one, other in copies], body)


def backward(where, grad, hidden, acts, decode, aux_grad, aux, second, groups):
    rows, width = acts.shape
    inner, n = hidden.shape[1], len(grad) * TILE
    n_decode = width // TILE
    row_block = lambda j: pl.BlockSpec((TILE, n), lambda g, where: (j, 0))
    size = rows // STEPS
    parts = (groups // 2, 2 * inner, width // groups)
    dealt = pl.BlockSpec(parts, lambda g, where: (0, 0, 0))
    whole = lambda array: pl.BlockSpec(array.shape, lambda g, where: (0, 0))
    return call(
        functools.partial(backward_kernel, groups, len(grad), n_decode),
        [shape(parts, BF16), shape(parts, BF16)],
        limit=44,
        flops=2 * rows * width * (n + 3 * inner),
        moved=2 * rows * (width + n + inner),
        grid_spec=pltpu.PrefetchScalarGridSpec(
            num_scalar_prefetch=1,
            grid=(STEPS,),
            in_specs=[
                *[pl.BlockSpec((size, TILE), lambda g, where: (g, 0))] * len(grad),
                *[row_block(j) for j in range(n_decode)],
                HBM,
                HBM,
                whole(aux_grad),
                whole(aux),
                whole(second),
            ],
            out_specs=[dealt, dealt],
            scratch_shapes=[
                pltpu.VMEM((rows, inner), BF16),
                pltpu.VMEM((rows, width), BF16),
                pltpu.VMEM((rows, width), BF16),
                pltpu.VMEM((rows, inner), BF16),
                pltpu.VMEM((aux_grad.shape[0], width), F32),
                pltpu.VMEM((inner, width), F32),
                pltpu.VMEM((inner, width), F32),
                pltpu.SemaphoreType.DMA((2, STEPS, 1)),
            ],
        ),
        name="backward",
    )(where, *grad, *[decode] * n_decode, hidden, acts, aux_grad, aux, second)


TOPS, DENOMS = 3, 19
DIGIT = 40


def to_digits(value):
    rest, lanes = value, []
    for _ in range(3):
        digit = rest.astype(BF16).astype(F32)
        lanes.append(digit[:, :DIGIT])
        rest = rest - digit
    lanes.append(jnp.zeros((value.shape[0], LANES - 3 * DIGIT), F32))
    return jnp.concatenate(lanes, axis=1).astype(BF16)


def from_digits(value):
    value = value.astype(F32)
    return sum(value[:, j * DIGIT : (j + 1) * DIGIT] for j in (2, 1, 0))


def labels_of(got, head):
    digits = got[:, head + LANES : head + LANES + 2].astype(F32)
    return (digits[:, 0:1] * LANES + digits[:, 1:2]).astype(jnp.int32)


def logits_kernel(where_ref, got_ref, klass_ref, sent_ref, logits_ref):
    groups, images, _ = got_ref.shape
    classes, head = klass_ref.shape
    got = got_ref[...].reshape(groups * images, -1)
    logits_ref[...] = dot(got[:, :head], klass_ref[...], COLS_1)
    logits = logits_ref[...]
    ids = lax.broadcasted_iota(jnp.int32, logits.shape, 1) + where_ref[ME] * classes
    hit = labels_of(got, head) == ids
    top = jnp.max(logits, axis=1, keepdims=True)
    expo = jnp.exp(logits - top)
    denom = jnp.sum(expo, axis=1, keepdims=True)
    own = jnp.sum(jnp.where(hit, expo, 0.0), axis=1, keepdims=True)
    rest = jnp.where(hit, 0.0, expo).astype(BF16)
    onehot = jnp.where(hit, 1.0, 0.0).astype(BF16)
    sent_ref[:, :, :head] = dot(rest, klass_ref[...]).astype(BF16).reshape(groups, images, head)
    sent_ref[:, :, head : 2 * head] = dot(onehot, klass_ref[...]).astype(BF16).reshape(groups, images, head)
    lane = lax.broadcasted_iota(jnp.int32, (images, LANES), 1)
    cut = lambda value, d: value[d * images : (d + 1) * images]
    common = jnp.zeros((images, LANES), F32)
    for d in range(groups):
        common = jnp.where(lane == TOPS + d, cut(top, d), common)
        common = jnp.where(lane == DENOMS + d, cut(denom, d), common)
    for d in range(groups):
        stats = jnp.where(lane == 1, cut(denom, d), jnp.where(lane == 2, cut(own, d), common))
        sent_ref[d, :, 2 * head :] = to_digits(jnp.where(lane == 0, cut(top, d), stats))


def class_logits(where, got, klass):
    groups, images, _ = got.shape
    classes, head = klass.shape
    return call(
        logits_kernel,
        shape((groups, images, 2 * head + LANES), BF16),
        limit=16,
        in_specs=[SMEM, VMEM, VMEM],
        scratch_shapes=[pltpu.VMEM((groups * images, classes), F32)],
        name="class_logits",
    )(where, got, klass)


def aux_kernel(norm, got_ref, aux_pre_ref, grad_ref, cut_ref):
    groups, images, _ = got_ref.shape
    head = aux_pre_ref.shape[1]
    stats = [from_digits(got_ref[d, :, 2 * head :]) for d in range(groups)]
    top = functools.reduce(jnp.maximum, [s[:, 0:1] for s in stats])
    scales = [jnp.exp(s[:, 0:1] - top) for s in stats]
    denom = sum(s[:, 1:2] * f for s, f in zip(stats, scales))
    own = sum(s[:, 2:3] * f for s, f in zip(stats, scales)) / denom
    rest = sum(got_ref[d, :, :head].astype(F32) * scales[d] for d in range(groups)) / (denom * norm)
    row = sum(got_ref[d, :, head : 2 * head].astype(F32) for d in range(groups))
    back = rest + row * ((own - 1.0) / norm).astype(BF16).astype(F32)
    aux_grad = jnp.where(aux_pre_ref[...] > 0, back, 0.0).astype(BF16)
    grad_ref[...] = aux_grad
    part = cut_ref.shape[1]
    for q in range(head // part):
        cut_ref[q * images : (q + 1) * images, :] = aux_grad[:, q * part : (q + 1) * part]


def aux_backward(got, aux_pre, part, norm):
    images, head = aux_pre.shape
    return call(
        functools.partial(aux_kernel, norm),
        [shape((images, head), BF16), shape((images * head // part, part), BF16)],
        limit=16,
        flops=2e10,
        name="aux_backward",
    )(got, aux_pre)


def class_kernel(norm, where_ref, klass_ref, got_ref, stats_ref, mine_ref, other_ref, class_ref, aux_ref):
    groups, images, _ = got_ref.shape
    head = class_ref.shape[1]
    classes, part = class_ref.shape[0], aux_ref.shape[0]
    got = got_ref[...].reshape(groups * images, -1)
    stats = [from_digits(stats_ref[e]) for e in range(groups)]
    tops, denoms = [], []
    for d in range(groups):
        top = functools.reduce(jnp.maximum, [s[:, TOPS + d : TOPS + d + 1] for s in stats])
        tops.append(top)
        denoms.append(sum(s[:, DENOMS + d : DENOMS + d + 1] * jnp.exp(s[:, TOPS + d : TOPS + d + 1] - top) for s in stats))
    top, denom = jnp.concatenate(tops, axis=0), jnp.concatenate(denoms, axis=0)
    logits = dot(got[:, :head], klass_ref[...], COLS_1)
    ids = lax.broadcasted_iota(jnp.int32, logits.shape, 1) + where_ref[ME] * classes
    onehot = jnp.where(labels_of(got, head) == ids, 1.0, 0.0)
    logit_grad = ((jnp.exp(logits - top) / denom - onehot) / norm).astype(BF16)
    class_ref[...] = dot(logit_grad, got[:, :head], ROWS_0)
    total = jnp.zeros(aux_ref.shape, F32)
    for d in range(groups):
        k, ref = d // 2, other_ref if d % 2 else mine_ref
        grad = jnp.concatenate([ref[k, q * images : (q + 1) * images] for q in range(head // part)], axis=1)
        pooled = got_ref[where_ref[ME] ^ d, :, head : head + part]
        total += dot(pooled, grad, ROWS_0).astype(BF16).astype(F32)
    aux_ref[...] = total


def class_backward(where, klass, got, partial, mine, other, norm):
    groups, images, wide = partial.shape
    classes, head = klass.shape
    whole = lambda *dims: pl.BlockSpec(dims, lambda i: (0,) * len(dims))
    part = mine.shape[2]
    return call(
        functools.partial(class_kernel, norm),
        [shape((classes, head), F32), shape((part, head), F32)],
        limit=20,
        flops=2 * groups * images * classes * head,
        moved=4 * classes * head,
        grid=(1,),
        in_specs=[
            SMEM,
            whole(*klass.shape),
            whole(*got.shape),
            pl.BlockSpec((groups, images, LANES), lambda i: (0, 0, wide // LANES - 1)),
            whole(*mine.shape),
            whole(*other.shape),
        ],
        out_specs=[whole(classes, head), whole(part, head)],
        name="class_backward",
    )(where, klass, got, partial, mine, other)


def chip_kernel(chips, below, collect, where_ref, keep_ref, got_ref, *refs):
    refs, outs = refs[: below + collect], refs[below + collect :]
    n = keep_ref.shape[1]
    chip = where_ref[ME] >> 1
    for k in range(chips):
        outs[k][:n] = (keep_ref[chip ^ k].astype(F32) + got_ref[chip ^ k].astype(F32)).astype(BF16)
        for ref in refs[:below]:
            outs[k][n:] = ref[...]
    if collect:
        size = outs[-1].shape[1]
        for k, ref in enumerate(refs[below:]):
            outs[-1][k] = ref[ref.shape[0] - size :]


def add_cores(where, keep, send, below=(), collect=(), size=0):
    chips, n, part = keep.shape
    rows = n + sum(e.shape[0] for e in below)
    outs = [shape((rows, part), BF16)] * chips
    if collect:
        outs.append(shape((len(collect), size, part), BF16))
    outs = call(
        functools.partial(chip_kernel, chips, len(below), len(collect)),
        outs,
        limit=16,
        in_specs=[SMEM, VMEM, VMEM, *[VMEM] * (len(below) + len(collect))],
        name="add_cores",
    )(where, keep, swap(send, "dp", 1), *below, *collect)
    return (outs[:chips], outs[chips]) if collect else outs


def exchange_chips(parts):
    return [parts[0]] + [swap(part, "dp", 2 * k) for k, part in enumerate(parts) if k]


def finish_kernel(inner, chips, *refs):
    early, last, (first_ref, second_ref, decode_ref) = refs[:chips], refs[chips : 2 * chips], refs[2 * chips :]
    n = decode_ref.shape[1]
    total = sum(ref[...].astype(F32) for ref in last)
    first_ref[...] = total[inner:].T
    tall, part = second_ref.shape[0], total.shape[1]
    for q in range(inner // tall):
        second_ref[:, q * part : (q + 1) * part] = total[q * tall : (q + 1) * tall]
    decode_ref[...] = sum(ref[:n].astype(F32) for ref in early).T


def finish(early, last, inner, groups, n):
    part = early[0].shape[1]
    return call(
        functools.partial(finish_kernel, inner, len(early)),
        [shape((part, inner), F32), shape((inner // groups, part * groups), F32), shape((part, n), F32)],
        limit=16,
        name="finish",
    )(*early, *last)


def local(acts, patches, labels, w_first, w_second, w_decode, w_aux, w_class):
    acts = acts[0].transpose(1, 0, 2)
    pix, images, width = acts.shape
    groups, count = lax.axis_size("dp"), lax.axis_size("section")
    me, section = lax.axis_index("dp"), lax.axis_index("section")
    scale = (groups * images * pix) ** -0.5
    norm = (groups * images) ** 0.5
    first, second, decode, aux, klass = w_first[0], w_second[0], w_decode[0], w_aux[0], w_class[0]
    inner = first.shape[1]
    n_decode = decode.shape[1]
    rows = pix * images

    paired = count == 4 and patches.shape[2] == 192
    if paired:
        near = [section ^ k for k in range(4)]
        tiles = [t for s in near for t in (3 * (s >> 1) + 2 * (s & 1), 3 * (s >> 1) + 1)]
        where = jnp.stack([section & 1, me & 1, me, *tiles]).astype(jnp.int32)
        turned = patches.transpose(0, 2, 1)
        halves = [pack(where, turned, h) for h in range(2)]
        x, y = [swap(halves[0], "section", 1)], [swap(halves[1], "section", 2)]
        first = after(first, halves[1])
    else:
        where = jnp.stack([section & 1, me & 1, me]).astype(jnp.int32)
        target = lax.all_gather(patches, "section", axis=2, tiled=True).transpose(1, 0, 2)

    hidden, feature, aux_pre, sent = forward(acts, first, second, aux, labels, groups)
    if paired:
        sent = after(sent, x[0])
        diagonal = [swap(after(x[0], aux_pre), "section", 2), swap(after(y[0], aux_pre), "section", 1)]
        x.append(swap(halves[1], "section", 1))
        y.insert(0, swap(halves[0], "section", 2))
        target = patch_operands([halves, x, y, diagonal], [0, 1, 2, 3], [0, 1, 2, 3])
    else:
        target = [target], [pl.BlockSpec((pix // STEPS, images, n_decode), lambda g, where: (g, 0, 0))]
    got = exchange(sent)
    recon = reconstruct([after(feature[0], sent), *feature[1:]], decode, n_decode // TILE)
    sent = class_logits(where, after(got, recon[0]), klass)
    partial = exchange(sent)
    grad, keep, send = residual(after(where, sent), feature, recon, *target, images, scale, groups)
    aux_grad, aux_cut = aux_backward(partial, aux_pre, width // groups, norm)
    chip_decode = add_cores(where, keep, send, [aux_cut])
    sum_decode = exchange_chips(chip_decode)
    keep, send = backward(
        where, grad, hidden, acts.reshape(rows, width), decode, after(aux_grad, chip_decode[0]), aux, second, groups
    )
    chip_last, mine = add_cores(where, keep, after(send, sum_decode), collect=sum_decode, size=aux_cut.shape[0])
    sum_last = exchange_chips(chip_last)
    grad_class, grad_aux = class_backward(where, klass, got, partial, mine, swap(mine, "dp", 1), norm)
    grad_first, grad_second, grad_decode = finish(sum_decode, sum_last, inner, groups, n_decode)
    return grad_first[None], grad_second[None], grad_decode[None], grad_aux[None], grad_class[None]


def solution(mesh):
    in_specs = (
        P("section", "dp", None, None),
        P("dp", None, "section"),
        P("dp"),
        P("section", None, None),
        P("section", None, None),
        P("section", None, None),
        P("section", None, None),
        P("section", "dp", None),
    )
    out_specs = (P("section", "dp", None),) * 5
    return jax.shard_map(local, mesh=mesh, in_specs=in_specs, out_specs=out_specs, check_vma=False)
```
